32 devices in a mesh: dp: 8 (over y, x, core), tensor: 4 (over z).
Axes of the slice: x: 2, y: 2, z: 4, core: 2. Of those that a mesh axis runs over, the one named last changes fastest.
Arguments:
- tokens: bfloat16 [16384, 512], P(('dp', 'tensor')), may hold values from -6 to 6
- memory: bfloat16 [16384, 512], P(('dp', 'tensor')), may hold values from -6 to 6
- cotangent: bfloat16 [16384, 512], P(('dp', 'tensor')), may hold values from -6 to 6
- tgt_lengths: int32 [16, 8], P('dp'), may hold values from 1 to 512, 1024 in all within a row
- mem_lengths: int32 [16, 8], P('dp'), may hold values from 1 to 512, 1024 in all within a row
- mem_keep: int32 [16, 1024], P('dp'), may hold values 0 or 1
- row_expert: int32 [16], P('dp'), may hold values from 0 to 15
- attn_weights: float32 [2, 4, 512, 512], P(None, None, 'dp', 'tensor')
- attn_moment: float32 [2, 4, 512, 512], P(None, None, 'dp', 'tensor')
- attn_second: float32 [2, 4, 512, 512], P(None, None, 'dp', 'tensor'), as said below
- expert_weights: float32 [16, 2, 512, 2048], P(None, None, 'dp', 'tensor')
- expert_moment: float32 [16, 2, 512, 2048], P(None, None, 'dp', 'tensor')
- expert_second: float32 [16, 2, 512, 2048], P(None, None, 'dp', 'tensor'), as said below
- norm_params: float32 [6, 512], P(None, 'dp'), as said below
- norm_moment: float32 [6, 512], P(None, 'dp')
- norm_second: float32 [6, 512], P(None, 'dp'), as said below
Outputs:
- layer_out: bfloat16 [16384, 512], P(('dp', 'tensor'))
- input_grad: bfloat16 [16384, 512], P(('dp', 'tensor'))
- memory_grad: bfloat16 [16384, 512], P(('dp', 'tensor'))
- attn_new: float32 [2, 4, 512, 512], P(None, None, 'dp', 'tensor')
- attn_moment_new: float32 [2, 4, 512, 512], P(None, None, 'dp', 'tensor')
- attn_second_new: float32 [2, 4, 512, 512], P(None, None, 'dp', 'tensor')
- expert_new: float32 [16, 2, 512, 2048], P(None, None, 'dp', 'tensor')
- expert_moment_new: float32 [16, 2, 512, 2048], P(None, None, 'dp', 'tensor')
- expert_second_new: float32 [16, 2, 512, 2048], P(None, None, 'dp', 'tensor')
- norm_new: float32 [6, 512], P(None, 'dp')
- norm_moment_new: float32 [6, 512], P(None, 'dp')
- norm_second_new: float32 [6, 512], P(None, 'dp')
- lamb_norms: float32 [2, 46], replicated
The draws below stay inside these ranges and needn't reach their ends.
Inputs may be any that keep to these rules, and one draw needn't show every extreme that they name: `attn_second`: second moments are positive. `expert_second`: second moments are positive. `norm_second`: second moments are positive. `norm_params`: rows 0, 2, 4 are gains near 1, rows 1, 3, 5 shifts.
All inputs are finite; a program needn't handle non-finite values. No bound on the sum of `mem_keep` on one device may be relied on, other than what follows from the above.
Results may differ from the reference program's by a relative error of at most 0.017.
The reference program's roundings to bfloat16 on the way count: a program that leaves them out, or rounds other values in their place, can miss the bound.
Values may be sent and summed in bfloat16 or wider, within the bound.
No kernel may reach another device: no remote copies, remote signals or barrier semaphores. Data moves between devices by JAX's collectives and lax.ppermute only.
A program may use at most 256 MiB of HBM per device.

```python
import math
import jax
import jax.numpy as jnp
import numpy as np
from jax import lax

D = 512
H = 8
HD = 64
FF = 2048
E = 16
LEN = 1024
MLEN = 1024
DOCS = 8
STEP = 10
ROWS = 16
TOKENS = 16384
MTOKENS = 16384


def attn_scale():
    return 0.3 * TOKENS ** 0.5


def expert_scale():
    return 0.4 * (TOKENS / E) ** 0.5


def norm_scale():
    return TOKENS ** 0.5


def rising(count, steep):
    places = jnp.arange(count, dtype=jnp.float32) / max(count - 1, 1)
    return jnp.sqrt((1.0 + steep * places) / (1.0 + 0.5 * steep))


def plane_profile(rows, cols, steep):
    return rising(rows, steep).reshape(1, 1, rows, 1) * rising(cols, steep).reshape(1, 1, 1, cols)


def draw_attn_weights(key, part):
    key = jax.random.fold_in(key, 11)
    shape = (2, 4, D, D)
    base = jnp.clip(jax.random.normal(key, shape, jnp.float32), -4.0, 4.0) * plane_profile(D, D, 2.0)
    slots = jnp.array([1.0, 1.0, 1.0, 4.0], jnp.float32).reshape(1, 4, 1, 1)
    return base * slots * D ** (-0.5)


def draw_expert_weights(key, part):
    key = jax.random.fold_in(key, 12)
    shape = (E, 2, D, FF)
    base = jnp.clip(jax.random.normal(key, shape, jnp.float32), -4.0, 4.0) * plane_profile(D, FF, 2.0)
    slots = jnp.array([D ** (-0.5), 1.5 * FF ** (-0.5)], jnp.float32).reshape(1, 2, 1, 1)
    return base * slots


def draw_norm_params(key, part):
    key = jax.random.fold_in(key, 13)
    shape = (6, D)
    base = jnp.clip(jax.random.normal(key, shape, jnp.float32), -3.0, 3.0)
    spread = jnp.array([0.15, 0.5, 0.15, 0.5, 0.15, 0.5], jnp.float32).reshape(6, 1)
    offset = jnp.array([1.0, 0.0, 1.0, 0.0, 1.0, 0.0], jnp.float32).reshape(6, 1)
    return offset + spread * base


def draw_attn_moment(key, part):
    key = jax.random.fold_in(key, 21)
    shape = (2, 4, D, D)
    base = jnp.clip(jax.random.normal(key, shape, jnp.float32), -4.0, 4.0) * plane_profile(D, D, 2.0)
    return 0.11 * attn_scale() * base


def draw_expert_moment(key, part):
    key = jax.random.fold_in(key, 22)
    shape = (E, 2, D, FF)
    base = jnp.clip(jax.random.normal(key, shape, jnp.float32), -4.0, 4.0) * plane_profile(D, FF, 2.0)
    return 0.11 * expert_scale() * base


def draw_norm_moment(key, part):
    key = jax.random.fold_in(key, 23)
    shape = (6, D)
    base = jnp.clip(jax.random.normal(key, shape, jnp.float32), -4.0, 4.0)
    return 0.11 * norm_scale() * base


def draw_attn_second(key, part):
    key = jax.random.fold_in(key, 31)
    shape = (2, 4, D, D)
    factor = jnp.exp(jax.random.uniform(key, shape, jnp.float32, -0.6931472, 2.0794415))
    return 0.001 / 0.999 * attn_scale() ** 2 * factor


def draw_expert_second(key, part):
    key = jax.random.fold_in(key, 32)
    shape = (E, 2, D, FF)
    factor = jnp.exp(jax.random.uniform(key, shape, jnp.float32, -0.6931472, 2.0794415))
    return 0.001 / 0.999 * expert_scale() ** 2 * factor


def draw_norm_second(key, part):
    key = jax.random.fold_in(key, 33)
    shape = (6, D)
    factor = jnp.exp(jax.random.uniform(key, shape, jnp.float32, -0.6931472, 2.0794415))
    return 0.001 / 0.999 * norm_scale() ** 2 * factor


def touch_ends(values, own_key, smallest, largest):
    spot = [jax.random.randint(jax.random.fold_in(own_key, axis), (), 0, length) for axis, length in enumerate(values.shape)]
    longest = values.shape.index(max(values.shape))
    beside = spot[:longest] + [(spot[longest] + 1) % values.shape[longest]] + spot[longest + 1:]
    return values.at[tuple(spot)].set(smallest).at[tuple(beside)].set(largest)


def steps_of(rng, shape, shards, smallest, high):
    def one(axis_at, shards_of):
        draws = jax.random.uniform(jax.random.fold_in(jax.random.fold_in(rng, 6), axis_at), (shards_of,), jnp.float32, smallest / len(shards), high / len(shards))
        return jnp.repeat(jnp.exp(draws), shape[axis_at] // shards_of).reshape((-1,) + (1,) * (len(shape) - axis_at - 1))

    level = one(*shards[0])
    for cut in shards[1:]:
        level = level * one(*cut)
    return level


def profile(count, total, most, lean):
    loads = [(1 << 20) // math.isqrt(grade ** lean) + 1 for grade in range(2, count + 1)]
    rest, holding = total - most - (count - 1), [1] * (count - 1)
    while rest > 0:
        free = [i for i in range(count - 1) if holding[i] < most]
        whole, budget = sum([loads[i] for i in free]), rest
        for i in free:
            more = min(most - holding[i], max(1, budget * loads[i] // whole), rest)
            holding[i] = holding[i] + more
            rest = rest - more
    return np.array([most] + holding)


def ragged_sizes(key, count, total, bound, lean):
    if count == 2:
        one = jax.random.randint(key, (), max(1, total - bound), min(bound, total - 1) + 1)
        return jnp.stack([one, total - one])
    sizes = jnp.asarray(profile(count, total, bound, lean), jnp.int32)
    twos = (count - 1) // 2
    giver, receiver = sizes[1:1 + 2 * twos:2], sizes[2:2 + 2 * twos:2]
    margin = jnp.minimum(giver - 1, bound - receiver)
    moved = jax.random.randint(jax.random.fold_in(key, 1), (twos,), 0, 1 << 20) % (margin + 1)
    sizes = sizes.at[1:1 + 2 * twos:2].set(giver - moved).at[2:2 + 2 * twos:2].set(receiver + moved)
    return sizes[jax.random.permutation(jax.random.fold_in(key, 2), count)]


def bell_draw(rng, dims, width, limit, shards=(), held_as=jnp.bfloat16):
    loudness = steps_of(rng, dims, shards, -0.22, 0.18) if shards else 1.0
    values = jax.random.normal(rng, dims, jnp.float32) * width * loudness
    return jnp.minimum(jnp.maximum(values, -limit), limit).astype(held_as)


def setup_inputs(seed: int = 0) -> dict:
    key_of = jax.random.split(jax.random.key(seed), 17)
    tokens = bell_draw(key_of[0], (TOKENS, D), 1.0, 6.0, ((0, 32),))
    memory = bell_draw(key_of[1], (MTOKENS, D), 1.0, 6.0, ((0, 32),))
    cotangent = bell_draw(key_of[2], (TOKENS, D), 1.0, 6.0, ((0, 32),))
    tgt_lengths = jax.vmap(lambda own: ragged_sizes(own, DOCS, LEN, LEN // 2, 1))(jax.random.split(key_of[3], ROWS)).reshape((ROWS, DOCS)).astype(jnp.int32)
    mem_lengths = jax.vmap(lambda own: ragged_sizes(own, DOCS, MLEN, MLEN // 2, 1))(jax.random.split(key_of[4], ROWS)).reshape((ROWS, DOCS)).astype(jnp.int32)
    mem_keep = touch_ends((jax.random.randint(key_of[5], (ROWS, MLEN), 0, 2) < 1).astype(jnp.int32), jax.random.fold_in(key_of[5], 1), 0, 1)
    row_expert = touch_ends(jax.random.randint(key_of[6], (ROWS,), 0, E), jax.random.fold_in(key_of[6], 1), 0, E - 1).astype(jnp.int32)
    attn_weights = draw_attn_weights(jax.random.fold_in(key_of[16], 71), 0)
    attn_moment = draw_attn_moment(jax.random.fold_in(key_of[16], 71), 0)
    attn_second = draw_attn_second(jax.random.fold_in(key_of[16], 71), 0)
    expert_weights = draw_expert_weights(jax.random.fold_in(key_of[16], 71), 0)
    expert_moment = draw_expert_moment(jax.random.fold_in(key_of[16], 71), 0)
    expert_second = draw_expert_second(jax.random.fold_in(key_of[16], 71), 0)
    norm_params = draw_norm_params(jax.random.fold_in(key_of[16], 71), 0)
    norm_moment = draw_norm_moment(jax.random.fold_in(key_of[16], 71), 0)
    norm_second = draw_norm_second(jax.random.fold_in(key_of[16], 71), 0)
    return {"tokens": tokens, "memory": memory, "cotangent": cotangent, "tgt_lengths": tgt_lengths, "mem_lengths": mem_lengths, "mem_keep": mem_keep, "row_expert": row_expert, "attn_weights": attn_weights, "attn_moment": attn_moment, "attn_second": attn_second, "expert_weights": expert_weights, "expert_moment": expert_moment, "expert_second": expert_second, "norm_params": norm_params, "norm_moment": norm_moment, "norm_second": norm_second}


@jax.custom_vjp
def low(v):
    return lax.optimization_barrier(v.astype(jnp.bfloat16)).astype(jnp.float32)

@jax.custom_vjp
def low_back(v):
    return v

def low_keep(v):
    return (low(v), None)

def low_pass(kept, grad):
    return (grad,)

def back_keep(v):
    return (v, None)

def back_low(kept, grad):
    return (low(grad),)
low.defvjp(low_keep, low_pass)
low_back.defvjp(back_keep, back_low)
highest = lax.Precision.HIGHEST
beta_one = 0.9
beta_two = 0.999
epsilon = 1e-06
decay = 0.01
rate = 0.2

def matmul(left_side, right_side):
    return jnp.dot(left_side, right_side, precision=highest, preferred_element_type=jnp.float32)

def norm_layer(values, gain_vec, shift_vec):
    centered = values - lax.optimization_barrier(jnp.mean(values, -1, keepdims=True))
    variance = lax.optimization_barrier(jnp.mean(centered * centered, -1, keepdims=True))
    return centered * lax.rsqrt(variance + 1e-05) * gain_vec + shift_vec

def doc_numbers(lengths, length_total):
    doc_ends = jnp.cumsum(lengths).astype(jnp.int32)
    places = jnp.arange(length_total, dtype=jnp.int32)
    numbers = lax.optimization_barrier(jnp.sum((places[:, None] >= doc_ends[None, :]).astype(jnp.int32), 1)).astype(jnp.int32)
    starts = (doc_ends - lengths).astype(jnp.int32)
    opening = jnp.any(places[:, None] == starts[None, :], 1)
    return (numbers, opening)

def attention(queries, key_rows, value_rows, allowed):
    query_count = queries.shape[0]
    heads_q = queries.reshape(query_count, H, HD)
    heads_k = key_rows.reshape(key_rows.shape[0], H, HD)
    heads_v = value_rows.reshape(value_rows.shape[0], H, HD)
    scores = jnp.einsum('qhd,khd->hqk', heads_q, heads_k, precision=highest) * HD ** (-0.5)
    scores = low_back(scores)
    scores = jnp.where(allowed[None], scores, -1e+30)
    prob_low = low(jax.nn.softmax(scores, -1))
    blended = jnp.einsum('hqk,khd->qhd', prob_low, heads_v, precision=highest)
    return low_back(low(blended.reshape(query_count, H * HD)))

def layer_row(attn_low, expert_low, norms, row_data):
    tokens_row, memory_row, tgt_len, mem_len, keep_row, expert = row_data
    doc_ids, _ = doc_numbers(tgt_len, LEN)
    mem_docs, opening = doc_numbers(mem_len, MLEN)
    places = jnp.arange(LEN, dtype=jnp.int32)
    self_allowed = (doc_ids[:, None] == doc_ids[None, :]) & (places[None, :] <= places[:, None])
    cross_allowed = (doc_ids[:, None] == mem_docs[None, :]) & ((keep_row == 1) | opening)[None, :]
    normed = low(norm_layer(tokens_row, norms[0], norms[1]))
    queries = low_back(low(matmul(normed, attn_low[0, 0])))
    key_rows = low_back(low(matmul(normed, attn_low[0, 1])))
    value_rows = low_back(low(matmul(normed, attn_low[0, 2])))
    blended = attention(queries, key_rows, value_rows, self_allowed)
    first_sum = tokens_row + low_back(matmul(blended, attn_low[0, 3].T))
    normed = low(norm_layer(first_sum, norms[2], norms[3]))
    queries = low_back(low(matmul(normed, attn_low[1, 0])))
    key_rows = low_back(low(matmul(memory_row, attn_low[1, 1])))
    value_rows = low_back(low(matmul(memory_row, attn_low[1, 2])))
    blended = attention(queries, key_rows, value_rows, cross_allowed)
    second_sum = first_sum + low_back(matmul(blended, attn_low[1, 3].T))
    normed = low(norm_layer(second_sum, norms[4], norms[5]))
    chosen = expert_low[expert]
    inner_act = low_back(matmul(normed, chosen[0]))
    hidden = low(jax.nn.gelu(inner_act))
    return second_sum + low_back(matmul(hidden, chosen[1].T))

def forward(tokens, memory, attn_weights, expert_weights, norm_params, tgt_lengths, mem_lengths, mem_keep, row_expert):
    attn_low = low(attn_weights)
    expert_low = low(expert_weights)
    row_inputs = (tokens.reshape(ROWS, LEN, D), memory.reshape(ROWS, MLEN, D), tgt_lengths, mem_lengths, mem_keep, row_expert)

    @jax.checkpoint
    def row_step(carried, row_data):
        return (carried, layer_row(attn_low, expert_low, norm_params, row_data))
    _, results = lax.scan(row_step, jnp.zeros((), jnp.float32), row_inputs)
    return results.reshape(TOKENS, D)

def lamb(weight, moment, second, grad, axes):
    moment = beta_one * moment + (1.0 - beta_one) * grad
    second = beta_two * second + (1.0 - beta_two) * grad * grad
    update = moment / (1.0 - beta_one ** STEP) / (jnp.sqrt(second / (1.0 - beta_two ** STEP)) + epsilon) + decay * weight
    weight_norm = jnp.sqrt(lax.optimization_barrier(jnp.sum(weight * weight, axes, keepdims=True)))
    update_norm = jnp.sqrt(lax.optimization_barrier(jnp.sum(update * update, axes, keepdims=True)))
    fresh_weight = weight - rate * (weight_norm / update_norm) * update
    return (fresh_weight, moment, second, weight_norm.reshape(-1), update_norm.reshape(-1))

def reference(tokens, memory, cotangent, tgt_lengths, mem_lengths, mem_keep, row_expert, attn_weights, attn_moment, attn_second, expert_weights, expert_moment, expert_second, norm_params, norm_moment, norm_second):

    def layer_fn(tokens_f, memory_f, attn_f, expert_f, norms_f):
        return forward(tokens_f, memory_f, attn_f, expert_f, norms_f, tgt_lengths, mem_lengths, mem_keep, row_expert)
    result, pullback = jax.vjp(layer_fn, tokens.astype(jnp.float32), memory.astype(jnp.float32), attn_weights, expert_weights, norm_params)
    grad_tokens, grad_memory, grad_attn, grad_expert, grad_norms = pullback(cotangent.astype(jnp.float32))
    attn_new, attn_first, attn_sec, attn_wn, attn_un = lamb(attn_weights, attn_moment, attn_second, grad_attn, (2, 3))
    expert_new, expert_first, expert_sec, expert_wn, expert_un = lamb(expert_weights, expert_moment, expert_second, grad_expert, (2, 3))
    norm_new, norm_first, norm_sec, norm_wn, norm_un = lamb(norm_params, norm_moment, norm_second, grad_norms, (1,))
    lamb_norms = jnp.stack([jnp.concatenate([attn_wn, expert_wn, norm_wn]), jnp.concatenate([attn_un, expert_un, norm_un])])
    return (result.astype(jnp.bfloat16), grad_tokens.astype(jnp.bfloat16), grad_memory.astype(jnp.bfloat16), attn_new, attn_first, attn_sec, expert_new, expert_first, expert_sec, norm_new, norm_first, norm_sec, lamb_norms)
```

```python
import jax
import jax.numpy as jnp
from jax import lax
from jax.sharding import Mesh
from jax.sharding import PartitionSpec as P

D = 512
HD = 64
E = 16
LEN = 1024
MLEN = 1024
STEP = 10


beta_one = 0.9
beta_two = 0.999
epsilon = 1e-06
decay = 0.01
rate = 0.2


def norm_layer(values, gain_vec, shift_vec):
    centered = values - jnp.mean(values, -1, keepdims=True)
    variance = jnp.mean(centered * centered, -1, keepdims=True)
    return centered * lax.rsqrt(variance + 1e-05) * gain_vec + shift_vec


def doc_numbers(lengths, length_total):
    doc_ends = jnp.cumsum(lengths)
    places = jnp.arange(length_total, dtype=jnp.int32)
    numbers = jnp.sum((places[:, None] >= doc_ends[None, :]).astype(jnp.int32), 1)
    starts = doc_ends - lengths
    opening = jnp.any(places[:, None] == starts[None, :], 1)
    return (numbers, opening)


def build_allowed(tgt_len, mem_len, keep_row, cross):
    doc_ids, _ = doc_numbers(tgt_len, LEN)
    if cross:
        mem_docs, opening = doc_numbers(mem_len, MLEN)
        return (doc_ids[:, None] == mem_docs[None, :]) & ((keep_row == 1) | opening)[None, :]
    places = jnp.arange(LEN, dtype=jnp.int32)
    return (doc_ids[:, None] == doc_ids[None, :]) & (places[None, :] <= places[:, None])


def gather_rows(values):
    return lax.all_gather(values, "tensor", axis=0, tiled=True)


def spread_rows(values):
    return lax.psum_scatter(values, "tensor", scatter_dimension=0, tiled=True)


def project(left_side, right_side):
    return jnp.dot(left_side, right_side, preferred_element_type=jnp.float32)


def project_back(left_side, right_side):
    return lax.dot_general(
        left_side, right_side, (((1,), (1,)), ((), ())), preferred_element_type=jnp.float32
    )


def outer_grad(left_side, right_side):
    return lax.dot_general(
        left_side, right_side, (((0,), (0,)), ((), ())), preferred_element_type=jnp.float32
    )


def attend_one(queries, key_rows, value_rows, allowed):
    head_count = queries.shape[1] // HD
    keys_h = key_rows.reshape(key_rows.shape[0], head_count, HD)
    values_h = value_rows.reshape(value_rows.shape[0], head_count, HD)
    block_rows = min(LEN, 512)
    outputs = []
    totals = []
    for begin_at in range(0, LEN, block_rows):
        queries_h = queries[begin_at : begin_at + block_rows].reshape(block_rows, head_count, HD)
        scores = jnp.einsum(
            "qhd,khd->hqk", queries_h, keys_h, preferred_element_type=jnp.float32
        ) * HD ** (-0.5)
        scores = jnp.where(allowed[None, begin_at : begin_at + block_rows], scores, -1e30)
        top_score = jnp.max(scores, -1, keepdims=True)
        weights = jnp.exp(scores - top_score)
        row_total = jnp.sum(weights, -1, keepdims=True)
        prob_low = (weights / row_total).astype(jnp.bfloat16)
        blended = jnp.einsum("hqk,khd->qhd", prob_low, values_h, preferred_element_type=jnp.float32)
        outputs.append(blended.reshape(block_rows, head_count * HD))
        totals.append((top_score + jnp.log(row_total))[..., 0])
    return (jnp.concatenate(outputs, 0), jnp.concatenate(totals, 1))


def attend_back_one(queries, key_rows, value_rows, upstream, log_totals, allowed):
    head_count = queries.shape[1] // HD
    scale = HD ** (-0.5)
    keys_h = key_rows.reshape(key_rows.shape[0], head_count, HD)
    values_h = value_rows.reshape(value_rows.shape[0], head_count, HD)
    key_grad = jnp.zeros(keys_h.shape, jnp.float32)
    value_grad = jnp.zeros(values_h.shape, jnp.float32)
    block_rows = min(LEN, 512)
    query_grads = []
    for begin_at in range(0, LEN, block_rows):
        queries_h = queries[begin_at : begin_at + block_rows].reshape(block_rows, head_count, HD)
        upstream_h = upstream[begin_at : begin_at + block_rows].reshape(block_rows, head_count, HD)
        scores = (
            jnp.einsum("qhd,khd->hqk", queries_h, keys_h, preferred_element_type=jnp.float32)
            * scale
        )
        scores = jnp.where(allowed[None, begin_at : begin_at + block_rows], scores, -1e30)
        probs_full = jnp.exp(scores - log_totals[:, begin_at : begin_at + block_rows, None])
        prob_grad = jnp.einsum(
            "qhd,khd->hqk", upstream_h, values_h, preferred_element_type=jnp.float32
        )
        weighted = jnp.sum(probs_full * prob_grad, -1, keepdims=True)
        score_grad = (probs_full * (prob_grad - weighted)).astype(jnp.bfloat16)
        query_part = (
            jnp.einsum("hqk,khd->qhd", score_grad, keys_h, preferred_element_type=jnp.float32)
            * scale
        )
        query_grads.append(query_part.astype(jnp.bfloat16).reshape(block_rows, head_count * HD))
        key_grad = (
            key_grad
            + jnp.einsum("hqk,qhd->khd", score_grad, queries_h, preferred_element_type=jnp.float32)
            * scale
        )
        value_grad = value_grad + jnp.einsum(
            "hqk,qhd->khd",
            probs_full.astype(jnp.bfloat16),
            upstream_h,
            preferred_element_type=jnp.float32,
        )
    width = head_count * HD
    return (
        jnp.concatenate(query_grads, 0),
        key_grad.astype(jnp.bfloat16).reshape(-1, width),
        value_grad.astype(jnp.bfloat16).reshape(-1, width),
    )


def attend_rows(queries, key_rows, value_rows, tgt_lengths, mem_lengths, mem_keep, cross):
    row_count = tgt_lengths.shape[0]
    width = queries.shape[1]

    def one_row(row_item):
        row_q, row_k, row_v, tgt_len, mem_len, keep_row = row_item
        return attend_one(row_q, row_k, row_v, build_allowed(tgt_len, mem_len, keep_row, cross))

    blended, log_totals = lax.map(
        one_row,
        (
            queries.reshape(row_count, LEN, width),
            key_rows.reshape(row_count, -1, width),
            value_rows.reshape(row_count, -1, width),
            tgt_lengths,
            mem_lengths,
            mem_keep,
        ),
    )
    return (blended.reshape(row_count * LEN, width), log_totals)


def attend_back_rows(
    queries, key_rows, value_rows, upstream, log_totals, tgt_lengths, mem_lengths, mem_keep, cross
):
    row_count = tgt_lengths.shape[0]
    width = queries.shape[1]

    def one_row(row_item):
        row_q, row_k, row_v, row_up, row_log, tgt_len, mem_len, keep_row = row_item
        return attend_back_one(
            row_q, row_k, row_v, row_up, row_log, build_allowed(tgt_len, mem_len, keep_row, cross)
        )

    query_grad, key_grad, value_grad = lax.map(
        one_row,
        (
            queries.reshape(row_count, LEN, width),
            key_rows.reshape(row_count, -1, width),
            value_rows.reshape(row_count, -1, width),
            upstream.reshape(row_count, LEN, width),
            log_totals,
            tgt_lengths,
            mem_lengths,
            mem_keep,
        ),
    )
    return (
        query_grad.reshape(-1, width),
        key_grad.reshape(-1, width),
        value_grad.reshape(-1, width),
    )


def lamb_pieces(weight, moment, second, grad, axes):
    moment = beta_one * moment + (1.0 - beta_one) * grad
    second = beta_two * second + (1.0 - beta_two) * grad * grad
    update = (
        moment / (1.0 - beta_one**STEP) / (jnp.sqrt(second / (1.0 - beta_two**STEP)) + epsilon)
        + decay * weight
    )
    return (moment, second, update, jnp.sum(weight * weight, axes), jnp.sum(update * update, axes))


def body(
    tokens,
    memory,
    cotangent,
    tgt_lengths,
    mem_lengths,
    mem_keep,
    row_expert,
    attn_weights,
    attn_moment,
    attn_second,
    expert_weights,
    expert_moment,
    expert_second,
    norm_params,
    norm_moment,
    norm_second,
):
    row_count = tgt_lengths.shape[0]
    attn_low, expert_low = (
        lax.all_gather(attn_weights.astype(jnp.bfloat16), "dp", axis=2, tiled=True),
        lax.all_gather(expert_weights.astype(jnp.bfloat16), "dp", axis=2, tiled=True),
    )
    row_low = expert_low[row_expert]
    norms = lax.all_gather(norm_params, "dp", axis=1, tiled=True)
    residual = tokens.astype(jnp.float32)
    normed_self, back_self = jax.vjp(norm_layer, residual, norms[0], norms[1])
    self_rows = gather_rows(normed_self.astype(jnp.bfloat16))
    self_qkv = jnp.einsum(
        "td,jdc->jtc", self_rows, attn_low[0, :3], preferred_element_type=jnp.float32
    ).astype(jnp.bfloat16)
    self_mix, self_log = attend_rows(
        self_qkv[0], self_qkv[1], self_qkv[2], tgt_lengths, mem_lengths, mem_keep, False
    )
    self_low = self_mix.astype(jnp.bfloat16)
    first_sum = residual + spread_rows(project_back(self_low, attn_low[0, 3]))
    normed_cross, back_cross = jax.vjp(norm_layer, first_sum, norms[2], norms[3])
    cross_rows = gather_rows(normed_cross.astype(jnp.bfloat16))
    memory_rows = gather_rows(memory)
    cross_queries = project(cross_rows, attn_low[1, 0]).astype(jnp.bfloat16)
    cross_kv = jnp.einsum(
        "td,jdc->jtc", memory_rows, attn_low[1, 1:3], preferred_element_type=jnp.float32
    ).astype(jnp.bfloat16)
    cross_mix, cross_log = attend_rows(
        cross_queries, cross_kv[0], cross_kv[1], tgt_lengths, mem_lengths, mem_keep, True
    )
    cross_low = cross_mix.astype(jnp.bfloat16)
    second_sum = first_sum + spread_rows(project_back(cross_low, attn_low[1, 3]))
    normed_ffn, back_ffn = jax.vjp(norm_layer, second_sum, norms[4], norms[5])
    ffn_rows = gather_rows(normed_ffn.astype(jnp.bfloat16))

    def expert_forward(row_item):
        row_in, chosen = row_item
        inner_act = project(row_in, chosen[0])
        hidden = jax.nn.gelu(inner_act).astype(jnp.bfloat16)
        return (inner_act, project_back(hidden, chosen[1]))

    inner_all, branch_all = lax.map(expert_forward, (ffn_rows.reshape(row_count, LEN, D), row_low))
    layer_out = (second_sum + spread_rows(branch_all.reshape(row_count * LEN, D))).astype(
        jnp.bfloat16
    )
    grad_ffn = cotangent.astype(jnp.float32)
    upstream_ffn = gather_rows(cotangent)
    ffn_again = gather_rows(normed_ffn.astype(jnp.bfloat16))

    def expert_backward(row_item):
        row_in, inner_act, upstream, chosen = row_item
        hidden, gelu_back = jax.vjp(jax.nn.gelu, inner_act)
        inner_grad = gelu_back(project(upstream, chosen[1]))[0].astype(jnp.bfloat16)
        pair_grads = jnp.stack(
            [outer_grad(row_in, inner_grad), outer_grad(upstream, hidden.astype(jnp.bfloat16))]
        )
        return (pair_grads, project_back(inner_grad, chosen[0]))

    row_grads, ffn_part = lax.map(
        expert_backward,
        (
            ffn_again.reshape(row_count, LEN, D),
            inner_all,
            upstream_ffn.reshape(row_count, LEN, D),
            row_low,
        ),
    )
    normed_ffn_grad = spread_rows(ffn_part.reshape(row_count * LEN, D))
    back_tokens, gain_ffn, shift_ffn = back_ffn(normed_ffn_grad)
    grad_cross = grad_ffn + back_tokens
    upstream_cross = gather_rows(grad_cross.astype(jnp.bfloat16))
    cross_again = gather_rows(normed_cross.astype(jnp.bfloat16))
    memory_again = gather_rows(memory)
    cross_up = project(upstream_cross, attn_low[1, 3]).astype(jnp.bfloat16)
    cross_dq, cross_dk, cross_dv = attend_back_rows(
        cross_queries,
        cross_kv[0],
        cross_kv[1],
        cross_up,
        cross_log,
        tgt_lengths,
        mem_lengths,
        mem_keep,
        True,
    )
    cross_grads = jnp.stack(
        [
            outer_grad(cross_again, cross_dq),
            outer_grad(memory_again, cross_dk),
            outer_grad(memory_again, cross_dv),
            outer_grad(upstream_cross, cross_low),
        ]
    )
    normed_cross_grad, memory_total = (
        lax.psum_scatter(
            project_back(cross_dq, attn_low[1, 0]), "tensor", scatter_dimension=0, tiled=True
        ),
        lax.psum_scatter(
            project_back(cross_dk, attn_low[1, 1]) + project_back(cross_dv, attn_low[1, 2]),
            "tensor",
            scatter_dimension=0,
            tiled=True,
        ),
    )
    back_tokens, gain_cross, shift_cross = back_cross(normed_cross_grad)
    grad_self = grad_cross + back_tokens
    upstream_self = gather_rows(grad_self.astype(jnp.bfloat16))
    self_again = gather_rows(normed_self.astype(jnp.bfloat16))
    self_up = project(upstream_self, attn_low[0, 3]).astype(jnp.bfloat16)
    self_dq, self_dk, self_dv = attend_back_rows(
        self_qkv[0],
        self_qkv[1],
        self_qkv[2],
        self_up,
        self_log,
        tgt_lengths,
        mem_lengths,
        mem_keep,
        False,
    )
    self_grads = jnp.stack(
        [
            outer_grad(self_again, self_dq),
            outer_grad(self_again, self_dk),
            outer_grad(self_again, self_dv),
            outer_grad(upstream_self, self_low),
        ]
    )
    normed_self_grad = spread_rows(
        project_back(self_dq, attn_low[0, 0])
        + project_back(self_dk, attn_low[0, 1])
        + project_back(self_dv, attn_low[0, 2])
    )
    back_tokens, gain_self, shift_self = back_self(normed_self_grad)
    input_grad = (grad_self + back_tokens).astype(jnp.bfloat16)
    attn_grad = jnp.stack([self_grads, cross_grads])
    norm_grad = jnp.stack([gain_self, shift_self, gain_cross, shift_cross, gain_ffn, shift_ffn])
    norm_total = lax.psum(norm_grad, "tensor")
    selector = (row_expert[:, None] == jnp.arange(E, dtype=jnp.int32)[None, :]).astype(jnp.float32)
    expert_grad = jnp.einsum("re,rjdf->ejdf", selector, row_grads, precision=lax.Precision.HIGHEST)
    expert_shard = lax.psum_scatter(expert_grad, "dp", scatter_dimension=2, tiled=True)
    attn_shard, norm_shard = (
        lax.psum_scatter(attn_grad, "dp", scatter_dimension=2, tiled=True),
        lax.psum_scatter(norm_total, "dp", scatter_dimension=1, tiled=True),
    )
    attn_pieces = lamb_pieces(attn_weights, attn_moment, attn_second, attn_shard, (2, 3))
    expert_pieces = lamb_pieces(expert_weights, expert_moment, expert_second, expert_shard, (2, 3))
    norm_pieces = lamb_pieces(norm_params, norm_moment, norm_second, norm_shard, (1,))
    copy_share = 1.0 / lax.axis_size("tensor")
    weight_squares = jnp.concatenate(
        [attn_pieces[3].reshape(-1), expert_pieces[3].reshape(-1), norm_pieces[3] * copy_share]
    )
    update_squares = jnp.concatenate(
        [attn_pieces[4].reshape(-1), expert_pieces[4].reshape(-1), norm_pieces[4] * copy_share]
    )
    weight_total, update_total = lax.psum((weight_squares, update_squares), ("dp", "tensor"))
    weight_norm = jnp.sqrt(weight_total)
    update_norm = jnp.sqrt(update_total)
    trust_ratio = weight_norm / update_norm
    attn_ratio = trust_ratio[:8].reshape(2, 4, 1, 1)
    expert_ratio = trust_ratio[8 : 8 + 2 * E].reshape(E, 2, 1, 1)
    norm_ratio = trust_ratio[8 + 2 * E :].reshape(6, 1)
    attn_new = attn_weights - rate * attn_ratio * attn_pieces[2]
    expert_new = expert_weights - rate * expert_ratio * expert_pieces[2]
    norm_new = norm_params - rate * norm_ratio * norm_pieces[2]
    lamb_norms = jnp.stack([weight_norm, update_norm])
    return (
        layer_out,
        input_grad,
        memory_total.astype(jnp.bfloat16),
        attn_new,
        attn_pieces[0],
        attn_pieces[1],
        expert_new,
        expert_pieces[0],
        expert_pieces[1],
        norm_new,
        norm_pieces[0],
        norm_pieces[1],
        lamb_norms,
    )


DEVICES = ("plane", "core", "tensor")
CHIP = ("core", "tensor")


def twin(values):
    return lax.ppermute(values, "core", ((0, 1), (1, 0)))


def pair_rows(mine):
    theirs = twin(mine)
    first = lax.axis_index("core") == 0
    return jnp.concatenate(
        [jnp.where(first, mine, theirs), jnp.where(first, theirs, mine)], 0
    )


def pair_sum(partial):
    half = partial.shape[0] // 2
    core = lax.axis_index("core")
    keep = lax.dynamic_slice_in_dim(partial, core * half, half, 0)
    give = lax.dynamic_slice_in_dim(partial, (1 - core) * half, half, 0)
    return keep + twin(give)


def exchange(values, axes):
    return lax.all_to_all(values, axes, 0, 0, tiled=True)


def swap_pairs(plane_count, tensor_count):
    pairs = []
    for plane in range(plane_count):
        for core in range(2):
            for place in range(tensor_count):
                target = (plane * 2 + place % 2) * tensor_count + place // 2 * 2 + core
                pairs.append(((plane * 2 + core) * tensor_count + place, target))
    return pairs


def fetch_attn(attn_low):
    rows, cols = attn_low.shape[1:]
    half = cols // 2
    tensor_count = lax.axis_size("tensor")
    plane_count = lax.axis_size("plane")
    parts = attn_low.reshape(2, 2, rows, 2, half)
    parts = jnp.moveaxis(parts, 3, 0)
    parts = jnp.moveaxis(parts, 2, 3).reshape(2, 1, 2, rows, cols)
    parts = jnp.broadcast_to(parts, (2, tensor_count, 2, rows, cols))
    chips = exchange(parts.reshape(2 * tensor_count, 2, rows, cols), CHIP)
    planes = jnp.broadcast_to(chips[None], (plane_count,) + chips.shape)
    planes = exchange(planes, "plane")
    planes = planes.reshape(plane_count, 2, tensor_count, 2, rows, cols)
    return planes.transpose(2, 3, 0, 1, 4, 5).reshape(
        tensor_count, 2, plane_count * 2 * rows, cols
    )


def send_attn(grads):
    tensor_count, _, full_rows, cols = grads.shape
    plane_count = lax.axis_size("plane")
    rows = full_rows // (2 * plane_count)
    parts = grads.reshape(tensor_count, 2, plane_count, 2, rows, cols)
    parts = parts.transpose(2, 3, 0, 1, 4, 5).astype(jnp.bfloat16)
    planes = exchange(parts, "plane").astype(jnp.float32).sum(0)
    chips = exchange(
        planes.astype(jnp.bfloat16).reshape(2 * tensor_count, 2, rows, cols), CHIP
    )
    total = chips.reshape(2, tensor_count, 2, rows, 2, cols // 2).astype(jnp.float32).sum(1)
    return total.transpose(1, 3, 2, 0, 4).reshape(4, rows, cols)


def heads_of(weights):
    count, rows, cols = weights.shape
    return jnp.moveaxis(weights, 0, 1).reshape(rows, count * cols)


def heads_apart(values, count):
    return jnp.moveaxis(values.reshape(values.shape[0], count, HD), 1, 0)


def body_rows(
    tokens,
    memory,
    cotangent,
    tgt_lengths,
    mem_lengths,
    mem_keep,
    row_expert,
    attn_weights,
    attn_moment,
    attn_second,
    expert_weights,
    expert_moment,
    expert_second,
    norm_params,
    norm_moment,
    norm_second,
):
    plane_count, tensor_count = lax.axis_size("plane"), lax.axis_size("tensor")
    devices = plane_count * 2 * tensor_count
    core, place = lax.axis_index("core"), lax.axis_index("tensor")
    moves = swap_pairs(plane_count, tensor_count)

    def swap(values):
        return lax.ppermute(values, DEVICES, moves)

    residual = swap(tokens).astype(jnp.float32)
    norm_rows = norm_params.shape[1]
    small = jnp.concatenate(
        [norm_params.reshape(-1), row_expert.astype(jnp.float32)]
    )
    small = exchange(
        jnp.broadcast_to(small[None], (plane_count * 2, small.shape[0])), ("plane", "core")
    )
    norms = jnp.moveaxis(small[:, : 6 * norm_rows].reshape(-1, 6, norm_rows), 0, 1).reshape(6, D)
    owner_expert = small[:, 6 * norm_rows :].astype(jnp.int32)
    chip_expert = (
        owner_expert.reshape(plane_count, 2, 2).transpose(0, 2, 1).reshape(plane_count, tensor_count)
    )
    self_weights = fetch_attn(attn_weights[0].astype(jnp.bfloat16))
    normed_self, back_self = jax.vjp(norm_layer, residual, norms[0], norms[1])
    self_rows = pair_rows(normed_self.astype(jnp.bfloat16))

    facts = jnp.concatenate([tgt_lengths, mem_lengths, mem_keep], 1)
    facts = jnp.where(core == place % 2, facts, twin(facts))
    facts = lax.dynamic_index_in_dim(facts, place // 2, 0, False)
    tgt_len, mem_len, keep_row = facts[:8], facts[8:16], facts[16:]
    self_allowed = build_allowed(tgt_len, mem_len, keep_row, False)
    cross_allowed = build_allowed(tgt_len, mem_len, keep_row, True)

    cross_weights = fetch_attn(attn_weights[1].astype(jnp.bfloat16))
    hidden_cols = expert_weights.shape[3] // 2
    chosen = expert_weights[chip_expert.reshape(-1)].astype(jnp.bfloat16)
    chosen = chosen.reshape(plane_count, tensor_count, 2, -1, 2, hidden_cols)
    chosen = exchange(
        chosen.transpose(0, 4, 1, 2, 3, 5).reshape(devices, 2, -1, hidden_cols), DEVICES
    )
    chosen = (
        chosen.reshape(plane_count * 2, tensor_count, 2, -1, hidden_cols)
        .transpose(2, 0, 3, 1, 4)
        .reshape(2, D, tensor_count * hidden_cols)
    )
    memory_rows = pair_rows(swap(memory))
    cotangent_own = swap(cotangent)
    cotangent_rows = pair_rows(cotangent_own)

    def pieces(weights):
        return [
            heads_of(weights[:, 0, :, :HD]),
            heads_of(weights[:, 0, :, HD:]),
            heads_of(weights[:, 1, :, :HD]),
            heads_of(weights[:, 1, :, HD:]),
        ]

    self_w = pieces(self_weights)
    cross_w = pieces(cross_weights)
    self_q, self_k, self_v = [project(self_rows, w).astype(jnp.bfloat16) for w in self_w[:3]]
    self_mix, self_log = attend_one(self_q, self_k, self_v, self_allowed)
    self_low = self_mix.astype(jnp.bfloat16)
    first_sum = residual + pair_sum(project_back(self_low, self_w[3]))
    normed_cross, back_cross = jax.vjp(norm_layer, first_sum, norms[2], norms[3])
    cross_rows = pair_rows(normed_cross.astype(jnp.bfloat16))
    cross_q = project(cross_rows, cross_w[0]).astype(jnp.bfloat16)
    cross_k, cross_v = [project(memory_rows, w).astype(jnp.bfloat16) for w in cross_w[1:3]]
    cross_mix, cross_log = attend_one(cross_q, cross_k, cross_v, cross_allowed)
    cross_low = cross_mix.astype(jnp.bfloat16)
    second_sum = first_sum + pair_sum(project_back(cross_low, cross_w[3]))
    normed_ffn, back_ffn = jax.vjp(norm_layer, second_sum, norms[4], norms[5])
    ffn_rows = pair_rows(normed_ffn.astype(jnp.bfloat16))

    inner = project(ffn_rows, chosen[0])
    hidden, gelu_back = jax.vjp(jax.nn.gelu, inner)
    hidden = hidden.astype(jnp.bfloat16)
    layer_out = (second_sum + pair_sum(project_back(hidden, chosen[1]))).astype(jnp.bfloat16)
    layer_out = swap(layer_out)
    inner_grad = gelu_back(project(cotangent_rows, chosen[1]))[0].astype(jnp.bfloat16)
    normed_ffn_grad = pair_sum(project_back(inner_grad, chosen[0]))
    row_grad = jnp.stack(
        [outer_grad(ffn_rows, inner_grad), outer_grad(cotangent_rows, hidden)]
    ).astype(jnp.bfloat16)
    row_grad = row_grad.reshape(2, plane_count * 2, -1, tensor_count, hidden_cols)
    row_grad = exchange(
        row_grad.transpose(1, 3, 0, 2, 4).reshape(devices, 2, -1, hidden_cols), DEVICES
    )
    back_tokens, gain_ffn, shift_ffn = back_ffn(normed_ffn_grad)
    grad_cross = cotangent_own.astype(jnp.float32) + back_tokens
    upstream_cross = pair_rows(grad_cross.astype(jnp.bfloat16))
    cross_up = project(upstream_cross, cross_w[3]).astype(jnp.bfloat16)
    cross_dq, cross_dk, cross_dv = attend_back_one(
        cross_q, cross_k, cross_v, cross_up, cross_log, cross_allowed
    )

    def packed(dq_in, dq, dk_in, dk, dv_in, dv, do_in, do):
        pair_qk = [
            heads_apart(outer_grad(dq_in, dq), tensor_count),
            heads_apart(outer_grad(dk_in, dk), tensor_count),
        ]
        pair_vo = [
            heads_apart(outer_grad(dv_in, dv), tensor_count),
            heads_apart(outer_grad(do_in, do), tensor_count),
        ]
        return jnp.stack(
            [jnp.concatenate(pair_qk, -1), jnp.concatenate(pair_vo, -1)], 1
        )

    cross_grad = send_attn(
        packed(
            cross_rows, cross_dq, memory_rows, cross_dk, memory_rows, cross_dv, upstream_cross, cross_low
        )
    )
    memory_grad = pair_sum(project_back(cross_dk, cross_w[1]) + project_back(cross_dv, cross_w[2]))
    memory_grad = swap(memory_grad.astype(jnp.bfloat16))
    back_tokens, gain_cross, shift_cross = back_cross(
        pair_sum(project_back(cross_dq, cross_w[0]))
    )
    grad_self = grad_cross + back_tokens
    upstream_self = pair_rows(grad_self.astype(jnp.bfloat16))
    self_up = project(upstream_self, self_w[3]).astype(jnp.bfloat16)
    self_dq, self_dk, self_dv = attend_back_one(
        self_q, self_k, self_v, self_up, self_log, self_allowed
    )
    self_grad = send_attn(
        packed(
            self_rows, self_dq, self_rows, self_dk, self_rows, self_dv, upstream_self, self_low
        )
    )
    back_tokens, gain_self, shift_self = back_self(
        pair_sum(
            project_back(self_dq, self_w[0])
            + project_back(self_dk, self_w[1])
            + project_back(self_dv, self_w[2])
        )
    )
    input_grad = swap((grad_self + back_tokens).astype(jnp.bfloat16))
    norm_grad = jnp.stack([gain_self, shift_self, gain_cross, shift_cross, gain_ffn, shift_ffn])
    norm_parts = jnp.moveaxis(norm_grad.reshape(6, plane_count * 2, norm_rows), 1, 0)
    norm_parts = jnp.broadcast_to(
        norm_parts.reshape(-1, 1, 6 * norm_rows), (plane_count * 2, tensor_count, 6 * norm_rows)
    )
    norm_shard = exchange(norm_parts.reshape(devices, 6 * norm_rows), DEVICES).sum(0)
    norm_shard = norm_shard.reshape(6, norm_rows)

    row_grad = row_grad.reshape(plane_count, 2, tensor_count, 2, -1, hidden_cols)
    selector = (chip_expert.reshape(-1)[None, :] == jnp.arange(E, dtype=jnp.int32)[:, None]).astype(
        jnp.bfloat16
    )
    row_grad = row_grad.transpose(0, 2, 3, 4, 1, 5).reshape(
        plane_count * tensor_count, 2, -1, 2 * hidden_cols
    )
    expert_shard = jnp.einsum(
        "er,rjdf->ejdf", selector, row_grad, preferred_element_type=jnp.float32
    )
    attn_shard = jnp.stack([self_grad, cross_grad])
    return finish(
        layer_out,
        input_grad,
        memory_grad,
        attn_shard,
        expert_shard,
        norm_shard,
        attn_weights,
        attn_moment,
        attn_second,
        expert_weights,
        expert_moment,
        expert_second,
        norm_params,
        norm_moment,
        norm_second,
    )


def finish(
    layer_out,
    input_grad,
    memory_grad,
    attn_shard,
    expert_shard,
    norm_shard,
    attn_weights,
    attn_moment,
    attn_second,
    expert_weights,
    expert_moment,
    expert_second,
    norm_params,
    norm_moment,
    norm_second,
):
    attn_pieces = lamb_pieces(attn_weights, attn_moment, attn_second, attn_shard, (2, 3))
    expert_pieces = lamb_pieces(expert_weights, expert_moment, expert_second, expert_shard, (2, 3))
    norm_pieces = lamb_pieces(norm_params, norm_moment, norm_second, norm_shard, (1,))
    copy_share = 1.0 / lax.axis_size("tensor")
    squares = jnp.concatenate(
        [
            attn_pieces[3].reshape(-1),
            expert_pieces[3].reshape(-1),
            norm_pieces[3] * copy_share,
            attn_pieces[4].reshape(-1),
            expert_pieces[4].reshape(-1),
            norm_pieces[4] * copy_share,
        ]
    )
    count = squares.shape[0] // 2
    devices = lax.axis_size("plane") * 2 * lax.axis_size("tensor")
    squares = exchange(jnp.broadcast_to(squares[None], (devices, 2 * count)), DEVICES).sum(0)
    lamb_norms = jnp.sqrt(squares).reshape(2, count)
    trust_ratio = lamb_norms[0] / lamb_norms[1]
    attn_ratio = trust_ratio[:8].reshape(2, 4, 1, 1)
    expert_ratio = trust_ratio[8 : 8 + 2 * E].reshape(E, 2, 1, 1)
    norm_ratio = trust_ratio[8 + 2 * E :].reshape(6, 1)
    return (
        layer_out,
        input_grad,
        memory_grad,
        attn_weights - rate * attn_ratio * attn_pieces[2],
        attn_pieces[0],
        attn_pieces[1],
        expert_weights - rate * expert_ratio * expert_pieces[2],
        expert_pieces[0],
        expert_pieces[1],
        norm_params - rate * norm_ratio * norm_pieces[2],
        norm_pieces[0],
        norm_pieces[1],
        lamb_norms,
    )


def specs(rows, dp):
    tokens = P((*dp, "tensor"), None)
    matrix = P(None, None, dp, "tensor")
    row_items = (P(dp, None),) * 3 + (P(dp),)
    return dict(
        in_specs=(tokens,) * 3 + row_items + (matrix,) * 6 + (P(None, dp),) * 3,
        out_specs=(tokens,) * 3 + (matrix,) * 6 + (P(None, dp),) * 3 + (P(),),
        check_vma=False,
    )


def solution(mesh):
    def run(*args):
        rows = args[3].shape[0]
        dp_count, tensor_count = mesh.shape["dp"], mesh.shape["tensor"]
        if rows // dp_count * 2 == tensor_count and tensor_count % 2 == 0:
            fine = Mesh(
                mesh.devices.reshape(dp_count // 2, 2, tensor_count), ("plane", "core", "tensor")
            )
            return jax.shard_map(body_rows, mesh=fine, **specs(rows, ("plane", "core")))(*args)
        return jax.shard_map(body, mesh=mesh, **specs(rows, ("dp",)))(*args)

    return run
```

```python
import jax
import jax.numpy as jnp
from jax import lax
from jax.experimental import pallas as pl
from jax.experimental.pallas import tpu as pltpu
from jax.sharding import Mesh
from jax.sharding import PartitionSpec as P

D = 512
HD = 64
E = 16
LEN = 1024
MLEN = 1024
STEP = 10


beta_one = 0.9
beta_two = 0.999
epsilon = 1e-06
decay = 0.01
rate = 0.2


def norm_layer(values, gain_vec, shift_vec):
    centered = values - jnp.mean(values, -1, keepdims=True)
    variance = jnp.mean(centered * centered, -1, keepdims=True)
    return centered * lax.rsqrt(variance + 1e-05) * gain_vec + shift_vec


def doc_numbers(lengths, length_total):
    doc_ends = jnp.cumsum(lengths)
    places = jnp.arange(length_total, dtype=jnp.int32)
    numbers = jnp.sum((places[:, None] >= doc_ends[None, :]).astype(jnp.int32), 1)
    starts = doc_ends - lengths
    opening = jnp.any(places[:, None] == starts[None, :], 1)
    return (numbers, opening)


def build_allowed(tgt_len, mem_len, keep_row, cross):
    doc_ids, _ = doc_numbers(tgt_len, LEN)
    if cross:
        mem_docs, opening = doc_numbers(mem_len, MLEN)
        return (doc_ids[:, None] == mem_docs[None, :]) & ((keep_row == 1) | opening)[None, :]
    places = jnp.arange(LEN, dtype=jnp.int32)
    return (doc_ids[:, None] == doc_ids[None, :]) & (places[None, :] <= places[:, None])


def gather_rows(values):
    return lax.all_gather(values, "tensor", axis=0, tiled=True)


def spread_rows(values):
    return lax.psum_scatter(values, "tensor", scatter_dimension=0, tiled=True)


def project(left_side, right_side):
    return jnp.dot(left_side, right_side, preferred_element_type=jnp.float32)


def project_back(left_side, right_side):
    return lax.dot_general(
        left_side, right_side, (((1,), (1,)), ((), ())), preferred_element_type=jnp.float32
    )


def outer_grad(left_side, right_side):
    return lax.dot_general(
        left_side, right_side, (((0,), (0,)), ((), ())), preferred_element_type=jnp.float32
    )


def attend_one(queries, key_rows, value_rows, allowed):
    head_count = queries.shape[1] // HD
    keys_h = key_rows.reshape(key_rows.shape[0], head_count, HD)
    values_h = value_rows.reshape(value_rows.shape[0], head_count, HD)
    block_rows = min(LEN, 512)
    outputs = []
    totals = []
    for begin_at in range(0, LEN, block_rows):
        queries_h = queries[begin_at : begin_at + block_rows].reshape(block_rows, head_count, HD)
        scores = jnp.einsum(
            "qhd,khd->hqk", queries_h, keys_h, preferred_element_type=jnp.float32
        ) * HD ** (-0.5)
        scores = jnp.where(allowed[None, begin_at : begin_at + block_rows], scores, -1e30)
        top_score = jnp.max(scores, -1, keepdims=True)
        weights = jnp.exp(scores - top_score)
        row_total = jnp.sum(weights, -1, keepdims=True)
        prob_low = (weights / row_total).astype(jnp.bfloat16)
        blended = jnp.einsum("hqk,khd->qhd", prob_low, values_h, preferred_element_type=jnp.float32)
        outputs.append(blended.reshape(block_rows, head_count * HD))
        totals.append((top_score + jnp.log(row_total))[..., 0])
    return (jnp.concatenate(outputs, 0), jnp.concatenate(totals, 1))


def attend_back_one(queries, key_rows, value_rows, upstream, log_totals, allowed):
    head_count = queries.shape[1] // HD
    scale = HD ** (-0.5)
    keys_h = key_rows.reshape(key_rows.shape[0], head_count, HD)
    values_h = value_rows.reshape(value_rows.shape[0], head_count, HD)
    key_grad = jnp.zeros(keys_h.shape, jnp.float32)
    value_grad = jnp.zeros(values_h.shape, jnp.float32)
    block_rows = min(LEN, 512)
    query_grads = []
    for begin_at in range(0, LEN, block_rows):
        queries_h = queries[begin_at : begin_at + block_rows].reshape(block_rows, head_count, HD)
        upstream_h = upstream[begin_at : begin_at + block_rows].reshape(block_rows, head_count, HD)
        scores = (
            jnp.einsum("qhd,khd->hqk", queries_h, keys_h, preferred_element_type=jnp.float32)
            * scale
        )
        scores = jnp.where(allowed[None, begin_at : begin_at + block_rows], scores, -1e30)
        probs_full = jnp.exp(scores - log_totals[:, begin_at : begin_at + block_rows, None])
        prob_grad = jnp.einsum(
            "qhd,khd->hqk", upstream_h, values_h, preferred_element_type=jnp.float32
        )
        weighted = jnp.sum(probs_full * prob_grad, -1, keepdims=True)
        score_grad = (probs_full * (prob_grad - weighted)).astype(jnp.bfloat16)
        query_part = (
            jnp.einsum("hqk,khd->qhd", score_grad, keys_h, preferred_element_type=jnp.float32)
            * scale
        )
        query_grads.append(query_part.astype(jnp.bfloat16).reshape(block_rows, head_count * HD))
        key_grad = (
            key_grad
            + jnp.einsum("hqk,qhd->khd", score_grad, queries_h, preferred_element_type=jnp.float32)
            * scale
        )
        value_grad = value_grad + jnp.einsum(
            "hqk,qhd->khd",
            probs_full.astype(jnp.bfloat16),
            upstream_h,
            preferred_element_type=jnp.float32,
        )
    width = head_count * HD
    return (
        jnp.concatenate(query_grads, 0),
        key_grad.astype(jnp.bfloat16).reshape(-1, width),
        value_grad.astype(jnp.bfloat16).reshape(-1, width),
    )


def attend_rows(queries, key_rows, value_rows, tgt_lengths, mem_lengths, mem_keep, cross):
    row_count = tgt_lengths.shape[0]
    width = queries.shape[1]

    def one_row(row_item):
        row_q, row_k, row_v, tgt_len, mem_len, keep_row = row_item
        return attend_one(row_q, row_k, row_v, build_allowed(tgt_len, mem_len, keep_row, cross))

    blended, log_totals = lax.map(
        one_row,
        (
            queries.reshape(row_count, LEN, width),
            key_rows.reshape(row_count, -1, width),
            value_rows.reshape(row_count, -1, width),
            tgt_lengths,
            mem_lengths,
            mem_keep,
        ),
    )
    return (blended.reshape(row_count * LEN, width), log_totals)


def attend_back_rows(
    queries, key_rows, value_rows, upstream, log_totals, tgt_lengths, mem_lengths, mem_keep, cross
):
    row_count = tgt_lengths.shape[0]
    width = queries.shape[1]

    def one_row(row_item):
        row_q, row_k, row_v, row_up, row_log, tgt_len, mem_len, keep_row = row_item
        return attend_back_one(
            row_q, row_k, row_v, row_up, row_log, build_allowed(tgt_len, mem_len, keep_row, cross)
        )

    query_grad, key_grad, value_grad = lax.map(
        one_row,
        (
            queries.reshape(row_count, LEN, width),
            key_rows.reshape(row_count, -1, width),
            value_rows.reshape(row_count, -1, width),
            upstream.reshape(row_count, LEN, width),
            log_totals,
            tgt_lengths,
            mem_lengths,
            mem_keep,
        ),
    )
    return (
        query_grad.reshape(-1, width),
        key_grad.reshape(-1, width),
        value_grad.reshape(-1, width),
    )


def lamb_pieces(weight, moment, second, grad, axes):
    moment = beta_one * moment + (1.0 - beta_one) * grad
    second = beta_two * second + (1.0 - beta_two) * grad * grad
    update = (
        moment / (1.0 - beta_one**STEP) / (jnp.sqrt(second / (1.0 - beta_two**STEP)) + epsilon)
        + decay * weight
    )
    return (moment, second, update, jnp.sum(weight * weight, axes), jnp.sum(update * update, axes))


def body(
    tokens,
    memory,
    cotangent,
    tgt_lengths,
    mem_lengths,
    mem_keep,
    row_expert,
    attn_weights,
    attn_moment,
    attn_second,
    expert_weights,
    expert_moment,
    expert_second,
    norm_params,
    norm_moment,
    norm_second,
):
    row_count = tgt_lengths.shape[0]
    attn_low, expert_low = (
        lax.all_gather(attn_weights.astype(jnp.bfloat16), "dp", axis=2, tiled=True),
        lax.all_gather(expert_weights.astype(jnp.bfloat16), "dp", axis=2, tiled=True),
    )
    row_low = expert_low[row_expert]
    norms = lax.all_gather(norm_params, "dp", axis=1, tiled=True)
    residual = tokens.astype(jnp.float32)
    normed_self, back_self = jax.vjp(norm_layer, residual, norms[0], norms[1])
    self_rows = gather_rows(normed_self.astype(jnp.bfloat16))
    self_qkv = jnp.einsum(
        "td,jdc->jtc", self_rows, attn_low[0, :3], preferred_element_type=jnp.float32
    ).astype(jnp.bfloat16)
    self_mix, self_log = attend_rows(
        self_qkv[0], self_qkv[1], self_qkv[2], tgt_lengths, mem_lengths, mem_keep, False
    )
    self_low = self_mix.astype(jnp.bfloat16)
    first_sum = residual + spread_rows(project_back(self_low, attn_low[0, 3]))
    normed_cross, back_cross = jax.vjp(norm_layer, first_sum, norms[2], norms[3])
    cross_rows = gather_rows(normed_cross.astype(jnp.bfloat16))
    memory_rows = gather_rows(memory)
    cross_queries = project(cross_rows, attn_low[1, 0]).astype(jnp.bfloat16)
    cross_kv = jnp.einsum(
        "td,jdc->jtc", memory_rows, attn_low[1, 1:3], preferred_element_type=jnp.float32
    ).astype(jnp.bfloat16)
    cross_mix, cross_log = attend_rows(
        cross_queries, cross_kv[0], cross_kv[1], tgt_lengths, mem_lengths, mem_keep, True
    )
    cross_low = cross_mix.astype(jnp.bfloat16)
    second_sum = first_sum + spread_rows(project_back(cross_low, attn_low[1, 3]))
    normed_ffn, back_ffn = jax.vjp(norm_layer, second_sum, norms[4], norms[5])
    ffn_rows = gather_rows(normed_ffn.astype(jnp.bfloat16))

    def expert_forward(row_item):
        row_in, chosen = row_item
        inner_act = project(row_in, chosen[0])
        hidden = jax.nn.gelu(inner_act).astype(jnp.bfloat16)
        return (inner_act, project_back(hidden, chosen[1]))

    inner_all, branch_all = lax.map(expert_forward, (ffn_rows.reshape(row_count, LEN, D), row_low))
    layer_out = (second_sum + spread_rows(branch_all.reshape(row_count * LEN, D))).astype(
        jnp.bfloat16
    )
    grad_ffn = cotangent.astype(jnp.float32)
    upstream_ffn = gather_rows(cotangent)
    ffn_again = gather_rows(normed_ffn.astype(jnp.bfloat16))

    def expert_backward(row_item):
        row_in, inner_act, upstream, chosen = row_item
        hidden, gelu_back = jax.vjp(jax.nn.gelu, inner_act)
        inner_grad = gelu_back(project(upstream, chosen[1]))[0].astype(jnp.bfloat16)
        pair_grads = jnp.stack(
            [outer_grad(row_in, inner_grad), outer_grad(upstream, hidden.astype(jnp.bfloat16))]
        )
        return (pair_grads, project_back(inner_grad, chosen[0]))

    row_grads, ffn_part = lax.map(
        expert_backward,
        (
            ffn_again.reshape(row_count, LEN, D),
            inner_all,
            upstream_ffn.reshape(row_count, LEN, D),
            row_low,
        ),
    )
    normed_ffn_grad = spread_rows(ffn_part.reshape(row_count * LEN, D))
    back_tokens, gain_ffn, shift_ffn = back_ffn(normed_ffn_grad)
    grad_cross = grad_ffn + back_tokens
    upstream_cross = gather_rows(grad_cross.astype(jnp.bfloat16))
    cross_again = gather_rows(normed_cross.astype(jnp.bfloat16))
    memory_again = gather_rows(memory)
    cross_up = project(upstream_cross, attn_low[1, 3]).astype(jnp.bfloat16)
    cross_dq, cross_dk, cross_dv = attend_back_rows(
        cross_queries,
        cross_kv[0],
        cross_kv[1],
        cross_up,
        cross_log,
        tgt_lengths,
        mem_lengths,
        mem_keep,
        True,
    )
    cross_grads = jnp.stack(
        [
            outer_grad(cross_again, cross_dq),
            outer_grad(memory_again, cross_dk),
            outer_grad(memory_again, cross_dv),
            outer_grad(upstream_cross, cross_low),
        ]
    )
    normed_cross_grad, memory_total = (
        lax.psum_scatter(
            project_back(cross_dq, attn_low[1, 0]), "tensor", scatter_dimension=0, tiled=True
        ),
        lax.psum_scatter(
            project_back(cross_dk, attn_low[1, 1]) + project_back(cross_dv, attn_low[1, 2]),
            "tensor",
            scatter_dimension=0,
            tiled=True,
        ),
    )
    back_tokens, gain_cross, shift_cross = back_cross(normed_cross_grad)
    grad_self = grad_cross + back_tokens
    upstream_self = gather_rows(grad_self.astype(jnp.bfloat16))
    self_again = gather_rows(normed_self.astype(jnp.bfloat16))
    self_up = project(upstream_self, attn_low[0, 3]).astype(jnp.bfloat16)
    self_dq, self_dk, self_dv = attend_back_rows(
        self_qkv[0],
        self_qkv[1],
        self_qkv[2],
        self_up,
        self_log,
        tgt_lengths,
        mem_lengths,
        mem_keep,
        False,
    )
    self_grads = jnp.stack(
        [
            outer_grad(self_again, self_dq),
            outer_grad(self_again, self_dk),
            outer_grad(self_again, self_dv),
            outer_grad(upstream_self, self_low),
        ]
    )
    normed_self_grad = spread_rows(
        project_back(self_dq, attn_low[0, 0])
        + project_back(self_dk, attn_low[0, 1])
        + project_back(self_dv, attn_low[0, 2])
    )
    back_tokens, gain_self, shift_self = back_self(normed_self_grad)
    input_grad = (grad_self + back_tokens).astype(jnp.bfloat16)
    attn_grad = jnp.stack([self_grads, cross_grads])
    norm_grad = jnp.stack([gain_self, shift_self, gain_cross, shift_cross, gain_ffn, shift_ffn])
    norm_total = lax.psum(norm_grad, "tensor")
    selector = (row_expert[:, None] == jnp.arange(E, dtype=jnp.int32)[None, :]).astype(jnp.float32)
    expert_grad = jnp.einsum("re,rjdf->ejdf", selector, row_grads, precision=lax.Precision.HIGHEST)
    expert_shard = lax.psum_scatter(expert_grad, "dp", scatter_dimension=2, tiled=True)
    attn_shard, norm_shard = (
        lax.psum_scatter(attn_grad, "dp", scatter_dimension=2, tiled=True),
        lax.psum_scatter(norm_total, "dp", scatter_dimension=1, tiled=True),
    )
    attn_pieces = lamb_pieces(attn_weights, attn_moment, attn_second, attn_shard, (2, 3))
    expert_pieces = lamb_pieces(expert_weights, expert_moment, expert_second, expert_shard, (2, 3))
    norm_pieces = lamb_pieces(norm_params, norm_moment, norm_second, norm_shard, (1,))
    copy_share = 1.0 / lax.axis_size("tensor")
    weight_squares = jnp.concatenate(
        [attn_pieces[3].reshape(-1), expert_pieces[3].reshape(-1), norm_pieces[3] * copy_share]
    )
    update_squares = jnp.concatenate(
        [attn_pieces[4].reshape(-1), expert_pieces[4].reshape(-1), norm_pieces[4] * copy_share]
    )
    weight_total, update_total = lax.psum((weight_squares, update_squares), ("dp", "tensor"))
    weight_norm = jnp.sqrt(weight_total)
    update_norm = jnp.sqrt(update_total)
    trust_ratio = weight_norm / update_norm
    attn_ratio = trust_ratio[:8].reshape(2, 4, 1, 1)
    expert_ratio = trust_ratio[8 : 8 + 2 * E].reshape(E, 2, 1, 1)
    norm_ratio = trust_ratio[8 + 2 * E :].reshape(6, 1)
    attn_new = attn_weights - rate * attn_ratio * attn_pieces[2]
    expert_new = expert_weights - rate * expert_ratio * expert_pieces[2]
    norm_new = norm_params - rate * norm_ratio * norm_pieces[2]
    lamb_norms = jnp.stack([weight_norm, update_norm])
    return (
        layer_out,
        input_grad,
        memory_total.astype(jnp.bfloat16),
        attn_new,
        attn_pieces[0],
        attn_pieces[1],
        expert_new,
        expert_pieces[0],
        expert_pieces[1],
        norm_new,
        norm_pieces[0],
        norm_pieces[1],
        lamb_norms,
    )


MEGA = 1024 * 1024
QUERY_BLOCK = 256
WINDOW_STEP = 256
FORWARD_MEGA = 24
BACKWARD_MEGA = 34
EXPERT_MEGA = 28
KERNEL_COST = pl.CostEstimate(flops=10**9, bytes_accessed=MEGA, transcendentals=0)
WHOLE = pl.BlockSpec(memory_space=pltpu.VMEM)
OUTSIDE = pl.BlockSpec(memory_space=pl.ANY)
SCALARS = pl.BlockSpec(memory_space=pltpu.SMEM)


def mm(left, right):
    return lax.dot_general(left, right, (((1,), (0,)), ((), ())), preferred_element_type=jnp.float32)


def mt(left, right):
    return lax.dot_general(left, right, (((1,), (1,)), ((), ())), preferred_element_type=jnp.float32)


def low(values):
    return values.astype(jnp.bfloat16)


def standardize(values):
    centered = values - jnp.mean(values, -1, keepdims=True)
    inverse = lax.rsqrt(jnp.mean(centered * centered, -1, keepdims=True) + 1e-05)
    return centered * inverse, inverse


def norm_back(values, grad, gain_vec):
    unit, inverse = standardize(values)
    inner = grad * gain_vec
    back = inverse * (
        inner
        - jnp.mean(inner, -1, keepdims=True)
        - unit * jnp.mean(inner * unit, -1, keepdims=True)
    )
    return back, jnp.sum(grad * unit, 0, keepdims=True), jnp.sum(grad, 0, keepdims=True)


def key_limits(facts, places, cross):
    zero = jnp.zeros(places.shape, jnp.int32)
    low_end, high_end, doc_end = zero, zero, 0
    for doc in range(8):
        begin, doc_end = doc_end, doc_end + facts[0, doc]
        if cross:
            low_end = low_end + jnp.where(places >= doc_end, facts[0, 8 + doc], 0)
            high_end = high_end + jnp.where(places >= begin, facts[0, 8 + doc], 0)
        else:
            low_end = jnp.where(places >= doc_end, doc_end, low_end)
    return low_end, (high_end if cross else places + 1)


def kept_keys(facts, keep, places):
    kept = keep == 1
    begin = 0
    for doc in range(8):
        kept = kept | (places == begin)
        begin = begin + facts[0, 8 + doc]
    return kept


def half_at(core_ref, other):
    half = LEN // 2
    core = core_ref[0, 0]
    return pl.ds(pl.multiple_of((1 - core if other else core) * half, half), half)


def key_windows(facts, cross, run):
    def block(index, _):
        first_query = pl.multiple_of(index * QUERY_BLOCK, QUERY_BLOCK)
        lowest, _ = key_limits(facts, first_query, cross)
        _, highest = key_limits(facts, first_query + QUERY_BLOCK - 1, cross)
        begin = lax.div(lowest, 128) * 128
        need = highest - begin
        for width in range(WINDOW_STEP, (MLEN if cross else 512 + QUERY_BLOCK) + 1, WINDOW_STEP):
            start = pl.multiple_of(jnp.minimum(begin, MLEN - width), 128)

            @pl.when((need <= width) & (need > width - WINDOW_STEP))
            def _(start=start, width=width):
                run(first_query, start, width)

        return 0

    lax.fori_loop(0, LEN // QUERY_BLOCK, block, 0)


def allowed_bias(facts, keep_ref, cross, keys_first, first_query, start, width):
    query_axis, key_axis = (1, 0) if keys_first else (0, 1)
    line = (1, QUERY_BLOCK) if keys_first else (QUERY_BLOCK, 1)
    places = first_query + lax.broadcasted_iota(jnp.int32, line, query_axis)
    low_end, high_end = key_limits(facts, places, cross)
    shape = (width, QUERY_BLOCK) if keys_first else (QUERY_BLOCK, width)
    keys = start + lax.broadcasted_iota(jnp.int32, shape, key_axis)
    if cross:
        line = (width, 1) if keys_first else (1, width)
        own = start + lax.broadcasted_iota(jnp.int32, line, key_axis)
        at = pl.ds(start, width)
        keep = keep_ref[at, :] if keys_first else keep_ref[:, at]
        keys = jnp.where(kept_keys(facts, keep, own), keys, -1)
    return jnp.where((keys >= low_end) & (keys < high_end), 0.0, -1e30)


def head_lanes(half):
    lane = lax.broadcasted_iota(jnp.int32, (1, 2 * HD), 1)
    return (lane < HD) if half == 0 else (lane >= HD)


def of_head(values, half):
    return jnp.where(head_lanes(half), values, jnp.zeros_like(values))


def gather_weights(w_ref, pack, first, second):
    shape = (w_ref.shape[0] * w_ref.shape[3], w_ref.shape[4])
    left = head_lanes(0)
    for pair in range(w_ref.shape[1] // 2):
        even = w_ref[:, 2 * pair, pack].reshape(shape)
        odd = w_ref[:, 2 * pair + 1, pack].reshape(shape)
        at = slice(pair * 2 * HD, (pair + 1) * 2 * HD)
        first[:, at] = jnp.where(left, even, odd)
        second[:, at] = jnp.where(left, odd, even)


def scatter_grads(w_ref, pack, first, second):
    left = head_lanes(0)
    for pair in range(w_ref.shape[1] // 2):
        at = slice(pair * 2 * HD, (pair + 1) * 2 * HD)
        shape = (w_ref.shape[0], w_ref.shape[3], w_ref.shape[4])
        w_ref[:, 2 * pair, pack] = low(jnp.where(left, first[:, at], second[:, at])).reshape(shape)
        w_ref[:, 2 * pair + 1, pack] = low(jnp.where(left, second[:, at], first[:, at])).reshape(
            shape
        )


def start_copies(sources, targets, sems):
    copies = [
        pltpu.make_async_copy(source, target, sems.at[place])
        for place, (source, target) in enumerate(zip(sources, targets))
    ]
    for copy in copies:
        copy.start()
    return copies


def forward_heads(
    facts, keep_ref, cross, rows, key_rows, w_ref, part_ref, kept, sems, scratch
):
    w_q, w_k, w_v, w_o, q_ref, k_ref, v_ref, o_ref, stats_ref = scratch
    query_rows = rows[-1]
    count = len(rows)
    copies = start_copies(rows, kept[:count], sems)
    gather_weights(w_ref, 0, w_q, w_v)
    gather_weights(w_ref, 1, w_k, w_o)
    q_ref[...] = low(mm(query_rows[...], w_q[...]))
    k_ref[...] = low(mm(key_rows[...], w_k[...]))
    v_ref[...] = low(mm(key_rows[...], w_v[...]))
    copies += start_copies(
        (q_ref, k_ref, v_ref), kept[count : count + 3], sems.at[pl.ds(count, 3)]
    )
    lane = lax.broadcasted_iota(jnp.int32, (1, 128), 1)

    def one(first_query, start, width):
        at, keys_at = pl.ds(first_query, QUERY_BLOCK), pl.ds(start, width)
        bias = allowed_bias(facts, keep_ref, cross, False, first_query, start, width)
        stats = jnp.zeros((QUERY_BLOCK, 128), jnp.float32)
        for pair in range(q_ref.shape[1] // (2 * HD)):
            tile = slice(pair * 2 * HD, (pair + 1) * 2 * HD)
            queries = q_ref[at, tile] * HD ** (-0.5)
            blended = []
            for half in (0, 1):
                scores = mt(of_head(queries, half), k_ref[keys_at, tile]) + bias
                top = jnp.max(scores, -1, keepdims=True)
                weights = jnp.exp(scores - top)
                total = jnp.sum(weights, -1, keepdims=True)
                blended.append(mm(low(weights), v_ref[keys_at, tile]) * (1.0 / total))
                stats = jnp.where(lane == 2 * pair + half, top + jnp.log(total), stats)
            o_ref[at, tile] = low(jnp.where(head_lanes(1), *blended))
        stats_ref[at, :] = stats

    key_windows(facts, cross, one)
    copies += start_copies((o_ref, stats_ref), kept[count + 3 :], sems.at[pl.ds(count + 3, 2)])
    part_ref[...] = mt(o_ref[...], w_o[...])
    for copy in copies:
        copy.wait()


def self_forward_kernel(core_ref, facts, mine, theirs, norms, w_ref, part_ref, *rest):
    kept, (sems, rows, *scratch) = rest[:6], rest[6:]
    for source, other in ((mine, False), (theirs, True)):
        unit, _ = standardize(source[...].astype(jnp.float32))
        rows[half_at(core_ref, other), :] = low(unit * norms[0:1, :] + norms[1:2, :])
    forward_heads(facts, None, False, (rows,), rows, w_ref, part_ref, kept, sems, scratch)


def cross_forward_kernel(
    core_ref,
    facts,
    keep_ref,
    mine,
    theirs,
    part_mine,
    part_theirs,
    memory_mine,
    memory_theirs,
    norms,
    w_ref,
    part_ref,
    *rest,
):
    kept, (sems, rows, total, memory_rows, *scratch) = rest[:7], rest[7:]
    for source, memory, other in ((mine, memory_mine, False), (theirs, memory_theirs, True)):
        at = half_at(core_ref, other)
        value = source[...].astype(jnp.float32) + (part_mine[at, :] + part_theirs[at, :])
        total[at, :] = value
        unit, _ = standardize(value)
        rows[at, :] = low(unit * norms[2:3, :] + norms[3:4, :])
        memory_rows[at, :] = memory[...]
    forward_heads(
        facts, keep_ref, True, (total, rows), memory_rows, w_ref, part_ref, kept, sems, scratch
    )


def attn_forward(name, kernel, scalars, wholes, weights, with_sum):
    heads = weights.shape[1]
    cols = heads * HD
    whole = jax.ShapeDtypeStruct((LEN, D), jnp.float32)
    head_shape = jax.ShapeDtypeStruct((LEN, cols), jnp.bfloat16)
    kept = (
        (whole,) * with_sum
        + (jax.ShapeDtypeStruct((LEN, D), jnp.bfloat16),)
        + (head_shape,) * 4
        + (jax.ShapeDtypeStruct((LEN, 128), jnp.float32),)
    )
    return pl.pallas_call(
        kernel,
        name=name,
        out_shape=(whole,) + kept,
        in_specs=[SCALARS] * len(scalars) + [WHOLE] * (len(wholes) + 1),
        out_specs=(WHOLE,) + (OUTSIDE,) * len(kept),
        scratch_shapes=[pltpu.SemaphoreType.DMA((len(kept),)), pltpu.VMEM((LEN, D), jnp.bfloat16)]
        + [pltpu.VMEM((LEN, D), jnp.float32), pltpu.VMEM((MLEN, D), jnp.bfloat16)] * with_sum
        + [pltpu.VMEM((D, cols), jnp.bfloat16)] * 4
        + [pltpu.VMEM((LEN, cols), jnp.bfloat16)] * 4
        + [pltpu.VMEM((LEN, 128), jnp.float32)],
        compiler_params=pltpu.CompilerParams(vmem_limit_bytes=FORWARD_MEGA * MEGA),
        cost_estimate=KERNEL_COST,
    )(*scalars, *wholes, weights)


def backward_heads(
    facts, keep_ref, cross, up_rows, w_ref, loads, heads_in, scratch
):
    w_q, w_k, w_v, w_o, up, keys_turned, turned_stats, q_turned, dq, k_sum, v_sum, dk, dv = scratch
    q_ref, k_ref, v_ref, _, stats_ref = heads_in
    gather_weights(w_ref, 0, w_q, w_v)
    gather_weights(w_ref, 1, w_k, w_o)
    scale = HD ** (-0.5)
    up[...] = low(mm(up_rows[...], w_o[...]))
    for copy in loads:
        copy.wait()
    keys_turned[...] = k_ref[...].T
    turned_stats[...] = stats_ref[...].T
    k_sum[...] = jnp.zeros_like(k_sum)
    v_sum[...] = jnp.zeros_like(v_sum)

    def one(first_query, start, width):
        at, keys_at = pl.ds(first_query, QUERY_BLOCK), pl.ds(start, width)
        bias = allowed_bias(facts, keep_ref, cross, True, first_query, start, width)
        for pair in range(q_ref.shape[1] // (2 * HD)):
            tile = slice(pair * 2 * HD, (pair + 1) * 2 * HD)
            key_add, value_add = [], []
            for half in (0, 1):
                head = 2 * pair + half
                queries, upstream = of_head(q_ref[at, tile], half), of_head(up[at, tile], 1 - half)
                scores = mt(k_ref[keys_at, tile], queries * scale) + bias
                probs = jnp.exp(scores - turned_stats[head : head + 1, at])
                prob_grad = mt(v_ref[keys_at, tile], upstream)
                weighted = jnp.sum(probs * prob_grad, 0, keepdims=True)
                score_grad = low(probs * (prob_grad - weighted))
                key_add.append(mm(score_grad, queries))
                value_add.append(mm(low(probs), upstream))
                lines = slice(head * HD, (head + 1) * HD)
                q_turned[lines, at] = low(mm(keys_turned[lines, keys_at], score_grad) * scale)
            k_sum[keys_at, tile] = k_sum[keys_at, tile] + (key_add[0] + key_add[1])
            v_sum[keys_at, tile] = v_sum[keys_at, tile] + (value_add[0] + value_add[1])

    key_windows(facts, cross, one)
    dq[...] = q_turned[...].T
    dk[...] = low(k_sum[...] * scale)
    dv[...] = low(v_sum[...])


def cross_backward_kernel(
    core_ref,
    facts,
    keep_ref,
    mine,
    theirs,
    part_mine,
    part_theirs,
    sum_ref,
    memory_mine,
    memory_theirs,
    norms,
    w_ref,
    *rest,
):
    kept, rest = rest[:6], rest[6:]
    (grad_out, part_ref, memory_keep, memory_give, w_grad_ref, norm_ref), rest = rest[:6], rest[6:]
    sems, (rows, *heads_in), rest = rest[0], rest[1:7], rest[7:]
    up_rows, turned, memory_turned, grad_ref, *scratch = rest
    loads = start_copies(kept, (rows, *heads_in), sems)
    gains = jnp.zeros((1, D), jnp.float32)
    shifts = jnp.zeros((1, D), jnp.float32)
    for source, memory, other in ((mine, memory_mine, False), (theirs, memory_theirs, True)):
        at = half_at(core_ref, other)
        back, gain, shift = norm_back(
            sum_ref[at, :], part_mine[at, :] + part_theirs[at, :], norms[4:5, :]
        )
        gains, shifts = gains + gain, shifts + shift
        total = source[...].astype(jnp.float32) + back
        grad_ref[at, :] = total
        up_rows[at, :] = low(total)
        memory_turned[:, at] = memory[...].T
    (leaving,) = start_copies((grad_ref,), (grad_out,), sems.at[pl.ds(6, 1)])
    norm_ref[0:1, :] = 0.5 * gains
    norm_ref[1:2, :] = 0.5 * shifts
    backward_heads(facts, keep_ref, True, up_rows, w_ref, loads, heads_in, scratch)
    w_q, w_k, w_v, *_ = scratch
    dq, _, _, dk, dv = scratch[-5:]
    part_ref[...] = mt(dq[...], w_q[...])
    for ref, other in ((memory_keep, False), (memory_give, True)):
        at = half_at(core_ref, other)
        ref[...] = mt(dk[at, :], w_k[...]) + mt(dv[at, :], w_v[...])
    turned[...] = rows[...].T
    scatter_grads(w_grad_ref, 0, mm(turned[...], dq[...]), mm(memory_turned[...], dv[...]))
    turned[...] = up_rows[...].T
    scatter_grads(w_grad_ref, 1, mm(memory_turned[...], dk[...]), mm(turned[...], heads_in[3][...]))
    leaving.wait()


def self_backward_kernel(
    core_ref,
    facts,
    grad_ref,
    part_mine,
    part_theirs,
    sum_ref,
    mine,
    theirs,
    ffn_norm,
    norms,
    w_ref,
    *rest,
):
    kept, rest = rest[:6], rest[6:]
    (own_grad, part_keep, part_give, w_grad_ref, norm_ref), rest = rest[:5], rest[5:]
    sems, (rows, *heads_in), rest = rest[0], rest[1:7], rest[7:]
    up_rows, turned, *scratch = rest
    loads = start_copies(kept, (rows, *heads_in), sems)
    gains = jnp.zeros((1, D), jnp.float32)
    shifts = jnp.zeros((1, D), jnp.float32)
    for other in (False, True):
        at = half_at(core_ref, other)
        back, gain, shift = norm_back(
            sum_ref[at, :], part_mine[at, :] + part_theirs[at, :], norms[2:3, :]
        )
        gains, shifts = gains + gain, shifts + shift
        total = grad_ref[at, :] + back
        if not other:
            own_grad[...] = total
        up_rows[at, :] = low(total)
    norm_ref[2:3, :] = 0.5 * gains
    norm_ref[3:4, :] = 0.5 * shifts
    norm_ref[4:6, :] = ffn_norm[...]
    backward_heads(facts, None, False, up_rows, w_ref, loads, heads_in, scratch)
    w_q, w_k, w_v, *_ = scratch
    dq, _, _, dk, dv = scratch[-5:]
    gains = jnp.zeros((1, D), jnp.float32)
    shifts = jnp.zeros((1, D), jnp.float32)
    for ref, source, other in ((part_keep, mine, False), (part_give, theirs, True)):
        at = half_at(core_ref, other)
        part = mt(dq[at, :], w_q[...]) + mt(dk[at, :], w_k[...]) + mt(dv[at, :], w_v[...])
        ref[...] = part
        unit, _ = standardize(source[...].astype(jnp.float32))
        gains = gains + jnp.sum(part * unit, 0, keepdims=True)
        shifts = shifts + jnp.sum(part, 0, keepdims=True)
    norm_ref[0:1, :] = gains
    norm_ref[1:2, :] = shifts
    turned[...] = rows[...].T
    scatter_grads(w_grad_ref, 0, mm(turned[...], dq[...]), mm(turned[...], dv[...]))
    key_grad = mm(turned[...], dk[...])
    turned[...] = up_rows[...].T
    scatter_grads(w_grad_ref, 1, key_grad, mm(turned[...], heads_in[3][...]))


def attn_backward(name, kernel, scalars, wholes, weights, kept, cross):
    heads = weights.shape[1]
    cols = heads * HD
    whole = jax.ShapeDtypeStruct((LEN, D), jnp.float32)
    half = jax.ShapeDtypeStruct((LEN // 2, D), jnp.float32)
    firsts = (whole, whole, half, half) if cross else (half, half, half)
    outs = firsts + (
        jax.ShapeDtypeStruct(weights.shape, jnp.bfloat16),
        jax.ShapeDtypeStruct((2 if cross else 6, D), jnp.float32),
    )
    return pl.pallas_call(
        kernel,
        name=name,
        out_shape=outs,
        in_specs=[SCALARS] * len(scalars) + [WHOLE] * (len(wholes) + 1) + [OUTSIDE] * len(kept),
        out_specs=(OUTSIDE,) * cross + (WHOLE,) * (len(outs) - cross),
        scratch_shapes=[pltpu.SemaphoreType.DMA((len(kept) + cross,))]
        + [pltpu.VMEM(array.shape, array.dtype) for array in kept]
        + [pltpu.VMEM((LEN, D), jnp.bfloat16), pltpu.VMEM((D, LEN), jnp.bfloat16)]
        + [pltpu.VMEM((D, MLEN), jnp.bfloat16), pltpu.VMEM((LEN, D), jnp.float32)] * cross
        + [pltpu.VMEM((D, cols), jnp.bfloat16)] * 4
        + [
            pltpu.VMEM((LEN, cols), jnp.bfloat16),
            pltpu.VMEM((cols, MLEN), jnp.bfloat16),
            pltpu.VMEM((128, LEN), jnp.float32),
            pltpu.VMEM((cols, LEN), jnp.bfloat16),
            pltpu.VMEM((LEN, cols), jnp.bfloat16),
            pltpu.VMEM((MLEN, cols), jnp.float32),
            pltpu.VMEM((MLEN, cols), jnp.float32),
            pltpu.VMEM((MLEN, cols), jnp.bfloat16),
            pltpu.VMEM((MLEN, cols), jnp.bfloat16),
        ],
        compiler_params=pltpu.CompilerParams(vmem_limit_bytes=BACKWARD_MEGA * MEGA),
        cost_estimate=KERNEL_COST,
    )(*scalars, *wholes, weights, *kept)


def add_to(ref, step, update):
    @pl.when(step == 0)
    def _():
        ref[...] = update

    @pl.when(step != 0)
    def _():
        ref[...] = ref[...] + update


def turn(values):
    return values.T


def gelu_pieces(values):
    factor = 0.7978845608028654
    square = values * values
    slope = jnp.tanh(factor * values * (1.0 + 0.044715 * square))
    half = 0.5 * (1.0 + slope)
    grad = half + 0.5 * values * (1.0 - slope * slope) * factor * (1.0 + 3 * 0.044715 * square)
    return values * half, grad


def expert_kernel(
    core_ref,
    mine,
    theirs,
    part_mine,
    part_theirs,
    first_sum,
    norms,
    w_ref,
    sum_out,
    grad_ref,
    out_keep,
    out_give,
    w_grad_ref,
    sum_ref,
    rows,
    rows_turned,
    up,
    up_turned,
    out_total,
    sem,
):
    step = pl.program_id(0)
    leaving = pltpu.make_async_copy(sum_ref, sum_out, sem)

    @pl.when(step == 0)
    def _():
        total = first_sum[...] + (part_mine[...] + part_theirs[...])
        sum_ref[...] = total
        leaving.start()
        unit, _ = standardize(total)
        normed = unit * norms[4:5, :] + norms[5:6, :]
        rows[...] = low(normed)
        rows_turned[...] = turn(rows[...])
        for source, other in ((mine, False), (theirs, True)):
            at = half_at(core_ref, other)
            up[at, :] = source[...]
            up_turned[:, at] = low(turn(source[...]))

    shape = (D, w_ref.shape[4])
    w_in, w_out = w_ref[:, 0, 0].reshape(shape), w_ref[:, 0, 1].reshape(shape)
    hidden, slope = gelu_pieces(mm(rows[...], w_in))
    hidden = low(hidden)
    inner_grad = low(slope * mm(up[...], w_out))
    grads = w_grad_ref.shape[0], -1, w_ref.shape[4]
    w_grad_ref[:, 0, 0] = low(mm(rows_turned[...], inner_grad)).reshape(grads)
    w_grad_ref[:, 0, 1] = low(mm(up_turned[...], hidden)).reshape(grads)
    add_to(grad_ref, step, mt(inner_grad, w_in))
    add_to(out_total, step, mt(hidden, w_out))

    @pl.when(step == pl.num_programs(0) - 1)
    def _():
        at = half_at(core_ref, False)
        out_keep[...] = sum_ref[at, :] + out_total[at, :]
        out_give[...] = out_total[half_at(core_ref, True), :]
        leaving.wait()


def expert_layer(scalars, wholes, weights):
    owners, steps, _, rows, cols = weights.shape
    whole = jax.ShapeDtypeStruct((LEN, D), jnp.float32)
    half = jax.ShapeDtypeStruct((LEN // 2, D), jnp.float32)
    w_spec = pl.BlockSpec((owners, 1, 2, rows, cols), lambda step: (0, step, 0, 0, 0))
    return pl.pallas_call(
        expert_kernel,
        name="expert",
        grid=(steps,),
        out_shape=(
            whole,
            whole,
            half,
            half,
            jax.ShapeDtypeStruct(weights.shape, jnp.bfloat16),
        ),
        in_specs=[SCALARS] * len(scalars) + [WHOLE] * len(wholes) + [w_spec],
        out_specs=(OUTSIDE,) + (WHOLE,) * 3 + (w_spec,),
        scratch_shapes=[
            pltpu.VMEM((LEN, D), jnp.float32),
            pltpu.VMEM((LEN, D), jnp.bfloat16),
            pltpu.VMEM((D, LEN), jnp.bfloat16),
            pltpu.VMEM((LEN, D), jnp.bfloat16),
            pltpu.VMEM((D, LEN), jnp.bfloat16),
            pltpu.VMEM((LEN, D), jnp.float32),
            pltpu.SemaphoreType.DMA,
        ],
        compiler_params=pltpu.CompilerParams(vmem_limit_bytes=EXPERT_MEGA * MEGA),
        cost_estimate=KERNEL_COST,
    )(*scalars, *wholes, weights)


def fetch_kernel(chosen, w_ref, out_ref):
    half = w_ref.shape[3] // 2
    for core in (0, 1):
        out_ref[0, core, 0] = low(w_ref[0, :, :, core * half : (core + 1) * half])


def pack_experts(chip_expert, weights, plane_count, tensor_count):
    _, pair, rows, cols = weights.shape
    out = (plane_count, 2, tensor_count, pair, rows, cols // 2)
    return pl.pallas_call(
        fetch_kernel,
        name="pack_experts",
        out_shape=jax.ShapeDtypeStruct(out, jnp.bfloat16),
        grid_spec=pltpu.PrefetchScalarGridSpec(
            num_scalar_prefetch=1,
            grid=(plane_count * tensor_count,),
            in_specs=[
                pl.BlockSpec((1, pair, rows, cols), lambda row, chosen: (chosen[row], 0, 0, 0))
            ],
            out_specs=pl.BlockSpec(
                (1, 2, 1, pair, rows, cols // 2),
                lambda row, chosen: (row // tensor_count, 0, row % tensor_count, 0, 0, 0),
            ),
        ),
        cost_estimate=KERNEL_COST,
    )(chip_expert, weights)


def lamb_update(weight, moment, second, grad):
    moment = beta_one * moment + (1.0 - beta_one) * grad
    second = beta_two * second + (1.0 - beta_two) * grad * grad
    update = (
        moment / (1.0 - beta_one**STEP) / (jnp.sqrt(second / (1.0 - beta_two**STEP)) + epsilon)
        + decay * weight
    )
    return moment, second, update


def expert_lamb_kernel(
    chosen, grads, w_ref, m_ref, v_ref, m_out, v_out, u_out, squares, total
):
    expert = pl.program_id(0)
    half = grads.shape[5]
    total[...] = jnp.zeros_like(total)
    for plane in range(grads.shape[0]):
        for place in range(grads.shape[2]):

            @pl.when(chosen[plane * grads.shape[2] + place] == expert)
            def _(plane=plane, place=place):
                for core in (0, 1):
                    at = slice(core * half, (core + 1) * half)
                    total[:, :, at] = total[:, :, at] + grads[plane, core, place].astype(
                        jnp.float32
                    )

    weight = w_ref[0]
    m_out[0], v_out[0], update = lamb_update(weight, m_ref[0], v_ref[0], total[...])
    u_out[0] = update
    squares[0] = jnp.concatenate(
        [jnp.sum(weight * weight, 1), jnp.sum(update * update, 1)], 0
    )


def expert_lamb(chip_expert, grads, weights, moments, seconds):
    experts, pair, rows, cols = weights.shape
    spec = pl.BlockSpec((1, pair, rows, cols), lambda expert, chosen: (expert, 0, 0, 0))
    return pl.pallas_call(
        expert_lamb_kernel,
        name="expert_lamb",
        out_shape=(jax.ShapeDtypeStruct(weights.shape, jnp.float32),) * 3
        + (jax.ShapeDtypeStruct((experts, 2 * pair, cols), jnp.float32),),
        grid_spec=pltpu.PrefetchScalarGridSpec(
            num_scalar_prefetch=1,
            grid=(experts,),
            in_specs=[WHOLE, spec, spec, spec],
            out_specs=(spec, spec, spec)
            + (pl.BlockSpec((1, 2 * pair, cols), lambda expert, chosen: (expert, 0, 0)),),
            scratch_shapes=[pltpu.VMEM((pair, rows, cols), jnp.float32)],
        ),
        compiler_params=pltpu.CompilerParams(vmem_limit_bytes=16 * MEGA),
        cost_estimate=KERNEL_COST,
    )(chip_expert, grads, weights, moments, seconds)


DEVICES = ("plane", "core", "tensor")
CHIP = ("core", "tensor")


def twin(values):
    return lax.ppermute(values, "core", ((0, 1), (1, 0)))


def exchange(values, axes):
    return lax.all_to_all(values, axes, 0, 0, tiled=True)


def swap_pairs(plane_count, tensor_count):
    pairs = []
    for plane in range(plane_count):
        for core in range(2):
            for place in range(tensor_count):
                target = (plane * 2 + place % 2) * tensor_count + place // 2 * 2 + core
                pairs.append(((plane * 2 + core) * tensor_count + place, target))
    return pairs


def to_planes(parts):
    count = lax.axis_size("plane")
    mine = lax.axis_index("plane")
    got = [lax.dynamic_index_in_dim(parts, mine, 0, False)]
    for step in range(1, count):
        there = lax.dynamic_index_in_dim(parts, mine ^ step, 0, False)
        got.append(lax.ppermute(there, "plane", [(k, k ^ step) for k in range(count)]))
    return got


def fetch_chip(attn_low):
    rows, cols = attn_low.shape[2:]
    tensor_count = lax.axis_size("tensor")
    parts = attn_low.reshape(2, 2, 2, rows, 2, cols // 2)
    odd = lax.axis_index("tensor") % 2
    parts = jnp.where(odd == 0, parts, parts[:, ::-1])
    parts = parts.transpose(4, 0, 2, 3, 1, 5).reshape(2, 1, 2, 2, rows, cols)
    parts = jnp.broadcast_to(parts, (2, tensor_count, 2, 2, rows, cols))
    chips = exchange(parts.reshape(2 * tensor_count, 2, 2, rows, cols), CHIP)
    return chips.transpose(1, 0, 2, 3, 4)


def fetch_planes(chips):
    count = lax.axis_size("plane")
    mine = lax.axis_index("plane")
    got = [chips] + [
        lax.ppermute(chips, "plane", [(k, k ^ step) for k in range(count)])
        for step in range(1, count)
    ]
    got = jnp.stack(got)
    order = jnp.arange(count) ^ mine
    got = got[order]
    rows, cols = chips.shape[2:]
    return got.reshape(count * 2, chips.shape[0] // 2, 2, rows, cols)


def sum_planes(grads):
    _, heads, _, rows, cols = grads.shape
    count = lax.axis_size("plane")
    got = to_planes(grads.reshape(count, 2 * heads, 2, rows, cols))
    return low(sum(part.astype(jnp.float32) for part in got))


def sum_chips(parts):
    rows, cols = parts.shape[3:]
    chips = exchange(parts, CHIP)
    total = chips.reshape(2, -1, 2, 2, rows, 2, cols // 2).astype(jnp.float32).sum(1)
    total = total.transpose(1, 4, 2, 3, 0, 5)
    odd = lax.axis_index("tensor") % 2
    return jnp.where(odd == 0, total, total[:, ::-1]).reshape(2, 4, rows, cols)


def sum_devices(values):
    def over(axis, flip):
        count = lax.axis_size(axis)
        return lax.ppermute(values, axis, [(k, k ^ flip) for k in range(count)])

    for axis in ("core", "plane", "tensor"):
        flip = 1
        while flip < lax.axis_size(axis):
            values = values + over(axis, flip)
            flip *= 2
    return values


def body_rows(
    tokens,
    memory,
    cotangent,
    tgt_lengths,
    mem_lengths,
    mem_keep,
    row_expert,
    attn_weights,
    attn_moment,
    attn_second,
    expert_weights,
    expert_moment,
    expert_second,
    norm_params,
    norm_moment,
    norm_second,
):
    plane_count, tensor_count = lax.axis_size("plane"), lax.axis_size("tensor")
    devices = plane_count * 2 * tensor_count
    core, place = lax.axis_index("core"), lax.axis_index("tensor")
    moves = swap_pairs(plane_count, tensor_count)

    def swap(values):
        return lax.ppermute(values, DEVICES, moves)

    norm_rows = norm_params.shape[1]
    small = jnp.concatenate([norm_params.reshape(-1), row_expert.astype(jnp.float32)])
    small = exchange(
        jnp.broadcast_to(small[None], (plane_count * 2, small.shape[0])), ("plane", "core")
    )
    norms = small[:, : 6 * norm_rows].reshape(-1, 6, norm_rows).transpose(1, 0, 2).reshape(6, D)
    owner_expert = small[:, 6 * norm_rows :].astype(jnp.int32)
    chip_expert = owner_expert.reshape(plane_count, 2, 2).transpose(0, 2, 1).reshape(-1)
    chips = fetch_chip(attn_weights.astype(jnp.bfloat16))
    self_weights = fetch_planes(chips[0])
    tokens_mine = swap(tokens)
    tokens_theirs = twin(tokens_mine)

    facts = jnp.concatenate([tgt_lengths, mem_lengths, mem_keep], 1)
    facts = jnp.where(core == place % 2, facts, twin(facts))
    facts = lax.dynamic_slice_in_dim(facts, place // 2, 1, 0)
    facts, keep = facts[:, :16], facts[:, 16:]
    core_ref = core.reshape(1, 1)

    hidden_cols = expert_weights.shape[3] // 2
    chosen = pack_experts(chip_expert, expert_weights, plane_count, tensor_count)
    chosen = exchange(chosen.reshape(devices, 2, -1, hidden_cols), DEVICES)
    chosen = chosen.reshape(plane_count * 2, tensor_count, 2, -1, hidden_cols)
    cross_weights = fetch_planes(chips[1])
    memory_mine = swap(memory)
    memory_theirs = twin(memory_mine)
    up_mine = swap(cotangent)
    up_theirs = twin(up_mine)

    self_part, *self_kept = attn_forward(
        "self_forward",
        self_forward_kernel,
        (core_ref, facts),
        (tokens_mine, tokens_theirs, norms),
        self_weights,
        False,
    )
    cross_part, first_sum, *cross_kept = attn_forward(
        "cross_forward",
        cross_forward_kernel,
        (core_ref, facts),
        (
            keep,
            tokens_mine,
            tokens_theirs,
            self_part,
            twin(self_part),
            memory_mine,
            memory_theirs,
            norms,
        ),
        cross_weights,
        True,
    )
    second_sum, ffn_part, out_keep, out_give, row_grad = expert_layer(
        (core_ref,),
        (up_mine, up_theirs, cross_part, twin(cross_part), first_sum, norms),
        chosen,
    )
    layer_out = swap((out_keep + twin(out_give)).astype(jnp.bfloat16))
    row_grad = exchange(row_grad.reshape(devices, 2, -1, hidden_cols), DEVICES)
    row_grad = row_grad.reshape(plane_count, 2, tensor_count, 2, -1, hidden_cols)
    grad_cross, cross_part, memory_keep, memory_give, cross_grad, ffn_norm = attn_backward(
        "cross_backward",
        cross_backward_kernel,
        (core_ref, facts),
        (
            keep.reshape(-1, 1),
            up_mine,
            up_theirs,
            ffn_part,
            twin(ffn_part),
            second_sum,
            memory_mine,
            memory_theirs,
            norms,
        ),
        cross_weights,
        cross_kept,
        True,
    )
    cross_grad = sum_planes(cross_grad)
    memory_grad = swap((memory_keep + twin(memory_give)).astype(jnp.bfloat16))
    own_grad, part_keep, part_give, self_grad, norm_grad = attn_backward(
        "self_backward",
        self_backward_kernel,
        (core_ref, facts),
        (
            grad_cross,
            cross_part,
            twin(cross_part),
            first_sum,
            tokens_mine,
            tokens_theirs,
            ffn_norm,
            norms,
        ),
        self_weights,
        self_kept,
        False,
    )
    self_grad = sum_planes(self_grad)
    attn_shard = sum_chips(jnp.stack([self_grad, cross_grad], 1))
    back, _, _ = norm_back(
        tokens_mine.astype(jnp.float32), part_keep + twin(part_give), norms[0:1]
    )
    input_grad = swap((own_grad + back).astype(jnp.bfloat16))
    norm_total = sum_devices(norm_grad)
    owner = (lax.axis_index("plane") * 2 + core) * norm_rows
    norm_shard = lax.dynamic_slice_in_dim(norm_total, owner, norm_rows, 1)
    expert_moment_new, expert_second_new, expert_update, expert_squares = expert_lamb(
        chip_expert, row_grad, expert_weights, expert_moment, expert_second
    )
    attn_moment_new, attn_second_new, attn_update = lamb_update(
        attn_weights, attn_moment, attn_second, attn_shard
    )
    norm_moment_new, norm_second_new, norm_update = lamb_update(
        norm_params, norm_moment, norm_second, norm_shard
    )
    share = 1.0 / tensor_count
    expert_squares = expert_squares.sum(-1).reshape(E, 2, 2)
    squares = jnp.concatenate(
        [
            jnp.sum(attn_weights * attn_weights, (2, 3)).reshape(-1),
            expert_squares[:, 0].reshape(-1),
            jnp.sum(norm_params * norm_params, 1) * share,
            jnp.sum(attn_update * attn_update, (2, 3)).reshape(-1),
            expert_squares[:, 1].reshape(-1),
            jnp.sum(norm_update * norm_update, 1) * share,
        ]
    )
    count = squares.shape[0] // 2
    squares = exchange(jnp.broadcast_to(squares[None], (devices, 2 * count)), DEVICES).sum(0)
    lamb_norms = jnp.sqrt(squares).reshape(2, count)
    step_size = rate * (lamb_norms[0] / lamb_norms[1])
    attn_step = step_size[:8].reshape(2, 4, 1, 1)
    expert_step = step_size[8 : 8 + 2 * E].reshape(E, 2, 1, 1)
    norm_step = step_size[8 + 2 * E :].reshape(6, 1)
    return (
        layer_out,
        input_grad,
        memory_grad,
        attn_weights - attn_step * attn_update,
        attn_moment_new,
        attn_second_new,
        expert_weights - expert_step * expert_update,
        expert_moment_new,
        expert_second_new,
        norm_params - norm_step * norm_update,
        norm_moment_new,
        norm_second_new,
        lamb_norms,
    )


def specs(rows, dp):
    tokens = P((*dp, "tensor"), None)
    matrix = P(None, None, dp, "tensor")
    row_items = (P(dp, None),) * 3 + (P(dp),)
    return dict(
        in_specs=(tokens,) * 3 + row_items + (matrix,) * 6 + (P(None, dp),) * 3,
        out_specs=(tokens,) * 3 + (matrix,) * 6 + (P(None, dp),) * 3 + (P(),),
        check_vma=False,
    )


def solution(mesh):
    def run(*args):
        rows = args[3].shape[0]
        dp_count, tensor_count = mesh.shape["dp"], mesh.shape["tensor"]
        if rows // dp_count * 2 == tensor_count and tensor_count % 2 == 0:
            fine = Mesh(
                mesh.devices.reshape(dp_count // 2, 2, tensor_count), ("plane", "core", "tensor")
            )
            return jax.shard_map(body_rows, mesh=fine, **specs(rows, ("plane", "core")))(*args)
        return jax.shard_map(body, mesh=mesh, **specs(rows, ("dp",)))(*args)

    return run
```

```python
import jax
import jax.numpy as jnp
from jax import lax
from jax.experimental import pallas as pl
from jax.experimental.pallas import tpu as pltpu
from jax.sharding import Mesh
from jax.sharding import PartitionSpec as P

D = 512
HD = 64
E = 16
LEN = 1024
MLEN = 1024
STEP = 10


beta_one = 0.9
beta_two = 0.999
epsilon = 1e-06
decay = 0.01
rate = 0.2


def norm_layer(values, gain_vec, shift_vec):
    centered = values - jnp.mean(values, -1, keepdims=True)
    variance = jnp.mean(centered * centered, -1, keepdims=True)
    return centered * lax.rsqrt(variance + 1e-05) * gain_vec + shift_vec


def doc_numbers(lengths, length_total):
    doc_ends = jnp.cumsum(lengths)
    places = jnp.arange(length_total, dtype=jnp.int32)
    numbers = jnp.sum((places[:, None] >= doc_ends[None, :]).astype(jnp.int32), 1)
    starts = doc_ends - lengths
    opening = jnp.any(places[:, None] == starts[None, :], 1)
    return (numbers, opening)


def build_allowed(tgt_len, mem_len, keep_row, cross):
    doc_ids, _ = doc_numbers(tgt_len, LEN)
    if cross:
        mem_docs, opening = doc_numbers(mem_len, MLEN)
        return (doc_ids[:, None] == mem_docs[None, :]) & ((keep_row == 1) | opening)[None, :]
    places = jnp.arange(LEN, dtype=jnp.int32)
    return (doc_ids[:, None] == doc_ids[None, :]) & (places[None, :] <= places[:, None])


def gather_rows(values):
    return lax.all_gather(values, "tensor", axis=0, tiled=True)


def spread_rows(values):
    return lax.psum_scatter(values, "tensor", scatter_dimension=0, tiled=True)


def project(left_side, right_side):
    return jnp.dot(left_side, right_side, preferred_element_type=jnp.float32)


def project_back(left_side, right_side):
    return lax.dot_general(
        left_side, right_side, (((1,), (1,)), ((), ())), preferred_element_type=jnp.float32
    )


def outer_grad(left_side, right_side):
    return lax.dot_general(
        left_side, right_side, (((0,), (0,)), ((), ())), preferred_element_type=jnp.float32
    )


def attend_one(queries, key_rows, value_rows, allowed):
    head_count = queries.shape[1] // HD
    keys_h = key_rows.reshape(key_rows.shape[0], head_count, HD)
    values_h = value_rows.reshape(value_rows.shape[0], head_count, HD)
    block_rows = min(LEN, 512)
    outputs = []
    totals = []
    for begin_at in range(0, LEN, block_rows):
        queries_h = queries[begin_at : begin_at + block_rows].reshape(block_rows, head_count, HD)
        scores = jnp.einsum(
            "qhd,khd->hqk", queries_h, keys_h, preferred_element_type=jnp.float32
        ) * HD ** (-0.5)
        scores = jnp.where(allowed[None, begin_at : begin_at + block_rows], scores, -1e30)
        top_score = jnp.max(scores, -1, keepdims=True)
        weights = jnp.exp(scores - top_score)
        row_total = jnp.sum(weights, -1, keepdims=True)
        prob_low = (weights / row_total).astype(jnp.bfloat16)
        blended = jnp.einsum("hqk,khd->qhd", prob_low, values_h, preferred_element_type=jnp.float32)
        outputs.append(blended.reshape(block_rows, head_count * HD))
        totals.append((top_score + jnp.log(row_total))[..., 0])
    return (jnp.concatenate(outputs, 0), jnp.concatenate(totals, 1))


def attend_back_one(queries, key_rows, value_rows, upstream, log_totals, allowed):
    head_count = queries.shape[1] // HD
    scale = HD ** (-0.5)
    keys_h = key_rows.reshape(key_rows.shape[0], head_count, HD)
    values_h = value_rows.reshape(value_rows.shape[0], head_count, HD)
    key_grad = jnp.zeros(keys_h.shape, jnp.float32)
    value_grad = jnp.zeros(values_h.shape, jnp.float32)
    block_rows = min(LEN, 512)
    query_grads = []
    for begin_at in range(0, LEN, block_rows):
        queries_h = queries[begin_at : begin_at + block_rows].reshape(block_rows, head_count, HD)
        upstream_h = upstream[begin_at : begin_at + block_rows].reshape(block_rows, head_count, HD)
        scores = (
            jnp.einsum("qhd,khd->hqk", queries_h, keys_h, preferred_element_type=jnp.float32)
            * scale
        )
        scores = jnp.where(allowed[None, begin_at : begin_at + block_rows], scores, -1e30)
        probs_full = jnp.exp(scores - log_totals[:, begin_at : begin_at + block_rows, None])
        prob_grad = jnp.einsum(
            "qhd,khd->hqk", upstream_h, values_h, preferred_element_type=jnp.float32
        )
        weighted = jnp.sum(probs_full * prob_grad, -1, keepdims=True)
        score_grad = (probs_full * (prob_grad - weighted)).astype(jnp.bfloat16)
        query_part = (
            jnp.einsum("hqk,khd->qhd", score_grad, keys_h, preferred_element_type=jnp.float32)
            * scale
        )
        query_grads.append(query_part.astype(jnp.bfloat16).reshape(block_rows, head_count * HD))
        key_grad = (
            key_grad
            + jnp.einsum("hqk,qhd->khd", score_grad, queries_h, preferred_element_type=jnp.float32)
            * scale
        )
        value_grad = value_grad + jnp.einsum(
            "hqk,qhd->khd",
            probs_full.astype(jnp.bfloat16),
            upstream_h,
            preferred_element_type=jnp.float32,
        )
    width = head_count * HD
    return (
        jnp.concatenate(query_grads, 0),
        key_grad.astype(jnp.bfloat16).reshape(-1, width),
        value_grad.astype(jnp.bfloat16).reshape(-1, width),
    )


def attend_rows(queries, key_rows, value_rows, tgt_lengths, mem_lengths, mem_keep, cross):
    row_count = tgt_lengths.shape[0]
    width = queries.shape[1]

    def one_row(row_item):
        row_q, row_k, row_v, tgt_len, mem_len, keep_row = row_item
        return attend_one(row_q, row_k, row_v, build_allowed(tgt_len, mem_len, keep_row, cross))

    blended, log_totals = lax.map(
        one_row,
        (
            queries.reshape(row_count, LEN, width),
            key_rows.reshape(row_count, -1, width),
            value_rows.reshape(row_count, -1, width),
            tgt_lengths,
            mem_lengths,
            mem_keep,
        ),
    )
    return (blended.reshape(row_count * LEN, width), log_totals)


def attend_back_rows(
    queries, key_rows, value_rows, upstream, log_totals, tgt_lengths, mem_lengths, mem_keep, cross
):
    row_count = tgt_lengths.shape[0]
    width = queries.shape[1]

    def one_row(row_item):
        row_q, row_k, row_v, row_up, row_log, tgt_len, mem_len, keep_row = row_item
        return attend_back_one(
            row_q, row_k, row_v, row_up, row_log, build_allowed(tgt_len, mem_len, keep_row, cross)
        )

    query_grad, key_grad, value_grad = lax.map(
        one_row,
        (
            queries.reshape(row_count, LEN, width),
            key_rows.reshape(row_count, -1, width),
            value_rows.reshape(row_count, -1, width),
            upstream.reshape(row_count, LEN, width),
            log_totals,
            tgt_lengths,
            mem_lengths,
            mem_keep,
        ),
    )
    return (
        query_grad.reshape(-1, width),
        key_grad.reshape(-1, width),
        value_grad.reshape(-1, width),
    )


def lamb_pieces(weight, moment, second, grad, axes):
    moment = beta_one * moment + (1.0 - beta_one) * grad
    second = beta_two * second + (1.0 - beta_two) * grad * grad
    update = (
        moment / (1.0 - beta_one**STEP) / (jnp.sqrt(second / (1.0 - beta_two**STEP)) + epsilon)
        + decay * weight
    )
    return (moment, second, update, jnp.sum(weight * weight, axes), jnp.sum(update * update, axes))


def body(
    tokens,
    memory,
    cotangent,
    tgt_lengths,
    mem_lengths,
    mem_keep,
    row_expert,
    attn_weights,
    attn_moment,
    attn_second,
    expert_weights,
    expert_moment,
    expert_second,
    norm_params,
    norm_moment,
    norm_second,
):
    row_count = tgt_lengths.shape[0]
    attn_low, expert_low = (
        lax.all_gather(attn_weights.astype(jnp.bfloat16), "dp", axis=2, tiled=True),
        lax.all_gather(expert_weights.astype(jnp.bfloat16), "dp", axis=2, tiled=True),
    )
    row_low = expert_low[row_expert]
    norms = lax.all_gather(norm_params, "dp", axis=1, tiled=True)
    residual = tokens.astype(jnp.float32)
    normed_self, back_self = jax.vjp(norm_layer, residual, norms[0], norms[1])
    self_rows = gather_rows(normed_self.astype(jnp.bfloat16))
    self_qkv = jnp.einsum(
        "td,jdc->jtc", self_rows, attn_low[0, :3], preferred_element_type=jnp.float32
    ).astype(jnp.bfloat16)
    self_mix, self_log = attend_rows(
        self_qkv[0], self_qkv[1], self_qkv[2], tgt_lengths, mem_lengths, mem_keep, False
    )
    self_low = self_mix.astype(jnp.bfloat16)
    first_sum = residual + spread_rows(project_back(self_low, attn_low[0, 3]))
    normed_cross, back_cross = jax.vjp(norm_layer, first_sum, norms[2], norms[3])
    cross_rows = gather_rows(normed_cross.astype(jnp.bfloat16))
    memory_rows = gather_rows(memory)
    cross_queries = project(cross_rows, attn_low[1, 0]).astype(jnp.bfloat16)
    cross_kv = jnp.einsum(
        "td,jdc->jtc", memory_rows, attn_low[1, 1:3], preferred_element_type=jnp.float32
    ).astype(jnp.bfloat16)
    cross_mix, cross_log = attend_rows(
        cross_queries, cross_kv[0], cross_kv[1], tgt_lengths, mem_lengths, mem_keep, True
    )
    cross_low = cross_mix.astype(jnp.bfloat16)
    second_sum = first_sum + spread_rows(project_back(cross_low, attn_low[1, 3]))
    normed_ffn, back_ffn = jax.vjp(norm_layer, second_sum, norms[4], norms[5])
    ffn_rows = gather_rows(normed_ffn.astype(jnp.bfloat16))

    def expert_forward(row_item):
        row_in, chosen = row_item
        inner_act = project(row_in, chosen[0])
        hidden = jax.nn.gelu(inner_act).astype(jnp.bfloat16)
        return (inner_act, project_back(hidden, chosen[1]))

    inner_all, branch_all = lax.map(expert_forward, (ffn_rows.reshape(row_count, LEN, D), row_low))
    layer_out = (second_sum + spread_rows(branch_all.reshape(row_count * LEN, D))).astype(
        jnp.bfloat16
    )
    grad_ffn = cotangent.astype(jnp.float32)
    upstream_ffn = gather_rows(cotangent)
    ffn_again = gather_rows(normed_ffn.astype(jnp.bfloat16))

    def expert_backward(row_item):
        row_in, inner_act, upstream, chosen = row_item
        hidden, gelu_back = jax.vjp(jax.nn.gelu, inner_act)
        inner_grad = gelu_back(project(upstream, chosen[1]))[0].astype(jnp.bfloat16)
        pair_grads = jnp.stack(
            [outer_grad(row_in, inner_grad), outer_grad(upstream, hidden.astype(jnp.bfloat16))]
        )
        return (pair_grads, project_back(inner_grad, chosen[0]))

    row_grads, ffn_part = lax.map(
        expert_backward,
        (
            ffn_again.reshape(row_count, LEN, D),
            inner_all,
            upstream_ffn.reshape(row_count, LEN, D),
            row_low,
        ),
    )
    normed_ffn_grad = spread_rows(ffn_part.reshape(row_count * LEN, D))
    back_tokens, gain_ffn, shift_ffn = back_ffn(normed_ffn_grad)
    grad_cross = grad_ffn + back_tokens
    upstream_cross = gather_rows(grad_cross.astype(jnp.bfloat16))
    cross_again = gather_rows(normed_cross.astype(jnp.bfloat16))
    memory_again = gather_rows(memory)
    cross_up = project(upstream_cross, attn_low[1, 3]).astype(jnp.bfloat16)
    cross_dq, cross_dk, cross_dv = attend_back_rows(
        cross_queries,
        cross_kv[0],
        cross_kv[1],
        cross_up,
        cross_log,
        tgt_lengths,
        mem_lengths,
        mem_keep,
        True,
    )
    cross_grads = jnp.stack(
        [
            outer_grad(cross_again, cross_dq),
            outer_grad(memory_again, cross_dk),
            outer_grad(memory_again, cross_dv),
            outer_grad(upstream_cross, cross_low),
        ]
    )
    normed_cross_grad, memory_total = (
        lax.psum_scatter(
            project_back(cross_dq, attn_low[1, 0]), "tensor", scatter_dimension=0, tiled=True
        ),
        lax.psum_scatter(
            project_back(cross_dk, attn_low[1, 1]) + project_back(cross_dv, attn_low[1, 2]),
            "tensor",
            scatter_dimension=0,
            tiled=True,
        ),
    )
    back_tokens, gain_cross, shift_cross = back_cross(normed_cross_grad)
    grad_self = grad_cross + back_tokens
    upstream_self = gather_rows(grad_self.astype(jnp.bfloat16))
    self_again = gather_rows(normed_self.astype(jnp.bfloat16))
    self_up = project(upstream_self, attn_low[0, 3]).astype(jnp.bfloat16)
    self_dq, self_dk, self_dv = attend_back_rows(
        self_qkv[0],
        self_qkv[1],
        self_qkv[2],
        self_up,
        self_log,
        tgt_lengths,
        mem_lengths,
        mem_keep,
        False,
    )
    self_grads = jnp.stack(
        [
            outer_grad(self_again, self_dq),
            outer_grad(self_again, self_dk),
            outer_grad(self_again, self_dv),
            outer_grad(upstream_self, self_low),
        ]
    )
    normed_self_grad = spread_rows(
        project_back(self_dq, attn_low[0, 0])
        + project_back(self_dk, attn_low[0, 1])
        + project_back(self_dv, attn_low[0, 2])
    )
    back_tokens, gain_self, shift_self = back_self(normed_self_grad)
    input_grad = (grad_self + back_tokens).astype(jnp.bfloat16)
    attn_grad = jnp.stack([self_grads, cross_grads])
    norm_grad = jnp.stack([gain_self, shift_self, gain_cross, shift_cross, gain_ffn, shift_ffn])
    norm_total = lax.psum(norm_grad, "tensor")
    selector = (row_expert[:, None] == jnp.arange(E, dtype=jnp.int32)[None, :]).astype(jnp.float32)
    expert_grad = jnp.einsum("re,rjdf->ejdf", selector, row_grads, precision=lax.Precision.HIGHEST)
    expert_shard = lax.psum_scatter(expert_grad, "dp", scatter_dimension=2, tiled=True)
    attn_shard, norm_shard = (
        lax.psum_scatter(attn_grad, "dp", scatter_dimension=2, tiled=True),
        lax.psum_scatter(norm_total, "dp", scatter_dimension=1, tiled=True),
    )
    attn_pieces = lamb_pieces(attn_weights, attn_moment, attn_second, attn_shard, (2, 3))
    expert_pieces = lamb_pieces(expert_weights, expert_moment, expert_second, expert_shard, (2, 3))
    norm_pieces = lamb_pieces(norm_params, norm_moment, norm_second, norm_shard, (1,))
    copy_share = 1.0 / lax.axis_size("tensor")
    weight_squares = jnp.concatenate(
        [attn_pieces[3].reshape(-1), expert_pieces[3].reshape(-1), norm_pieces[3] * copy_share]
    )
    update_squares = jnp.concatenate(
        [attn_pieces[4].reshape(-1), expert_pieces[4].reshape(-1), norm_pieces[4] * copy_share]
    )
    weight_total, update_total = lax.psum((weight_squares, update_squares), ("dp", "tensor"))
    weight_norm = jnp.sqrt(weight_total)
    update_norm = jnp.sqrt(update_total)
    trust_ratio = weight_norm / update_norm
    attn_ratio = trust_ratio[:8].reshape(2, 4, 1, 1)
    expert_ratio = trust_ratio[8 : 8 + 2 * E].reshape(E, 2, 1, 1)
    norm_ratio = trust_ratio[8 + 2 * E :].reshape(6, 1)
    attn_new = attn_weights - rate * attn_ratio * attn_pieces[2]
    expert_new = expert_weights - rate * expert_ratio * expert_pieces[2]
    norm_new = norm_params - rate * norm_ratio * norm_pieces[2]
    lamb_norms = jnp.stack([weight_norm, update_norm])
    return (
        layer_out,
        input_grad,
        memory_total.astype(jnp.bfloat16),
        attn_new,
        attn_pieces[0],
        attn_pieces[1],
        expert_new,
        expert_pieces[0],
        expert_pieces[1],
        norm_new,
        norm_pieces[0],
        norm_pieces[1],
        lamb_norms,
    )


MEGA = 1024 * 1024
QUERY_BLOCK = 256
WINDOW_STEP = 256
KERNEL_MEGA = 52
PART = jnp.bfloat16
SUM = jnp.bfloat16
HALVES = (slice(0, LEN // 2), slice(LEN // 2, LEN))
KERNEL_COST = pl.CostEstimate(flops=10**6, bytes_accessed=1024, transcendentals=0)
WHOLE = pl.BlockSpec(memory_space=pltpu.VMEM)
OUTSIDE = pl.BlockSpec(memory_space=pltpu.HBM)


def outside(shape, dtype):
    return pltpu.HBM(shape, dtype)


def stay_outside(arrays):
    return [pltpu.with_memory_space_constraint(array, pltpu.HBM) for array in arrays]


SCALARS = pl.BlockSpec(memory_space=pltpu.SMEM)


def mm(left, right):
    return lax.dot_general(left, right, (((1,), (0,)), ((), ())), preferred_element_type=jnp.float32)


def mt(left, right):
    return lax.dot_general(left, right, (((1,), (1,)), ((), ())), preferred_element_type=jnp.float32)


def low(values):
    return values.astype(jnp.bfloat16)


def standardize(values):
    centered = values - jnp.mean(values, -1, keepdims=True)
    inverse = lax.rsqrt(jnp.mean(centered * centered, -1, keepdims=True) + 1e-05)
    return centered * inverse, inverse


def norm_back(values, grad, gain_vec):
    unit, inverse = standardize(values)
    inner = grad * gain_vec
    back = inverse * (
        inner
        - jnp.mean(inner, -1, keepdims=True)
        - unit * jnp.mean(inner * unit, -1, keepdims=True)
    )
    return back, jnp.sum(grad * unit, 0, keepdims=True), jnp.sum(grad, 0, keepdims=True)


def key_limits(facts, places, cross):
    zero = jnp.zeros(places.shape, jnp.int32)
    low_end, high_end, doc_end = zero, zero, 0
    for doc in range(8):
        begin, doc_end = doc_end, doc_end + facts[0, doc]
        if cross:
            low_end = low_end + jnp.where(places >= doc_end, facts[0, 8 + doc], 0)
            high_end = high_end + jnp.where(places >= begin, facts[0, 8 + doc], 0)
        else:
            low_end = jnp.where(places >= doc_end, doc_end, low_end)
    return low_end, (high_end if cross else places + 1)


def kept_keys(facts, keep, places):
    kept = keep == 1
    begin = 0
    for doc in range(8):
        kept = kept | (places == begin)
        begin = begin + facts[0, 8 + doc]
    return kept


def key_windows(facts, cross, run):
    def block(index, _):
        first_query = pl.multiple_of(index * QUERY_BLOCK, QUERY_BLOCK)
        lowest, _ = key_limits(facts, first_query, cross)
        _, highest = key_limits(facts, first_query + QUERY_BLOCK - 1, cross)
        begin = lax.div(lowest, 128) * 128
        need = highest - begin
        for width in range(WINDOW_STEP, (MLEN if cross else 512 + QUERY_BLOCK) + 1, WINDOW_STEP):
            start = pl.multiple_of(jnp.minimum(begin, MLEN - width), 128)

            @pl.when((need <= width) & (need > width - WINDOW_STEP))
            def _(start=start, width=width):
                run(first_query, start, width)

        return 0

    lax.fori_loop(0, LEN // QUERY_BLOCK, block, 0)


def allowed_bias(facts, keep_ref, cross, keys_first, first_query, start, width):
    query_axis, key_axis = (1, 0) if keys_first else (0, 1)
    line = (1, QUERY_BLOCK) if keys_first else (QUERY_BLOCK, 1)
    places = first_query + lax.broadcasted_iota(jnp.int32, line, query_axis)
    low_end, high_end = key_limits(facts, places, cross)
    shape = (width, QUERY_BLOCK) if keys_first else (QUERY_BLOCK, width)
    keys = start + lax.broadcasted_iota(jnp.int32, shape, key_axis)
    if cross:
        line = (width, 1) if keys_first else (1, width)
        own = start + lax.broadcasted_iota(jnp.int32, line, key_axis)
        at = pl.ds(start, width)
        keep = keep_ref[at, 0:1] if keys_first else keep_ref[0:1, at]
        keys = jnp.where(kept_keys(facts, keep, own), keys, -1)
    return jnp.where((keys >= low_end) & (keys < high_end), 0.0, -1e30)


def head_lanes(half):
    lane = lax.broadcasted_iota(jnp.int32, (1, 2 * HD), 1)
    return (lane < HD) if half == 0 else (lane >= HD)


def of_head(values, half):
    return jnp.where(head_lanes(half), values, jnp.zeros_like(values))


def gather_weights(plane, w_refs, pack, first, second):
    left = head_lanes(0)
    cores, rows = 2, D // (2 * len(w_refs))
    heads = w_refs[0].shape[0] // cores
    lines = slice(pack * rows, (pack + 1) * rows)
    for distance, w_ref in enumerate(w_refs):
        for core in range(cores):
            begin = pl.multiple_of(((plane ^ distance) * cores + core) * rows, rows)
            for pair in range(heads // 2):
                even = w_ref[core * heads + 2 * pair, lines]
                odd = w_ref[core * heads + 2 * pair + 1, lines]
                at = slice(pair * 2 * HD, (pair + 1) * 2 * HD)
                first[pl.ds(begin, rows), at] = jnp.where(left, even, odd)
                second[pl.ds(begin, rows), at] = jnp.where(left, odd, even)


def scatter_grads(plane, g_refs, pack, held, values):
    first, second = held
    first[:D, :], second[:D, :] = values
    left = head_lanes(0)
    cores, rows = 2, D // (2 * len(g_refs))
    heads = g_refs[0].shape[0] // cores
    lines = slice(pack * rows, (pack + 1) * rows)
    for distance, g_ref in enumerate(g_refs):
        for core in range(cores):
            begin = pl.multiple_of(((plane ^ distance) * cores + core) * rows, rows)
            for pair in range(heads // 2):
                at = slice(pair * 2 * HD, (pair + 1) * 2 * HD)
                one, two = first[pl.ds(begin, rows), at], second[pl.ds(begin, rows), at]
                g_ref[core * heads + 2 * pair, lines] = low(jnp.where(left, one, two))
                g_ref[core * heads + 2 * pair + 1, lines] = low(jnp.where(left, two, one))


def gather_norms(plane, w_refs, norms):
    left = head_lanes(0)
    heads = w_refs[0].shape[0] // 2
    first = 2 * D // (2 * len(w_refs))
    for distance, w_ref in enumerate(w_refs):
        parts = []
        for core in (0, 1):
            parts.append(join_norms(w_ref[core * heads, first : first + 16]))
        at = pl.ds(pl.multiple_of((plane ^ distance) * 2 * HD, 2 * HD), 2 * HD)
        norms[:, at] = jnp.where(left, *parts)


def split_norms(values):
    high = low(values).astype(jnp.float32)
    middle = low(values - high).astype(jnp.float32)
    least = low(values - high - middle).astype(jnp.float32)
    return low(jnp.concatenate([jnp.where(head_lanes(0), high, middle), least], 0))


def join_norms(held):
    held = held.astype(jnp.float32)
    return (held[0:8] + pltpu.roll(held[0:8], HD, 1)) + held[8:16]


def scatter_norms(plane, g_refs, norms):
    heads = g_refs[0].shape[0] // 2
    first = D // len(g_refs)
    for distance, g_ref in enumerate(g_refs):
        at = pl.ds(pl.multiple_of((plane ^ distance) * 2 * HD, 2 * HD), 2 * HD)
        tile = norms[:, at]
        for core in (0, 1):
            values = jnp.where(head_lanes(core), tile, pltpu.roll(tile, HD, 1))
            for head in range(heads):
                g_ref[core * heads + head, first : first + 16] = split_norms(values)


class Moved:
    def __init__(self, values):
        self.values, self.shape, self.dtype = values, values.shape, values.dtype


class Arriving:
    def __init__(self, held, copies):
        self.held, self.copies = held, list(copies)

    def half(self, which):
        copy, self.copies[which] = self.copies[which], None
        if copy is not None:
            copy.wait()
        return self.held

    def get(self):
        for which in range(len(self.copies)):
            self.half(which)
        return self.held


class Leaving:
    def __init__(self, held, copies):
        self.held, self.copies, self.sent = held, list(copies), 0

    def send(self, upto=None):
        while self.sent < (len(self.copies) if upto is None else upto):
            self.copies[self.sent].start()
            self.sent += 1

    def finish(self):
        self.send()
        for copy in self.copies:
            copy.wait()


def half_at(core_ref, other):
    half = LEN // 2
    core = core_ref[0, 0]
    return pl.ds(pl.multiple_of((1 - core if other else core) * half, half), half)


def copies_of(kind, refs, held, core_ref, sems):
    if kind == "one":
        pairs = [(refs[0], held)]
    elif kind == "halves":
        pairs = [(refs[0].at[at], held.at[at]) for at in HALVES]
    else:
        pairs = [(ref, held.at[half_at(core_ref, other)]) for ref, other in zip(refs, (False, True))]
    return pairs, [next(sems) for _ in pairs]


def staged_call(body, name, scalars, inputs, outputs, scratch):
    in_count = sum(len(arrays) for _, arrays in inputs)
    shapes = []
    for kind, shape, dtype in outputs:
        if kind == "cores":
            shapes += [outside((shape[0] // 2, *shape[1:]), dtype)] * 2
        elif kind == "own":
            shapes += [outside((shape[0] // 2, *shape[1:]), dtype)]
        else:
            shapes += [outside(shape, dtype)]
    held_in = []
    for kind, arrays in inputs:
        rows, *others = arrays[0].shape
        rows = 2 * rows if kind == "cores" else rows
        held_in.append(pltpu.VMEM((rows, *others), arrays[0].dtype))
    held_out = [pltpu.VMEM(shape, dtype) for _, shape, dtype in outputs]
    waits = 2 * (len(inputs) + len(outputs))

    def kernel(*refs):
        refs = list(refs)

        def take(count):
            taken = refs[:count]
            del refs[:count]
            return taken

        scalar_refs, in_refs, out_refs = take(len(scalars)), take(in_count), take(len(shapes))
        in_held, out_held, (sem_ref,) = take(len(inputs)), take(len(outputs)), take(1)
        sems = (sem_ref.at[place] for place in range(waits))
        core_ref = scalar_refs[0]
        arrivals = []
        for (kind, arrays), held in zip(inputs, in_held):
            mine, in_refs = in_refs[: len(arrays)], in_refs[len(arrays) :]
            pairs, own = copies_of(kind, mine, held, core_ref, sems)
            copies = [pltpu.make_async_copy(a, b, sem) for (a, b), sem in zip(pairs, own)]
            for copy in copies:
                copy.start()
            arrivals.append(Arriving(held, copies))
        departures = []
        for (kind, _, _), held in zip(outputs, out_held):
            mine = out_refs[: 2 if kind == "cores" else 1]
            out_refs = out_refs[len(mine) :]
            pairs, own = copies_of("cores" if kind == "own" else kind, mine, held, core_ref, sems)
            copies = [pltpu.make_async_copy(b, a, sem) for (a, b), sem in zip(pairs, own)]
            departures.append(Leaving(held, copies))
        body(scalar_refs, arrivals, departures, refs)
        for arrival in arrivals:
            arrival.get()
        for departure in departures:
            departure.finish()

    arrays = [array for _, group in inputs for array in group]
    moved = [place for place, array in enumerate(arrays) if isinstance(array, Moved)]
    arrays = [array.values if isinstance(array, Moved) else array for array in arrays]
    arrays = [
        array if place in moved else stay_outside([array])[0] for place, array in enumerate(arrays)
    ]
    return pl.pallas_call(
        kernel,
        name=name,
        out_shape=tuple(shapes),
        in_specs=[SCALARS] * len(scalars) + [OUTSIDE] * in_count,
        out_specs=(OUTSIDE,) * len(shapes),
        scratch_shapes=held_in + held_out + [pltpu.SemaphoreType.DMA((waits,))] + scratch,
        compiler_params=pltpu.CompilerParams(vmem_limit_bytes=KERNEL_MEGA * MEGA),
        cost_estimate=KERNEL_COST,
    )(*scalars, *arrays)


def forward_heads(plane, facts, keep_ref, cross, query_rows, key_rows, w_refs, outs, scratch):
    w_q, w_k, w_v, w_o, stats_ref = scratch
    part, queries_out, keys_out, values_out, blended_out, stats_out = outs
    q_ref, k_ref, v_ref, o_ref = (
        out.held for out in (queries_out, keys_out, values_out, blended_out)
    )
    w_refs = [w_ref.get() for w_ref in w_refs]
    gather_weights(plane, w_refs, 0, w_q, w_v)
    gather_weights(plane, w_refs, 1, w_k, w_o)
    for out, rows, weights in (
        (queries_out, query_rows, w_q),
        (keys_out, key_rows, w_k),
        (values_out, key_rows, w_v),
    ):
        out.held[...] = low(mm(rows[...], weights[...]))
        out.send()
    lane = lax.broadcasted_iota(jnp.int32, (1, 128), 1)

    def one(first_query, start, width):
        at, keys_at = pl.ds(first_query, QUERY_BLOCK), pl.ds(start, width)
        bias = allowed_bias(facts, keep_ref, cross, False, first_query, start, width)
        stats = jnp.zeros((QUERY_BLOCK, 128), jnp.float32)
        for pair in range(q_ref.shape[1] // (2 * HD)):
            tile = slice(pair * 2 * HD, (pair + 1) * 2 * HD)
            queries = q_ref[at, tile] * HD ** (-0.5)
            blended = []
            for half in (0, 1):
                scores = mt(of_head(queries, half), k_ref[keys_at, tile]) + bias
                top = jnp.max(scores, -1, keepdims=True)
                weights = jnp.exp(scores - top)
                total = jnp.sum(weights, -1, keepdims=True)
                blended.append(mm(low(weights), v_ref[keys_at, tile]) * (1.0 / total))
                stats = jnp.where(lane == 2 * pair + half, top + jnp.log(total), stats)
            o_ref[at, tile] = low(jnp.where(head_lanes(1), *blended))
        stats_ref[at, :] = stats

    key_windows(facts, cross, one)
    for which, at in enumerate(HALVES):
        part.held[at, :] = mt(o_ref[at, :], w_o[...]).astype(PART)
        part.send(which + 1)
    blended_out.send()
    stats_out.held[...] = stats_ref[...].T[0:8]


def self_forward_body(scalars, ins, outs, scratch):
    core_ref, facts = scalars
    tokens, *w_refs = ins
    part, norms, rows, *heads = outs
    plane = core_ref[0, 1]
    tokens = tokens.get()
    units = [standardize(tokens[at, :].astype(jnp.float32))[0] for at in HALVES]
    gather_norms(plane, [w_ref.get() for w_ref in w_refs], norms.held)
    norms.send()
    for at, unit in zip(HALVES, units):
        rows.held[at, :] = low(unit * norms.held[0:1, :] + norms.held[1:2, :])
    rows.send()
    forward_heads(
        plane, facts, None, False, rows.held, rows.held, w_refs, (part, *heads), scratch
    )


def cross_forward_body(scalars, ins, outs, scratch):
    core_ref, facts = scalars
    part_mine, part_theirs, tokens, norms, keep, memory, *w_refs = ins
    part, total, rows, *heads = outs
    tokens, norms = tokens.get(), norms.get()
    for which, at in enumerate(HALVES):
        ours = part_mine.half(which)[at, :].astype(jnp.float32)
        value = tokens[at, :].astype(jnp.float32) + (
            ours + part_theirs.half(which)[at, :].astype(jnp.float32)
        )
        total.held[at, :] = value.astype(SUM)
        total.send(which + 1)
        unit, _ = standardize(value)
        rows.held[at, :] = low(unit * norms[2:3, :] + norms[3:4, :])
    rows.send()
    forward_heads(
        core_ref[0, 1],
        facts,
        keep.get(),
        True,
        rows.held,
        memory.get(),
        w_refs,
        (part, *heads),
        scratch,
    )


def attn_forward(name, body, scalars, inputs, weights, extra):
    cols = weights[0].shape[0] // 2 * HD
    bfloat16 = jnp.bfloat16
    outputs = [
        ("halves", (LEN, D), PART),
        extra,
        ("one", (LEN, D), bfloat16),
        *[("one", (LEN, cols), bfloat16)] * 4,
        ("one", (8, LEN), jnp.float32),
    ]
    scratch = [pltpu.VMEM((D, cols), bfloat16)] * 4 + [pltpu.VMEM((LEN, 128), jnp.float32)]
    inputs = inputs + [("one", (Moved(block),)) for block in weights]
    return staged_call(body, name, scalars, inputs, outputs, scratch)


def backward_heads(plane, facts, keep_ref, cross, up_rows, w_refs, heads, scratch):
    w_q, w_k, w_v, w_o, up, keys_turned, q_turned, dq, k_sum, v_sum, dk, dv = scratch
    w_refs = [w_ref.get() for w_ref in w_refs]
    gather_weights(plane, w_refs, 0, w_q, w_v)
    gather_weights(plane, w_refs, 1, w_k, w_o)
    scale = HD ** (-0.5)
    up[...] = low(mm(up_rows[...], w_o[...]))
    q_ref, k_ref, v_ref, _, stats_ref = (head.get() for head in heads)
    keys_turned[...] = k_ref[...].T
    k_sum[...] = jnp.zeros_like(k_sum)
    v_sum[...] = jnp.zeros_like(v_sum)

    def one(first_query, start, width):
        at, keys_at = pl.ds(first_query, QUERY_BLOCK), pl.ds(start, width)
        bias = allowed_bias(facts, keep_ref, cross, True, first_query, start, width)
        for pair in range(q_ref.shape[1] // (2 * HD)):
            tile = slice(pair * 2 * HD, (pair + 1) * 2 * HD)
            key_add, value_add = [], []
            for half in (0, 1):
                head = 2 * pair + half
                queries, upstream = of_head(q_ref[at, tile], half), of_head(up[at, tile], 1 - half)
                scores = mt(k_ref[keys_at, tile], queries * scale) + bias
                probs = jnp.exp(scores - stats_ref[head : head + 1, at])
                prob_grad = mt(v_ref[keys_at, tile], upstream)
                weighted = jnp.sum(probs * prob_grad, 0, keepdims=True)
                score_grad = low(probs * (prob_grad - weighted))
                key_add.append(mm(score_grad, queries))
                value_add.append(mm(low(probs), upstream))
                lines = slice(head * HD, (head + 1) * HD)
                q_turned[lines, at] = low(mm(keys_turned[lines, keys_at], score_grad) * scale)
            k_sum[keys_at, tile] = k_sum[keys_at, tile] + (key_add[0] + key_add[1])
            v_sum[keys_at, tile] = v_sum[keys_at, tile] + (value_add[0] + value_add[1])

    key_windows(facts, cross, one)
    dq[...] = q_turned[...].T
    dk[...] = low(k_sum[...] * scale)
    dv[...] = low(v_sum[...])


def norm_step(parts, total, norms, row, upstream, finish):
    gains = jnp.zeros((1, D), jnp.float32)
    shifts = jnp.zeros((1, D), jnp.float32)
    for which, at in enumerate(HALVES):
        mine, theirs = (part.half(which)[at, :].astype(jnp.float32) for part in parts)
        back, gain, shift = norm_back(
            total.half(which)[at, :].astype(jnp.float32), mine + theirs, norms[row : row + 1, :]
        )
        gains, shifts = gains + gain, shifts + shift
        finish(which, at, upstream(which, at) + back)
    return gains, shifts


def cross_backward_body(scalars, ins, outs, scratch):
    core_ref, facts = scalars
    part_mine, part_theirs, total, cotangent, norms, keep, memory, *rest = ins
    planes = len(rest) - 6
    w_refs, (rows, *heads) = rest[:planes], rest[planes:]
    up_rows, part, memory_part, norm_out, *g_outs = outs
    turned, memory_turned, keep_turned, *scratch = scratch
    keep_turned[...] = jnp.broadcast_to(keep.get()[...], (128, MLEN)).T
    norms, cotangent = norms.get(), cotangent.get()
    plane = core_ref[0, 1]

    def finish(which, at, value):
        up_rows.held[at, :] = low(value)
        up_rows.send(which + 1)

    gains, shifts = norm_step(
        (part_mine, part_theirs),
        total,
        norms,
        4,
        lambda which, at: cotangent[at, :].astype(jnp.float32),
        finish,
    )
    norm_out.held[0:1, :] = 0.5 * gains
    norm_out.held[1:2, :] = 0.5 * shifts
    norm_out.send()
    backward_heads(plane, facts, keep_turned, True, up_rows.held, w_refs, heads, scratch)
    w_q, w_k, w_v, *_ = scratch
    dq, *held, dk, dv = scratch[-5:]
    for which, at in enumerate(HALVES):
        part.held[at, :] = mt(dq[at, :], w_q[...]).astype(PART)
        part.send(which + 1)
    memory_part.held[...] = low(mt(dk[...], w_k[...]) + mt(dv[...], w_v[...]))
    memory_part.send()
    g_refs = [out.held for out in g_outs]
    turned[...] = rows.get()[...].T
    memory_turned[...] = memory.get()[...].T
    scatter_grads(
        plane, g_refs, 0, held, (mm(turned[...], dq[...]), mm(memory_turned[...], dv[...]))
    )
    turned[...] = up_rows.held[...].T
    out_grad = mm(turned[...], heads[3].get()[...])
    scatter_grads(plane, g_refs, 1, held, (mm(memory_turned[...], dk[...]), out_grad))


def self_backward_body(scalars, ins, outs, scratch):
    core_ref, facts = scalars
    part_mine, part_theirs, total, grad, tokens, ffn_norm, norms, *rest = ins
    planes = len(rest) - 6
    w_refs, (rows, *heads) = rest[:planes], rest[planes:]
    grad_out, part, *g_outs = outs
    norm_grad, up_rows, turned, *scratch = scratch
    norms = norms.get()
    plane = core_ref[0, 1]

    def finish(which, at, value):
        grad_out.held[at, :] = value
        up_rows[at, :] = low(value)

    gains, shifts = norm_step(
        (part_mine, part_theirs),
        total,
        norms,
        2,
        lambda which, at: grad.half(which)[at, :].astype(jnp.float32),
        finish,
    )
    grad_out.send()
    norm_grad[2:3, :] = 0.5 * gains
    norm_grad[3:4, :] = 0.5 * shifts
    norm_grad[4:6, :] = ffn_norm.get()[...]
    norm_grad[6:8, :] = jnp.zeros((2, D), jnp.float32)
    backward_heads(plane, facts, None, False, up_rows, w_refs, heads, scratch)
    w_q, w_k, w_v, *_ = scratch
    dq, *held, dk, dv = scratch[-5:]
    tokens = tokens.get()
    gains = jnp.zeros((1, D), jnp.float32)
    shifts = jnp.zeros((1, D), jnp.float32)
    for at in HALVES:
        value = mt(dq[at, :], w_q[...]) + mt(dk[at, :], w_k[...]) + mt(dv[at, :], w_v[...])
        part.held[at, :] = value
        unit, _ = standardize(tokens[at, :].astype(jnp.float32))
        gains = gains + jnp.sum(value * unit, 0, keepdims=True)
        shifts = shifts + jnp.sum(value, 0, keepdims=True)
    part.send()
    norm_grad[0:1, :] = gains
    norm_grad[1:2, :] = shifts
    g_refs = [out.held for out in g_outs]
    scatter_norms(plane, g_refs, norm_grad)
    turned[...] = rows.get()[...].T
    scatter_grads(plane, g_refs, 0, held, (mm(turned[...], dq[...]), mm(turned[...], dv[...])))
    key_grad = mm(turned[...], dk[...])
    turned[...] = up_rows[...].T
    scatter_grads(plane, g_refs, 1, held, (key_grad, mm(turned[...], heads[3].get()[...])))


def attn_backward(name, body, scalars, inputs, weights, kept, outputs, cross):
    cols = weights[0].shape[0] // 2 * HD
    bfloat16 = jnp.bfloat16
    block = (weights[0].shape[0], D // len(weights) + (0 if cross else 16), 2 * HD)
    outputs = outputs + [("one", block, bfloat16)] * len(weights)
    scratch = [pltpu.VMEM((D, LEN), bfloat16)]
    if not cross:
        scratch = [pltpu.VMEM((8, D), jnp.float32), pltpu.VMEM((LEN, D), bfloat16)] + scratch
    if cross:
        scratch += [pltpu.VMEM((D, MLEN), bfloat16), pltpu.VMEM((MLEN, 128), jnp.int32)]
    scratch += [pltpu.VMEM((D, cols), bfloat16)] * 4 + [
        pltpu.VMEM((LEN, cols), bfloat16),
        pltpu.VMEM((cols, MLEN), bfloat16),
        pltpu.VMEM((cols, LEN), bfloat16),
        pltpu.VMEM((LEN, cols), bfloat16),
        pltpu.VMEM((MLEN, cols), jnp.float32),
        pltpu.VMEM((MLEN, cols), jnp.float32),
        pltpu.VMEM((MLEN, cols), bfloat16),
        pltpu.VMEM((MLEN, cols), bfloat16),
    ]
    inputs = inputs + [("one", (array,)) for array in (*map(Moved, weights), *kept)]
    return staged_call(body, name, scalars, inputs, outputs, scratch)


def add_to(ref, step, update):
    @pl.when(step == 0)
    def _():
        ref[...] = update

    @pl.when(step != 0)
    def _():
        ref[...] = ref[...] + update


def gelu_pieces(values):
    factor = 0.7978845608028654
    square = values * values
    slope = jnp.tanh(factor * values * (1.0 + 0.044715 * square))
    half = 0.5 * (1.0 + slope)
    grad = half + 0.5 * values * (1.0 - slope * slope) * factor * (1.0 + 3 * 0.044715 * square)
    return values * half, grad


def expert_kernel(
    core_ref,
    mine,
    theirs,
    part_mine,
    part_theirs,
    first_sum,
    norms,
    in_ref,
    out_ref,
    sum_out,
    grad_out,
    out_keep,
    out_give,
    w_grad_ref,
    ours,
    others,
    sum_ref,
    exact,
    rows,
    rows_turned,
    up,
    up_turned,
    grad_ref,
    out_total,
    grad_low,
    sems,
    out_sems,
):
    step = pl.program_id(0)

    def leaving(place):
        held, target = (
            (sum_ref, sum_out),
            (grad_low, grad_out),
            (out_total.at[half_at(core_ref, False)], out_keep),
            (out_total.at[half_at(core_ref, True)], out_give),
        )[place]
        return pltpu.make_async_copy(held, target, out_sems.at[place])

    @pl.when(step == 0)
    def _():
        up_copies = [
            pltpu.make_async_copy(a, up.at[half_at(core_ref, other)], sems.at[place])
            for place, (a, other) in enumerate(((mine, False), (theirs, True)))
        ]
        copies = [
            pltpu.make_async_copy(a.at[at], b.at[at], sems.at[2 + 3 * which + place])
            for which, at in enumerate(HALVES)
            for place, (a, b) in enumerate(
                ((part_mine, ours), (part_theirs, others), (first_sum, sum_ref))
            )
        ]
        for copy in copies[:3] + up_copies + copies[3:]:
            copy.start()
        for which, at in enumerate(HALVES):
            for copy in copies[3 * which : 3 * which + 3]:
                copy.wait()
            total = sum_ref[at, :].astype(jnp.float32) + (
                ours[at, :].astype(jnp.float32) + others[at, :].astype(jnp.float32)
            )
            exact[at, :] = total
            sum_ref[at, :] = total.astype(SUM)
            unit, _ = standardize(total)
            rows[at, :] = low(unit * norms[4:5, :] + norms[5:6, :])
            rows_turned[:, at] = rows[at, :].T
        leaving(0).start()
        for copy in up_copies:
            copy.wait()
        up_turned[...] = up[...].T

    shape = (D, in_ref.shape[3])
    w_in, w_out = in_ref[:, 0].reshape(shape), out_ref[:, 0].reshape(shape)
    hidden, slope = gelu_pieces(mm(rows[...], w_in))
    hidden = low(hidden)
    inner_grad = low(slope * mm(up[...], w_out))
    add_to(grad_ref, step, mt(inner_grad, w_in))
    add_to(out_total, step, mt(hidden, w_out))

    @pl.when(step == pl.num_programs(0) - 1)
    def _():
        grad_low[...] = grad_ref[...].astype(PART)
        at = half_at(core_ref, False)
        out_total[at, :] = out_total[at, :] + exact[at, :]
        for place in (1, 2, 3):
            leaving(place).start()

    grads = w_grad_ref.shape[0], -1, in_ref.shape[3]
    w_grad_ref[:, 0, 0] = low(mm(rows_turned[...], inner_grad)).reshape(grads)
    w_grad_ref[:, 0, 1] = low(mm(up_turned[...], hidden)).reshape(grads)

    @pl.when(step == pl.num_programs(0) - 1)
    def _():
        for place in range(4):
            leaving(place).wait()


def expert_layer(core_ref, rows, parts, first_sum, norms, weights):
    owners, steps, line_count, cols = weights[0].shape
    half = outside((LEN // 2, D), jnp.float32)
    w_spec = pl.BlockSpec((owners, 1, line_count, cols), lambda step: (0, step, 0, 0))
    g_shape = (owners, steps, 2, line_count, cols)
    g_spec = pl.BlockSpec((owners, 1, 2, line_count, cols), lambda step: (0, step, 0, 0, 0))
    low_rows, low_turned = pltpu.VMEM((LEN, D), jnp.bfloat16), pltpu.VMEM((D, LEN), jnp.bfloat16)
    wide = pltpu.VMEM((LEN, D), jnp.float32)
    return pl.pallas_call(
        expert_kernel,
        name="expert",
        grid=(steps,),
        out_shape=(
            outside((LEN, D), SUM),
            outside((LEN, D), PART),
            half,
            half,
            outside(g_shape, jnp.bfloat16),
        ),
        in_specs=[SCALARS] + [OUTSIDE] * 5 + [WHOLE, w_spec, w_spec],
        out_specs=(OUTSIDE,) * 4 + (g_spec,),
        scratch_shapes=[pltpu.VMEM((LEN, D), PART)] * 2
        + [pltpu.VMEM((LEN, D), SUM), wide, low_rows, low_turned, low_rows, low_turned]
        + [wide, wide, pltpu.VMEM((LEN, D), PART)]
        + [pltpu.SemaphoreType.DMA((8,)), pltpu.SemaphoreType.DMA((4,))],
        compiler_params=pltpu.CompilerParams(vmem_limit_bytes=KERNEL_MEGA * MEGA),
        cost_estimate=KERNEL_COST,
    )(
        core_ref,
        *stay_outside(rows[:1]),
        rows[1],
        *stay_outside(parts[:1]),
        parts[1],
        *stay_outside((first_sum, norms, *weights)),
    )


def pack_attn_kernel(places, weights, norms, out_ref):
    odd = places[0, 0] == 1
    left = head_lanes(0)
    rows = weights.shape[2]
    count = norms.shape[0]
    values = jnp.concatenate(
        [norms[...], jnp.zeros((8 - count, norms.shape[1]), jnp.float32)], 0
    )
    facts = split_norms(jnp.concatenate([values, values], 1))
    blocks = out_ref.shape[0] // 2
    for core in (0, 1):
        for branch in range(weights.shape[0]):
            for pack in (0, 1):
                first, second = weights[branch, pack], weights[branch, 2 + pack]
                one = jnp.where(odd, second, first)
                two = jnp.where(odd, first, second)
                if core == 0:
                    tile = jnp.where(left, one, pltpu.roll(two, HD, 1))
                else:
                    tile = jnp.where(left, pltpu.roll(one, HD, 1), two)
                begin = pack * rows + branch * (2 * rows + 16)
                for block in range(blocks):
                    out_ref[core * blocks + block, begin : begin + rows] = low(tile)
        for block in range(blocks):
            out_ref[core * blocks + block, 2 * rows : 2 * rows + 16] = facts


def pack_attn(odd, weights, norms, tensor_count):
    shape = (2 * tensor_count, 4 * weights.shape[2] + 16, 2 * HD)
    return pl.pallas_call(
        pack_attn_kernel,
        name="pack_attn",
        out_shape=outside(shape, jnp.bfloat16),
        in_specs=[SCALARS, WHOLE, WHOLE],
        out_specs=WHOLE,
        compiler_params=pltpu.CompilerParams(vmem_limit_bytes=16 * MEGA),
        cost_estimate=KERNEL_COST,
    )(odd, *stay_outside((weights, norms)))


def pack_experts_kernel(chosen, weights, in_ref, out_ref, held, sems):
    places, half = in_ref.shape[2], in_ref.shape[4]
    copies = [
        pltpu.make_async_copy(weights.at[chosen[0, row]], held.at[row], sems.at[row])
        for row in range(held.shape[0])
    ]
    for copy in copies:
        copy.start()
    for row, copy in enumerate(copies):
        copy.wait()
        for core in (0, 1):
            at = slice(core * half, (core + 1) * half)
            in_ref[row // places, core, row % places] = low(held[row, 0, :, at])
            out_ref[row // places, core, row % places] = low(held[row, 1, :, at])


def pack_experts(chip_expert, weights, plane_count, tensor_count):
    _, pair, rows, cols = weights.shape
    count = plane_count * tensor_count
    out = outside((plane_count, 2, tensor_count, rows, cols // 2), jnp.bfloat16)
    return pl.pallas_call(
        pack_experts_kernel,
        name="pack_experts",
        out_shape=(out, out),
        in_specs=[SCALARS, OUTSIDE],
        out_specs=(WHOLE, WHOLE),
        scratch_shapes=[
            pltpu.VMEM((count, pair, rows, cols), jnp.float32),
            pltpu.SemaphoreType.DMA((count,)),
        ],
        compiler_params=pltpu.CompilerParams(vmem_limit_bytes=16 * MEGA),
        cost_estimate=KERNEL_COST,
    )(chip_expert, *stay_outside((weights,)))


def sum_planes_kernel(*refs):
    *parts, out_ref = refs
    count = len(parts) // 2
    rows = parts[count].shape[1]

    def total(blocks, index, lines):
        return sum(block[index, lines].astype(jnp.float32) for block in blocks)

    for index in range(out_ref.shape[0]):
        out_ref[index, :rows] = low(total(parts[:count], index, slice(0, rows)))
        norms = sum(join_norms(block[index, rows : rows + 16]) for block in parts[:count])
        out_ref[index, rows : rows + 16] = split_norms(norms)
        out_ref[index, rows + 16 :] = low(total(parts[count:], index, slice(0, rows)))


def sum_planes(self_parts, cross_parts):
    blocks, rows, cols = self_parts[0].shape
    shape = (blocks, rows + cross_parts[0].shape[1], cols)
    return pl.pallas_call(
        sum_planes_kernel,
        name="sum_planes",
        out_shape=outside(shape, jnp.bfloat16),
        in_specs=[WHOLE] * (len(self_parts) + len(cross_parts)),
        out_specs=WHOLE,
        compiler_params=pltpu.CompilerParams(vmem_limit_bytes=16 * MEGA),
        cost_estimate=KERNEL_COST,
    )(*self_parts, *cross_parts)


def lamb_update(weight, moment, second, grad):
    moment = beta_one * moment + (1.0 - beta_one) * grad
    second = beta_two * second + (1.0 - beta_two) * grad * grad
    update = (
        moment / (1.0 - beta_one**STEP) / (jnp.sqrt(second / (1.0 - beta_two**STEP)) + epsilon)
        + decay * weight
    )
    return moment, second, update


def expert_lamb_kernel(
    chosen, grads, w_ref, m_ref, v_ref, m_out, v_out, u_out, squares, total
):
    step = pl.program_id(0)
    half = grads.shape[5]
    group = w_ref.shape[0]
    for own in range(group):
        expert = step * group + own
        total[...] = jnp.zeros_like(total)
        for plane in range(grads.shape[0]):
            for place in range(grads.shape[2]):

                @pl.when(chosen[plane * grads.shape[2] + place] == expert)
                def _(plane=plane, place=place):
                    for core in (0, 1):
                        at = slice(core * half, (core + 1) * half)
                        total[:, :, at] = total[:, :, at] + grads[plane, core, place].astype(
                            jnp.float32
                        )

        weight = w_ref[own]
        m_out[own], v_out[own], update = lamb_update(weight, m_ref[own], v_ref[own], total[...])
        u_out[own] = low(update)
        squares[own] = jnp.concatenate(
            [jnp.sum(weight * weight, 1), jnp.sum(update * update, 1)], 0
        )


def expert_lamb(chip_expert, grads, weights, moments, seconds):
    experts, pair, rows, cols = weights.shape
    group = 4
    spec = pl.BlockSpec((group, pair, rows, cols), lambda step, chosen: (step, 0, 0, 0))
    return pl.pallas_call(
        expert_lamb_kernel,
        name="expert_lamb",
        out_shape=(outside(weights.shape, jnp.float32),) * 2
        + (outside(weights.shape, jnp.bfloat16),)
        + (jax.ShapeDtypeStruct((experts, 2 * pair, cols), jnp.float32),),
        grid_spec=pltpu.PrefetchScalarGridSpec(
            num_scalar_prefetch=1,
            grid=(experts // group,),
            in_specs=[WHOLE, spec, spec, spec],
            out_specs=(spec, spec, spec)
            + (pl.BlockSpec((group, 2 * pair, cols), lambda step, chosen: (step, 0, 0)),),
            scratch_shapes=[pltpu.VMEM((pair, rows, cols), jnp.float32)],
        ),
        compiler_params=pltpu.CompilerParams(vmem_limit_bytes=24 * MEGA),
        cost_estimate=KERNEL_COST,
    )(chip_expert, *stay_outside((grads, weights, moments, seconds)))


def owner_lamb_kernel(odd, chips, *refs):
    w_ref, m_ref, v_ref, norms, norm_m, norm_v, *outs = refs
    m_out, v_out, u_out, squares, norm_m_out, norm_v_out, norm_u_out, norm_squares = outs
    heads = chips.shape[0] // 2
    left = head_lanes(0)
    rows = w_ref.shape[2]
    for branch in range(w_ref.shape[0]):
        for pack in (0, 1):
            begin = pack * rows + branch * (2 * rows + 16)
            totals = []
            for core in (0, 1):
                totals.append(
                    sum(
                        chips[core * heads + head, begin : begin + rows].astype(jnp.float32)
                        for head in range(heads)
                    )
                )
            first = jnp.where(left, totals[0], pltpu.roll(totals[1], HD, 1))
            second = jnp.where(left, pltpu.roll(totals[0], HD, 1), totals[1])
            swapped = odd[0, 0] == 1
            for kind, grad in (
                (0, jnp.where(swapped, second, first)),
                (1, jnp.where(swapped, first, second)),
            ):
                matrix = 2 * kind + pack
                weight = w_ref[branch, matrix]
                m_out[branch, matrix], v_out[branch, matrix], update = lamb_update(
                    weight, m_ref[branch, matrix], v_ref[branch, matrix], grad
                )
                u_out[branch, matrix] = update
                squares[branch, matrix, 0:1] = jnp.sum(weight * weight, 0, keepdims=True)
                squares[branch, matrix, 1:2] = jnp.sum(update * update, 0, keepdims=True)
    grad = sum(join_norms(chips[index, 2 * rows : 2 * rows + 16]) for index in range(2 * heads))
    count, cols = norms.shape
    norm_m_out[...], norm_v_out[...], update = lamb_update(
        norms[...], norm_m[...], norm_v[...], grad[:count, :cols]
    )
    norm_u_out[...] = update
    norm_squares[0] = norms[...] * norms[...]
    norm_squares[1] = update * update


def owner_lamb(odd, chips, attn, norm):
    matrices, norms = attn[0].shape, norm[0].shape
    return pl.pallas_call(
        owner_lamb_kernel,
        name="owner_lamb",
        out_shape=(outside(matrices, jnp.float32),) * 3
        + (jax.ShapeDtypeStruct((*matrices[:2], 2, matrices[3]), jnp.float32),)
        + (jax.ShapeDtypeStruct(norms, jnp.float32),) * 3
        + (jax.ShapeDtypeStruct((2, *norms), jnp.float32),),
        in_specs=[SCALARS] + [WHOLE] * 7,
        out_specs=(WHOLE,) * 8,
        compiler_params=pltpu.CompilerParams(vmem_limit_bytes=16 * MEGA),
        cost_estimate=KERNEL_COST,
    )(odd, *stay_outside((chips, *attn, *norm)))


def final_step_kernel(sizes, w_ref, u_ref, attn, attn_u, norms, norm_u, *outs):
    out_ref, attn_out, norm_out = outs
    step = pl.program_id(0)
    group, pair = out_ref.shape[:2]
    attn_count = attn.shape[0] * attn.shape[1]
    for own in range(group):
        for kind in range(pair):
            size = sizes[0, attn_count + (step * group + own) * pair + kind]
            out_ref[own, kind] = w_ref[own, kind] - size * u_ref[own, kind].astype(jnp.float32)

    @pl.when(step == 0)
    def _():
        for branch in range(attn.shape[0]):
            for matrix in range(attn.shape[1]):
                size = sizes[0, branch * attn.shape[1] + matrix]
                attn_out[branch, matrix] = attn[branch, matrix] - size * attn_u[branch, matrix]
        first = sizes.shape[1] - norms.shape[0]
        for row in range(norms.shape[0]):
            at = slice(row, row + 1)
            norm_out[at, :] = norms[at, :] - sizes[0, first + row] * norm_u[at, :]


def final_step(sizes, weights, updates, attn, norm):
    experts, pair, rows, cols = weights.shape
    group = 4
    spec = pl.BlockSpec((group, pair, rows, cols), lambda step: (step, 0, 0, 0))
    return pl.pallas_call(
        final_step_kernel,
        name="final_step",
        grid=(experts // group,),
        out_shape=(
            outside(weights.shape, jnp.float32),
            outside(attn[0].shape, jnp.float32),
            jax.ShapeDtypeStruct(norm[0].shape, jnp.float32),
        ),
        in_specs=[SCALARS, spec, spec] + [WHOLE] * 4,
        out_specs=(spec, WHOLE, WHOLE),
        compiler_params=pltpu.CompilerParams(vmem_limit_bytes=24 * MEGA),
        cost_estimate=KERNEL_COST,
    )(sizes, *stay_outside((weights, updates, *attn, *norm)))


DEVICES = ("plane", "core", "tensor")
CHIP = ("core", "tensor")


def twin(values):
    return lax.ppermute(values, "core", ((0, 1), (1, 0)))


def exchange(values, axes):
    return lax.all_to_all(values, axes, 0, 0, tiled=True)


def swap_pairs(plane_count, tensor_count):
    pairs = []
    for plane in range(plane_count):
        for core in range(2):
            for place in range(tensor_count):
                target = (plane * 2 + place % 2) * tensor_count + place // 2 * 2 + core
                pairs.append(((plane * 2 + core) * tensor_count + place, target))
    return pairs


def other_planes(blocks):
    planes = range(lax.axis_size("plane"))
    return [
        lax.ppermute(block, "plane", [(k, k ^ distance) for k in planes]) if distance else block
        for distance, block in enumerate(blocks)
    ]


def sum_devices(values, axes):
    for axis in axes:
        count, flip = lax.axis_size(axis), 1
        while flip < count:
            values = values + lax.ppermute(values, axis, [(k, k ^ flip) for k in range(count)])
            flip *= 2
    return values


def body_rows(
    tokens,
    memory,
    cotangent,
    tgt_lengths,
    mem_lengths,
    mem_keep,
    row_expert,
    attn_weights,
    attn_moment,
    attn_second,
    expert_weights,
    expert_moment,
    expert_second,
    norm_params,
    norm_moment,
    norm_second,
):
    plane_count, tensor_count = lax.axis_size("plane"), lax.axis_size("tensor")
    devices = plane_count * 2 * tensor_count
    core, place = lax.axis_index("core"), lax.axis_index("tensor")
    moves = swap_pairs(plane_count, tensor_count)

    def swap(values):
        return lax.ppermute(values, DEVICES, moves)

    plane = lax.axis_index("plane")
    core_ref = jnp.stack([core, plane]).reshape(1, 2)
    odd = (place % 2).reshape(1, 1)
    packed = pack_attn(odd, attn_weights, norm_params, tensor_count)
    tokens_mine = swap(tokens)
    owned = jnp.arange(plane_count * 2)[:, None] == plane * 2 + core
    owner_expert = sum_devices(jnp.where(owned, row_expert[None], 0), ("core", "plane"))
    chip_expert = owner_expert.reshape(plane_count, 2, 2).transpose(0, 2, 1).reshape(1, -1)
    expert_in, expert_out = pack_experts(chip_expert, expert_weights, plane_count, tensor_count)
    facts = jnp.concatenate([tgt_lengths, mem_lengths, mem_keep], 1)
    facts = jnp.where(core == place % 2, facts, twin(facts))
    facts = lax.dynamic_slice_in_dim(facts, place // 2, 1, 0)
    facts, keep = facts[:, :16], facts[:, 16:]
    chips = exchange(packed, CHIP)
    tokens_theirs = twin(tokens_mine)
    chips, tokens_mine, tokens_theirs, facts, keep, memory, cotangent, expert_in, expert_out = (
        lax.optimization_barrier(
            (chips, tokens_mine, tokens_theirs, facts, keep, memory, cotangent, expert_in, expert_out)
        )
    )
    self_lines = 2 * attn_weights.shape[2] + 16
    self_weights = other_planes([chips[:, :self_lines]] * plane_count)
    cross_weights = other_planes([chips[:, self_lines:]] * plane_count)
    memory_mine = swap(memory)
    up_mine = swap(cotangent)
    memory_mine, up_mine, expert_in, expert_out, *self_weights = lax.optimization_barrier(
        (memory_mine, up_mine, expert_in, expert_out, *self_weights)
    )
    hidden_cols = expert_weights.shape[3] // 2
    expert_shape = (plane_count * 2, tensor_count, -1, hidden_cols)
    expert_in = exchange(expert_in.reshape(devices, -1, hidden_cols), DEVICES)
    tokens_row = ("cores", (tokens_mine, Moved(tokens_theirs)))

    def halves(*arrays):
        return [("halves", (array,)) for array in arrays]

    self_part, norms, *self_kept = attn_forward(
        "self_forward",
        self_forward_body,
        (core_ref, facts),
        [tokens_row],
        self_weights,
        ("one", (8, D), jnp.float32),
    )
    self_part, memory_mine, up_mine, expert_in, expert_out, *cross_weights = (
        lax.optimization_barrier(
            (self_part, memory_mine, up_mine, expert_in, expert_out, *cross_weights)
        )
    )
    memory_row = ("cores", (memory_mine, Moved(twin(memory_mine))))
    up_theirs = twin(up_mine)
    up_row = ("cores", (up_mine, Moved(up_theirs)))
    expert_out = exchange(expert_out.reshape(devices, -1, hidden_cols), DEVICES)
    norms_in = ("one", (norms,))
    cross_part, first_sum, *cross_kept = attn_forward(
        "cross_forward",
        cross_forward_body,
        (core_ref, facts),
        [*halves(self_part, Moved(twin(self_part))), tokens_row, norms_in, ("one", (keep,)), memory_row],
        cross_weights,
        ("halves", (LEN, D), SUM),
    )
    cross_part, expert_out = lax.optimization_barrier((cross_part, expert_out))
    second_sum, ffn_part, out_keep, out_give, row_grad = expert_layer(
        core_ref,
        (up_mine, up_theirs),
        (cross_part, twin(cross_part)),
        first_sum,
        norms,
        (expert_in.reshape(expert_shape), expert_out.reshape(expert_shape)),
    )
    layer_out = swap(low(out_keep + twin(out_give)))
    row_grad = exchange(row_grad.reshape(devices, 2, -1, hidden_cols), DEVICES)
    row_grad = row_grad.reshape(plane_count, 2, tensor_count, 2, -1, hidden_cols)
    grad_cross, cross_part, memory_keep, memory_give, ffn_norm, *cross_grad = attn_backward(
        "cross_backward",
        cross_backward_body,
        (core_ref, facts),
        [*halves(ffn_part, Moved(twin(ffn_part)), second_sum), up_row, norms_in, ("one", (keep,)), memory_row],
        cross_weights,
        cross_kept,
        [
            ("halves", (LEN, D), SUM),
            ("halves", (LEN, D), PART),
            ("cores", (LEN, D), jnp.bfloat16),
            ("one", (2, D), jnp.float32),
        ],
        True,
    )
    cross_grad = other_planes(cross_grad)
    own_grad, part_keep, part_give, *self_grad = attn_backward(
        "self_backward",
        self_backward_body,
        (core_ref, facts),
        [
            *halves(cross_part, Moved(twin(cross_part)), first_sum, grad_cross),
            tokens_row,
            ("one", (ffn_norm,)),
            norms_in,
        ],
        self_weights,
        self_kept,
        [("own", (LEN, D), jnp.float32), ("cores", (LEN, D), jnp.float32)],
        False,
    )
    self_grad, memory_give, cross_grad = lax.optimization_barrier(
        (self_grad, memory_give, cross_grad)
    )
    row_grad, part_give = lax.optimization_barrier((row_grad, part_give))
    expert_moment_new, expert_second_new, expert_update, expert_squares = expert_lamb(
        chip_expert.reshape(-1), row_grad, expert_weights, expert_moment, expert_second
    )
    memory_grad = swap(
        low(memory_keep.astype(jnp.float32) + twin(memory_give).astype(jnp.float32))
    )
    planes = other_planes(self_grad)
    expert_squares, layer_out, memory_grad, *planes = lax.optimization_barrier(
        (expert_squares, layer_out, memory_grad, *planes)
    )
    chips = sum_planes(planes, cross_grad)
    part_give, chips = lax.optimization_barrier((part_give, chips))
    chips = exchange(chips, CHIP)
    back, _, _ = norm_back(
        tokens_mine.astype(jnp.float32), part_keep + twin(part_give), norms[0:1]
    )
    input_grad = low(own_grad + back)
    expert_squares = expert_squares.sum(-1).reshape(E, 2, 2).transpose(1, 0, 2).reshape(2, -1)
    input_grad, chips = lax.optimization_barrier((input_grad, chips))
    input_grad = swap(input_grad)
    attn_moment_new, attn_second_new, attn_update, attn_squares, *norm_outs = owner_lamb(
        odd,
        chips,
        (attn_weights, attn_moment, attn_second),
        (norm_params, norm_moment, norm_second),
    )
    norm_moment_new, norm_second_new, norm_update, norm_squares = norm_outs
    attn_squares = attn_squares.sum(-1).reshape(8, 2).T
    norm_squares = norm_squares.sum(-1) / tensor_count
    squares = jnp.concatenate([attn_squares, expert_squares, norm_squares], 1)
    count = squares.shape[1]
    squares = jnp.broadcast_to(squares.reshape(1, -1), (devices, 2 * count))
    lamb_norms = jnp.sqrt(exchange(squares, DEVICES).sum(0)).reshape(2, count)
    sizes = (rate * (lamb_norms[0] / lamb_norms[1])).reshape(1, -1)
    expert_new, attn_new, norm_new = final_step(
        sizes,
        expert_weights,
        expert_update,
        (attn_weights, attn_update),
        (norm_params, norm_update),
    )
    return (
        layer_out,
        input_grad,
        memory_grad,
        attn_new,
        attn_moment_new,
        attn_second_new,
        expert_new,
        expert_moment_new,
        expert_second_new,
        norm_new,
        norm_moment_new,
        norm_second_new,
        lamb_norms,
    )


def specs(rows, dp):
    tokens = P((*dp, "tensor"), None)
    matrix = P(None, None, dp, "tensor")
    row_items = (P(dp, None),) * 3 + (P(dp),)
    return dict(
        in_specs=(tokens,) * 3 + row_items + (matrix,) * 6 + (P(None, dp),) * 3,
        out_specs=(tokens,) * 3 + (matrix,) * 6 + (P(None, dp),) * 3 + (P(),),
        check_vma=False,
    )


def solution(mesh):
    def run(*args):
        rows = args[3].shape[0]
        dp_count, tensor_count = mesh.shape["dp"], mesh.shape["tensor"]
        if rows // dp_count * 2 == tensor_count and tensor_count % 2 == 0:
            fine = Mesh(
                mesh.devices.reshape(dp_count // 2, 2, tensor_count), ("plane", "core", "tensor")
            )
            return jax.shard_map(body_rows, mesh=fine, **specs(rows, ("plane", "core")))(*args)
        return jax.shard_map(body, mesh=mesh, **specs(rows, ("dp",)))(*args)

    return run
```

```python
import jax
import jax.numpy as jnp
from jax import lax
from jax.experimental import pallas as pl
from jax.experimental.pallas import tpu as pltpu
from jax.sharding import Mesh
from jax.sharding import PartitionSpec as P

D = 512
HD = 64
E = 16
LEN = 1024
MLEN = 1024
STEP = 10


beta_one = 0.9
beta_two = 0.999
epsilon = 1e-06
decay = 0.01
rate = 0.2


def norm_layer(values, gain_vec, shift_vec):
    centered = values - jnp.mean(values, -1, keepdims=True)
    variance = jnp.mean(centered * centered, -1, keepdims=True)
    return centered * lax.rsqrt(variance + 1e-05) * gain_vec + shift_vec


def doc_numbers(lengths, length_total):
    doc_ends = jnp.cumsum(lengths)
    places = jnp.arange(length_total, dtype=jnp.int32)
    numbers = jnp.sum((places[:, None] >= doc_ends[None, :]).astype(jnp.int32), 1)
    starts = doc_ends - lengths
    opening = jnp.any(places[:, None] == starts[None, :], 1)
    return (numbers, opening)


def build_allowed(tgt_len, mem_len, keep_row, cross):
    doc_ids, _ = doc_numbers(tgt_len, LEN)
    if cross:
        mem_docs, opening = doc_numbers(mem_len, MLEN)
        return (doc_ids[:, None] == mem_docs[None, :]) & ((keep_row == 1) | opening)[None, :]
    places = jnp.arange(LEN, dtype=jnp.int32)
    return (doc_ids[:, None] == doc_ids[None, :]) & (places[None, :] <= places[:, None])


def gather_rows(values):
    return lax.all_gather(values, "tensor", axis=0, tiled=True)


def spread_rows(values):
    return lax.psum_scatter(values, "tensor", scatter_dimension=0, tiled=True)


def project(left_side, right_side):
    return jnp.dot(left_side, right_side, preferred_element_type=jnp.float32)


def project_back(left_side, right_side):
    return lax.dot_general(
        left_side, right_side, (((1,), (1,)), ((), ())), preferred_element_type=jnp.float32
    )


def outer_grad(left_side, right_side):
    return lax.dot_general(
        left_side, right_side, (((0,), (0,)), ((), ())), preferred_element_type=jnp.float32
    )


def attend_one(queries, key_rows, value_rows, allowed):
    head_count = queries.shape[1] // HD
    keys_h = key_rows.reshape(key_rows.shape[0], head_count, HD)
    values_h = value_rows.reshape(value_rows.shape[0], head_count, HD)
    block_rows = min(LEN, 512)
    outputs = []
    totals = []
    for begin_at in range(0, LEN, block_rows):
        queries_h = queries[begin_at : begin_at + block_rows].reshape(block_rows, head_count, HD)
        scores = jnp.einsum(
            "qhd,khd->hqk", queries_h, keys_h, preferred_element_type=jnp.float32
        ) * HD ** (-0.5)
        scores = jnp.where(allowed[None, begin_at : begin_at + block_rows], scores, -1e30)
        top_score = jnp.max(scores, -1, keepdims=True)
        weights = jnp.exp(scores - top_score)
        row_total = jnp.sum(weights, -1, keepdims=True)
        prob_low = (weights / row_total).astype(jnp.bfloat16)
        blended = jnp.einsum("hqk,khd->qhd", prob_low, values_h, preferred_element_type=jnp.float32)
        outputs.append(blended.reshape(block_rows, head_count * HD))
        totals.append((top_score + jnp.log(row_total))[..., 0])
    return (jnp.concatenate(outputs, 0), jnp.concatenate(totals, 1))


def attend_back_one(queries, key_rows, value_rows, upstream, log_totals, allowed):
    head_count = queries.shape[1] // HD
    scale = HD ** (-0.5)
    keys_h = key_rows.reshape(key_rows.shape[0], head_count, HD)
    values_h = value_rows.reshape(value_rows.shape[0], head_count, HD)
    key_grad = jnp.zeros(keys_h.shape, jnp.float32)
    value_grad = jnp.zeros(values_h.shape, jnp.float32)
    block_rows = min(LEN, 512)
    query_grads = []
    for begin_at in range(0, LEN, block_rows):
        queries_h = queries[begin_at : begin_at + block_rows].reshape(block_rows, head_count, HD)
        upstream_h = upstream[begin_at : begin_at + block_rows].reshape(block_rows, head_count, HD)
        scores = (
            jnp.einsum("qhd,khd->hqk", queries_h, keys_h, preferred_element_type=jnp.float32)
            * scale
        )
        scores = jnp.where(allowed[None, begin_at : begin_at + block_rows], scores, -1e30)
        probs_full = jnp.exp(scores - log_totals[:, begin_at : begin_at + block_rows, None])
        prob_grad = jnp.einsum(
            "qhd,khd->hqk", upstream_h, values_h, preferred_element_type=jnp.float32
        )
        weighted = jnp.sum(probs_full * prob_grad, -1, keepdims=True)
        score_grad = (probs_full * (prob_grad - weighted)).astype(jnp.bfloat16)
        query_part = (
            jnp.einsum("hqk,khd->qhd", score_grad, keys_h, preferred_element_type=jnp.float32)
            * scale
        )
        query_grads.append(query_part.astype(jnp.bfloat16).reshape(block_rows, head_count * HD))
        key_grad = (
            key_grad
            + jnp.einsum("hqk,qhd->khd", score_grad, queries_h, preferred_element_type=jnp.float32)
            * scale
        )
        value_grad = value_grad + jnp.einsum(
            "hqk,qhd->khd",
            probs_full.astype(jnp.bfloat16),
            upstream_h,
            preferred_element_type=jnp.float32,
        )
    width = head_count * HD
    return (
        jnp.concatenate(query_grads, 0),
        key_grad.astype(jnp.bfloat16).reshape(-1, width),
        value_grad.astype(jnp.bfloat16).reshape(-1, width),
    )


def attend_rows(queries, key_rows, value_rows, tgt_lengths, mem_lengths, mem_keep, cross):
    row_count = tgt_lengths.shape[0]
    width = queries.shape[1]

    def one_row(row_item):
        row_q, row_k, row_v, tgt_len, mem_len, keep_row = row_item
        return attend_one(row_q, row_k, row_v, build_allowed(tgt_len, mem_len, keep_row, cross))

    blended, log_totals = lax.map(
        one_row,
        (
            queries.reshape(row_count, LEN, width),
            key_rows.reshape(row_count, -1, width),
            value_rows.reshape(row_count, -1, width),
            tgt_lengths,
            mem_lengths,
            mem_keep,
        ),
    )
    return (blended.reshape(row_count * LEN, width), log_totals)


def attend_back_rows(
    queries, key_rows, value_rows, upstream, log_totals, tgt_lengths, mem_lengths, mem_keep, cross
):
    row_count = tgt_lengths.shape[0]
    width = queries.shape[1]

    def one_row(row_item):
        row_q, row_k, row_v, row_up, row_log, tgt_len, mem_len, keep_row = row_item
        return attend_back_one(
            row_q, row_k, row_v, row_up, row_log, build_allowed(tgt_len, mem_len, keep_row, cross)
        )

    query_grad, key_grad, value_grad = lax.map(
        one_row,
        (
            queries.reshape(row_count, LEN, width),
            key_rows.reshape(row_count, -1, width),
            value_rows.reshape(row_count, -1, width),
            upstream.reshape(row_count, LEN, width),
            log_totals,
            tgt_lengths,
            mem_lengths,
            mem_keep,
        ),
    )
    return (
        query_grad.reshape(-1, width),
        key_grad.reshape(-1, width),
        value_grad.reshape(-1, width),
    )


def lamb_pieces(weight, moment, second, grad, axes):
    moment = beta_one * moment + (1.0 - beta_one) * grad
    second = beta_two * second + (1.0 - beta_two) * grad * grad
    update = (
        moment / (1.0 - beta_one**STEP) / (jnp.sqrt(second / (1.0 - beta_two**STEP)) + epsilon)
        + decay * weight
    )
    return (moment, second, update, jnp.sum(weight * weight, axes), jnp.sum(update * update, axes))


def body(
    tokens,
    memory,
    cotangent,
    tgt_lengths,
    mem_lengths,
    mem_keep,
    row_expert,
    attn_weights,
    attn_moment,
    attn_second,
    expert_weights,
    expert_moment,
    expert_second,
    norm_params,
    norm_moment,
    norm_second,
):
    row_count = tgt_lengths.shape[0]
    attn_low, expert_low = (
        lax.all_gather(attn_weights.astype(jnp.bfloat16), "dp", axis=2, tiled=True),
        lax.all_gather(expert_weights.astype(jnp.bfloat16), "dp", axis=2, tiled=True),
    )
    row_low = expert_low[row_expert]
    norms = lax.all_gather(norm_params, "dp", axis=1, tiled=True)
    residual = tokens.astype(jnp.float32)
    normed_self, back_self = jax.vjp(norm_layer, residual, norms[0], norms[1])
    self_rows = gather_rows(normed_self.astype(jnp.bfloat16))
    self_qkv = jnp.einsum(
        "td,jdc->jtc", self_rows, attn_low[0, :3], preferred_element_type=jnp.float32
    ).astype(jnp.bfloat16)
    self_mix, self_log = attend_rows(
        self_qkv[0], self_qkv[1], self_qkv[2], tgt_lengths, mem_lengths, mem_keep, False
    )
    self_low = self_mix.astype(jnp.bfloat16)
    first_sum = residual + spread_rows(project_back(self_low, attn_low[0, 3]))
    normed_cross, back_cross = jax.vjp(norm_layer, first_sum, norms[2], norms[3])
    cross_rows = gather_rows(normed_cross.astype(jnp.bfloat16))
    memory_rows = gather_rows(memory)
    cross_queries = project(cross_rows, attn_low[1, 0]).astype(jnp.bfloat16)
    cross_kv = jnp.einsum(
        "td,jdc->jtc", memory_rows, attn_low[1, 1:3], preferred_element_type=jnp.float32
    ).astype(jnp.bfloat16)
    cross_mix, cross_log = attend_rows(
        cross_queries, cross_kv[0], cross_kv[1], tgt_lengths, mem_lengths, mem_keep, True
    )
    cross_low = cross_mix.astype(jnp.bfloat16)
    second_sum = first_sum + spread_rows(project_back(cross_low, attn_low[1, 3]))
    normed_ffn, back_ffn = jax.vjp(norm_layer, second_sum, norms[4], norms[5])
    ffn_rows = gather_rows(normed_ffn.astype(jnp.bfloat16))

    def expert_forward(row_item):
        row_in, chosen = row_item
        inner_act = project(row_in, chosen[0])
        hidden = jax.nn.gelu(inner_act).astype(jnp.bfloat16)
        return (inner_act, project_back(hidden, chosen[1]))

    inner_all, branch_all = lax.map(expert_forward, (ffn_rows.reshape(row_count, LEN, D), row_low))
    layer_out = (second_sum + spread_rows(branch_all.reshape(row_count * LEN, D))).astype(
        jnp.bfloat16
    )
    grad_ffn = cotangent.astype(jnp.float32)
    upstream_ffn = gather_rows(cotangent)
    ffn_again = gather_rows(normed_ffn.astype(jnp.bfloat16))

    def expert_backward(row_item):
        row_in, inner_act, upstream, chosen = row_item
        hidden, gelu_back = jax.vjp(jax.nn.gelu, inner_act)
        inner_grad = gelu_back(project(upstream, chosen[1]))[0].astype(jnp.bfloat16)
        pair_grads = jnp.stack(
            [outer_grad(row_in, inner_grad), outer_grad(upstream, hidden.astype(jnp.bfloat16))]
        )
        return (pair_grads, project_back(inner_grad, chosen[0]))

    row_grads, ffn_part = lax.map(
        expert_backward,
        (
            ffn_again.reshape(row_count, LEN, D),
            inner_all,
            upstream_ffn.reshape(row_count, LEN, D),
            row_low,
        ),
    )
    normed_ffn_grad = spread_rows(ffn_part.reshape(row_count * LEN, D))
    back_tokens, gain_ffn, shift_ffn = back_ffn(normed_ffn_grad)
    grad_cross = grad_ffn + back_tokens
    upstream_cross = gather_rows(grad_cross.astype(jnp.bfloat16))
    cross_again = gather_rows(normed_cross.astype(jnp.bfloat16))
    memory_again = gather_rows(memory)
    cross_up = project(upstream_cross, attn_low[1, 3]).astype(jnp.bfloat16)
    cross_dq, cross_dk, cross_dv = attend_back_rows(
        cross_queries,
        cross_kv[0],
        cross_kv[1],
        cross_up,
        cross_log,
        tgt_lengths,
        mem_lengths,
        mem_keep,
        True,
    )
    cross_grads = jnp.stack(
        [
            outer_grad(cross_again, cross_dq),
            outer_grad(memory_again, cross_dk),
            outer_grad(memory_again, cross_dv),
            outer_grad(upstream_cross, cross_low),
        ]
    )
    normed_cross_grad, memory_total = (
        lax.psum_scatter(
            project_back(cross_dq, attn_low[1, 0]), "tensor", scatter_dimension=0, tiled=True
        ),
        lax.psum_scatter(
            project_back(cross_dk, attn_low[1, 1]) + project_back(cross_dv, attn_low[1, 2]),
            "tensor",
            scatter_dimension=0,
            tiled=True,
        ),
    )
    back_tokens, gain_cross, shift_cross = back_cross(normed_cross_grad)
    grad_self = grad_cross + back_tokens
    upstream_self = gather_rows(grad_self.astype(jnp.bfloat16))
    self_again = gather_rows(normed_self.astype(jnp.bfloat16))
    self_up = project(upstream_self, attn_low[0, 3]).astype(jnp.bfloat16)
    self_dq, self_dk, self_dv = attend_back_rows(
        self_qkv[0],
        self_qkv[1],
        self_qkv[2],
        self_up,
        self_log,
        tgt_lengths,
        mem_lengths,
        mem_keep,
        False,
    )
    self_grads = jnp.stack(
        [
            outer_grad(self_again, self_dq),
            outer_grad(self_again, self_dk),
            outer_grad(self_again, self_dv),
            outer_grad(upstream_self, self_low),
        ]
    )
    normed_self_grad = spread_rows(
        project_back(self_dq, attn_low[0, 0])
        + project_back(self_dk, attn_low[0, 1])
        + project_back(self_dv, attn_low[0, 2])
    )
    back_tokens, gain_self, shift_self = back_self(normed_self_grad)
    input_grad = (grad_self + back_tokens).astype(jnp.bfloat16)
    attn_grad = jnp.stack([self_grads, cross_grads])
    norm_grad = jnp.stack([gain_self, shift_self, gain_cross, shift_cross, gain_ffn, shift_ffn])
    norm_total = lax.psum(norm_grad, "tensor")
    selector = (row_expert[:, None] == jnp.arange(E, dtype=jnp.int32)[None, :]).astype(jnp.float32)
    expert_grad = jnp.einsum("re,rjdf->ejdf", selector, row_grads, precision=lax.Precision.HIGHEST)
    expert_shard = lax.psum_scatter(expert_grad, "dp", scatter_dimension=2, tiled=True)
    attn_shard, norm_shard = (
        lax.psum_scatter(attn_grad, "dp", scatter_dimension=2, tiled=True),
        lax.psum_scatter(norm_total, "dp", scatter_dimension=1, tiled=True),
    )
    attn_pieces = lamb_pieces(attn_weights, attn_moment, attn_second, attn_shard, (2, 3))
    expert_pieces = lamb_pieces(expert_weights, expert_moment, expert_second, expert_shard, (2, 3))
    norm_pieces = lamb_pieces(norm_params, norm_moment, norm_second, norm_shard, (1,))
    copy_share = 1.0 / lax.axis_size("tensor")
    weight_squares = jnp.concatenate(
        [attn_pieces[3].reshape(-1), expert_pieces[3].reshape(-1), norm_pieces[3] * copy_share]
    )
    update_squares = jnp.concatenate(
        [attn_pieces[4].reshape(-1), expert_pieces[4].reshape(-1), norm_pieces[4] * copy_share]
    )
    weight_total, update_total = lax.psum((weight_squares, update_squares), ("dp", "tensor"))
    weight_norm = jnp.sqrt(weight_total)
    update_norm = jnp.sqrt(update_total)
    trust_ratio = weight_norm / update_norm
    attn_ratio = trust_ratio[:8].reshape(2, 4, 1, 1)
    expert_ratio = trust_ratio[8 : 8 + 2 * E].reshape(E, 2, 1, 1)
    norm_ratio = trust_ratio[8 + 2 * E :].reshape(6, 1)
    attn_new = attn_weights - rate * attn_ratio * attn_pieces[2]
    expert_new = expert_weights - rate * expert_ratio * expert_pieces[2]
    norm_new = norm_params - rate * norm_ratio * norm_pieces[2]
    lamb_norms = jnp.stack([weight_norm, update_norm])
    return (
        layer_out,
        input_grad,
        memory_total.astype(jnp.bfloat16),
        attn_new,
        attn_pieces[0],
        attn_pieces[1],
        expert_new,
        expert_pieces[0],
        expert_pieces[1],
        norm_new,
        norm_pieces[0],
        norm_pieces[1],
        lamb_norms,
    )


MEGA = 1024 * 1024
QUERY_BLOCK = 256
WINDOW_STEPS = {False: 128, True: 256}
KERNEL_MEGA = 36
PART = jnp.bfloat16
SUM = jnp.bfloat16
HALVES = (slice(0, LEN // 2), slice(LEN // 2, LEN))
KERNEL_COST = pl.CostEstimate(flops=10**6, bytes_accessed=1024, transcendentals=0)
WHOLE = pl.BlockSpec(memory_space=pltpu.VMEM)
OUTSIDE = pl.BlockSpec(memory_space=pltpu.HBM)
ANYWHERE = pl.BlockSpec(memory_space=pl.ANY)


def outside(shape, dtype):
    return pltpu.HBM(shape, dtype)


def stay_outside(arrays):
    return [pltpu.with_memory_space_constraint(array, pltpu.HBM) for array in arrays]


SCALARS = pl.BlockSpec(memory_space=pltpu.SMEM)


def mm(left, right):
    return lax.dot_general(left, right, (((1,), (0,)), ((), ())), preferred_element_type=jnp.float32)


def mt(left, right):
    return lax.dot_general(left, right, (((1,), (1,)), ((), ())), preferred_element_type=jnp.float32)


def tm(left, right):
    return lax.dot_general(left, right, (((0,), (0,)), ((), ())), preferred_element_type=jnp.float32)


def low(values):
    return values.astype(jnp.bfloat16)


def standardize(values):
    centered = values - jnp.mean(values, -1, keepdims=True)
    inverse = lax.rsqrt(jnp.mean(centered * centered, -1, keepdims=True) + 1e-05)
    return centered * inverse, inverse


def norm_back(values, grad, gain_vec):
    unit, inverse = standardize(values)
    inner = grad * gain_vec
    back = inverse * (
        inner
        - jnp.mean(inner, -1, keepdims=True)
        - unit * jnp.mean(inner * unit, -1, keepdims=True)
    )
    return back, jnp.sum(grad * unit, 0, keepdims=True), jnp.sum(grad, 0, keepdims=True)


def key_limits(facts, places, cross):
    zero = jnp.zeros(places.shape, jnp.int32)
    low_end, high_end, doc_end = zero, zero, 0
    for doc in range(8):
        begin, doc_end = doc_end, doc_end + facts[0, doc]
        if cross:
            low_end = low_end + jnp.where(places >= doc_end, facts[0, 8 + doc], 0)
            high_end = high_end + jnp.where(places >= begin, facts[0, 8 + doc], 0)
        else:
            low_end = jnp.where(places >= doc_end, doc_end, low_end)
    return low_end, (high_end if cross else places + 1)


def kept_keys(facts, keep, places):
    kept = keep == 1
    begin = 0
    for doc in range(8):
        kept = kept | (places == begin)
        begin = begin + facts[0, 8 + doc]
    return kept


def key_windows(facts, cross, run):
    def block(index, _):
        first_query = pl.multiple_of(index * QUERY_BLOCK, QUERY_BLOCK)
        lowest, _ = key_limits(facts, first_query, cross)
        _, highest = key_limits(facts, first_query + QUERY_BLOCK - 1, cross)
        begin = lax.div(lowest, 128) * 128
        need = highest - begin
        unit = WINDOW_STEPS[cross]
        for width in range(unit, (MLEN if cross else 512 + QUERY_BLOCK) + 1, unit):
            start = pl.multiple_of(jnp.minimum(begin, MLEN - width), 128)

            @pl.when((need <= width) & (need > width - unit))
            def _(start=start, width=width):
                run(first_query, start, width)

        return 0

    lax.fori_loop(0, LEN // QUERY_BLOCK, block, 0)


def allowed_bias(facts, keep_ref, cross, first_query, start, width):
    places = first_query + lax.broadcasted_iota(jnp.int32, (1, QUERY_BLOCK), 1)
    low_end, high_end = key_limits(facts, places, cross)
    keys = start + lax.broadcasted_iota(jnp.int32, (width, QUERY_BLOCK), 0)
    if cross:
        own = start + lax.broadcasted_iota(jnp.int32, (width, 1), 0)
        keys = jnp.where(kept_keys(facts, keep_ref[pl.ds(start, width), 0:1], own), keys, -1)
    return jnp.where((keys >= low_end) & (keys < high_end), 0.0, -1e30)


def head_lanes(half):
    lane = lax.broadcasted_iota(jnp.int32, (1, 2 * HD), 1)
    return (lane < HD) if half == 0 else (lane >= HD)


def head_tile(head):
    return slice(head // 2 * 2 * HD, (head // 2 + 1) * 2 * HD)


def value_lines(head):
    return slice((head ^ 1) * HD, ((head ^ 1) + 1) * HD)


def of_head(values, half):
    return jnp.where(head_lanes(half), values, jnp.zeros_like(values))


def gather_weights(plane, w_refs, pack, first, second):
    left = head_lanes(0)
    cores, rows = 2, D // (2 * len(w_refs))
    heads = w_refs[0].shape[0] // cores
    lines = slice(pack * rows, (pack + 1) * rows)
    for distance, w_ref in enumerate(w_refs):
        for core in range(cores):
            begin = pl.multiple_of(((plane ^ distance) * cores + core) * rows, rows)
            for pair in range(heads // 2):
                even = w_ref[core * heads + 2 * pair, lines]
                odd = w_ref[core * heads + 2 * pair + 1, lines]
                at = slice(pair * 2 * HD, (pair + 1) * 2 * HD)
                first[pl.ds(begin, rows), at] = jnp.where(left, even, odd)
                second[pl.ds(begin, rows), at] = jnp.where(left, odd, even)


def scatter_grads(plane, g_refs, pack, held, values):
    first, second = held
    first[:D, :], second[:D, :] = values
    left = head_lanes(0)
    cores, rows = 2, D // (2 * len(g_refs))
    heads = g_refs[0].shape[0] // cores
    lines = slice(pack * rows, (pack + 1) * rows)
    for distance, g_ref in enumerate(g_refs):
        for core in range(cores):
            begin = pl.multiple_of(((plane ^ distance) * cores + core) * rows, rows)
            for pair in range(heads // 2):
                at = slice(pair * 2 * HD, (pair + 1) * 2 * HD)
                one, two = first[pl.ds(begin, rows), at], second[pl.ds(begin, rows), at]
                g_ref[core * heads + 2 * pair, lines] = low(jnp.where(left, one, two))
                g_ref[core * heads + 2 * pair + 1, lines] = low(jnp.where(left, two, one))


def gather_norms(plane, w_refs, norms):
    left = head_lanes(0)
    heads = w_refs[0].shape[0] // 2
    first = 2 * D // (2 * len(w_refs))
    for distance, w_ref in enumerate(w_refs):
        parts = []
        for core in (0, 1):
            parts.append(join_norms(w_ref[core * heads, first : first + 16]))
        at = pl.ds(pl.multiple_of((plane ^ distance) * 2 * HD, 2 * HD), 2 * HD)
        norms[:, at] = jnp.where(left, *parts)


def split_norms(values):
    high = low(values).astype(jnp.float32)
    middle = low(values - high).astype(jnp.float32)
    least = low(values - high - middle).astype(jnp.float32)
    return low(jnp.concatenate([jnp.where(head_lanes(0), high, middle), least], 0))


def join_norms(held):
    held = held.astype(jnp.float32)
    return (held[0:8] + pltpu.roll(held[0:8], HD, 1)) + held[8:16]


def scatter_norms(plane, g_refs, norms):
    heads = g_refs[0].shape[0] // 2
    first = D // len(g_refs)
    for distance, g_ref in enumerate(g_refs):
        at = pl.ds(pl.multiple_of((plane ^ distance) * 2 * HD, 2 * HD), 2 * HD)
        tile = norms[:, at]
        for core in (0, 1):
            values = jnp.where(head_lanes(core), tile, pltpu.roll(tile, HD, 1))
            for head in range(heads):
                g_ref[core * heads + head, first : first + 16] = split_norms(values)


class Moved:
    def __init__(self, values):
        self.values, self.shape, self.dtype = values, values.shape, values.dtype


class Arriving:
    def __init__(self, held, copies):
        self.held, self.copies = held, list(copies)

    def half(self, which):
        copy, self.copies[which] = self.copies[which], None
        if copy is not None:
            copy.wait()
        return self.held

    def get(self):
        for which in range(len(self.copies)):
            self.half(which)
        return self.held


class Leaving:
    def __init__(self, held, copies):
        self.held, self.copies, self.sent = held, list(copies), 0

    def send(self, upto=None):
        while self.sent < (len(self.copies) if upto is None else upto):
            self.copies[self.sent].start()
            self.sent += 1

    def finish(self):
        for copy in self.copies:
            copy.wait()


def half_at(core_ref, other):
    half = LEN // 2
    core = core_ref[0, 0]
    return pl.ds(pl.multiple_of((1 - core if other else core) * half, half), half)


def copies_of(kind, refs, held, core_ref, sems):
    if kind in ("one", "small"):
        pairs = [(refs[0], held)]
    elif kind == "halves":
        pairs = [(refs[0].at[at], held.at[at]) for at in HALVES]
    else:
        pairs = [(ref, held.at[half_at(core_ref, other)]) for ref, other in zip(refs, (False, True))]
    return pairs, [next(sems) for _ in pairs]


def staged_call(body, name, scalars, inputs, outputs, scratch):
    in_count = sum(len(arrays) for _, arrays in inputs)
    shapes = []
    for kind, shape, dtype in outputs:
        if kind == "cores":
            shapes += [outside((shape[0] // 2, *shape[1:]), dtype)] * 2
        elif kind == "own":
            shapes += [outside((shape[0] // 2, *shape[1:]), dtype)]
        else:
            shapes += [outside(shape, dtype)]
    held_in = []
    for kind, arrays in inputs:
        rows, *others = arrays[0].shape
        rows = 2 * rows if kind == "cores" else rows
        held_in.append(pltpu.VMEM((rows, *others), arrays[0].dtype))
    held_out = [pltpu.VMEM(shape, dtype) for _, shape, dtype in outputs]
    waits = 2 * (len(inputs) + len(outputs))

    def kernel(*refs):
        refs = list(refs)

        def take(count):
            taken = refs[:count]
            del refs[:count]
            return taken

        scalar_refs, in_refs, out_refs = take(len(scalars)), take(in_count), take(len(shapes))
        in_held, out_held, (sem_ref,) = take(len(inputs)), take(len(outputs)), take(1)
        sems = (sem_ref.at[place] for place in range(waits))
        core_ref = scalar_refs[0]
        arrivals, starts = [], []
        for (kind, arrays), held in zip(inputs, in_held):
            mine, in_refs = in_refs[: len(arrays)], in_refs[len(arrays) :]
            pairs, own = copies_of(kind, mine, held, core_ref, sems)
            copies = [pltpu.make_async_copy(a, b, sem) for (a, b), sem in zip(pairs, own)]
            turn = {"small": (0,), "halves": (1, 2), "cores": (2, 2), "one": (3,)}[kind]
            starts += zip(turn, copies)
            arrivals.append(Arriving(held, copies))
        for _, copy in sorted(starts, key=lambda item: item[0]):
            copy.start()
        departures = []
        for (kind, _, _), held in zip(outputs, out_held):
            mine = out_refs[: 2 if kind == "cores" else 1]
            out_refs = out_refs[len(mine) :]
            pairs, own = copies_of("cores" if kind == "own" else kind, mine, held, core_ref, sems)
            copies = [pltpu.make_async_copy(b, a, sem) for (a, b), sem in zip(pairs, own)]
            departures.append(Leaving(held, copies))
        body(scalar_refs, arrivals, departures, refs)
        for arrival in arrivals:
            arrival.get()
        for departure in departures:
            departure.send()
        for departure in departures:
            departure.finish()

    arrays = [array for _, group in inputs for array in group]
    moved = [place for place, array in enumerate(arrays) if isinstance(array, Moved)]
    arrays = [array.values if isinstance(array, Moved) else array for array in arrays]
    arrays = [
        array if place in moved else stay_outside([array])[0] for place, array in enumerate(arrays)
    ]
    return pl.pallas_call(
        kernel,
        name=name,
        out_shape=tuple(shapes),
        in_specs=[SCALARS] * len(scalars)
        + [ANYWHERE if place in moved else OUTSIDE for place in range(in_count)],
        out_specs=(OUTSIDE,) * len(shapes),
        scratch_shapes=held_in + held_out + [pltpu.SemaphoreType.DMA((waits,))] + scratch,
        compiler_params=pltpu.CompilerParams(vmem_limit_bytes=KERNEL_MEGA * MEGA),
        cost_estimate=KERNEL_COST,
    )(*scalars, *arrays)


def forward_heads(plane, facts, keep_ref, cross, query_rows, key_rows, w_refs, outs, scratch):
    w_q, w_k, w_v, w_o, values_turned, blended_turned = scratch
    part, queries_out, keys_out, values_out, blended_out, stats_out = outs
    q_ref, k_ref, o_ref, stats_ref = (
        out.held for out in (queries_out, keys_out, blended_out, stats_out)
    )
    w_refs = [w_ref.get() for w_ref in w_refs]
    gather_weights(plane, w_refs, 0, w_q, w_v)
    gather_weights(plane, w_refs, 1, w_k, w_o)
    for out, rows, weights in (
        (queries_out, query_rows, w_q),
        (keys_out, key_rows, w_k),
        (values_out, key_rows, w_v),
    ):
        out.held[...] = low(mm(rows[...], weights[...]))
        out.send()
    values_turned[...] = values_out.held[...].T
    stats_ref[...] = jnp.zeros_like(stats_ref)
    heads = q_ref.shape[1] // HD

    def one(first_query, start, width):
        at, keys_at = pl.ds(first_query, QUERY_BLOCK), pl.ds(start, width)
        bias = allowed_bias(facts, keep_ref, cross, first_query, start, width)
        scores = []
        for head in range(heads):
            tile = head_tile(head)
            queries = of_head(q_ref[at, tile] * HD ** (-0.5), head % 2)
            scores.append(mt(k_ref[keys_at, tile], queries) + bias)
        done = []
        for head in range(heads):
            top = jnp.max(scores[head], 0, keepdims=True)
            weights = jnp.exp(scores[head] - top)
            total = jnp.sum(weights, 0, keepdims=True)
            stats_ref[head : head + 1, at] = top + jnp.log(total)
            done.append((low(weights), 1.0 / total))
        for head, (weights, share) in enumerate(done):
            lines = value_lines(head)
            blended_turned[lines, at] = low(mm(values_turned[lines, keys_at], weights) * share)

    key_windows(facts, cross, one)
    for which, at in enumerate(HALVES):
        o_ref[at, :] = blended_turned[:, at].T
        part.held[at, :] = mt(o_ref[at, :], w_o[...]).astype(PART)
        part.send(which + 1)


def self_forward_body(scalars, ins, outs, scratch):
    core_ref, facts = scalars
    tokens, *w_refs = ins
    part, norms, rows, *heads = outs
    plane = core_ref[0, 1]
    tokens = tokens.get()
    units = [standardize(tokens[at, :].astype(jnp.float32))[0] for at in HALVES]
    gather_norms(plane, [w_ref.get() for w_ref in w_refs], norms.held)
    norms.send()
    for at, unit in zip(HALVES, units):
        rows.held[at, :] = low(unit * norms.held[0:1, :] + norms.held[1:2, :])
    rows.send()
    forward_heads(
        plane, facts, None, False, rows.held, rows.held, w_refs, (part, *heads), scratch
    )


def cross_forward_body(scalars, ins, outs, scratch):
    core_ref, facts = scalars
    part_mine, part_theirs, tokens, norms, keep, memory, *w_refs = ins
    part, total, rows, *heads = outs
    tokens, norms = tokens.get(), norms.get()
    for which, at in enumerate(HALVES):
        ours = part_mine.half(which)[at, :].astype(jnp.float32)
        value = tokens[at, :].astype(jnp.float32) + (
            ours + part_theirs.half(which)[at, :].astype(jnp.float32)
        )
        total.held[at, :] = value.astype(SUM)
        total.send(which + 1)
        unit, _ = standardize(value)
        rows.held[at, :] = low(unit * norms[2:3, :] + norms[3:4, :])
    rows.send()
    keep_turned, *scratch = scratch
    keep_turned[...] = jnp.broadcast_to(keep.get()[...], (128, MLEN)).T
    forward_heads(
        core_ref[0, 1],
        facts,
        keep_turned,
        True,
        rows.held,
        memory.get(),
        w_refs,
        (part, *heads),
        scratch,
    )


def attn_forward(name, body, scalars, inputs, weights, extra, cross):
    cols = weights[0].shape[0] // 2 * HD
    bfloat16 = jnp.bfloat16
    outputs = [
        ("halves", (LEN, D), PART),
        extra,
        ("one", (LEN, D), bfloat16),
        *[("one", (LEN, cols), bfloat16)] * 4,
        ("one", (8, LEN), jnp.float32),
    ]
    scratch = [pltpu.VMEM((D, cols), bfloat16)] * 4
    scratch += [pltpu.VMEM((cols, MLEN), bfloat16), pltpu.VMEM((cols, LEN), bfloat16)]
    if cross:
        scratch = [pltpu.VMEM((MLEN, 128), jnp.int32)] + scratch
    inputs = inputs + [("one", (Moved(block),)) for block in weights]
    return staged_call(body, name, scalars, inputs, outputs, scratch)


def backward_heads(plane, facts, keep_ref, cross, up_rows, w_refs, heads, scratch):
    w_q, w_k, w_v, w_o, weighted, up, keys_turned, q_turned, dq, k_sum, v_sum, dk, dv = scratch
    w_refs = [w_ref.get() for w_ref in w_refs]
    gather_weights(plane, w_refs, 0, w_q, w_v)
    gather_weights(plane, w_refs, 1, w_k, w_o)
    scale = HD ** (-0.5)
    up[...] = low(mm(up_rows[...], w_o[...]))
    q_ref, k_ref, v_ref, o_ref, stats_ref = (head.get() for head in heads)
    keys_turned[...] = k_ref[...].T
    k_sum[...] = jnp.zeros_like(k_sum)
    v_sum[...] = jnp.zeros_like(v_sum)

    products = (up[...].astype(jnp.float32) * o_ref[...].astype(jnp.float32)).T
    heads = q_ref.shape[1] // HD
    for head in range(heads):
        weighted[head : head + 1, :] = jnp.sum(products[value_lines(head), :], 0, keepdims=True)

    def one(first_query, start, width):
        at, keys_at = pl.ds(first_query, QUERY_BLOCK), pl.ds(start, width)
        bias = allowed_bias(facts, keep_ref, cross, first_query, start, width)
        ready, done, adds = [], [], []
        for head in range(heads):
            tile = head_tile(head)
            queries = of_head(q_ref[at, tile], head % 2)
            upstream = of_head(up[at, tile], 1 - head % 2)
            scores = mt(k_ref[keys_at, tile], queries * scale)
            ready.append((queries, upstream, scores, mt(v_ref[keys_at, tile], upstream)))
        for head, (_, _, scores, prob_grad) in enumerate(ready):
            probs = jnp.exp(scores + bias - stats_ref[head : head + 1, at])
            score_grad = low(probs * (prob_grad - weighted[head : head + 1, at]))
            done.append((low(probs), score_grad))
        for head, (probs, score_grad) in enumerate(done):
            queries, upstream, _, _ = ready[head]
            lines = slice(head * HD, (head + 1) * HD)
            q_turned[lines, at] = low(mm(keys_turned[lines, keys_at], score_grad) * scale)
            adds.append((mm(score_grad, queries), mm(probs, upstream)))
        for head in range(0, heads, 2):
            tile = head_tile(head)
            (key_one, value_one), (key_two, value_two) = adds[head : head + 2]
            k_sum[keys_at, tile] = k_sum[keys_at, tile] + (key_one + key_two)
            v_sum[keys_at, tile] = v_sum[keys_at, tile] + (value_one + value_two)

    key_windows(facts, cross, one)
    dq[...] = q_turned[...].T
    dk[...] = low(k_sum[...] * scale)
    dv[...] = low(v_sum[...])


def norm_step(parts, total, norms, row, upstream, finish):
    gains = jnp.zeros((1, D), jnp.float32)
    shifts = jnp.zeros((1, D), jnp.float32)
    for which, at in enumerate(HALVES):
        mine, theirs = (part.half(which)[at, :].astype(jnp.float32) for part in parts)
        back, gain, shift = norm_back(
            total.half(which)[at, :].astype(jnp.float32), mine + theirs, norms[row : row + 1, :]
        )
        gains, shifts = gains + gain, shifts + shift
        finish(which, at, upstream(which, at) + back)
    return gains, shifts


def cross_backward_body(scalars, ins, outs, scratch):
    core_ref, facts = scalars
    part_mine, part_theirs, total, cotangent, norms, keep, memory, *rest = ins
    planes = len(rest) - 6
    w_refs, (rows, *heads) = rest[:planes], rest[planes:]
    up_rows, part, memory_part, norm_out, *g_outs = outs
    turned, memory_turned, keep_turned, *scratch = scratch
    keep_turned[...] = jnp.broadcast_to(keep.get()[...], (128, MLEN)).T
    norms, cotangent = norms.get(), cotangent.get()
    plane = core_ref[0, 1]

    def finish(which, at, value):
        up_rows.held[at, :] = low(value)
        up_rows.send(which + 1)

    gains, shifts = norm_step(
        (part_mine, part_theirs),
        total,
        norms,
        4,
        lambda which, at: cotangent[at, :].astype(jnp.float32),
        finish,
    )
    norm_out.held[0:1, :] = 0.5 * gains
    norm_out.held[1:2, :] = 0.5 * shifts
    norm_out.send()
    backward_heads(plane, facts, keep_turned, True, up_rows.held, w_refs, heads, scratch)
    w_q, w_k, w_v, *_ = scratch
    dq, *held, dk, dv = scratch[-5:]
    for which, at in enumerate(HALVES):
        part.held[at, :] = mt(dq[at, :], w_q[...]).astype(PART)
        part.send(which + 1)
    memory_part.held[...] = low(mt(dk[...], w_k[...]) + mt(dv[...], w_v[...]))
    memory_part.send()
    g_refs = [out.held for out in g_outs]
    turned[...] = rows.get()[...].T
    memory_turned[...] = memory.get()[...].T
    scatter_grads(
        plane, g_refs, 0, held, (mm(turned[...], dq[...]), mm(memory_turned[...], dv[...]))
    )
    turned[...] = up_rows.held[...].T
    out_grad = mm(turned[...], heads[3].get()[...])
    scatter_grads(plane, g_refs, 1, held, (mm(memory_turned[...], dk[...]), out_grad))


def self_backward_body(scalars, ins, outs, scratch):
    core_ref, facts = scalars
    part_mine, part_theirs, total, grad, tokens, ffn_norm, norms, *rest = ins
    planes = len(rest) - 6
    w_refs, (rows, *heads) = rest[:planes], rest[planes:]
    grad_out, part, *g_outs = outs
    norm_grad, up_rows, turned, *scratch = scratch
    norms = norms.get()
    plane = core_ref[0, 1]

    def finish(which, at, value):
        grad_out.held[at, :] = value
        up_rows[at, :] = low(value)

    gains, shifts = norm_step(
        (part_mine, part_theirs),
        total,
        norms,
        2,
        lambda which, at: grad.half(which)[at, :].astype(jnp.float32),
        finish,
    )
    grad_out.send()
    norm_grad[2:3, :] = 0.5 * gains
    norm_grad[3:4, :] = 0.5 * shifts
    norm_grad[4:6, :] = ffn_norm.get()[...]
    norm_grad[6:8, :] = jnp.zeros((2, D), jnp.float32)
    backward_heads(plane, facts, None, False, up_rows, w_refs, heads, scratch)
    w_q, w_k, w_v, *_ = scratch
    dq, *held, dk, dv = scratch[-5:]
    tokens = tokens.get()
    gains = jnp.zeros((1, D), jnp.float32)
    shifts = jnp.zeros((1, D), jnp.float32)
    for at in HALVES:
        value = mt(dq[at, :], w_q[...]) + mt(dk[at, :], w_k[...]) + mt(dv[at, :], w_v[...])
        part.held[at, :] = value
        unit, _ = standardize(tokens[at, :].astype(jnp.float32))
        gains = gains + jnp.sum(value * unit, 0, keepdims=True)
        shifts = shifts + jnp.sum(value, 0, keepdims=True)
    part.send()
    norm_grad[0:1, :] = gains
    norm_grad[1:2, :] = shifts
    g_refs = [out.held for out in g_outs]
    scatter_norms(plane, g_refs, norm_grad)
    turned[...] = rows.get()[...].T
    scatter_grads(plane, g_refs, 0, held, (mm(turned[...], dq[...]), mm(turned[...], dv[...])))
    key_grad = mm(turned[...], dk[...])
    turned[...] = up_rows[...].T
    scatter_grads(plane, g_refs, 1, held, (key_grad, mm(turned[...], heads[3].get()[...])))


def attn_backward(name, body, scalars, inputs, weights, kept, outputs, cross):
    cols = weights[0].shape[0] // 2 * HD
    bfloat16 = jnp.bfloat16
    block = (weights[0].shape[0], D // len(weights) + (0 if cross else 16), 2 * HD)
    outputs = outputs + [("one", block, bfloat16)] * len(weights)
    scratch = [pltpu.VMEM((D, LEN), bfloat16)]
    if not cross:
        scratch = [pltpu.VMEM((8, D), jnp.float32), pltpu.VMEM((LEN, D), bfloat16)] + scratch
    if cross:
        scratch += [pltpu.VMEM((D, MLEN), bfloat16), pltpu.VMEM((MLEN, 128), jnp.int32)]
    scratch += [pltpu.VMEM((D, cols), bfloat16)] * 4 + [
        pltpu.VMEM((8, LEN), jnp.float32),
        pltpu.VMEM((LEN, cols), bfloat16),
        pltpu.VMEM((cols, MLEN), bfloat16),
        pltpu.VMEM((cols, LEN), bfloat16),
        pltpu.VMEM((LEN, cols), bfloat16),
        pltpu.VMEM((MLEN, cols), jnp.float32),
        pltpu.VMEM((MLEN, cols), jnp.float32),
        pltpu.VMEM((MLEN, cols), bfloat16),
        pltpu.VMEM((MLEN, cols), bfloat16),
    ]
    inputs = inputs + [("one", (array,)) for array in (*map(Moved, weights), *kept)]
    return staged_call(body, name, scalars, inputs, outputs, scratch)


def add_to(ref, step, update):
    @pl.when(step == 0)
    def _():
        ref[...] = update

    @pl.when(step != 0)
    def _():
        ref[...] = ref[...] + update


def gelu_pieces(values):
    factor = 0.7978845608028654
    square = values * values
    slope = jnp.tanh(factor * values * (1.0 + 0.044715 * square))
    half = 0.5 * (1.0 + slope)
    grad = half + 0.5 * values * (1.0 - slope * slope) * factor * (1.0 + 3 * 0.044715 * square)
    return values * half, grad


def expert_kernel(
    core_ref,
    mine,
    theirs,
    part_mine,
    part_theirs,
    first_sum,
    norms,
    w_ref,
    sum_out,
    grad_out,
    out_keep,
    out_give,
    w_grad_ref,
    ours,
    others,
    sum_ref,
    exact,
    rows,
    up,
    grad_ref,
    out_total,
    grad_low,
    sems,
    out_sems,
):
    step = pl.program_id(0)

    def leaving(place):
        held, target = (
            (sum_ref, sum_out),
            (grad_low, grad_out),
            (out_total.at[half_at(core_ref, False)], out_keep),
            (out_total.at[half_at(core_ref, True)], out_give),
        )[place]
        return pltpu.make_async_copy(held, target, out_sems.at[place])

    @pl.when(step == 0)
    def _():
        up_copies = [
            pltpu.make_async_copy(a, up.at[half_at(core_ref, other)], sems.at[place])
            for place, (a, other) in enumerate(((mine, False), (theirs, True)))
        ]
        copies = [
            pltpu.make_async_copy(a.at[at], b.at[at], sems.at[2 + 3 * which + place])
            for which, at in enumerate(HALVES)
            for place, (a, b) in enumerate(
                ((part_mine, ours), (part_theirs, others), (first_sum, sum_ref))
            )
        ]
        for copy in copies[:3] + up_copies + copies[3:]:
            copy.start()
        for which, at in enumerate(HALVES):
            for copy in copies[3 * which : 3 * which + 3]:
                copy.wait()
            total = sum_ref[at, :].astype(jnp.float32) + (
                ours[at, :].astype(jnp.float32) + others[at, :].astype(jnp.float32)
            )
            exact[at, :] = total
            sum_ref[at, :] = total.astype(SUM)
            unit, _ = standardize(total)
            rows[at, :] = low(unit * norms[4:5, :] + norms[5:6, :])
        leaving(0).start()
        for copy in up_copies:
            copy.wait()

    shape = (D, w_ref.shape[4])
    w_in, w_out = w_ref[:, 0, 0].reshape(shape), w_ref[:, 0, 1].reshape(shape)
    back = mm(up[...], w_out)
    hidden, slope = gelu_pieces(mm(rows[...], w_in))
    hidden = low(hidden)
    inner_grad = low(slope * back)
    add_to(grad_ref, step, mt(inner_grad, w_in))
    add_to(out_total, step, mt(hidden, w_out))

    @pl.when(step == pl.num_programs(0) - 1)
    def _():
        grad_low[...] = grad_ref[...].astype(PART)
        at = half_at(core_ref, False)
        out_total[at, :] = out_total[at, :] + exact[at, :]
        for place in (1, 2, 3):
            leaving(place).start()

    grads = w_grad_ref.shape[0], -1, w_ref.shape[4]
    w_grad_ref[:, 0, 0] = low(tm(rows[...], inner_grad)).reshape(grads)
    w_grad_ref[:, 0, 1] = low(tm(up[...], hidden)).reshape(grads)

    @pl.when(step == pl.num_programs(0) - 1)
    def _():
        for place in range(4):
            leaving(place).wait()


def expert_layer(core_ref, rows, parts, first_sum, norms, weights):
    owners, steps, _, line_count, cols = weights.shape
    half = outside((LEN // 2, D), jnp.float32)
    w_spec = pl.BlockSpec((owners, 1, 2, line_count, cols), lambda step: (0, step, 0, 0, 0))
    low_rows = pltpu.VMEM((LEN, D), jnp.bfloat16)
    wide = pltpu.VMEM((LEN, D), jnp.float32)
    return pl.pallas_call(
        expert_kernel,
        name="expert",
        grid=(steps,),
        out_shape=(
            outside((LEN, D), SUM),
            outside((LEN, D), PART),
            half,
            half,
            outside(weights.shape, jnp.bfloat16),
        ),
        in_specs=[SCALARS, OUTSIDE, ANYWHERE, OUTSIDE, ANYWHERE, OUTSIDE, WHOLE, w_spec],
        out_specs=(OUTSIDE,) * 4 + (w_spec,),
        scratch_shapes=[pltpu.VMEM((LEN, D), PART)] * 2
        + [pltpu.VMEM((LEN, D), SUM), wide, low_rows, low_rows]
        + [wide, wide, pltpu.VMEM((LEN, D), PART)]
        + [pltpu.SemaphoreType.DMA((8,)), pltpu.SemaphoreType.DMA((4,))],
        compiler_params=pltpu.CompilerParams(vmem_limit_bytes=KERNEL_MEGA * MEGA),
        cost_estimate=KERNEL_COST,
    )(
        core_ref,
        *stay_outside(rows[:1]),
        rows[1],
        *stay_outside(parts[:1]),
        parts[1],
        *stay_outside((first_sum, norms, weights)),
    )


def pack_attn_kernel(places, weights, norms, out_ref):
    odd = places[0, 0] == 1
    left = head_lanes(0)
    rows = weights.shape[2]
    count = norms.shape[0]
    values = jnp.concatenate(
        [norms[...], jnp.zeros((8 - count, norms.shape[1]), jnp.float32)], 0
    )
    facts = split_norms(jnp.concatenate([values, values], 1))
    blocks = out_ref.shape[0] // 2
    for core in (0, 1):
        for branch in range(weights.shape[0]):
            for pack in (0, 1):
                first, second = weights[branch, pack], weights[branch, 2 + pack]
                one = jnp.where(odd, second, first)
                two = jnp.where(odd, first, second)
                if core == 0:
                    tile = jnp.where(left, one, pltpu.roll(two, HD, 1))
                else:
                    tile = jnp.where(left, pltpu.roll(one, HD, 1), two)
                begin = pack * rows + branch * (2 * rows + 16)
                for block in range(blocks):
                    out_ref[core * blocks + block, begin : begin + rows] = low(tile)
        for block in range(blocks):
            out_ref[core * blocks + block, 2 * rows : 2 * rows + 16] = facts


def pack_attn(odd, weights, norms, tensor_count):
    shape = (2 * tensor_count, 4 * weights.shape[2] + 16, 2 * HD)
    return pl.pallas_call(
        pack_attn_kernel,
        name="pack_attn",
        out_shape=outside(shape, jnp.bfloat16),
        in_specs=[SCALARS, WHOLE, WHOLE],
        out_specs=WHOLE,
        compiler_params=pltpu.CompilerParams(vmem_limit_bytes=16 * MEGA),
        cost_estimate=KERNEL_COST,
    )(odd, *stay_outside((weights, norms)))


def pack_experts_kernel(chosen, weights, out_ref, held, sems):
    places, half = out_ref.shape[2], out_ref.shape[5]
    copies = [
        pltpu.make_async_copy(weights.at[chosen[0, row]], held.at[row], sems.at[row])
        for row in range(held.shape[0])
    ]
    for copy in copies:
        copy.start()
    for row, copy in enumerate(copies):
        copy.wait()
        for core in (0, 1):
            at = slice(core * half, (core + 1) * half)
            out_ref[row // places, core, row % places] = low(held[row, :, :, at])


def pack_experts(chip_expert, weights, plane_count, tensor_count):
    _, pair, rows, cols = weights.shape
    count = plane_count * tensor_count
    out = outside((plane_count, 2, tensor_count, pair, rows, cols // 2), jnp.bfloat16)
    return pl.pallas_call(
        pack_experts_kernel,
        name="pack_experts",
        out_shape=out,
        in_specs=[SCALARS, OUTSIDE],
        out_specs=WHOLE,
        scratch_shapes=[
            pltpu.VMEM((count, pair, rows, cols), jnp.float32),
            pltpu.SemaphoreType.DMA((count,)),
        ],
        compiler_params=pltpu.CompilerParams(vmem_limit_bytes=16 * MEGA),
        cost_estimate=KERNEL_COST,
    )(chip_expert, *stay_outside((weights,)))


def sum_planes_kernel(*refs):
    *parts, out_ref = refs
    count = len(parts) // 2
    rows = parts[count].shape[1]

    def total(blocks, index, lines):
        return sum(block[index, lines].astype(jnp.float32) for block in blocks)

    for index in range(out_ref.shape[0]):
        out_ref[index, :rows] = low(total(parts[:count], index, slice(0, rows)))
        norms = sum(join_norms(block[index, rows : rows + 16]) for block in parts[:count])
        out_ref[index, rows : rows + 16] = split_norms(norms)
        out_ref[index, rows + 16 :] = low(total(parts[count:], index, slice(0, rows)))


def sum_planes(self_parts, cross_parts):
    blocks, rows, cols = self_parts[0].shape
    shape = (blocks, rows + cross_parts[0].shape[1], cols)
    return pl.pallas_call(
        sum_planes_kernel,
        name="sum_planes",
        out_shape=outside(shape, jnp.bfloat16),
        in_specs=[WHOLE] * (len(self_parts) + len(cross_parts)),
        out_specs=WHOLE,
        compiler_params=pltpu.CompilerParams(vmem_limit_bytes=16 * MEGA),
        cost_estimate=KERNEL_COST,
    )(*self_parts, *cross_parts)


def lamb_update(weight, moment, second, grad):
    moment = beta_one * moment + (1.0 - beta_one) * grad
    second = beta_two * second + (1.0 - beta_two) * grad * grad
    update = (
        moment / (1.0 - beta_one**STEP) / (jnp.sqrt(second / (1.0 - beta_two**STEP)) + epsilon)
        + decay * weight
    )
    return moment, second, update


def expert_lamb_kernel(
    chosen, grads, w_ref, m_ref, v_ref, m_out, v_out, u_out, squares, total
):
    step = pl.program_id(0)
    half = grads.shape[5]
    group = w_ref.shape[0]
    for own in range(group):
        expert = step * group + own
        total[...] = jnp.zeros_like(total)
        for plane in range(grads.shape[0]):
            for place in range(grads.shape[2]):

                @pl.when(chosen[plane * grads.shape[2] + place] == expert)
                def _(plane=plane, place=place):
                    for core in (0, 1):
                        at = slice(core * half, (core + 1) * half)
                        total[:, :, at] = total[:, :, at] + grads[plane, core, place].astype(
                            jnp.float32
                        )

        weight = w_ref[own]
        m_out[own], v_out[own], update = lamb_update(weight, m_ref[own], v_ref[own], total[...])
        u_out[own] = low(update)
        squares[own] = jnp.concatenate(
            [jnp.sum(weight * weight, 1), jnp.sum(update * update, 1)], 0
        )


def expert_lamb(chip_expert, grads, weights, moments, seconds):
    experts, pair, rows, cols = weights.shape
    group = 4
    spec = pl.BlockSpec((group, pair, rows, cols), lambda step, chosen: (step, 0, 0, 0))
    return pl.pallas_call(
        expert_lamb_kernel,
        name="expert_lamb",
        out_shape=(outside(weights.shape, jnp.float32),) * 2
        + (outside(weights.shape, jnp.bfloat16),)
        + (jax.ShapeDtypeStruct((experts, 2 * pair, cols), jnp.float32),),
        grid_spec=pltpu.PrefetchScalarGridSpec(
            num_scalar_prefetch=1,
            grid=(experts // group,),
            in_specs=[WHOLE, spec, spec, spec],
            out_specs=(spec, spec, spec)
            + (pl.BlockSpec((group, 2 * pair, cols), lambda step, chosen: (step, 0, 0)),),
            scratch_shapes=[pltpu.VMEM((pair, rows, cols), jnp.float32)],
        ),
        compiler_params=pltpu.CompilerParams(vmem_limit_bytes=24 * MEGA),
        cost_estimate=KERNEL_COST,
    )(chip_expert, *stay_outside((grads, weights, moments, seconds)))


def owner_lamb_kernel(odd, chips, *refs):
    w_ref, m_ref, v_ref, norms, norm_m, norm_v, *outs = refs
    m_out, v_out, u_out, squares, norm_m_out, norm_v_out, norm_u_out, norm_squares = outs
    heads = chips.shape[0] // 2
    left = head_lanes(0)
    rows = w_ref.shape[2]
    for branch in range(w_ref.shape[0]):
        for pack in (0, 1):
            begin = pack * rows + branch * (2 * rows + 16)
            totals = []
            for core in (0, 1):
                totals.append(
                    sum(
                        chips[core * heads + head, begin : begin + rows].astype(jnp.float32)
                        for head in range(heads)
                    )
                )
            first = jnp.where(left, totals[0], pltpu.roll(totals[1], HD, 1))
            second = jnp.where(left, pltpu.roll(totals[0], HD, 1), totals[1])
            swapped = odd[0, 0] == 1
            for kind, grad in (
                (0, jnp.where(swapped, second, first)),
                (1, jnp.where(swapped, first, second)),
            ):
                matrix = 2 * kind + pack
                weight = w_ref[branch, matrix]
                m_out[branch, matrix], v_out[branch, matrix], update = lamb_update(
                    weight, m_ref[branch, matrix], v_ref[branch, matrix], grad
                )
                u_out[branch, matrix] = update
                squares[branch, matrix, 0:1] = jnp.sum(weight * weight, 0, keepdims=True)
                squares[branch, matrix, 1:2] = jnp.sum(update * update, 0, keepdims=True)
    grad = sum(join_norms(chips[index, 2 * rows : 2 * rows + 16]) for index in range(2 * heads))
    count, cols = norms.shape
    norm_m_out[...], norm_v_out[...], update = lamb_update(
        norms[...], norm_m[...], norm_v[...], grad[:count, :cols]
    )
    norm_u_out[...] = update
    norm_squares[0] = norms[...] * norms[...]
    norm_squares[1] = update * update


def owner_lamb(odd, chips, attn, norm):
    matrices, norms = attn[0].shape, norm[0].shape
    return pl.pallas_call(
        owner_lamb_kernel,
        name="owner_lamb",
        out_shape=(outside(matrices, jnp.float32),) * 3
        + (jax.ShapeDtypeStruct((*matrices[:2], 2, matrices[3]), jnp.float32),)
        + (jax.ShapeDtypeStruct(norms, jnp.float32),) * 3
        + (jax.ShapeDtypeStruct((2, *norms), jnp.float32),),
        in_specs=[SCALARS] + [WHOLE] * 7,
        out_specs=(WHOLE,) * 8,
        compiler_params=pltpu.CompilerParams(vmem_limit_bytes=16 * MEGA),
        cost_estimate=KERNEL_COST,
    )(odd, *stay_outside((chips, *attn, *norm)))


def final_step_kernel(sizes, moves, w_ref, u_ref, attn, attn_u, norms, norm_u, *rest):
    count = (len(rest) - 4) // 3
    sources, (out_ref, attn_out, norm_out) = rest[: 2 * count], rest[2 * count : 2 * count + 3]
    settled, sems = rest[2 * count + 3 : -1], rest[-1]
    step = pl.program_id(0)

    def settle(source, place):
        return pltpu.make_async_copy(source, settled[place], sems.at[place])

    for place in range(count):
        for source, moved in zip(sources[2 * place : 2 * place + 2], (0, 1)):

            @pl.when((step == 0) & (moves[0, 0] == moved))
            def _(source=source, place=place):
                settle(source, place).start()

    @pl.when(step == pl.num_programs(0) - 1)
    def _():
        for place in range(count):
            settle(sources[2 * place], place).wait()

    group, pair = out_ref.shape[:2]
    attn_count = attn.shape[0] * attn.shape[1]
    for own in range(group):
        for kind in range(pair):
            size = sizes[0, attn_count + (step * group + own) * pair + kind]
            out_ref[own, kind] = w_ref[own, kind] - size * u_ref[own, kind].astype(jnp.float32)

    @pl.when(step == 0)
    def _():
        for branch in range(attn.shape[0]):
            for matrix in range(attn.shape[1]):
                size = sizes[0, branch * attn.shape[1] + matrix]
                attn_out[branch, matrix] = attn[branch, matrix] - size * attn_u[branch, matrix]
        first = sizes.shape[1] - norms.shape[0]
        for row in range(norms.shape[0]):
            at = slice(row, row + 1)
            norm_out[at, :] = norms[at, :] - sizes[0, first + row] * norm_u[at, :]


def final_step(sizes, moves, weights, updates, attn, norm, landed):
    experts, pair, rows, cols = weights.shape
    group = 4
    spec = pl.BlockSpec((group, pair, rows, cols), lambda step: (step, 0, 0, 0))
    return pl.pallas_call(
        final_step_kernel,
        name="final_step",
        grid=(experts // group,),
        out_shape=(
            outside(weights.shape, jnp.float32),
            outside(attn[0].shape, jnp.float32),
            jax.ShapeDtypeStruct(norm[0].shape, jnp.float32),
        )
        + tuple(outside(array.shape, array.dtype) for array in landed[::2]),
        in_specs=[SCALARS, SCALARS, spec, spec] + [WHOLE] * 4 + [ANYWHERE] * len(landed),
        out_specs=(spec, WHOLE, WHOLE) + (OUTSIDE,) * (len(landed) // 2),
        scratch_shapes=[pltpu.SemaphoreType.DMA((len(landed) // 2,))],
        compiler_params=pltpu.CompilerParams(vmem_limit_bytes=24 * MEGA),
        cost_estimate=KERNEL_COST,
    )(sizes, moves, *stay_outside((weights, updates, *attn, *norm)), *landed)


DEVICES = ("plane", "core", "tensor")
CHIP = ("core", "tensor")


def twin(values):
    return lax.ppermute(values, "core", ((0, 1), (1, 0)))


def exchange(values, axes):
    return lax.all_to_all(values, axes, 0, 0, tiled=True)


def swap_pairs(plane_count, tensor_count):
    pairs = []
    for plane in range(plane_count):
        for core in range(2):
            for place in range(tensor_count):
                target = (plane * 2 + place % 2) * tensor_count + place // 2 * 2 + core
                here = (plane * 2 + core) * tensor_count + place
                if target != here:
                    pairs.append((here, target))
    return pairs


def other_planes(blocks):
    planes = range(lax.axis_size("plane"))
    return [
        lax.ppermute(block, "plane", [(k, k ^ distance) for k in planes]) if distance else block
        for distance, block in enumerate(blocks)
    ]


def sum_devices(values, axes):
    for axis in axes:
        count, flip = lax.axis_size(axis), 1
        while flip < count:
            values = values + lax.ppermute(values, axis, [(k, k ^ flip) for k in range(count)])
            flip *= 2
    return values


def body_rows(
    tokens,
    memory,
    cotangent,
    tgt_lengths,
    mem_lengths,
    mem_keep,
    row_expert,
    attn_weights,
    attn_moment,
    attn_second,
    expert_weights,
    expert_moment,
    expert_second,
    norm_params,
    norm_moment,
    norm_second,
):
    plane_count, tensor_count = lax.axis_size("plane"), lax.axis_size("tensor")
    devices = plane_count * 2 * tensor_count
    core, place = lax.axis_index("core"), lax.axis_index("tensor")
    moves = swap_pairs(plane_count, tensor_count)

    moving = core != place % 2

    def swap(values):
        return lax.ppermute(values, DEVICES, moves)

    def own_row(values):
        return jnp.where(moving, swap(values), values)

    plane = lax.axis_index("plane")
    core_ref = jnp.stack([core, plane]).reshape(1, 2)
    odd = (place % 2).reshape(1, 1)
    packed = pack_attn(odd, attn_weights, norm_params, tensor_count)
    tokens_mine = own_row(tokens)
    owned = jnp.arange(plane_count * 2)[:, None] == plane * 2 + core
    owner_expert = sum_devices(jnp.where(owned, row_expert[None], 0), ("core", "plane"))
    chip_expert = owner_expert.reshape(plane_count, 2, 2).transpose(0, 2, 1).reshape(1, -1)
    facts = jnp.concatenate([tgt_lengths, mem_lengths, mem_keep], 1)
    facts = jnp.where(core == place % 2, facts, twin(facts))
    facts = lax.dynamic_slice_in_dim(facts, place // 2, 1, 0)
    facts, keep = facts[:, :16], facts[:, 16:]
    chips = exchange(packed, CHIP)
    tokens_theirs = twin(tokens_mine)
    chips, tokens_mine, tokens_theirs, memory, cotangent, chip_expert = lax.optimization_barrier(
        (chips, tokens_mine, tokens_theirs, memory, cotangent, chip_expert)
    )
    self_lines = 2 * attn_weights.shape[2] + 16
    self_weights = other_planes([chips[:, :self_lines]] * plane_count)
    memory_mine = own_row(memory)
    up_mine = own_row(cotangent)
    cross_weights = other_planes([chips[:, self_lines:]] * plane_count)
    chosen = pack_experts(chip_expert, expert_weights, plane_count, tensor_count)
    memory_mine, up_mine, chosen, *self_weights = lax.optimization_barrier(
        (memory_mine, up_mine, chosen, *self_weights)
    )
    hidden_cols = expert_weights.shape[3] // 2
    chosen = exchange(chosen.reshape(devices, 2, -1, hidden_cols), DEVICES)
    chosen = chosen.reshape(plane_count * 2, tensor_count, 2, -1, hidden_cols)
    tokens_row = ("cores", (tokens_mine, Moved(tokens_theirs)))

    def halves(*arrays):
        return [("halves", (array,)) for array in arrays]

    self_part, norms, *self_kept = attn_forward(
        "self_forward",
        self_forward_body,
        (core_ref, facts),
        [tokens_row],
        self_weights,
        ("one", (8, D), jnp.float32),
        False,
    )
    self_part, memory_mine, up_mine, *cross_weights = lax.optimization_barrier(
        (self_part, memory_mine, up_mine, *cross_weights)
    )
    memory_row = ("cores", (memory_mine, Moved(twin(memory_mine))))
    up_theirs = twin(up_mine)
    up_row = ("cores", (up_mine, Moved(up_theirs)))
    norms_in, keep_in = ("small", (norms,)), ("small", (keep,))
    cross_part, first_sum, *cross_kept = attn_forward(
        "cross_forward",
        cross_forward_body,
        (core_ref, facts),
        [*halves(self_part, Moved(twin(self_part))), tokens_row, norms_in, keep_in, memory_row],
        cross_weights,
        ("halves", (LEN, D), SUM),
        True,
    )
    second_sum, ffn_part, out_keep, out_give, row_grad = expert_layer(
        core_ref,
        (up_mine, up_theirs),
        (cross_part, twin(cross_part)),
        first_sum,
        norms,
        chosen,
    )
    layer_low = low(out_keep + twin(out_give))
    layer_out = swap(layer_low)
    row_grad = exchange(row_grad.reshape(devices, 2, -1, hidden_cols), DEVICES)
    row_grad = row_grad.reshape(plane_count, 2, tensor_count, 2, -1, hidden_cols)
    grad_cross, cross_part, memory_keep, memory_give, ffn_norm, *cross_grad = attn_backward(
        "cross_backward",
        cross_backward_body,
        (core_ref, facts),
        [*halves(ffn_part, Moved(twin(ffn_part)), second_sum), up_row, norms_in, keep_in, memory_row],
        cross_weights,
        cross_kept,
        [
            ("halves", (LEN, D), SUM),
            ("halves", (LEN, D), PART),
            ("cores", (LEN, D), jnp.bfloat16),
            ("one", (2, D), jnp.float32),
        ],
        True,
    )
    cross_grad = other_planes(cross_grad)
    own_grad, part_keep, part_give, *self_grad = attn_backward(
        "self_backward",
        self_backward_body,
        (core_ref, facts),
        [
            *halves(cross_part, Moved(twin(cross_part)), first_sum, grad_cross),
            tokens_row,
            ("small", (ffn_norm,)),
            norms_in,
        ],
        self_weights,
        self_kept,
        [("own", (LEN, D), jnp.float32), ("cores", (LEN, D), jnp.float32)],
        False,
    )
    self_grad, memory_give, cross_grad = lax.optimization_barrier(
        (self_grad, memory_give, cross_grad)
    )
    memory_low = low(memory_keep.astype(jnp.float32) + twin(memory_give).astype(jnp.float32))
    memory_grad = swap(memory_low)
    planes = other_planes(self_grad)
    back, _, _ = norm_back(
        tokens_mine.astype(jnp.float32), part_keep + twin(part_give), norms[0:1]
    )
    input_low = low(own_grad + back)
    input_grad = swap(input_low)
    input_grad, layer_out, memory_grad, *planes = lax.optimization_barrier(
        (input_grad, layer_out, memory_grad, *planes)
    )
    chips = sum_planes(planes, cross_grad)
    row_grad, chips = lax.optimization_barrier((row_grad, chips))
    chips = exchange(chips, CHIP)
    expert_moment_new, expert_second_new, expert_update, expert_squares = expert_lamb(
        chip_expert.reshape(-1), row_grad, expert_weights, expert_moment, expert_second
    )
    expert_squares = expert_squares.sum(-1).reshape(E, 2, 2).transpose(1, 0, 2).reshape(2, -1)
    attn_moment_new, attn_second_new, attn_update, attn_squares, *norm_outs = owner_lamb(
        odd,
        chips,
        (attn_weights, attn_moment, attn_second),
        (norm_params, norm_moment, norm_second),
    )
    norm_moment_new, norm_second_new, norm_update, norm_squares = norm_outs
    attn_squares = attn_squares.sum(-1).reshape(8, 2).T
    norm_squares = norm_squares.sum(-1) / tensor_count
    squares = jnp.concatenate([attn_squares, expert_squares, norm_squares], 1)
    count = squares.shape[1]
    squares = jnp.broadcast_to(squares.reshape(1, -1), (devices, 2 * count))
    lamb_norms = jnp.sqrt(exchange(squares, DEVICES).sum(0)).reshape(2, count)
    sizes = (rate * (lamb_norms[0] / lamb_norms[1])).reshape(1, -1)
    expert_new, attn_new, norm_new, layer_out, memory_grad, input_grad = final_step(
        sizes,
        moving.astype(jnp.int32).reshape(1, 1),
        expert_weights,
        expert_update,
        (attn_weights, attn_update),
        (norm_params, norm_update),
        (layer_low, layer_out, memory_low, memory_grad, input_low, input_grad),
    )
    return (
        layer_out,
        input_grad,
        memory_grad,
        attn_new,
        attn_moment_new,
        attn_second_new,
        expert_new,
        expert_moment_new,
        expert_second_new,
        norm_new,
        norm_moment_new,
        norm_second_new,
        lamb_norms,
    )


def specs(rows, dp):
    tokens = P((*dp, "tensor"), None)
    matrix = P(None, None, dp, "tensor")
    row_items = (P(dp, None),) * 3 + (P(dp),)
    return dict(
        in_specs=(tokens,) * 3 + row_items + (matrix,) * 6 + (P(None, dp),) * 3,
        out_specs=(tokens,) * 3 + (matrix,) * 6 + (P(None, dp),) * 3 + (P(),),
        check_vma=False,
    )


def solution(mesh):
    def run(*args):
        rows = args[3].shape[0]
        dp_count, tensor_count = mesh.shape["dp"], mesh.shape["tensor"]
        if rows // dp_count * 2 == tensor_count and tensor_count % 2 == 0:
            fine = Mesh(
                mesh.devices.reshape(dp_count // 2, 2, tensor_count), ("plane", "core", "tensor")
            )
            return jax.shard_map(body_rows, mesh=fine, **specs(rows, ("plane", "core")))(*args)
        return jax.shard_map(body, mesh=mesh, **specs(rows, ("dp",)))(*args)

    return run
```

```python
import jax
import jax.numpy as jnp
from jax import lax
from jax.experimental import pallas as pl
from jax.experimental.pallas import tpu as pltpu
from jax.sharding import Mesh
from jax.sharding import PartitionSpec as P

D = 512
HD = 64
E = 16
LEN = 1024
MLEN = 1024
STEP = 10


beta_one = 0.9
beta_two = 0.999
epsilon = 1e-06
decay = 0.01
rate = 0.2


def norm_layer(values, gain_vec, shift_vec):
    centered = values - jnp.mean(values, -1, keepdims=True)
    variance = jnp.mean(centered * centered, -1, keepdims=True)
    return centered * lax.rsqrt(variance + 1e-05) * gain_vec + shift_vec


def doc_numbers(lengths, length_total):
    doc_ends = jnp.cumsum(lengths)
    places = jnp.arange(length_total, dtype=jnp.int32)
    numbers = jnp.sum((places[:, None] >= doc_ends[None, :]).astype(jnp.int32), 1)
    starts = doc_ends - lengths
    opening = jnp.any(places[:, None] == starts[None, :], 1)
    return (numbers, opening)


def build_allowed(tgt_len, mem_len, keep_row, cross):
    doc_ids, _ = doc_numbers(tgt_len, LEN)
    if cross:
        mem_docs, opening = doc_numbers(mem_len, MLEN)
        return (doc_ids[:, None] == mem_docs[None, :]) & ((keep_row == 1) | opening)[None, :]
    places = jnp.arange(LEN, dtype=jnp.int32)
    return (doc_ids[:, None] == doc_ids[None, :]) & (places[None, :] <= places[:, None])


def gather_rows(values):
    return lax.all_gather(values, "tensor", axis=0, tiled=True)


def spread_rows(values):
    return lax.psum_scatter(values, "tensor", scatter_dimension=0, tiled=True)


def project(left_side, right_side):
    return jnp.dot(left_side, right_side, preferred_element_type=jnp.float32)


def project_back(left_side, right_side):
    return lax.dot_general(
        left_side, right_side, (((1,), (1,)), ((), ())), preferred_element_type=jnp.float32
    )


def outer_grad(left_side, right_side):
    return lax.dot_general(
        left_side, right_side, (((0,), (0,)), ((), ())), preferred_element_type=jnp.float32
    )


def attend_one(queries, key_rows, value_rows, allowed):
    head_count = queries.shape[1] // HD
    keys_h = key_rows.reshape(key_rows.shape[0], head_count, HD)
    values_h = value_rows.reshape(value_rows.shape[0], head_count, HD)
    block_rows = min(LEN, 512)
    outputs = []
    totals = []
    for begin_at in range(0, LEN, block_rows):
        queries_h = queries[begin_at : begin_at + block_rows].reshape(block_rows, head_count, HD)
        scores = jnp.einsum(
            "qhd,khd->hqk", queries_h, keys_h, preferred_element_type=jnp.float32
        ) * HD ** (-0.5)
        scores = jnp.where(allowed[None, begin_at : begin_at + block_rows], scores, -1e30)
        top_score = jnp.max(scores, -1, keepdims=True)
        weights = jnp.exp(scores - top_score)
        row_total = jnp.sum(weights, -1, keepdims=True)
        prob_low = (weights / row_total).astype(jnp.bfloat16)
        blended = jnp.einsum("hqk,khd->qhd", prob_low, values_h, preferred_element_type=jnp.float32)
        outputs.append(blended.reshape(block_rows, head_count * HD))
        totals.append((top_score + jnp.log(row_total))[..., 0])
    return (jnp.concatenate(outputs, 0), jnp.concatenate(totals, 1))


def attend_back_one(queries, key_rows, value_rows, upstream, log_totals, allowed):
    head_count = queries.shape[1] // HD
    scale = HD ** (-0.5)
    keys_h = key_rows.reshape(key_rows.shape[0], head_count, HD)
    values_h = value_rows.reshape(value_rows.shape[0], head_count, HD)
    key_grad = jnp.zeros(keys_h.shape, jnp.float32)
    value_grad = jnp.zeros(values_h.shape, jnp.float32)
    block_rows = min(LEN, 512)
    query_grads = []
    for begin_at in range(0, LEN, block_rows):
        queries_h = queries[begin_at : begin_at + block_rows].reshape(block_rows, head_count, HD)
        upstream_h = upstream[begin_at : begin_at + block_rows].reshape(block_rows, head_count, HD)
        scores = (
            jnp.einsum("qhd,khd->hqk", queries_h, keys_h, preferred_element_type=jnp.float32)
            * scale
        )
        scores = jnp.where(allowed[None, begin_at : begin_at + block_rows], scores, -1e30)
        probs_full = jnp.exp(scores - log_totals[:, begin_at : begin_at + block_rows, None])
        prob_grad = jnp.einsum(
            "qhd,khd->hqk", upstream_h, values_h, preferred_element_type=jnp.float32
        )
        weighted = jnp.sum(probs_full * prob_grad, -1, keepdims=True)
        score_grad = (probs_full * (prob_grad - weighted)).astype(jnp.bfloat16)
        query_part = (
            jnp.einsum("hqk,khd->qhd", score_grad, keys_h, preferred_element_type=jnp.float32)
            * scale
        )
        query_grads.append(query_part.astype(jnp.bfloat16).reshape(block_rows, head_count * HD))
        key_grad = (
            key_grad
            + jnp.einsum("hqk,qhd->khd", score_grad, queries_h, preferred_element_type=jnp.float32)
            * scale
        )
        value_grad = value_grad + jnp.einsum(
            "hqk,qhd->khd",
            probs_full.astype(jnp.bfloat16),
            upstream_h,
            preferred_element_type=jnp.float32,
        )
    width = head_count * HD
    return (
        jnp.concatenate(query_grads, 0),
        key_grad.astype(jnp.bfloat16).reshape(-1, width),
        value_grad.astype(jnp.bfloat16).reshape(-1, width),
    )


def attend_rows(queries, key_rows, value_rows, tgt_lengths, mem_lengths, mem_keep, cross):
    row_count = tgt_lengths.shape[0]
    width = queries.shape[1]

    def one_row(row_item):
        row_q, row_k, row_v, tgt_len, mem_len, keep_row = row_item
        return attend_one(row_q, row_k, row_v, build_allowed(tgt_len, mem_len, keep_row, cross))

    blended, log_totals = lax.map(
        one_row,
        (
            queries.reshape(row_count, LEN, width),
            key_rows.reshape(row_count, -1, width),
            value_rows.reshape(row_count, -1, width),
            tgt_lengths,
            mem_lengths,
            mem_keep,
        ),
    )
    return (blended.reshape(row_count * LEN, width), log_totals)


def attend_back_rows(
    queries, key_rows, value_rows, upstream, log_totals, tgt_lengths, mem_lengths, mem_keep, cross
):
    row_count = tgt_lengths.shape[0]
    width = queries.shape[1]

    def one_row(row_item):
        row_q, row_k, row_v, row_up, row_log, tgt_len, mem_len, keep_row = row_item
        return attend_back_one(
            row_q, row_k, row_v, row_up, row_log, build_allowed(tgt_len, mem_len, keep_row, cross)
        )

    query_grad, key_grad, value_grad = lax.map(
        one_row,
        (
            queries.reshape(row_count, LEN, width),
            key_rows.reshape(row_count, -1, width),
            value_rows.reshape(row_count, -1, width),
            upstream.reshape(row_count, LEN, width),
            log_totals,
            tgt_lengths,
            mem_lengths,
            mem_keep,
        ),
    )
    return (
        query_grad.reshape(-1, width),
        key_grad.reshape(-1, width),
        value_grad.reshape(-1, width),
    )


def lamb_pieces(weight, moment, second, grad, axes):
    moment = beta_one * moment + (1.0 - beta_one) * grad
    second = beta_two * second + (1.0 - beta_two) * grad * grad
    update = (
        moment / (1.0 - beta_one**STEP) / (jnp.sqrt(second / (1.0 - beta_two**STEP)) + epsilon)
        + decay * weight
    )
    return (moment, second, update, jnp.sum(weight * weight, axes), jnp.sum(update * update, axes))


def body(
    tokens,
    memory,
    cotangent,
    tgt_lengths,
    mem_lengths,
    mem_keep,
    row_expert,
    attn_weights,
    attn_moment,
    attn_second,
    expert_weights,
    expert_moment,
    expert_second,
    norm_params,
    norm_moment,
    norm_second,
):
    row_count = tgt_lengths.shape[0]
    attn_low, expert_low = (
        lax.all_gather(attn_weights.astype(jnp.bfloat16), "dp", axis=2, tiled=True),
        lax.all_gather(expert_weights.astype(jnp.bfloat16), "dp", axis=2, tiled=True),
    )
    row_low = expert_low[row_expert]
    norms = lax.all_gather(norm_params, "dp", axis=1, tiled=True)
    residual = tokens.astype(jnp.float32)
    normed_self, back_self = jax.vjp(norm_layer, residual, norms[0], norms[1])
    self_rows = gather_rows(normed_self.astype(jnp.bfloat16))
    self_qkv = jnp.einsum(
        "td,jdc->jtc", self_rows, attn_low[0, :3], preferred_element_type=jnp.float32
    ).astype(jnp.bfloat16)
    self_mix, self_log = attend_rows(
        self_qkv[0], self_qkv[1], self_qkv[2], tgt_lengths, mem_lengths, mem_keep, False
    )
    self_low = self_mix.astype(jnp.bfloat16)
    first_sum = residual + spread_rows(project_back(self_low, attn_low[0, 3]))
    normed_cross, back_cross = jax.vjp(norm_layer, first_sum, norms[2], norms[3])
    cross_rows = gather_rows(normed_cross.astype(jnp.bfloat16))
    memory_rows = gather_rows(memory)
    cross_queries = project(cross_rows, attn_low[1, 0]).astype(jnp.bfloat16)
    cross_kv = jnp.einsum(
        "td,jdc->jtc", memory_rows, attn_low[1, 1:3], preferred_element_type=jnp.float32
    ).astype(jnp.bfloat16)
    cross_mix, cross_log = attend_rows(
        cross_queries, cross_kv[0], cross_kv[1], tgt_lengths, mem_lengths, mem_keep, True
    )
    cross_low = cross_mix.astype(jnp.bfloat16)
    second_sum = first_sum + spread_rows(project_back(cross_low, attn_low[1, 3]))
    normed_ffn, back_ffn = jax.vjp(norm_layer, second_sum, norms[4], norms[5])
    ffn_rows = gather_rows(normed_ffn.astype(jnp.bfloat16))

    def expert_forward(row_item):
        row_in, chosen = row_item
        inner_act = project(row_in, chosen[0])
        hidden = jax.nn.gelu(inner_act).astype(jnp.bfloat16)
        return (inner_act, project_back(hidden, chosen[1]))

    inner_all, branch_all = lax.map(expert_forward, (ffn_rows.reshape(row_count, LEN, D), row_low))
    layer_out = (second_sum + spread_rows(branch_all.reshape(row_count * LEN, D))).astype(
        jnp.bfloat16
    )
    grad_ffn = cotangent.astype(jnp.float32)
    upstream_ffn = gather_rows(cotangent)
    ffn_again = gather_rows(normed_ffn.astype(jnp.bfloat16))

    def expert_backward(row_item):
        row_in, inner_act, upstream, chosen = row_item
        hidden, gelu_back = jax.vjp(jax.nn.gelu, inner_act)
        inner_grad = gelu_back(project(upstream, chosen[1]))[0].astype(jnp.bfloat16)
        pair_grads = jnp.stack(
            [outer_grad(row_in, inner_grad), outer_grad(upstream, hidden.astype(jnp.bfloat16))]
        )
        return (pair_grads, project_back(inner_grad, chosen[0]))

    row_grads, ffn_part = lax.map(
        expert_backward,
        (
            ffn_again.reshape(row_count, LEN, D),
            inner_all,
            upstream_ffn.reshape(row_count, LEN, D),
            row_low,
        ),
    )
    normed_ffn_grad = spread_rows(ffn_part.reshape(row_count * LEN, D))
    back_tokens, gain_ffn, shift_ffn = back_ffn(normed_ffn_grad)
    grad_cross = grad_ffn + back_tokens
    upstream_cross = gather_rows(grad_cross.astype(jnp.bfloat16))
    cross_again = gather_rows(normed_cross.astype(jnp.bfloat16))
    memory_again = gather_rows(memory)
    cross_up = project(upstream_cross, attn_low[1, 3]).astype(jnp.bfloat16)
    cross_dq, cross_dk, cross_dv = attend_back_rows(
        cross_queries,
        cross_kv[0],
        cross_kv[1],
        cross_up,
        cross_log,
        tgt_lengths,
        mem_lengths,
        mem_keep,
        True,
    )
    cross_grads = jnp.stack(
        [
            outer_grad(cross_again, cross_dq),
            outer_grad(memory_again, cross_dk),
            outer_grad(memory_again, cross_dv),
            outer_grad(upstream_cross, cross_low),
        ]
    )
    normed_cross_grad, memory_total = (
        lax.psum_scatter(
            project_back(cross_dq, attn_low[1, 0]), "tensor", scatter_dimension=0, tiled=True
        ),
        lax.psum_scatter(
            project_back(cross_dk, attn_low[1, 1]) + project_back(cross_dv, attn_low[1, 2]),
            "tensor",
            scatter_dimension=0,
            tiled=True,
        ),
    )
    back_tokens, gain_cross, shift_cross = back_cross(normed_cross_grad)
    grad_self = grad_cross + back_tokens
    upstream_self = gather_rows(grad_self.astype(jnp.bfloat16))
    self_again = gather_rows(normed_self.astype(jnp.bfloat16))
    self_up = project(upstream_self, attn_low[0, 3]).astype(jnp.bfloat16)
    self_dq, self_dk, self_dv = attend_back_rows(
        self_qkv[0],
        self_qkv[1],
        self_qkv[2],
        self_up,
        self_log,
        tgt_lengths,
        mem_lengths,
        mem_keep,
        False,
    )
    self_grads = jnp.stack(
        [
            outer_grad(self_again, self_dq),
            outer_grad(self_again, self_dk),
            outer_grad(self_again, self_dv),
            outer_grad(upstream_self, self_low),
        ]
    )
    normed_self_grad = spread_rows(
        project_back(self_dq, attn_low[0, 0])
        + project_back(self_dk, attn_low[0, 1])
        + project_back(self_dv, attn_low[0, 2])
    )
    back_tokens, gain_self, shift_self = back_self(normed_self_grad)
    input_grad = (grad_self + back_tokens).astype(jnp.bfloat16)
    attn_grad = jnp.stack([self_grads, cross_grads])
    norm_grad = jnp.stack([gain_self, shift_self, gain_cross, shift_cross, gain_ffn, shift_ffn])
    norm_total = lax.psum(norm_grad, "tensor")
    selector = (row_expert[:, None] == jnp.arange(E, dtype=jnp.int32)[None, :]).astype(jnp.float32)
    expert_grad = jnp.einsum("re,rjdf->ejdf", selector, row_grads, precision=lax.Precision.HIGHEST)
    expert_shard = lax.psum_scatter(expert_grad, "dp", scatter_dimension=2, tiled=True)
    attn_shard, norm_shard = (
        lax.psum_scatter(attn_grad, "dp", scatter_dimension=2, tiled=True),
        lax.psum_scatter(norm_total, "dp", scatter_dimension=1, tiled=True),
    )
    attn_pieces = lamb_pieces(attn_weights, attn_moment, attn_second, attn_shard, (2, 3))
    expert_pieces = lamb_pieces(expert_weights, expert_moment, expert_second, expert_shard, (2, 3))
    norm_pieces = lamb_pieces(norm_params, norm_moment, norm_second, norm_shard, (1,))
    copy_share = 1.0 / lax.axis_size("tensor")
    weight_squares = jnp.concatenate(
        [attn_pieces[3].reshape(-1), expert_pieces[3].reshape(-1), norm_pieces[3] * copy_share]
    )
    update_squares = jnp.concatenate(
        [attn_pieces[4].reshape(-1), expert_pieces[4].reshape(-1), norm_pieces[4] * copy_share]
    )
    weight_total, update_total = lax.psum((weight_squares, update_squares), ("dp", "tensor"))
    weight_norm = jnp.sqrt(weight_total)
    update_norm = jnp.sqrt(update_total)
    trust_ratio = weight_norm / update_norm
    attn_ratio = trust_ratio[:8].reshape(2, 4, 1, 1)
    expert_ratio = trust_ratio[8 : 8 + 2 * E].reshape(E, 2, 1, 1)
    norm_ratio = trust_ratio[8 + 2 * E :].reshape(6, 1)
    attn_new = attn_weights - rate * attn_ratio * attn_pieces[2]
    expert_new = expert_weights - rate * expert_ratio * expert_pieces[2]
    norm_new = norm_params - rate * norm_ratio * norm_pieces[2]
    lamb_norms = jnp.stack([weight_norm, update_norm])
    return (
        layer_out,
        input_grad,
        memory_total.astype(jnp.bfloat16),
        attn_new,
        attn_pieces[0],
        attn_pieces[1],
        expert_new,
        expert_pieces[0],
        expert_pieces[1],
        norm_new,
        norm_pieces[0],
        norm_pieces[1],
        lamb_norms,
    )


MEGA = 1024 * 1024
QUERY_BLOCK = 256
WINDOW_STEPS = {False: 128, True: 256}
FORWARD_MEGA, BACKWARD_MEGA, EXPERT_MEGA = 26, 36, 28
PART = jnp.bfloat16
SUM = jnp.bfloat16
HALVES = (slice(0, LEN // 2), slice(LEN // 2, LEN))
KERNEL_COST = pl.CostEstimate(flops=10**6, bytes_accessed=1024, transcendentals=0)
WHOLE = pl.BlockSpec(memory_space=pltpu.VMEM)
OUTSIDE = pl.BlockSpec(memory_space=pltpu.HBM)
ANYWHERE = pl.BlockSpec(memory_space=pl.ANY)


def outside(shape, dtype):
    return pltpu.HBM(shape, dtype)


def stay_outside(arrays):
    return [pltpu.with_memory_space_constraint(array, pltpu.HBM) for array in arrays]


SCALARS = pl.BlockSpec(memory_space=pltpu.SMEM)


def mm(left, right):
    return lax.dot_general(left, right, (((1,), (0,)), ((), ())), preferred_element_type=jnp.float32)


def mt(left, right):
    return lax.dot_general(left, right, (((1,), (1,)), ((), ())), preferred_element_type=jnp.float32)


def tm(left, right):
    return lax.dot_general(left, right, (((0,), (0,)), ((), ())), preferred_element_type=jnp.float32)


def low(values):
    return values.astype(jnp.bfloat16)


def standardize(values):
    centered = values - jnp.mean(values, -1, keepdims=True)
    inverse = lax.rsqrt(jnp.mean(centered * centered, -1, keepdims=True) + 1e-05)
    return centered * inverse, inverse


def norm_back(values, grad, gain_vec):
    unit, inverse = standardize(values)
    inner = grad * gain_vec
    back = inverse * (
        inner
        - jnp.mean(inner, -1, keepdims=True)
        - unit * jnp.mean(inner * unit, -1, keepdims=True)
    )
    return back, jnp.sum(grad * unit, 0, keepdims=True), jnp.sum(grad, 0, keepdims=True)


def key_limits(facts, places, cross):
    zero = jnp.zeros(places.shape, jnp.int32)
    low_end, high_end, doc_end = zero, zero, 0
    for doc in range(8):
        begin, doc_end = doc_end, doc_end + facts[0, doc]
        if cross:
            low_end = low_end + jnp.where(places >= doc_end, facts[0, 8 + doc], 0)
            high_end = high_end + jnp.where(places >= begin, facts[0, 8 + doc], 0)
        else:
            low_end = jnp.where(places >= doc_end, doc_end, low_end)
    return low_end, (high_end if cross else places + 1)


def kept_keys(facts, keep, places):
    kept = keep == 1
    begin = 0
    for doc in range(8):
        kept = kept | (places == begin)
        begin = begin + facts[0, 8 + doc]
    return kept


def key_windows(facts, cross, run):
    def block(index, _):
        first_query = pl.multiple_of(index * QUERY_BLOCK, QUERY_BLOCK)
        lowest, _ = key_limits(facts, first_query, cross)
        _, highest = key_limits(facts, first_query + QUERY_BLOCK - 1, cross)
        begin = lax.div(lowest, 128) * 128
        need = highest - begin
        unit = WINDOW_STEPS[cross]
        for width in range(unit, (MLEN if cross else 512 + QUERY_BLOCK) + 1, unit):
            start = pl.multiple_of(jnp.minimum(begin, MLEN - width), 128)

            @pl.when((need <= width) & (need > width - unit))
            def _(start=start, width=width):
                run(first_query, start, width)

        return 0

    lax.fori_loop(0, LEN // QUERY_BLOCK, block, 0)


def allowed_bias(facts, keep_ref, cross, first_query, start, width):
    places = first_query + lax.broadcasted_iota(jnp.int32, (1, QUERY_BLOCK), 1)
    low_end, high_end = key_limits(facts, places, cross)
    keys = start + lax.broadcasted_iota(jnp.int32, (width, QUERY_BLOCK), 0)
    if cross:
        own = start + lax.broadcasted_iota(jnp.int32, (width, 1), 0)
        keys = jnp.where(kept_keys(facts, keep_ref[pl.ds(start, width), 0:1], own), keys, -1)
    return jnp.where((keys >= low_end) & (keys < high_end), 0.0, -1e30)


def head_lanes(half):
    lane = lax.broadcasted_iota(jnp.int32, (1, 2 * HD), 1)
    return (lane < HD) if half == 0 else (lane >= HD)


def head_tile(head):
    return slice(head // 2 * 2 * HD, (head // 2 + 1) * 2 * HD)


def value_lines(head):
    return slice((head ^ 1) * HD, ((head ^ 1) + 1) * HD)


def of_head(values, half):
    return jnp.where(head_lanes(half), values, jnp.zeros_like(values))


def gather_weights(plane, w_refs, pack, first, second):
    left = head_lanes(0)
    cores, rows = 2, D // (2 * len(w_refs))
    heads = w_refs[0].shape[0] // cores
    lines = slice(pack * rows, (pack + 1) * rows)
    for distance, w_ref in enumerate(w_refs):
        for core in range(cores):
            begin = pl.multiple_of(((plane ^ distance) * cores + core) * rows, rows)
            for pair in range(heads // 2):
                even = w_ref[core * heads + 2 * pair, lines]
                odd = w_ref[core * heads + 2 * pair + 1, lines]
                at = slice(pair * 2 * HD, (pair + 1) * 2 * HD)
                first[pl.ds(begin, rows), at] = jnp.where(left, even, odd)
                second[pl.ds(begin, rows), at] = jnp.where(left, odd, even)


def scatter_grads(plane, g_refs, pack, held, values):
    first, second = held
    first[:D, :], second[:D, :] = values
    left = head_lanes(0)
    cores, rows = 2, D // (2 * len(g_refs))
    heads = g_refs[0].shape[0] // cores
    lines = slice(pack * rows, (pack + 1) * rows)
    for distance, g_ref in enumerate(g_refs):
        for core in range(cores):
            begin = pl.multiple_of(((plane ^ distance) * cores + core) * rows, rows)
            for pair in range(heads // 2):
                at = slice(pair * 2 * HD, (pair + 1) * 2 * HD)
                one, two = first[pl.ds(begin, rows), at], second[pl.ds(begin, rows), at]
                g_ref[core * heads + 2 * pair, lines] = low(jnp.where(left, one, two))
                g_ref[core * heads + 2 * pair + 1, lines] = low(jnp.where(left, two, one))


def gather_norms(plane, w_refs, norms):
    left = head_lanes(0)
    heads = w_refs[0].shape[0] // 2
    first = 2 * D // (2 * len(w_refs))
    for distance, w_ref in enumerate(w_refs):
        parts = []
        for core in (0, 1):
            parts.append(join_norms(w_ref[core * heads, first : first + 16]))
        at = pl.ds(pl.multiple_of((plane ^ distance) * 2 * HD, 2 * HD), 2 * HD)
        norms[:, at] = jnp.where(left, *parts)


def split_norms(values):
    high = low(values).astype(jnp.float32)
    middle = low(values - high).astype(jnp.float32)
    least = low(values - high - middle).astype(jnp.float32)
    return low(jnp.concatenate([jnp.where(head_lanes(0), high, middle), least], 0))


def join_norms(held):
    held = held.astype(jnp.float32)
    return (held[0:8] + pltpu.roll(held[0:8], HD, 1)) + held[8:16]


def scatter_norms(plane, g_refs, norms):
    heads = g_refs[0].shape[0] // 2
    first = D // len(g_refs)
    for distance, g_ref in enumerate(g_refs):
        at = pl.ds(pl.multiple_of((plane ^ distance) * 2 * HD, 2 * HD), 2 * HD)
        tile = norms[:, at]
        for core in (0, 1):
            values = jnp.where(head_lanes(core), tile, pltpu.roll(tile, HD, 1))
            for head in range(heads):
                g_ref[core * heads + head, first : first + 16] = split_norms(values)


class Moved:
    def __init__(self, values):
        self.values, self.shape, self.dtype = values, values.shape, values.dtype


class Arriving:
    def __init__(self, held, copies):
        self.held, self.copies = held, list(copies)

    def half(self, which):
        copy, self.copies[which] = self.copies[which], None
        if copy is not None:
            copy.wait()
        return self.held

    def get(self):
        for which in range(len(self.copies)):
            self.half(which)
        return self.held


class Leaving:
    def __init__(self, held, copies):
        self.held, self.copies, self.sent = held, list(copies), 0

    def send(self, upto=None):
        while self.sent < (len(self.copies) if upto is None else upto):
            self.copies[self.sent].start()
            self.sent += 1

    def finish(self):
        for copy in self.copies:
            copy.wait()


def half_at(core_ref, other):
    half = LEN // 2
    core = core_ref[0, 0]
    return pl.ds(pl.multiple_of((1 - core if other else core) * half, half), half)


def copies_of(kind, refs, held, core_ref, sems):
    if kind in ("one", "small"):
        pairs = [(refs[0], held)]
    elif kind == "halves":
        pairs = [(refs[0].at[at], held.at[at]) for at in HALVES]
    else:
        pairs = [(ref, held.at[half_at(core_ref, other)]) for ref, other in zip(refs, (False, True))]
    return pairs, [next(sems) for _ in pairs]


def staged_call(body, name, scalars, inputs, outputs, scratch, mega):
    in_count = sum(len(arrays) for _, arrays in inputs)
    shapes = []
    for kind, shape, dtype in outputs:
        if kind == "cores":
            shapes += [outside((shape[0] // 2, *shape[1:]), dtype)] * 2
        elif kind == "own":
            shapes += [outside((shape[0] // 2, *shape[1:]), dtype)]
        else:
            shapes += [outside(shape, dtype)]
    held_in = []
    for kind, arrays in inputs:
        rows, *others = arrays[0].shape
        rows = 2 * rows if kind == "cores" else rows
        held_in.append(pltpu.VMEM((rows, *others), arrays[0].dtype))
    held_out = [pltpu.VMEM(shape, dtype) for _, shape, dtype in outputs]
    waits = 2 * (len(inputs) + len(outputs))

    def kernel(*refs):
        refs = list(refs)

        def take(count):
            taken = refs[:count]
            del refs[:count]
            return taken

        scalar_refs, in_refs, out_refs = take(len(scalars)), take(in_count), take(len(shapes))
        in_held, out_held, (sem_ref,) = take(len(inputs)), take(len(outputs)), take(1)
        sems = (sem_ref.at[place] for place in range(waits))
        core_ref = scalar_refs[0]
        arrivals, starts = [], []
        for (kind, arrays), held in zip(inputs, in_held):
            mine, in_refs = in_refs[: len(arrays)], in_refs[len(arrays) :]
            pairs, own = copies_of(kind, mine, held, core_ref, sems)
            copies = [pltpu.make_async_copy(a, b, sem) for (a, b), sem in zip(pairs, own)]
            turn = {"small": (0,), "halves": (1, 2), "cores": (2, 2), "one": (3,)}[kind]
            starts += zip(turn, copies)
            arrivals.append(Arriving(held, copies))
        for _, copy in sorted(starts, key=lambda item: item[0]):
            copy.start()
        departures = []
        for (kind, _, _), held in zip(outputs, out_held):
            mine = out_refs[: 2 if kind == "cores" else 1]
            out_refs = out_refs[len(mine) :]
            pairs, own = copies_of("cores" if kind == "own" else kind, mine, held, core_ref, sems)
            copies = [pltpu.make_async_copy(b, a, sem) for (a, b), sem in zip(pairs, own)]
            departures.append(Leaving(held, copies))
        body(scalar_refs, arrivals, departures, refs)
        for arrival in arrivals:
            arrival.get()
        for departure in departures:
            departure.send()
        for departure in departures:
            departure.finish()

    arrays = [array for _, group in inputs for array in group]
    moved = [place for place, array in enumerate(arrays) if isinstance(array, Moved)]
    arrays = [array.values if isinstance(array, Moved) else array for array in arrays]
    arrays = [
        array if place in moved else stay_outside([array])[0] for place, array in enumerate(arrays)
    ]
    return pl.pallas_call(
        kernel,
        name=name,
        out_shape=tuple(shapes),
        in_specs=[SCALARS] * len(scalars)
        + [ANYWHERE if place in moved else OUTSIDE for place in range(in_count)],
        out_specs=(OUTSIDE,) * len(shapes),
        scratch_shapes=held_in + held_out + [pltpu.SemaphoreType.DMA((waits,))] + scratch,
        compiler_params=pltpu.CompilerParams(vmem_limit_bytes=mega * MEGA),
        cost_estimate=KERNEL_COST,
    )(*scalars, *arrays)


def forward_heads(plane, facts, keep_ref, cross, query_rows, key_rows, w_refs, outs, scratch):
    w_q, w_k, w_v, w_o, values_turned, blended_turned = scratch
    part, queries_out, keys_out, values_out, blended_out, stats_out = outs
    q_ref, k_ref, o_ref, stats_ref = (
        out.held for out in (queries_out, keys_out, blended_out, stats_out)
    )
    w_refs = [w_ref.get() for w_ref in w_refs]
    gather_weights(plane, w_refs, 0, w_q, w_v)
    gather_weights(plane, w_refs, 1, w_k, w_o)
    for out, rows, weights in (
        (queries_out, query_rows, w_q),
        (keys_out, key_rows, w_k),
        (values_out, key_rows, w_v),
    ):
        out.held[...] = low(mm(rows[...], weights[...]))
        out.send()
    values_turned[...] = values_out.held[...].T
    stats_ref[...] = jnp.zeros_like(stats_ref)
    heads = q_ref.shape[1] // HD

    def one(first_query, start, width):
        at, keys_at = pl.ds(first_query, QUERY_BLOCK), pl.ds(start, width)
        bias = allowed_bias(facts, keep_ref, cross, first_query, start, width)
        scores = []
        for head in range(heads):
            tile = head_tile(head)
            queries = of_head(q_ref[at, tile] * HD ** (-0.5), head % 2)
            scores.append(mt(k_ref[keys_at, tile], queries) + bias)
        done = []
        for head in range(heads):
            top = jnp.max(scores[head], 0, keepdims=True)
            weights = jnp.exp(scores[head] - top)
            total = jnp.sum(weights, 0, keepdims=True)
            stats_ref[head : head + 1, at] = top + jnp.log(total)
            done.append((low(weights), 1.0 / total))
        for head, (weights, share) in enumerate(done):
            lines = value_lines(head)
            blended_turned[lines, at] = low(mm(values_turned[lines, keys_at], weights) * share)

    key_windows(facts, cross, one)
    for which, at in enumerate(HALVES):
        o_ref[at, :] = blended_turned[:, at].T
        part.held[at, :] = mt(o_ref[at, :], w_o[...]).astype(PART)
        part.send(which + 1)


def self_forward_body(scalars, ins, outs, scratch):
    core_ref, facts = scalars
    tokens, *w_refs = ins
    part, norms, rows, *heads = outs
    plane = core_ref[0, 1]
    tokens = tokens.get()
    units = [standardize(tokens[at, :].astype(jnp.float32))[0] for at in HALVES]
    gather_norms(plane, [w_ref.get() for w_ref in w_refs], norms.held)
    norms.send()
    for at, unit in zip(HALVES, units):
        rows.held[at, :] = low(unit * norms.held[0:1, :] + norms.held[1:2, :])
    rows.send()
    forward_heads(
        plane, facts, None, False, rows.held, rows.held, w_refs, (part, *heads), scratch
    )


def cross_forward_body(scalars, ins, outs, scratch):
    core_ref, facts = scalars
    part_mine, part_theirs, tokens, norms, keep, memory, *w_refs = ins
    part, total, rows, *heads = outs
    tokens, norms = tokens.get(), norms.get()
    for which, at in enumerate(HALVES):
        ours = part_mine.half(which)[at, :].astype(jnp.float32)
        value = tokens[at, :].astype(jnp.float32) + (
            ours + part_theirs.half(which)[at, :].astype(jnp.float32)
        )
        total.held[at, :] = value.astype(SUM)
        total.send(which + 1)
        unit, _ = standardize(value)
        rows.held[at, :] = low(unit * norms[2:3, :] + norms[3:4, :])
    rows.send()
    keep_turned, *scratch = scratch
    keep_turned[...] = jnp.broadcast_to(keep.get()[...], (128, MLEN)).T
    forward_heads(
        core_ref[0, 1],
        facts,
        keep_turned,
        True,
        rows.held,
        memory.get(),
        w_refs,
        (part, *heads),
        scratch,
    )


def attn_forward(name, body, scalars, inputs, weights, extra, cross):
    cols = weights[0].shape[0] // 2 * HD
    bfloat16 = jnp.bfloat16
    outputs = [
        ("halves", (LEN, D), PART),
        extra,
        ("one", (LEN, D), bfloat16),
        *[("one", (LEN, cols), bfloat16)] * 4,
        ("one", (8, LEN), jnp.float32),
    ]
    scratch = [pltpu.VMEM((D, cols), bfloat16)] * 4
    scratch += [pltpu.VMEM((cols, MLEN), bfloat16), pltpu.VMEM((cols, LEN), bfloat16)]
    if cross:
        scratch = [pltpu.VMEM((MLEN, 128), jnp.int32)] + scratch
    inputs = inputs + [("one", (Moved(block),)) for block in weights]
    return staged_call(body, name, scalars, inputs, outputs, scratch, FORWARD_MEGA)


def backward_heads(plane, facts, keep_ref, cross, up_rows, w_refs, heads, scratch):
    w_q, w_k, w_v, w_o, weighted, up, keys_turned, q_turned, dq, k_sum, v_sum, dk, dv = scratch
    w_refs = [w_ref.get() for w_ref in w_refs]
    gather_weights(plane, w_refs, 0, w_q, w_v)
    gather_weights(plane, w_refs, 1, w_k, w_o)
    scale = HD ** (-0.5)
    up[...] = low(mm(up_rows[...], w_o[...]))
    q_ref, k_ref, v_ref, o_ref, stats_ref = (head.get() for head in heads)
    keys_turned[...] = k_ref[...].T
    k_sum[...] = jnp.zeros_like(k_sum)
    v_sum[...] = jnp.zeros_like(v_sum)

    products = (up[...].astype(jnp.float32) * o_ref[...].astype(jnp.float32)).T
    heads = q_ref.shape[1] // HD
    for head in range(heads):
        weighted[head : head + 1, :] = jnp.sum(products[value_lines(head), :], 0, keepdims=True)

    def one(first_query, start, width):
        at, keys_at = pl.ds(first_query, QUERY_BLOCK), pl.ds(start, width)
        bias = allowed_bias(facts, keep_ref, cross, first_query, start, width)
        ready, done, adds = [], [], []
        for head in range(heads):
            tile = head_tile(head)
            queries = of_head(q_ref[at, tile], head % 2)
            upstream = of_head(up[at, tile], 1 - head % 2)
            scores = mt(k_ref[keys_at, tile], queries * scale)
            ready.append((queries, upstream, scores, mt(v_ref[keys_at, tile], upstream)))
        for head, (_, _, scores, prob_grad) in enumerate(ready):
            probs = jnp.exp(scores + bias - stats_ref[head : head + 1, at])
            score_grad = low(probs * (prob_grad - weighted[head : head + 1, at]))
            done.append((low(probs), score_grad))
        for head, (probs, score_grad) in enumerate(done):
            queries, upstream, _, _ = ready[head]
            lines = slice(head * HD, (head + 1) * HD)
            q_turned[lines, at] = low(mm(keys_turned[lines, keys_at], score_grad) * scale)
            adds.append((mm(score_grad, queries), mm(probs, upstream)))
        for head in range(0, heads, 2):
            tile = head_tile(head)
            (key_one, value_one), (key_two, value_two) = adds[head : head + 2]
            k_sum[keys_at, tile] = k_sum[keys_at, tile] + (key_one + key_two)
            v_sum[keys_at, tile] = v_sum[keys_at, tile] + (value_one + value_two)

    key_windows(facts, cross, one)
    dq[...] = q_turned[...].T
    dk[...] = low(k_sum[...] * scale)
    dv[...] = low(v_sum[...])


def norm_step(parts, total, norms, row, upstream, finish):
    gains = jnp.zeros((1, D), jnp.float32)
    shifts = jnp.zeros((1, D), jnp.float32)
    for which, at in enumerate(HALVES):
        mine, theirs = (part.half(which)[at, :].astype(jnp.float32) for part in parts)
        back, gain, shift = norm_back(
            total.half(which)[at, :].astype(jnp.float32), mine + theirs, norms[row : row + 1, :]
        )
        gains, shifts = gains + gain, shifts + shift
        finish(which, at, upstream(which, at) + back)
    return gains, shifts


def cross_backward_body(scalars, ins, outs, scratch):
    core_ref, facts = scalars
    part_mine, part_theirs, total, cotangent, norms, keep, memory, *rest = ins
    planes = len(rest) - 6
    w_refs, (rows, *heads) = rest[:planes], rest[planes:]
    up_rows, part, memory_part, norm_out, *g_outs = outs
    turned, memory_turned, keep_turned, *scratch = scratch
    keep_turned[...] = jnp.broadcast_to(keep.get()[...], (128, MLEN)).T
    norms, cotangent = norms.get(), cotangent.get()
    plane = core_ref[0, 1]

    def finish(which, at, value):
        up_rows.held[at, :] = low(value)
        up_rows.send(which + 1)

    gains, shifts = norm_step(
        (part_mine, part_theirs),
        total,
        norms,
        4,
        lambda which, at: cotangent[at, :].astype(jnp.float32),
        finish,
    )
    norm_out.held[0:1, :] = 0.5 * gains
    norm_out.held[1:2, :] = 0.5 * shifts
    norm_out.send()
    backward_heads(plane, facts, keep_turned, True, up_rows.held, w_refs, heads, scratch)
    w_q, w_k, w_v, *_ = scratch
    dq, *held, dk, dv = scratch[-5:]
    for which, at in enumerate(HALVES):
        part.held[at, :] = mt(dq[at, :], w_q[...]).astype(PART)
        part.send(which + 1)
    memory_part.held[...] = low(mt(dk[...], w_k[...]) + mt(dv[...], w_v[...]))
    memory_part.send()
    g_refs = [out.held for out in g_outs]
    turned[...] = rows.get()[...].T
    memory_turned[...] = memory.get()[...].T
    scatter_grads(
        plane, g_refs, 0, held, (mm(turned[...], dq[...]), mm(memory_turned[...], dv[...]))
    )
    turned[...] = up_rows.held[...].T
    out_grad = mm(turned[...], heads[3].get()[...])
    scatter_grads(plane, g_refs, 1, held, (mm(memory_turned[...], dk[...]), out_grad))


def self_backward_body(scalars, ins, outs, scratch):
    core_ref, facts = scalars
    part_mine, part_theirs, total, grad, tokens, ffn_norm, norms, *rest = ins
    planes = len(rest) - 6
    w_refs, (rows, *heads) = rest[:planes], rest[planes:]
    grad_out, part, *g_outs = outs
    norm_grad, up_rows, turned, *scratch = scratch
    norms = norms.get()
    plane = core_ref[0, 1]

    def finish(which, at, value):
        grad_out.held[at, :] = value
        up_rows[at, :] = low(value)

    gains, shifts = norm_step(
        (part_mine, part_theirs),
        total,
        norms,
        2,
        lambda which, at: grad.half(which)[at, :].astype(jnp.float32),
        finish,
    )
    grad_out.send()
    norm_grad[2:3, :] = 0.5 * gains
    norm_grad[3:4, :] = 0.5 * shifts
    norm_grad[4:6, :] = ffn_norm.get()[...]
    norm_grad[6:8, :] = jnp.zeros((2, D), jnp.float32)
    backward_heads(plane, facts, None, False, up_rows, w_refs, heads, scratch)
    w_q, w_k, w_v, *_ = scratch
    dq, *held, dk, dv = scratch[-5:]
    tokens = tokens.get()
    gains = jnp.zeros((1, D), jnp.float32)
    shifts = jnp.zeros((1, D), jnp.float32)
    for at in HALVES:
        value = mt(dq[at, :], w_q[...]) + mt(dk[at, :], w_k[...]) + mt(dv[at, :], w_v[...])
        part.held[at, :] = value
        unit, _ = standardize(tokens[at, :].astype(jnp.float32))
        gains = gains + jnp.sum(value * unit, 0, keepdims=True)
        shifts = shifts + jnp.sum(value, 0, keepdims=True)
    part.send()
    norm_grad[0:1, :] = gains
    norm_grad[1:2, :] = shifts
    g_refs = [out.held for out in g_outs]
    scatter_norms(plane, g_refs, norm_grad)
    turned[...] = rows.get()[...].T
    scatter_grads(plane, g_refs, 0, held, (mm(turned[...], dq[...]), mm(turned[...], dv[...])))
    key_grad = mm(turned[...], dk[...])
    turned[...] = up_rows[...].T
    scatter_grads(plane, g_refs, 1, held, (key_grad, mm(turned[...], heads[3].get()[...])))


def attn_backward(name, body, scalars, inputs, weights, kept, outputs, cross):
    cols = weights[0].shape[0] // 2 * HD
    bfloat16 = jnp.bfloat16
    block = (weights[0].shape[0], D // len(weights) + (0 if cross else 16), 2 * HD)
    outputs = outputs + [("one", block, bfloat16)] * len(weights)
    scratch = [pltpu.VMEM((D, LEN), bfloat16)]
    if not cross:
        scratch = [pltpu.VMEM((8, D), jnp.float32), pltpu.VMEM((LEN, D), bfloat16)] + scratch
    if cross:
        scratch += [pltpu.VMEM((D, MLEN), bfloat16), pltpu.VMEM((MLEN, 128), jnp.int32)]
    scratch += [pltpu.VMEM((D, cols), bfloat16)] * 4 + [
        pltpu.VMEM((8, LEN), jnp.float32),
        pltpu.VMEM((LEN, cols), bfloat16),
        pltpu.VMEM((cols, MLEN), bfloat16),
        pltpu.VMEM((cols, LEN), bfloat16),
        pltpu.VMEM((LEN, cols), bfloat16),
        pltpu.VMEM((MLEN, cols), jnp.float32),
        pltpu.VMEM((MLEN, cols), jnp.float32),
        pltpu.VMEM((MLEN, cols), bfloat16),
        pltpu.VMEM((MLEN, cols), bfloat16),
    ]
    inputs = inputs + [("one", (array,)) for array in (*map(Moved, weights), *kept)]
    return staged_call(body, name, scalars, inputs, outputs, scratch, BACKWARD_MEGA)


def add_to(ref, step, update):
    @pl.when(step == 0)
    def _():
        ref[...] = update

    @pl.when(step != 0)
    def _():
        ref[...] = ref[...] + update


def gelu_pieces(values):
    factor = 0.7978845608028654
    square = values * values
    slope = jnp.tanh(factor * values * (1.0 + 0.044715 * square))
    half = 0.5 * (1.0 + slope)
    grad = half + 0.5 * values * (1.0 - slope * slope) * factor * (1.0 + 3 * 0.044715 * square)
    return values * half, grad


def expert_kernel(
    core_ref,
    mine,
    theirs,
    part_mine,
    part_theirs,
    first_sum,
    norms,
    w_ref,
    sum_out,
    grad_out,
    out_keep,
    out_give,
    w_grad_ref,
    ours,
    others,
    sum_ref,
    exact,
    rows,
    up,
    grad_ref,
    out_total,
    grad_low,
    sems,
    out_sems,
):
    step = pl.program_id(0)

    def leaving(place):
        held, target = (
            (sum_ref, sum_out),
            (grad_low, grad_out),
            (out_total.at[half_at(core_ref, False)], out_keep),
            (out_total.at[half_at(core_ref, True)], out_give),
        )[place]
        return pltpu.make_async_copy(held, target, out_sems.at[place])

    @pl.when(step == 0)
    def _():
        up_copies = [
            pltpu.make_async_copy(a, up.at[half_at(core_ref, other)], sems.at[place])
            for place, (a, other) in enumerate(((mine, False), (theirs, True)))
        ]
        copies = [
            pltpu.make_async_copy(a.at[at], b.at[at], sems.at[2 + 3 * which + place])
            for which, at in enumerate(HALVES)
            for place, (a, b) in enumerate(
                ((part_mine, ours), (part_theirs, others), (first_sum, sum_ref))
            )
        ]
        for copy in copies[:3] + up_copies + copies[3:]:
            copy.start()
        for which, at in enumerate(HALVES):
            for copy in copies[3 * which : 3 * which + 3]:
                copy.wait()
            total = sum_ref[at, :].astype(jnp.float32) + (
                ours[at, :].astype(jnp.float32) + others[at, :].astype(jnp.float32)
            )
            exact[at, :] = total
            sum_ref[at, :] = total.astype(SUM)
            unit, _ = standardize(total)
            rows[at, :] = low(unit * norms[4:5, :] + norms[5:6, :])
        leaving(0).start()
        for copy in up_copies:
            copy.wait()

    shape = (D, w_ref.shape[4])
    w_in, w_out = w_ref[:, 0, 0].reshape(shape), w_ref[:, 0, 1].reshape(shape)
    back = mm(up[...], w_out)
    hidden, slope = gelu_pieces(mm(rows[...], w_in))
    hidden = low(hidden)
    inner_grad = low(slope * back)
    add_to(grad_ref, step, mt(inner_grad, w_in))
    add_to(out_total, step, mt(hidden, w_out))

    @pl.when(step == pl.num_programs(0) - 1)
    def _():
        grad_low[...] = grad_ref[...].astype(PART)
        at = half_at(core_ref, False)
        out_total[at, :] = out_total[at, :] + exact[at, :]
        for place in (1, 2, 3):
            leaving(place).start()

    grads = w_grad_ref.shape[0], -1, w_ref.shape[4]
    w_grad_ref[:, 0, 0] = low(tm(rows[...], inner_grad)).reshape(grads)
    w_grad_ref[:, 0, 1] = low(tm(up[...], hidden)).reshape(grads)

    @pl.when(step == pl.num_programs(0) - 1)
    def _():
        for place in range(4):
            leaving(place).wait()


def expert_layer(core_ref, rows, parts, first_sum, norms, weights):
    owners, steps, _, line_count, cols = weights.shape
    half = outside((LEN // 2, D), jnp.float32)
    w_spec = pl.BlockSpec((owners, 1, 2, line_count, cols), lambda step: (0, step, 0, 0, 0))
    low_rows = pltpu.VMEM((LEN, D), jnp.bfloat16)
    wide = pltpu.VMEM((LEN, D), jnp.float32)
    return pl.pallas_call(
        expert_kernel,
        name="expert",
        grid=(steps,),
        out_shape=(
            outside((LEN, D), SUM),
            outside((LEN, D), PART),
            half,
            half,
            outside(weights.shape, jnp.bfloat16),
        ),
        in_specs=[SCALARS, OUTSIDE, ANYWHERE, OUTSIDE, OUTSIDE, OUTSIDE, WHOLE, w_spec],
        out_specs=(OUTSIDE,) * 4 + (w_spec,),
        scratch_shapes=[pltpu.VMEM((LEN, D), PART)] * 2
        + [pltpu.VMEM((LEN, D), SUM), wide, low_rows, low_rows]
        + [wide, wide, pltpu.VMEM((LEN, D), PART)]
        + [pltpu.SemaphoreType.DMA((8,)), pltpu.SemaphoreType.DMA((4,))],
        compiler_params=pltpu.CompilerParams(vmem_limit_bytes=EXPERT_MEGA * MEGA),
        cost_estimate=KERNEL_COST,
    )(
        core_ref,
        *stay_outside(rows[:1]),
        rows[1],
        *stay_outside(parts),
        *stay_outside((first_sum, norms, weights)),
    )


def pack_attn_kernel(places, weights, norms, out_ref):
    odd = places[0, 0] == 1
    left = head_lanes(0)
    rows = weights.shape[2]
    count = norms.shape[0]
    values = jnp.concatenate(
        [norms[...], jnp.zeros((8 - count, norms.shape[1]), jnp.float32)], 0
    )
    facts = split_norms(jnp.concatenate([values, values], 1))
    blocks = out_ref.shape[0] // 2
    for core in (0, 1):
        for branch in range(weights.shape[0]):
            for pack in (0, 1):
                first, second = weights[branch, pack], weights[branch, 2 + pack]
                one = jnp.where(odd, second, first)
                two = jnp.where(odd, first, second)
                if core == 0:
                    tile = jnp.where(left, one, pltpu.roll(two, HD, 1))
                else:
                    tile = jnp.where(left, pltpu.roll(one, HD, 1), two)
                begin = pack * rows + branch * (2 * rows + 16)
                for block in range(blocks):
                    out_ref[core * blocks + block, begin : begin + rows] = low(tile)
        for block in range(blocks):
            out_ref[core * blocks + block, 2 * rows : 2 * rows + 16] = facts


def pack_attn(odd, weights, norms, tensor_count):
    shape = (2 * tensor_count, 4 * weights.shape[2] + 16, 2 * HD)
    return pl.pallas_call(
        pack_attn_kernel,
        name="pack_attn",
        out_shape=outside(shape, jnp.bfloat16),
        in_specs=[SCALARS, WHOLE, WHOLE],
        out_specs=WHOLE,
        compiler_params=pltpu.CompilerParams(vmem_limit_bytes=16 * MEGA),
        cost_estimate=KERNEL_COST,
    )(odd, *stay_outside((weights, norms)))


def pack_experts_kernel(chosen, weights, out_ref, held, sems):
    places, half = out_ref.shape[2], out_ref.shape[5]
    copies = [
        pltpu.make_async_copy(weights.at[chosen[0, row]], held.at[row], sems.at[row])
        for row in range(held.shape[0])
    ]
    for copy in copies:
        copy.start()
    for row, copy in enumerate(copies):
        copy.wait()
        for core in (0, 1):
            at = slice(core * half, (core + 1) * half)
            out_ref[row // places, core, row % places] = low(held[row, :, :, at])


def pack_experts(chip_expert, weights, plane_count, tensor_count):
    _, pair, rows, cols = weights.shape
    count = plane_count * tensor_count
    out = outside((plane_count, 2, tensor_count, pair, rows, cols // 2), jnp.bfloat16)
    return pl.pallas_call(
        pack_experts_kernel,
        name="pack_experts",
        out_shape=out,
        in_specs=[SCALARS, OUTSIDE],
        out_specs=WHOLE,
        scratch_shapes=[
            pltpu.VMEM((count, pair, rows, cols), jnp.float32),
            pltpu.SemaphoreType.DMA((count,)),
        ],
        compiler_params=pltpu.CompilerParams(vmem_limit_bytes=16 * MEGA),
        cost_estimate=KERNEL_COST,
    )(chip_expert, *stay_outside((weights,)))


def sum_planes_kernel(*refs):
    *parts, out_ref = refs
    count = len(parts) // 2
    rows = parts[count].shape[1]

    def total(blocks, index, lines):
        return sum(block[index, lines].astype(jnp.float32) for block in blocks)

    for index in range(out_ref.shape[0]):
        out_ref[index, :rows] = low(total(parts[:count], index, slice(0, rows)))
        norms = sum(join_norms(block[index, rows : rows + 16]) for block in parts[:count])
        out_ref[index, rows : rows + 16] = split_norms(norms)
        out_ref[index, rows + 16 :] = low(total(parts[count:], index, slice(0, rows)))


def sum_planes(self_parts, cross_parts):
    blocks, rows, cols = self_parts[0].shape
    shape = (blocks, rows + cross_parts[0].shape[1], cols)
    return pl.pallas_call(
        sum_planes_kernel,
        name="sum_planes",
        out_shape=outside(shape, jnp.bfloat16),
        in_specs=[WHOLE] * (len(self_parts) + len(cross_parts)),
        out_specs=WHOLE,
        compiler_params=pltpu.CompilerParams(vmem_limit_bytes=16 * MEGA),
        cost_estimate=KERNEL_COST,
    )(*self_parts, *cross_parts)


def lamb_update(weight, moment, second, grad):
    moment = beta_one * moment + (1.0 - beta_one) * grad
    second = beta_two * second + (1.0 - beta_two) * grad * grad
    update = (
        moment / (1.0 - beta_one**STEP) / (jnp.sqrt(second / (1.0 - beta_two**STEP)) + epsilon)
        + decay * weight
    )
    return moment, second, update


def expert_lamb_kernel(
    chosen, grads, w_ref, m_ref, v_ref, m_out, v_out, u_out, squares, total
):
    step = pl.program_id(0)
    half = grads.shape[5]
    group = w_ref.shape[0]
    for own in range(group):
        expert = step * group + own
        total[...] = jnp.zeros_like(total)
        for plane in range(grads.shape[0]):
            for place in range(grads.shape[2]):

                @pl.when(chosen[plane * grads.shape[2] + place] == expert)
                def _(plane=plane, place=place):
                    for core in (0, 1):
                        at = slice(core * half, (core + 1) * half)
                        total[:, :, at] = total[:, :, at] + grads[plane, core, place].astype(
                            jnp.float32
                        )

        weight = w_ref[own]
        m_out[own], v_out[own], update = lamb_update(weight, m_ref[own], v_ref[own], total[...])
        u_out[own] = low(update)
        squares[own] = jnp.concatenate(
            [jnp.sum(weight * weight, 1), jnp.sum(update * update, 1)], 0
        )


def expert_lamb(chip_expert, grads, weights, moments, seconds):
    experts, pair, rows, cols = weights.shape
    group = 4
    spec = pl.BlockSpec((group, pair, rows, cols), lambda step, chosen: (step, 0, 0, 0))
    return pl.pallas_call(
        expert_lamb_kernel,
        name="expert_lamb",
        out_shape=(outside(weights.shape, jnp.float32),) * 2
        + (outside(weights.shape, jnp.bfloat16),)
        + (jax.ShapeDtypeStruct((experts, 2 * pair, cols), jnp.float32),),
        grid_spec=pltpu.PrefetchScalarGridSpec(
            num_scalar_prefetch=1,
            grid=(experts // group,),
            in_specs=[WHOLE, spec, spec, spec],
            out_specs=(spec, spec, spec)
            + (pl.BlockSpec((group, 2 * pair, cols), lambda step, chosen: (step, 0, 0)),),
            scratch_shapes=[pltpu.VMEM((pair, rows, cols), jnp.float32)],
        ),
        compiler_params=pltpu.CompilerParams(vmem_limit_bytes=24 * MEGA),
        cost_estimate=KERNEL_COST,
    )(chip_expert, *stay_outside((grads, weights, moments, seconds)))


def owner_lamb_kernel(odd, chips, *refs):
    w_ref, m_ref, v_ref, norms, norm_m, norm_v, *outs = refs
    m_out, v_out, u_out, squares, norm_m_out, norm_v_out, norm_u_out, norm_squares = outs
    heads = chips.shape[0] // 2
    left = head_lanes(0)
    rows = w_ref.shape[2]
    for branch in range(w_ref.shape[0]):
        for pack in (0, 1):
            begin = pack * rows + branch * (2 * rows + 16)
            totals = []
            for core in (0, 1):
                totals.append(
                    sum(
                        chips[core * heads + head, begin : begin + rows].astype(jnp.float32)
                        for head in range(heads)
                    )
                )
            first = jnp.where(left, totals[0], pltpu.roll(totals[1], HD, 1))
            second = jnp.where(left, pltpu.roll(totals[0], HD, 1), totals[1])
            swapped = odd[0, 0] == 1
            for kind, grad in (
                (0, jnp.where(swapped, second, first)),
                (1, jnp.where(swapped, first, second)),
            ):
                matrix = 2 * kind + pack
                weight = w_ref[branch, matrix]
                m_out[branch, matrix], v_out[branch, matrix], update = lamb_update(
                    weight, m_ref[branch, matrix], v_ref[branch, matrix], grad
                )
                u_out[branch, matrix] = update
                squares[branch, matrix, 0:1] = jnp.sum(weight * weight, 0, keepdims=True)
                squares[branch, matrix, 1:2] = jnp.sum(update * update, 0, keepdims=True)
    grad = sum(join_norms(chips[index, 2 * rows : 2 * rows + 16]) for index in range(2 * heads))
    count, cols = norms.shape
    norm_m_out[...], norm_v_out[...], update = lamb_update(
        norms[...], norm_m[...], norm_v[...], grad[:count, :cols]
    )
    norm_u_out[...] = update
    norm_squares[0] = norms[...] * norms[...]
    norm_squares[1] = update * update


def owner_lamb(odd, chips, attn, norm):
    matrices, norms = attn[0].shape, norm[0].shape
    return pl.pallas_call(
        owner_lamb_kernel,
        name="owner_lamb",
        out_shape=(outside(matrices, jnp.float32),) * 3
        + (jax.ShapeDtypeStruct((*matrices[:2], 2, matrices[3]), jnp.float32),)
        + (jax.ShapeDtypeStruct(norms, jnp.float32),) * 3
        + (jax.ShapeDtypeStruct((2, *norms), jnp.float32),),
        in_specs=[SCALARS] + [WHOLE] * 7,
        out_specs=(WHOLE,) * 8,
        compiler_params=pltpu.CompilerParams(vmem_limit_bytes=16 * MEGA),
        cost_estimate=KERNEL_COST,
    )(odd, *stay_outside((chips, *attn, *norm)))


def final_step_kernel(sizes, moves, w_ref, u_ref, attn, attn_u, norms, norm_u, *rest):
    count = (len(rest) - 4) // 3
    sources, (out_ref, attn_out, norm_out) = rest[: 2 * count], rest[2 * count : 2 * count + 3]
    settled, sems = rest[2 * count + 3 : -1], rest[-1]
    step = pl.program_id(0)

    def settle(source, place):
        return pltpu.make_async_copy(source, settled[place], sems.at[place])

    for place in range(count):
        for source, moved in zip(sources[2 * place : 2 * place + 2], (0, 1)):

            @pl.when((step == 0) & (moves[0, 0] == moved))
            def _(source=source, place=place):
                settle(source, place).start()

    @pl.when(step == pl.num_programs(0) - 1)
    def _():
        for place in range(count):
            settle(sources[2 * place], place).wait()

    group, pair = out_ref.shape[:2]
    attn_count = attn.shape[0] * attn.shape[1]
    for own in range(group):
        for kind in range(pair):
            size = sizes[0, attn_count + (step * group + own) * pair + kind]
            out_ref[own, kind] = w_ref[own, kind] - size * u_ref[own, kind].astype(jnp.float32)

    @pl.when(step == 0)
    def _():
        for branch in range(attn.shape[0]):
            for matrix in range(attn.shape[1]):
                size = sizes[0, branch * attn.shape[1] + matrix]
                attn_out[branch, matrix] = attn[branch, matrix] - size * attn_u[branch, matrix]
        first = sizes.shape[1] - norms.shape[0]
        for row in range(norms.shape[0]):
            at = slice(row, row + 1)
            norm_out[at, :] = norms[at, :] - sizes[0, first + row] * norm_u[at, :]


def final_step(sizes, moves, weights, updates, attn, norm, landed):
    experts, pair, rows, cols = weights.shape
    group = 4
    spec = pl.BlockSpec((group, pair, rows, cols), lambda step: (step, 0, 0, 0))
    return pl.pallas_call(
        final_step_kernel,
        name="final_step",
        grid=(experts // group,),
        out_shape=(
            outside(weights.shape, jnp.float32),
            outside(attn[0].shape, jnp.float32),
            jax.ShapeDtypeStruct(norm[0].shape, jnp.float32),
        )
        + tuple(outside(array.shape, array.dtype) for array in landed[::2]),
        in_specs=[SCALARS, SCALARS, spec, spec] + [WHOLE] * 4 + [ANYWHERE] * len(landed),
        out_specs=(spec, WHOLE, WHOLE) + (OUTSIDE,) * (len(landed) // 2),
        scratch_shapes=[pltpu.SemaphoreType.DMA((len(landed) // 2,))],
        compiler_params=pltpu.CompilerParams(vmem_limit_bytes=24 * MEGA),
        cost_estimate=KERNEL_COST,
    )(sizes, moves, *stay_outside((weights, updates, *attn, *norm)), *landed)


DEVICES = ("plane", "core", "tensor")
CHIP = ("core", "tensor")


def twin(values):
    return lax.ppermute(values, "core", ((0, 1), (1, 0)))


def exchange(values, axes):
    return lax.all_to_all(values, axes, 0, 0, tiled=True)


def swap_pairs(plane_count, tensor_count):
    pairs = []
    for plane in range(plane_count):
        for core in range(2):
            for place in range(tensor_count):
                target = (plane * 2 + place % 2) * tensor_count + place // 2 * 2 + core
                here = (plane * 2 + core) * tensor_count + place
                if target != here:
                    pairs.append((here, target))
    return pairs


def other_planes(blocks):
    planes = range(lax.axis_size("plane"))
    return [
        lax.ppermute(block, "plane", [(k, k ^ distance) for k in planes]) if distance else block
        for distance, block in enumerate(blocks)
    ]


def sum_devices(values, axes):
    for axis in axes:
        count, flip = lax.axis_size(axis), 1
        while flip < count:
            values = values + lax.ppermute(values, axis, [(k, k ^ flip) for k in range(count)])
            flip *= 2
    return values


def body_rows(
    tokens,
    memory,
    cotangent,
    tgt_lengths,
    mem_lengths,
    mem_keep,
    row_expert,
    attn_weights,
    attn_moment,
    attn_second,
    expert_weights,
    expert_moment,
    expert_second,
    norm_params,
    norm_moment,
    norm_second,
):
    plane_count, tensor_count = lax.axis_size("plane"), lax.axis_size("tensor")
    devices = plane_count * 2 * tensor_count
    core, place = lax.axis_index("core"), lax.axis_index("tensor")
    moves = swap_pairs(plane_count, tensor_count)

    moving = core != place % 2

    def swap(values):
        return lax.ppermute(values, DEVICES, moves)

    def own_row(values):
        return jnp.where(moving, swap(values), values)

    plane = lax.axis_index("plane")
    core_ref = jnp.stack([core, plane]).reshape(1, 2)
    odd = (place % 2).reshape(1, 1)
    packed = pack_attn(odd, attn_weights, norm_params, tensor_count)
    tokens_mine = own_row(tokens)
    owned = jnp.arange(plane_count * 2)[:, None] == plane * 2 + core
    owner_expert = sum_devices(jnp.where(owned, row_expert[None], 0), ("core", "plane"))
    chip_expert = owner_expert.reshape(plane_count, 2, 2).transpose(0, 2, 1).reshape(1, -1)
    facts = jnp.concatenate([tgt_lengths, mem_lengths, mem_keep], 1)
    facts = jnp.where(core == place % 2, facts, twin(facts))
    facts = lax.dynamic_slice_in_dim(facts, place // 2, 1, 0)
    facts, keep = facts[:, :16], facts[:, 16:]
    chips = exchange(packed, CHIP)
    tokens_theirs = twin(tokens_mine)
    chips, tokens_mine, tokens_theirs, memory, cotangent, chip_expert = lax.optimization_barrier(
        (chips, tokens_mine, tokens_theirs, memory, cotangent, chip_expert)
    )
    self_lines = 2 * attn_weights.shape[2] + 16
    self_weights = other_planes([chips[:, :self_lines]] * plane_count)
    memory_mine = own_row(memory)
    up_mine = own_row(cotangent)
    cross_weights = other_planes([chips[:, self_lines:]] * plane_count)
    chosen = pack_experts(chip_expert, expert_weights, plane_count, tensor_count)
    memory_mine, up_mine, chosen, *self_weights = lax.optimization_barrier(
        (memory_mine, up_mine, chosen, *self_weights)
    )
    hidden_cols = expert_weights.shape[3] // 2
    chosen = exchange(chosen.reshape(devices, 2, -1, hidden_cols), DEVICES)
    chosen = chosen.reshape(plane_count * 2, tensor_count, 2, -1, hidden_cols)
    tokens_row = ("cores", (tokens_mine, Moved(tokens_theirs)))

    def halves(*arrays):
        return [("halves", (array,)) for array in arrays]

    self_part, norms, *self_kept = attn_forward(
        "self_forward",
        self_forward_body,
        (core_ref, facts),
        [tokens_row],
        self_weights,
        ("one", (8, D), jnp.float32),
        False,
    )
    self_theirs = twin(self_part)
    memory_mine, up_mine, self_theirs, *cross_weights = lax.optimization_barrier(
        (memory_mine, up_mine, self_theirs, *cross_weights)
    )
    memory_row = ("cores", (memory_mine, Moved(twin(memory_mine))))
    up_theirs = twin(up_mine)
    up_row = ("cores", (up_mine, Moved(up_theirs)))
    norms_in, keep_in = ("small", (norms,)), ("small", (keep,))
    cross_part, first_sum, *cross_kept = attn_forward(
        "cross_forward",
        cross_forward_body,
        (core_ref, facts),
        [*halves(self_part, Moved(self_theirs)), tokens_row, norms_in, keep_in, memory_row],
        cross_weights,
        ("halves", (LEN, D), SUM),
        True,
    )
    second_sum, ffn_part, out_keep, out_give, row_grad = expert_layer(
        core_ref,
        (up_mine, up_theirs),
        (cross_part, twin(cross_part)),
        first_sum,
        norms,
        chosen,
    )
    layer_low = low(out_keep + twin(out_give))
    layer_out = swap(layer_low)
    row_grad = exchange(row_grad.reshape(devices, 2, -1, hidden_cols), DEVICES)
    row_grad = row_grad.reshape(plane_count, 2, tensor_count, 2, -1, hidden_cols)
    grad_cross, cross_part, memory_keep, memory_give, ffn_norm, *cross_grad = attn_backward(
        "cross_backward",
        cross_backward_body,
        (core_ref, facts),
        [*halves(ffn_part, Moved(twin(ffn_part)), second_sum), up_row, norms_in, keep_in, memory_row],
        cross_weights,
        cross_kept,
        [
            ("halves", (LEN, D), SUM),
            ("halves", (LEN, D), PART),
            ("cores", (LEN, D), jnp.bfloat16),
            ("one", (2, D), jnp.float32),
        ],
        True,
    )
    cross_grad = other_planes(cross_grad)
    own_grad, part_keep, part_give, *self_grad = attn_backward(
        "self_backward",
        self_backward_body,
        (core_ref, facts),
        [
            *halves(cross_part, Moved(twin(cross_part)), first_sum, grad_cross),
            tokens_row,
            ("small", (ffn_norm,)),
            norms_in,
        ],
        self_weights,
        self_kept,
        [("own", (LEN, D), jnp.float32), ("cores", (LEN, D), jnp.float32)],
        False,
    )
    self_grad, memory_give, cross_grad = lax.optimization_barrier(
        (self_grad, memory_give, cross_grad)
    )
    memory_low = low(memory_keep.astype(jnp.float32) + twin(memory_give).astype(jnp.float32))
    memory_grad = swap(memory_low)
    planes = other_planes(self_grad)
    back, _, _ = norm_back(
        tokens_mine.astype(jnp.float32), part_keep + twin(part_give), norms[0:1]
    )
    input_low = low(own_grad + back)
    input_grad = swap(input_low)
    input_grad, layer_out, memory_grad, *planes = lax.optimization_barrier(
        (input_grad, layer_out, memory_grad, *planes)
    )
    chips = sum_planes(planes, cross_grad)
    row_grad, chips = lax.optimization_barrier((row_grad, chips))
    chips = exchange(chips, CHIP)
    expert_moment_new, expert_second_new, expert_update, expert_squares = expert_lamb(
        chip_expert.reshape(-1), row_grad, expert_weights, expert_moment, expert_second
    )
    expert_squares = expert_squares.sum(-1).reshape(E, 2, 2).transpose(1, 0, 2).reshape(2, -1)
    attn_moment_new, attn_second_new, attn_update, attn_squares, *norm_outs = owner_lamb(
        odd,
        chips,
        (attn_weights, attn_moment, attn_second),
        (norm_params, norm_moment, norm_second),
    )
    norm_moment_new, norm_second_new, norm_update, norm_squares = norm_outs
    attn_squares = attn_squares.sum(-1).reshape(8, 2).T
    norm_squares = norm_squares.sum(-1) / tensor_count
    squares = jnp.concatenate([attn_squares, expert_squares, norm_squares], 1)
    count = squares.shape[1]
    squares = jnp.broadcast_to(squares.reshape(1, -1), (devices, 2 * count))
    lamb_norms = jnp.sqrt(exchange(squares, DEVICES).sum(0)).reshape(2, count)
    sizes = (rate * (lamb_norms[0] / lamb_norms[1])).reshape(1, -1)
    expert_new, attn_new, norm_new, layer_out, memory_grad, input_grad = final_step(
        sizes,
        moving.astype(jnp.int32).reshape(1, 1),
        expert_weights,
        expert_update,
        (attn_weights, attn_update),
        (norm_params, norm_update),
        (layer_low, layer_out, memory_low, memory_grad, input_low, input_grad),
    )
    return (
        layer_out,
        input_grad,
        memory_grad,
        attn_new,
        attn_moment_new,
        attn_second_new,
        expert_new,
        expert_moment_new,
        expert_second_new,
        norm_new,
        norm_moment_new,
        norm_second_new,
        lamb_norms,
    )


def specs(rows, dp):
    tokens = P((*dp, "tensor"), None)
    matrix = P(None, None, dp, "tensor")
    row_items = (P(dp, None),) * 3 + (P(dp),)
    return dict(
        in_specs=(tokens,) * 3 + row_items + (matrix,) * 6 + (P(None, dp),) * 3,
        out_specs=(tokens,) * 3 + (matrix,) * 6 + (P(None, dp),) * 3 + (P(),),
        check_vma=False,
    )


def solution(mesh):
    def run(*args):
        rows = args[3].shape[0]
        dp_count, tensor_count = mesh.shape["dp"], mesh.shape["tensor"]
        if rows // dp_count * 2 == tensor_count and tensor_count % 2 == 0:
            fine = Mesh(
                mesh.devices.reshape(dp_count // 2, 2, tensor_count), ("plane", "core", "tensor")
            )
            return jax.shard_map(body_rows, mesh=fine, **specs(rows, ("plane", "core")))(*args)
        return jax.shard_map(body, mesh=mesh, **specs(rows, ("dp",)))(*args)

    return run
```

```python
import jax
import jax.numpy as jnp
from jax import lax
from jax.experimental import pallas as pl
from jax.experimental.pallas import tpu as pltpu
from jax.sharding import Mesh
from jax.sharding import PartitionSpec as P

D = 512
HD = 64
E = 16
LEN = 1024
MLEN = 1024
STEP = 10


beta_one = 0.9
beta_two = 0.999
epsilon = 1e-06
decay = 0.01
rate = 0.2


def norm_layer(values, gain_vec, shift_vec):
    centered = values - jnp.mean(values, -1, keepdims=True)
    variance = jnp.mean(centered * centered, -1, keepdims=True)
    return centered * lax.rsqrt(variance + 1e-05) * gain_vec + shift_vec


def doc_numbers(lengths, length_total):
    doc_ends = jnp.cumsum(lengths)
    places = jnp.arange(length_total, dtype=jnp.int32)
    numbers = jnp.sum((places[:, None] >= doc_ends[None, :]).astype(jnp.int32), 1)
    starts = doc_ends - lengths
    opening = jnp.any(places[:, None] == starts[None, :], 1)
    return (numbers, opening)


def build_allowed(tgt_len, mem_len, keep_row, cross):
    doc_ids, _ = doc_numbers(tgt_len, LEN)
    if cross:
        mem_docs, opening = doc_numbers(mem_len, MLEN)
        return (doc_ids[:, None] == mem_docs[None, :]) & ((keep_row == 1) | opening)[None, :]
    places = jnp.arange(LEN, dtype=jnp.int32)
    return (doc_ids[:, None] == doc_ids[None, :]) & (places[None, :] <= places[:, None])


def gather_rows(values):
    return lax.all_gather(values, "tensor", axis=0, tiled=True)


def spread_rows(values):
    return lax.psum_scatter(values, "tensor", scatter_dimension=0, tiled=True)


def project(left_side, right_side):
    return jnp.dot(left_side, right_side, preferred_element_type=jnp.float32)


def project_back(left_side, right_side):
    return lax.dot_general(
        left_side, right_side, (((1,), (1,)), ((), ())), preferred_element_type=jnp.float32
    )


def outer_grad(left_side, right_side):
    return lax.dot_general(
        left_side, right_side, (((0,), (0,)), ((), ())), preferred_element_type=jnp.float32
    )


def attend_one(queries, key_rows, value_rows, allowed):
    head_count = queries.shape[1] // HD
    keys_h = key_rows.reshape(key_rows.shape[0], head_count, HD)
    values_h = value_rows.reshape(value_rows.shape[0], head_count, HD)
    block_rows = min(LEN, 512)
    outputs = []
    totals = []
    for begin_at in range(0, LEN, block_rows):
        queries_h = queries[begin_at : begin_at + block_rows].reshape(block_rows, head_count, HD)
        scores = jnp.einsum(
            "qhd,khd->hqk", queries_h, keys_h, preferred_element_type=jnp.float32
        ) * HD ** (-0.5)
        scores = jnp.where(allowed[None, begin_at : begin_at + block_rows], scores, -1e30)
        top_score = jnp.max(scores, -1, keepdims=True)
        weights = jnp.exp(scores - top_score)
        row_total = jnp.sum(weights, -1, keepdims=True)
        prob_low = (weights / row_total).astype(jnp.bfloat16)
        blended = jnp.einsum("hqk,khd->qhd", prob_low, values_h, preferred_element_type=jnp.float32)
        outputs.append(blended.reshape(block_rows, head_count * HD))
        totals.append((top_score + jnp.log(row_total))[..., 0])
    return (jnp.concatenate(outputs, 0), jnp.concatenate(totals, 1))


def attend_back_one(queries, key_rows, value_rows, upstream, log_totals, allowed):
    head_count = queries.shape[1] // HD
    scale = HD ** (-0.5)
    keys_h = key_rows.reshape(key_rows.shape[0], head_count, HD)
    values_h = value_rows.reshape(value_rows.shape[0], head_count, HD)
    key_grad = jnp.zeros(keys_h.shape, jnp.float32)
    value_grad = jnp.zeros(values_h.shape, jnp.float32)
    block_rows = min(LEN, 512)
    query_grads = []
    for begin_at in range(0, LEN, block_rows):
        queries_h = queries[begin_at : begin_at + block_rows].reshape(block_rows, head_count, HD)
        upstream_h = upstream[begin_at : begin_at + block_rows].reshape(block_rows, head_count, HD)
        scores = (
            jnp.einsum("qhd,khd->hqk", queries_h, keys_h, preferred_element_type=jnp.float32)
            * scale
        )
        scores = jnp.where(allowed[None, begin_at : begin_at + block_rows], scores, -1e30)
        probs_full = jnp.exp(scores - log_totals[:, begin_at : begin_at + block_rows, None])
        prob_grad = jnp.einsum(
            "qhd,khd->hqk", upstream_h, values_h, preferred_element_type=jnp.float32
        )
        weighted = jnp.sum(probs_full * prob_grad, -1, keepdims=True)
        score_grad = (probs_full * (prob_grad - weighted)).astype(jnp.bfloat16)
        query_part = (
            jnp.einsum("hqk,khd->qhd", score_grad, keys_h, preferred_element_type=jnp.float32)
            * scale
        )
        query_grads.append(query_part.astype(jnp.bfloat16).reshape(block_rows, head_count * HD))
        key_grad = (
            key_grad
            + jnp.einsum("hqk,qhd->khd", score_grad, queries_h, preferred_element_type=jnp.float32)
            * scale
        )
        value_grad = value_grad + jnp.einsum(
            "hqk,qhd->khd",
            probs_full.astype(jnp.bfloat16),
            upstream_h,
            preferred_element_type=jnp.float32,
        )
    width = head_count * HD
    return (
        jnp.concatenate(query_grads, 0),
        key_grad.astype(jnp.bfloat16).reshape(-1, width),
        value_grad.astype(jnp.bfloat16).reshape(-1, width),
    )


def attend_rows(queries, key_rows, value_rows, tgt_lengths, mem_lengths, mem_keep, cross):
    row_count = tgt_lengths.shape[0]
    width = queries.shape[1]

    def one_row(row_item):
        row_q, row_k, row_v, tgt_len, mem_len, keep_row = row_item
        return attend_one(row_q, row_k, row_v, build_allowed(tgt_len, mem_len, keep_row, cross))

    blended, log_totals = lax.map(
        one_row,
        (
            queries.reshape(row_count, LEN, width),
            key_rows.reshape(row_count, -1, width),
            value_rows.reshape(row_count, -1, width),
            tgt_lengths,
            mem_lengths,
            mem_keep,
        ),
    )
    return (blended.reshape(row_count * LEN, width), log_totals)


def attend_back_rows(
    queries, key_rows, value_rows, upstream, log_totals, tgt_lengths, mem_lengths, mem_keep, cross
):
    row_count = tgt_lengths.shape[0]
    width = queries.shape[1]

    def one_row(row_item):
        row_q, row_k, row_v, row_up, row_log, tgt_len, mem_len, keep_row = row_item
        return attend_back_one(
            row_q, row_k, row_v, row_up, row_log, build_allowed(tgt_len, mem_len, keep_row, cross)
        )

    query_grad, key_grad, value_grad = lax.map(
        one_row,
        (
            queries.reshape(row_count, LEN, width),
            key_rows.reshape(row_count, -1, width),
            value_rows.reshape(row_count, -1, width),
            upstream.reshape(row_count, LEN, width),
            log_totals,
            tgt_lengths,
            mem_lengths,
            mem_keep,
        ),
    )
    return (
        query_grad.reshape(-1, width),
        key_grad.reshape(-1, width),
        value_grad.reshape(-1, width),
    )


def lamb_pieces(weight, moment, second, grad, axes):
    moment = beta_one * moment + (1.0 - beta_one) * grad
    second = beta_two * second + (1.0 - beta_two) * grad * grad
    update = (
        moment / (1.0 - beta_one**STEP) / (jnp.sqrt(second / (1.0 - beta_two**STEP)) + epsilon)
        + decay * weight
    )
    return (moment, second, update, jnp.sum(weight * weight, axes), jnp.sum(update * update, axes))


def body(
    tokens,
    memory,
    cotangent,
    tgt_lengths,
    mem_lengths,
    mem_keep,
    row_expert,
    attn_weights,
    attn_moment,
    attn_second,
    expert_weights,
    expert_moment,
    expert_second,
    norm_params,
    norm_moment,
    norm_second,
):
    row_count = tgt_lengths.shape[0]
    attn_low, expert_low = (
        lax.all_gather(attn_weights.astype(jnp.bfloat16), "dp", axis=2, tiled=True),
        lax.all_gather(expert_weights.astype(jnp.bfloat16), "dp", axis=2, tiled=True),
    )
    row_low = expert_low[row_expert]
    norms = lax.all_gather(norm_params, "dp", axis=1, tiled=True)
    residual = tokens.astype(jnp.float32)
    normed_self, back_self = jax.vjp(norm_layer, residual, norms[0], norms[1])
    self_rows = gather_rows(normed_self.astype(jnp.bfloat16))
    self_qkv = jnp.einsum(
        "td,jdc->jtc", self_rows, attn_low[0, :3], preferred_element_type=jnp.float32
    ).astype(jnp.bfloat16)
    self_mix, self_log = attend_rows(
        self_qkv[0], self_qkv[1], self_qkv[2], tgt_lengths, mem_lengths, mem_keep, False
    )
    self_low = self_mix.astype(jnp.bfloat16)
    first_sum = residual + spread_rows(project_back(self_low, attn_low[0, 3]))
    normed_cross, back_cross = jax.vjp(norm_layer, first_sum, norms[2], norms[3])
    cross_rows = gather_rows(normed_cross.astype(jnp.bfloat16))
    memory_rows = gather_rows(memory)
    cross_queries = project(cross_rows, attn_low[1, 0]).astype(jnp.bfloat16)
    cross_kv = jnp.einsum(
        "td,jdc->jtc", memory_rows, attn_low[1, 1:3], preferred_element_type=jnp.float32
    ).astype(jnp.bfloat16)
    cross_mix, cross_log = attend_rows(
        cross_queries, cross_kv[0], cross_kv[1], tgt_lengths, mem_lengths, mem_keep, True
    )
    cross_low = cross_mix.astype(jnp.bfloat16)
    second_sum = first_sum + spread_rows(project_back(cross_low, attn_low[1, 3]))
    normed_ffn, back_ffn = jax.vjp(norm_layer, second_sum, norms[4], norms[5])
    ffn_rows = gather_rows(normed_ffn.astype(jnp.bfloat16))

    def expert_forward(row_item):
        row_in, chosen = row_item
        inner_act = project(row_in, chosen[0])
        hidden = jax.nn.gelu(inner_act).astype(jnp.bfloat16)
        return (inner_act, project_back(hidden, chosen[1]))

    inner_all, branch_all = lax.map(expert_forward, (ffn_rows.reshape(row_count, LEN, D), row_low))
    layer_out = (second_sum + spread_rows(branch_all.reshape(row_count * LEN, D))).astype(
        jnp.bfloat16
    )
    grad_ffn = cotangent.astype(jnp.float32)
    upstream_ffn = gather_rows(cotangent)
    ffn_again = gather_rows(normed_ffn.astype(jnp.bfloat16))

    def expert_backward(row_item):
        row_in, inner_act, upstream, chosen = row_item
        hidden, gelu_back = jax.vjp(jax.nn.gelu, inner_act)
        inner_grad = gelu_back(project(upstream, chosen[1]))[0].astype(jnp.bfloat16)
        pair_grads = jnp.stack(
            [outer_grad(row_in, inner_grad), outer_grad(upstream, hidden.astype(jnp.bfloat16))]
        )
        return (pair_grads, project_back(inner_grad, chosen[0]))

    row_grads, ffn_part = lax.map(
        expert_backward,
        (
            ffn_again.reshape(row_count, LEN, D),
            inner_all,
            upstream_ffn.reshape(row_count, LEN, D),
            row_low,
        ),
    )
    normed_ffn_grad = spread_rows(ffn_part.reshape(row_count * LEN, D))
    back_tokens, gain_ffn, shift_ffn = back_ffn(normed_ffn_grad)
    grad_cross = grad_ffn + back_tokens
    upstream_cross = gather_rows(grad_cross.astype(jnp.bfloat16))
    cross_again = gather_rows(normed_cross.astype(jnp.bfloat16))
    memory_again = gather_rows(memory)
    cross_up = project(upstream_cross, attn_low[1, 3]).astype(jnp.bfloat16)
    cross_dq, cross_dk, cross_dv = attend_back_rows(
        cross_queries,
        cross_kv[0],
        cross_kv[1],
        cross_up,
        cross_log,
        tgt_lengths,
        mem_lengths,
        mem_keep,
        True,
    )
    cross_grads = jnp.stack(
        [
            outer_grad(cross_again, cross_dq),
            outer_grad(memory_again, cross_dk),
            outer_grad(memory_again, cross_dv),
            outer_grad(upstream_cross, cross_low),
        ]
    )
    normed_cross_grad, memory_total = (
        lax.psum_scatter(
            project_back(cross_dq, attn_low[1, 0]), "tensor", scatter_dimension=0, tiled=True
        ),
        lax.psum_scatter(
            project_back(cross_dk, attn_low[1, 1]) + project_back(cross_dv, attn_low[1, 2]),
            "tensor",
            scatter_dimension=0,
            tiled=True,
        ),
    )
    back_tokens, gain_cross, shift_cross = back_cross(normed_cross_grad)
    grad_self = grad_cross + back_tokens
    upstream_self = gather_rows(grad_self.astype(jnp.bfloat16))
    self_again = gather_rows(normed_self.astype(jnp.bfloat16))
    self_up = project(upstream_self, attn_low[0, 3]).astype(jnp.bfloat16)
    self_dq, self_dk, self_dv = attend_back_rows(
        self_qkv[0],
        self_qkv[1],
        self_qkv[2],
        self_up,
        self_log,
        tgt_lengths,
        mem_lengths,
        mem_keep,
        False,
    )
    self_grads = jnp.stack(
        [
            outer_grad(self_again, self_dq),
            outer_grad(self_again, self_dk),
            outer_grad(self_again, self_dv),
            outer_grad(upstream_self, self_low),
        ]
    )
    normed_self_grad = spread_rows(
        project_back(self_dq, attn_low[0, 0])
        + project_back(self_dk, attn_low[0, 1])
        + project_back(self_dv, attn_low[0, 2])
    )
    back_tokens, gain_self, shift_self = back_self(normed_self_grad)
    input_grad = (grad_self + back_tokens).astype(jnp.bfloat16)
    attn_grad = jnp.stack([self_grads, cross_grads])
    norm_grad = jnp.stack([gain_self, shift_self, gain_cross, shift_cross, gain_ffn, shift_ffn])
    norm_total = lax.psum(norm_grad, "tensor")
    selector = (row_expert[:, None] == jnp.arange(E, dtype=jnp.int32)[None, :]).astype(jnp.float32)
    expert_grad = jnp.einsum("re,rjdf->ejdf", selector, row_grads, precision=lax.Precision.HIGHEST)
    expert_shard = lax.psum_scatter(expert_grad, "dp", scatter_dimension=2, tiled=True)
    attn_shard, norm_shard = (
        lax.psum_scatter(attn_grad, "dp", scatter_dimension=2, tiled=True),
        lax.psum_scatter(norm_total, "dp", scatter_dimension=1, tiled=True),
    )
    attn_pieces = lamb_pieces(attn_weights, attn_moment, attn_second, attn_shard, (2, 3))
    expert_pieces = lamb_pieces(expert_weights, expert_moment, expert_second, expert_shard, (2, 3))
    norm_pieces = lamb_pieces(norm_params, norm_moment, norm_second, norm_shard, (1,))
    copy_share = 1.0 / lax.axis_size("tensor")
    weight_squares = jnp.concatenate(
        [attn_pieces[3].reshape(-1), expert_pieces[3].reshape(-1), norm_pieces[3] * copy_share]
    )
    update_squares = jnp.concatenate(
        [attn_pieces[4].reshape(-1), expert_pieces[4].reshape(-1), norm_pieces[4] * copy_share]
    )
    weight_total, update_total = lax.psum((weight_squares, update_squares), ("dp", "tensor"))
    weight_norm = jnp.sqrt(weight_total)
    update_norm = jnp.sqrt(update_total)
    trust_ratio = weight_norm / update_norm
    attn_ratio = trust_ratio[:8].reshape(2, 4, 1, 1)
    expert_ratio = trust_ratio[8 : 8 + 2 * E].reshape(E, 2, 1, 1)
    norm_ratio = trust_ratio[8 + 2 * E :].reshape(6, 1)
    attn_new = attn_weights - rate * attn_ratio * attn_pieces[2]
    expert_new = expert_weights - rate * expert_ratio * expert_pieces[2]
    norm_new = norm_params - rate * norm_ratio * norm_pieces[2]
    lamb_norms = jnp.stack([weight_norm, update_norm])
    return (
        layer_out,
        input_grad,
        memory_total.astype(jnp.bfloat16),
        attn_new,
        attn_pieces[0],
        attn_pieces[1],
        expert_new,
        expert_pieces[0],
        expert_pieces[1],
        norm_new,
        norm_pieces[0],
        norm_pieces[1],
        lamb_norms,
    )


MEGA = 1024 * 1024
QUERY_BLOCK = 256
WINDOW_STEPS = {False: 128, True: 256}
FORWARD_MEGA, BACKWARD_MEGA, EXPERT_MEGA = 26, 36, 28
PART = jnp.bfloat16
SUM = jnp.bfloat16
HALVES = (slice(0, LEN // 2), slice(LEN // 2, LEN))
KERNEL_COST = pl.CostEstimate(flops=10**6, bytes_accessed=1024, transcendentals=0)
WHOLE = pl.BlockSpec(memory_space=pltpu.VMEM)
OUTSIDE = pl.BlockSpec(memory_space=pltpu.HBM)
ANYWHERE = pl.BlockSpec(memory_space=pl.ANY)


def outside(shape, dtype):
    return pltpu.HBM(shape, dtype)


def stay_outside(arrays):
    return [pltpu.with_memory_space_constraint(array, pltpu.HBM) for array in arrays]


SCALARS = pl.BlockSpec(memory_space=pltpu.SMEM)


def mm(left, right):
    return lax.dot_general(left, right, (((1,), (0,)), ((), ())), preferred_element_type=jnp.float32)


def mt(left, right):
    return lax.dot_general(left, right, (((1,), (1,)), ((), ())), preferred_element_type=jnp.float32)


def tm(left, right):
    return lax.dot_general(left, right, (((0,), (0,)), ((), ())), preferred_element_type=jnp.float32)


def low(values):
    return values.astype(jnp.bfloat16)


def standardize(values):
    centered = values - jnp.mean(values, -1, keepdims=True)
    inverse = lax.rsqrt(jnp.mean(centered * centered, -1, keepdims=True) + 1e-05)
    return centered * inverse, inverse


def norm_back(values, grad, gain_vec):
    unit, inverse = standardize(values)
    inner = grad * gain_vec
    back = inverse * (
        inner
        - jnp.mean(inner, -1, keepdims=True)
        - unit * jnp.mean(inner * unit, -1, keepdims=True)
    )
    return back, jnp.sum(grad * unit, 0, keepdims=True), jnp.sum(grad, 0, keepdims=True)


def key_limits(facts, places, cross):
    zero = jnp.zeros(places.shape, jnp.int32)
    low_end, high_end, doc_end = zero, zero, 0
    for doc in range(8):
        begin, doc_end = doc_end, doc_end + facts[0, doc]
        if cross:
            low_end = low_end + jnp.where(places >= doc_end, facts[0, 8 + doc], 0)
            high_end = high_end + jnp.where(places >= begin, facts[0, 8 + doc], 0)
        else:
            low_end = jnp.where(places >= doc_end, doc_end, low_end)
    return low_end, (high_end if cross else places + 1)


def kept_keys(facts, keep, places):
    kept = keep == 1
    begin = 0
    for doc in range(8):
        kept = kept | (places == begin)
        begin = begin + facts[0, 8 + doc]
    return kept


def key_windows(facts, cross, run):
    def block(index, _):
        first_query = pl.multiple_of(index * QUERY_BLOCK, QUERY_BLOCK)
        lowest, _ = key_limits(facts, first_query, cross)
        _, highest = key_limits(facts, first_query + QUERY_BLOCK - 1, cross)
        begin = lax.div(lowest, 128) * 128
        need = highest - begin
        unit = WINDOW_STEPS[cross]
        for width in range(unit, (MLEN if cross else 512 + QUERY_BLOCK) + 1, unit):
            start = pl.multiple_of(jnp.minimum(begin, MLEN - width), 128)

            @pl.when((need <= width) & (need > width - unit))
            def _(start=start, width=width):
                run(first_query, start, width)

        return 0

    lax.fori_loop(0, LEN // QUERY_BLOCK, block, 0)


def allowed_bias(facts, keep_ref, cross, first_query, start, width):
    places = first_query + lax.broadcasted_iota(jnp.int32, (1, QUERY_BLOCK), 1)
    low_end, high_end = key_limits(facts, places, cross)
    keys = start + lax.broadcasted_iota(jnp.int32, (width, QUERY_BLOCK), 0)
    if cross:
        own = start + lax.broadcasted_iota(jnp.int32, (width, 1), 0)
        keys = jnp.where(kept_keys(facts, keep_ref[pl.ds(start, width), 0:1], own), keys, -1)
    return jnp.where((keys >= low_end) & (keys < high_end), 0.0, -1e30)


def head_lanes(half):
    lane = lax.broadcasted_iota(jnp.int32, (1, 2 * HD), 1)
    return (lane < HD) if half == 0 else (lane >= HD)


def head_tile(head):
    return slice(head // 2 * 2 * HD, (head // 2 + 1) * 2 * HD)


def value_lines(head):
    return slice((head ^ 1) * HD, ((head ^ 1) + 1) * HD)


def of_head(values, half):
    return jnp.where(head_lanes(half), values, jnp.zeros_like(values))


def gather_weights(plane, w_refs, pack, first, second):
    left = head_lanes(0)
    cores, rows = 2, D // (2 * len(w_refs))
    heads = w_refs[0].shape[0] // cores
    lines = slice(pack * rows, (pack + 1) * rows)
    for distance, w_ref in enumerate(w_refs):
        for core in range(cores):
            begin = pl.multiple_of(((plane ^ distance) * cores + core) * rows, rows)
            for pair in range(heads // 2):
                even = w_ref[core * heads + 2 * pair, lines]
                odd = w_ref[core * heads + 2 * pair + 1, lines]
                at = slice(pair * 2 * HD, (pair + 1) * 2 * HD)
                first[pl.ds(begin, rows), at] = jnp.where(left, even, odd)
                second[pl.ds(begin, rows), at] = jnp.where(left, odd, even)


def scatter_grads(plane, g_refs, pack, held, values):
    first, second = held
    first[:D, :], second[:D, :] = values
    left = head_lanes(0)
    cores, rows = 2, D // (2 * len(g_refs))
    heads = g_refs[0].shape[0] // cores
    lines = slice(pack * rows, (pack + 1) * rows)
    for distance, g_ref in enumerate(g_refs):
        for core in range(cores):
            begin = pl.multiple_of(((plane ^ distance) * cores + core) * rows, rows)
            for pair in range(heads // 2):
                at = slice(pair * 2 * HD, (pair + 1) * 2 * HD)
                one, two = first[pl.ds(begin, rows), at], second[pl.ds(begin, rows), at]
                g_ref[core * heads + 2 * pair, lines] = low(jnp.where(left, one, two))
                g_ref[core * heads + 2 * pair + 1, lines] = low(jnp.where(left, two, one))


def gather_norms(plane, w_refs, norms):
    left = head_lanes(0)
    heads = w_refs[0].shape[0] // 2
    first = 2 * D // (2 * len(w_refs))
    for distance, w_ref in enumerate(w_refs):
        parts = []
        for core in (0, 1):
            parts.append(join_norms(w_ref[core * heads, first : first + 16]))
        at = pl.ds(pl.multiple_of((plane ^ distance) * 2 * HD, 2 * HD), 2 * HD)
        norms[:, at] = jnp.where(left, *parts)


def split_norms(values):
    high = low(values).astype(jnp.float32)
    middle = low(values - high).astype(jnp.float32)
    least = low(values - high - middle).astype(jnp.float32)
    return low(jnp.concatenate([jnp.where(head_lanes(0), high, middle), least], 0))


def join_norms(held):
    held = held.astype(jnp.float32)
    return (held[0:8] + pltpu.roll(held[0:8], HD, 1)) + held[8:16]


def scatter_norms(plane, g_refs, norms):
    heads = g_refs[0].shape[0] // 2
    first = D // len(g_refs)
    for distance, g_ref in enumerate(g_refs):
        at = pl.ds(pl.multiple_of((plane ^ distance) * 2 * HD, 2 * HD), 2 * HD)
        tile = norms[:, at]
        for core in (0, 1):
            values = jnp.where(head_lanes(core), tile, pltpu.roll(tile, HD, 1))
            for head in range(heads):
                g_ref[core * heads + head, first : first + 16] = split_norms(values)


class Moved:
    def __init__(self, values):
        self.values, self.shape, self.dtype = values, values.shape, values.dtype


class Arriving:
    def __init__(self, held, copies):
        self.held, self.copies = held, list(copies)

    def half(self, which):
        copy, self.copies[which] = self.copies[which], None
        if copy is not None:
            copy.wait()
        return self.held

    def get(self):
        for which in range(len(self.copies)):
            self.half(which)
        return self.held


class Leaving:
    def __init__(self, held, copies):
        self.held, self.copies, self.sent = held, list(copies), 0

    def send(self, upto=None):
        while self.sent < (len(self.copies) if upto is None else upto):
            self.copies[self.sent].start()
            self.sent += 1

    def finish(self):
        for copy in self.copies:
            copy.wait()


def half_at(core_ref, other):
    half = LEN // 2
    core = core_ref[0, 0]
    return pl.ds(pl.multiple_of((1 - core if other else core) * half, half), half)


def copies_of(kind, refs, held, core_ref, sems):
    if kind in ("one", "small"):
        pairs = [(refs[0], held)]
    elif kind == "halves":
        pairs = [(refs[0].at[at], held.at[at]) for at in HALVES]
    else:
        pairs = [(ref, held.at[half_at(core_ref, other)]) for ref, other in zip(refs, (False, True))]
    return pairs, [next(sems) for _ in pairs]


def staged_call(body, name, scalars, inputs, outputs, scratch, mega):
    in_count = sum(len(arrays) for _, arrays in inputs)
    shapes = []
    for kind, shape, dtype in outputs:
        if kind == "cores":
            shapes += [outside((shape[0] // 2, *shape[1:]), dtype)] * 2
        elif kind == "own":
            shapes += [outside((shape[0] // 2, *shape[1:]), dtype)]
        else:
            shapes += [outside(shape, dtype)]
    held_in = []
    for kind, arrays in inputs:
        rows, *others = arrays[0].shape
        rows = 2 * rows if kind == "cores" else rows
        held_in.append(pltpu.VMEM((rows, *others), arrays[0].dtype))
    held_out = [pltpu.VMEM(shape, dtype) for _, shape, dtype in outputs]
    waits = 2 * (len(inputs) + len(outputs))

    def kernel(*refs):
        refs = list(refs)

        def take(count):
            taken = refs[:count]
            del refs[:count]
            return taken

        scalar_refs, in_refs, out_refs = take(len(scalars)), take(in_count), take(len(shapes))
        in_held, out_held, (sem_ref,) = take(len(inputs)), take(len(outputs)), take(1)
        sems = (sem_ref.at[place] for place in range(waits))
        core_ref = scalar_refs[0]
        arrivals, starts = [], []
        for (kind, arrays), held in zip(inputs, in_held):
            mine, in_refs = in_refs[: len(arrays)], in_refs[len(arrays) :]
            pairs, own = copies_of(kind, mine, held, core_ref, sems)
            copies = [pltpu.make_async_copy(a, b, sem) for (a, b), sem in zip(pairs, own)]
            turn = {"small": (0,), "halves": (1, 2), "cores": (2, 2), "one": (3,)}[kind]
            starts += zip(turn, copies)
            arrivals.append(Arriving(held, copies))
        for _, copy in sorted(starts, key=lambda item: item[0]):
            copy.start()
        departures = []
        for (kind, _, _), held in zip(outputs, out_held):
            mine = out_refs[: 2 if kind == "cores" else 1]
            out_refs = out_refs[len(mine) :]
            pairs, own = copies_of("cores" if kind == "own" else kind, mine, held, core_ref, sems)
            copies = [pltpu.make_async_copy(b, a, sem) for (a, b), sem in zip(pairs, own)]
            departures.append(Leaving(held, copies))
        body(scalar_refs, arrivals, departures, refs)
        for arrival in arrivals:
            arrival.get()
        for departure in departures:
            departure.send()
        for departure in departures:
            departure.finish()

    arrays = [array for _, group in inputs for array in group]
    moved = [place for place, array in enumerate(arrays) if isinstance(array, Moved)]
    arrays = [array.values if isinstance(array, Moved) else array for array in arrays]
    arrays = [
        array if place in moved else stay_outside([array])[0] for place, array in enumerate(arrays)
    ]
    return pl.pallas_call(
        kernel,
        name=name,
        out_shape=tuple(shapes),
        in_specs=[SCALARS] * len(scalars)
        + [ANYWHERE if place in moved else OUTSIDE for place in range(in_count)],
        out_specs=(OUTSIDE,) * len(shapes),
        scratch_shapes=held_in + held_out + [pltpu.SemaphoreType.DMA((waits,))] + scratch,
        compiler_params=pltpu.CompilerParams(vmem_limit_bytes=mega * MEGA),
        cost_estimate=KERNEL_COST,
    )(*scalars, *arrays)


def forward_heads(plane, facts, keep_ref, cross, query_rows, key_rows, w_refs, outs, scratch):
    w_q, w_k, w_v, w_o, values_turned, blended_turned = scratch
    part, queries_out, keys_out, values_out, blended_out, stats_out = outs
    q_ref, k_ref, o_ref, stats_ref = (
        out.held for out in (queries_out, keys_out, blended_out, stats_out)
    )
    w_refs = [w_ref.get() for w_ref in w_refs]
    gather_weights(plane, w_refs, 0, w_q, w_v)
    gather_weights(plane, w_refs, 1, w_k, w_o)
    for out, rows, weights in (
        (queries_out, query_rows, w_q),
        (keys_out, key_rows, w_k),
        (values_out, key_rows, w_v),
    ):
        out.held[...] = low(mm(rows[...], weights[...]))
        out.send()
    values_turned[...] = values_out.held[...].T
    stats_ref[...] = jnp.zeros_like(stats_ref)
    heads = q_ref.shape[1] // HD

    def one(first_query, start, width):
        at, keys_at = pl.ds(first_query, QUERY_BLOCK), pl.ds(start, width)
        bias = allowed_bias(facts, keep_ref, cross, first_query, start, width)
        scores = []
        for head in range(heads):
            tile = head_tile(head)
            queries = of_head(q_ref[at, tile] * HD ** (-0.5), head % 2)
            scores.append(mt(k_ref[keys_at, tile], queries) + bias)
        done = []
        for head in range(heads):
            top = jnp.max(scores[head], 0, keepdims=True)
            weights = jnp.exp(scores[head] - top)
            total = jnp.sum(weights, 0, keepdims=True)
            stats_ref[head : head + 1, at] = top + jnp.log(total)
            done.append((low(weights), 1.0 / total))
        for head, (weights, share) in enumerate(done):
            lines = value_lines(head)
            blended_turned[lines, at] = low(mm(values_turned[lines, keys_at], weights) * share)

    key_windows(facts, cross, one)
    for which, at in enumerate(HALVES):
        o_ref[at, :] = blended_turned[:, at].T
        part.held[at, :] = mt(o_ref[at, :], w_o[...]).astype(PART)
        part.send(which + 1)


def self_forward_body(scalars, ins, outs, scratch):
    core_ref, facts = scalars
    tokens, *w_refs = ins
    part, norms, rows, *heads = outs
    plane = core_ref[0, 1]
    tokens = tokens.get()
    units = [standardize(tokens[at, :].astype(jnp.float32))[0] for at in HALVES]
    gather_norms(plane, [w_ref.get() for w_ref in w_refs], norms.held)
    norms.send()
    for at, unit in zip(HALVES, units):
        rows.held[at, :] = low(unit * norms.held[0:1, :] + norms.held[1:2, :])
    rows.send()
    forward_heads(
        plane, facts, None, False, rows.held, rows.held, w_refs, (part, *heads), scratch
    )


def cross_forward_body(scalars, ins, outs, scratch):
    core_ref, facts = scalars
    part_mine, part_theirs, tokens, norms, keep, memory, *w_refs = ins
    part, total, rows, *heads = outs
    tokens, norms = tokens.get(), norms.get()
    for which, at in enumerate(HALVES):
        ours = part_mine.half(which)[at, :].astype(jnp.float32)
        value = tokens[at, :].astype(jnp.float32) + (
            ours + part_theirs.half(which)[at, :].astype(jnp.float32)
        )
        total.held[at, :] = value.astype(SUM)
        total.send(which + 1)
        unit, _ = standardize(value)
        rows.held[at, :] = low(unit * norms[2:3, :] + norms[3:4, :])
    rows.send()
    keep_turned, *scratch = scratch
    keep_turned[...] = jnp.broadcast_to(keep.get()[...], (128, MLEN)).T
    forward_heads(
        core_ref[0, 1],
        facts,
        keep_turned,
        True,
        rows.held,
        memory.get(),
        w_refs,
        (part, *heads),
        scratch,
    )


def attn_forward(name, body, scalars, inputs, weights, extra, cross):
    cols = weights[0].shape[0] // 2 * HD
    bfloat16 = jnp.bfloat16
    outputs = [
        ("halves", (LEN, D), PART),
        extra,
        ("one", (LEN, D), bfloat16),
        *[("one", (LEN, cols), bfloat16)] * 4,
        ("one", (8, LEN), jnp.float32),
    ]
    scratch = [pltpu.VMEM((D, cols), bfloat16)] * 4
    scratch += [pltpu.VMEM((cols, MLEN), bfloat16), pltpu.VMEM((cols, LEN), bfloat16)]
    if cross:
        scratch = [pltpu.VMEM((MLEN, 128), jnp.int32)] + scratch
    inputs = inputs + [("one", (Moved(block),)) for block in weights]
    return staged_call(body, name, scalars, inputs, outputs, scratch, FORWARD_MEGA)


def backward_heads(plane, facts, keep_ref, cross, up_rows, w_refs, heads, scratch):
    w_q, w_k, w_v, w_o, weighted, up, keys_turned, q_turned, dq, k_sum, v_sum, dk, dv = scratch
    w_refs = [w_ref.get() for w_ref in w_refs]
    gather_weights(plane, w_refs, 0, w_q, w_v)
    gather_weights(plane, w_refs, 1, w_k, w_o)
    scale = HD ** (-0.5)
    up[...] = low(mm(up_rows[...], w_o[...]))
    q_ref, k_ref, v_ref, o_ref, stats_ref = (head.get() for head in heads)
    keys_turned[...] = k_ref[...].T
    k_sum[...] = jnp.zeros_like(k_sum)
    v_sum[...] = jnp.zeros_like(v_sum)

    products = (up[...].astype(jnp.float32) * o_ref[...].astype(jnp.float32)).T
    heads = q_ref.shape[1] // HD
    for head in range(heads):
        weighted[head : head + 1, :] = jnp.sum(products[value_lines(head), :], 0, keepdims=True)

    def one(first_query, start, width):
        at, keys_at = pl.ds(first_query, QUERY_BLOCK), pl.ds(start, width)
        bias = allowed_bias(facts, keep_ref, cross, first_query, start, width)
        ready, done, adds = [], [], []
        for head in range(heads):
            tile = head_tile(head)
            queries = of_head(q_ref[at, tile], head % 2)
            upstream = of_head(up[at, tile], 1 - head % 2)
            scores = mt(k_ref[keys_at, tile], queries * scale)
            ready.append((queries, upstream, scores, mt(v_ref[keys_at, tile], upstream)))
        for head, (_, _, scores, prob_grad) in enumerate(ready):
            probs = jnp.exp(scores + bias - stats_ref[head : head + 1, at])
            score_grad = low(probs * (prob_grad - weighted[head : head + 1, at]))
            done.append((low(probs), score_grad))
        for head, (probs, score_grad) in enumerate(done):
            queries, upstream, _, _ = ready[head]
            lines = slice(head * HD, (head + 1) * HD)
            q_turned[lines, at] = low(mm(keys_turned[lines, keys_at], score_grad) * scale)
            adds.append((mm(score_grad, queries), mm(probs, upstream)))
        for head in range(0, heads, 2):
            tile = head_tile(head)
            (key_one, value_one), (key_two, value_two) = adds[head : head + 2]
            k_sum[keys_at, tile] = k_sum[keys_at, tile] + (key_one + key_two)
            v_sum[keys_at, tile] = v_sum[keys_at, tile] + (value_one + value_two)

    key_windows(facts, cross, one)
    dq[...] = q_turned[...].T
    dk[...] = low(k_sum[...] * scale)
    dv[...] = low(v_sum[...])


def norm_step(parts, total, norms, row, upstream, finish):
    gains = jnp.zeros((1, D), jnp.float32)
    shifts = jnp.zeros((1, D), jnp.float32)
    for which, at in enumerate(HALVES):
        mine, theirs = (part.half(which)[at, :].astype(jnp.float32) for part in parts)
        back, gain, shift = norm_back(
            total.half(which)[at, :].astype(jnp.float32), mine + theirs, norms[row : row + 1, :]
        )
        gains, shifts = gains + gain, shifts + shift
        finish(which, at, upstream(which, at) + back)
    return gains, shifts


def cross_backward_body(scalars, ins, outs, scratch):
    core_ref, facts = scalars
    part_mine, part_theirs, total, cotangent, norms, keep, memory, *rest = ins
    planes = len(rest) - 6
    w_refs, (rows, *heads) = rest[:planes], rest[planes:]
    up_rows, part, memory_part, norm_out, *g_outs = outs
    turned, memory_turned, keep_turned, *scratch = scratch
    keep_turned[...] = jnp.broadcast_to(keep.get()[...], (128, MLEN)).T
    norms, cotangent = norms.get(), cotangent.get()
    plane = core_ref[0, 1]

    def finish(which, at, value):
        up_rows.held[at, :] = low(value)
        up_rows.send(which + 1)

    gains, shifts = norm_step(
        (part_mine, part_theirs),
        total,
        norms,
        4,
        lambda which, at: cotangent[at, :].astype(jnp.float32),
        finish,
    )
    norm_out.held[0:1, :] = 0.5 * gains
    norm_out.held[1:2, :] = 0.5 * shifts
    norm_out.send()
    backward_heads(plane, facts, keep_turned, True, up_rows.held, w_refs, heads, scratch)
    w_q, w_k, w_v, *_ = scratch
    dq, *held, dk, dv = scratch[-5:]
    for which, at in enumerate(HALVES):
        part.held[at, :] = mt(dq[at, :], w_q[...]).astype(PART)
        part.send(which + 1)
    memory_part.held[...] = low(mt(dk[...], w_k[...]) + mt(dv[...], w_v[...]))
    memory_part.send()
    g_refs = [out.held for out in g_outs]
    turned[...] = rows.get()[...].T
    memory_turned[...] = memory.get()[...].T
    scatter_grads(
        plane, g_refs, 0, held, (mm(turned[...], dq[...]), mm(memory_turned[...], dv[...]))
    )
    turned[...] = up_rows.held[...].T
    out_grad = mm(turned[...], heads[3].get()[...])
    scatter_grads(plane, g_refs, 1, held, (mm(memory_turned[...], dk[...]), out_grad))


def self_backward_body(scalars, ins, outs, scratch):
    core_ref, facts = scalars
    part_mine, part_theirs, total, grad, tokens, ffn_norm, norms, *rest = ins
    planes = len(rest) - 6
    w_refs, (rows, *heads) = rest[:planes], rest[planes:]
    grad_out, part, *g_outs = outs
    norm_grad, up_rows, turned, *scratch = scratch
    norms = norms.get()
    plane = core_ref[0, 1]

    def finish(which, at, value):
        grad_out.held[at, :] = value
        up_rows[at, :] = low(value)

    gains, shifts = norm_step(
        (part_mine, part_theirs),
        total,
        norms,
        2,
        lambda which, at: grad.half(which)[at, :].astype(jnp.float32),
        finish,
    )
    grad_out.send()
    norm_grad[2:3, :] = 0.5 * gains
    norm_grad[3:4, :] = 0.5 * shifts
    norm_grad[4:6, :] = ffn_norm.get()[...]
    norm_grad[6:8, :] = jnp.zeros((2, D), jnp.float32)
    backward_heads(plane, facts, None, False, up_rows, w_refs, heads, scratch)
    w_q, w_k, w_v, *_ = scratch
    dq, *held, dk, dv = scratch[-5:]
    tokens = tokens.get()
    gains = jnp.zeros((1, D), jnp.float32)
    shifts = jnp.zeros((1, D), jnp.float32)
    for at in HALVES:
        value = mt(dq[at, :], w_q[...]) + mt(dk[at, :], w_k[...]) + mt(dv[at, :], w_v[...])
        part.held[at, :] = value
        unit, _ = standardize(tokens[at, :].astype(jnp.float32))
        gains = gains + jnp.sum(value * unit, 0, keepdims=True)
        shifts = shifts + jnp.sum(value, 0, keepdims=True)
    part.send()
    norm_grad[0:1, :] = gains
    norm_grad[1:2, :] = shifts
    g_refs = [out.held for out in g_outs]
    scatter_norms(plane, g_refs, norm_grad)
    turned[...] = rows.get()[...].T
    scatter_grads(plane, g_refs, 0, held, (mm(turned[...], dq[...]), mm(turned[...], dv[...])))
    key_grad = mm(turned[...], dk[...])
    turned[...] = up_rows[...].T
    scatter_grads(plane, g_refs, 1, held, (key_grad, mm(turned[...], heads[3].get()[...])))


def attn_backward(name, body, scalars, inputs, weights, kept, outputs, cross):
    cols = weights[0].shape[0] // 2 * HD
    bfloat16 = jnp.bfloat16
    block = (weights[0].shape[0], D // len(weights) + (0 if cross else 16), 2 * HD)
    outputs = outputs + [("one", block, bfloat16)] * len(weights)
    scratch = [pltpu.VMEM((D, LEN), bfloat16)]
    if not cross:
        scratch = [pltpu.VMEM((8, D), jnp.float32), pltpu.VMEM((LEN, D), bfloat16)] + scratch
    if cross:
        scratch += [pltpu.VMEM((D, MLEN), bfloat16), pltpu.VMEM((MLEN, 128), jnp.int32)]
    scratch += [pltpu.VMEM((D, cols), bfloat16)] * 4 + [
        pltpu.VMEM((8, LEN), jnp.float32),
        pltpu.VMEM((LEN, cols), bfloat16),
        pltpu.VMEM((cols, MLEN), bfloat16),
        pltpu.VMEM((cols, LEN), bfloat16),
        pltpu.VMEM((LEN, cols), bfloat16),
        pltpu.VMEM((MLEN, cols), jnp.float32),
        pltpu.VMEM((MLEN, cols), jnp.float32),
        pltpu.VMEM((MLEN, cols), bfloat16),
        pltpu.VMEM((MLEN, cols), bfloat16),
    ]
    inputs = inputs + [("one", (array,)) for array in (*map(Moved, weights), *kept)]
    return staged_call(body, name, scalars, inputs, outputs, scratch, BACKWARD_MEGA)


def add_to(ref, step, update):
    @pl.when(step == 0)
    def _():
        ref[...] = update

    @pl.when(step != 0)
    def _():
        ref[...] = ref[...] + update


def gelu_pieces(values):
    factor = 0.7978845608028654
    square = values * values
    slope = jnp.tanh(factor * values * (1.0 + 0.044715 * square))
    half = 0.5 * (1.0 + slope)
    grad = half + 0.5 * values * (1.0 - slope * slope) * factor * (1.0 + 3 * 0.044715 * square)
    return values * half, grad


def expert_kernel(
    core_ref,
    mine,
    theirs,
    part_mine,
    part_theirs,
    first_sum,
    norms,
    w_ref,
    sum_out,
    grad_out,
    out_keep,
    out_give,
    w_grad_ref,
    ours,
    others,
    sum_ref,
    exact,
    rows,
    up,
    grad_ref,
    out_total,
    grad_low,
    sems,
    out_sems,
):
    step = pl.program_id(0)

    def leaving(place):
        held, target = (
            (sum_ref, sum_out),
            (grad_low, grad_out),
            (out_total.at[half_at(core_ref, False)], out_keep),
            (out_total.at[half_at(core_ref, True)], out_give),
        )[place]
        return pltpu.make_async_copy(held, target, out_sems.at[place])

    @pl.when(step == 0)
    def _():
        up_copies = [
            pltpu.make_async_copy(a, up.at[half_at(core_ref, other)], sems.at[place])
            for place, (a, other) in enumerate(((mine, False), (theirs, True)))
        ]
        copies = [
            pltpu.make_async_copy(a.at[at], b.at[at], sems.at[2 + 3 * which + place])
            for which, at in enumerate(HALVES)
            for place, (a, b) in enumerate(
                ((part_mine, ours), (part_theirs, others), (first_sum, sum_ref))
            )
        ]
        for copy in copies[:3] + up_copies + copies[3:]:
            copy.start()
        for which, at in enumerate(HALVES):
            for copy in copies[3 * which : 3 * which + 3]:
                copy.wait()
            total = sum_ref[at, :].astype(jnp.float32) + (
                ours[at, :].astype(jnp.float32) + others[at, :].astype(jnp.float32)
            )
            exact[at, :] = total
            sum_ref[at, :] = total.astype(SUM)
            unit, _ = standardize(total)
            rows[at, :] = low(unit * norms[4:5, :] + norms[5:6, :])
        leaving(0).start()
        for copy in up_copies:
            copy.wait()

    shape = (D, w_ref.shape[4])
    w_in, w_out = w_ref[:, 0, 0].reshape(shape), w_ref[:, 0, 1].reshape(shape)
    back = mm(up[...], w_out)
    hidden, slope = gelu_pieces(mm(rows[...], w_in))
    hidden = low(hidden)
    inner_grad = low(slope * back)
    add_to(grad_ref, step, mt(inner_grad, w_in))
    add_to(out_total, step, mt(hidden, w_out))

    @pl.when(step == pl.num_programs(0) - 1)
    def _():
        grad_low[...] = grad_ref[...].astype(PART)
        at = half_at(core_ref, False)
        out_total[at, :] = out_total[at, :] + exact[at, :]
        for place in (1, 2, 3):
            leaving(place).start()

    grads = w_grad_ref.shape[0], -1, w_ref.shape[4]
    w_grad_ref[:, 0, 0] = low(tm(rows[...], inner_grad)).reshape(grads)
    w_grad_ref[:, 0, 1] = low(tm(up[...], hidden)).reshape(grads)

    @pl.when(step == pl.num_programs(0) - 1)
    def _():
        for place in range(4):
            leaving(place).wait()


def expert_layer(core_ref, rows, parts, first_sum, norms, weights):
    owners, steps, _, line_count, cols = weights.shape
    half = outside((LEN // 2, D), jnp.float32)
    w_spec = pl.BlockSpec((owners, 1, 2, line_count, cols), lambda step: (0, step, 0, 0, 0))
    low_rows = pltpu.VMEM((LEN, D), jnp.bfloat16)
    wide = pltpu.VMEM((LEN, D), jnp.float32)
    return pl.pallas_call(
        expert_kernel,
        name="expert",
        grid=(steps,),
        out_shape=(
            outside((LEN, D), SUM),
            outside((LEN, D), PART),
            half,
            half,
            outside(weights.shape, jnp.bfloat16),
        ),
        in_specs=[SCALARS, OUTSIDE, ANYWHERE, OUTSIDE, OUTSIDE, OUTSIDE, WHOLE, w_spec],
        out_specs=(OUTSIDE,) * 4 + (w_spec,),
        scratch_shapes=[pltpu.VMEM((LEN, D), PART)] * 2
        + [pltpu.VMEM((LEN, D), SUM), wide, low_rows, low_rows]
        + [wide, wide, pltpu.VMEM((LEN, D), PART)]
        + [pltpu.SemaphoreType.DMA((8,)), pltpu.SemaphoreType.DMA((4,))],
        compiler_params=pltpu.CompilerParams(vmem_limit_bytes=EXPERT_MEGA * MEGA),
        cost_estimate=KERNEL_COST,
    )(
        core_ref,
        *stay_outside(rows[:1]),
        rows[1],
        *stay_outside(parts),
        *stay_outside((first_sum, norms, weights)),
    )


def pack_attn_kernel(places, weights, norms, out_ref):
    odd = places[0, 0] == 1
    left = head_lanes(0)
    rows = weights.shape[2]
    count = norms.shape[0]
    values = jnp.concatenate(
        [norms[...], jnp.zeros((8 - count, norms.shape[1]), jnp.float32)], 0
    )
    facts = split_norms(jnp.concatenate([values, values], 1))
    blocks = out_ref.shape[0] // 2
    for core in (0, 1):
        for branch in range(weights.shape[0]):
            for pack in (0, 1):
                first, second = weights[branch, pack], weights[branch, 2 + pack]
                one = jnp.where(odd, second, first)
                two = jnp.where(odd, first, second)
                if core == 0:
                    tile = jnp.where(left, one, pltpu.roll(two, HD, 1))
                else:
                    tile = jnp.where(left, pltpu.roll(one, HD, 1), two)
                begin = pack * rows + branch * (2 * rows + 16)
                for block in range(blocks):
                    out_ref[core * blocks + block, begin : begin + rows] = low(tile)
        for block in range(blocks):
            out_ref[core * blocks + block, 2 * rows : 2 * rows + 16] = facts


def pack_attn(odd, weights, norms, tensor_count):
    shape = (2 * tensor_count, 4 * weights.shape[2] + 16, 2 * HD)
    return pl.pallas_call(
        pack_attn_kernel,
        name="pack_attn",
        out_shape=outside(shape, jnp.bfloat16),
        in_specs=[SCALARS, WHOLE, WHOLE],
        out_specs=WHOLE,
        compiler_params=pltpu.CompilerParams(vmem_limit_bytes=16 * MEGA),
        cost_estimate=KERNEL_COST,
    )(odd, *stay_outside((weights, norms)))


def pack_experts_kernel(chosen, weights, out_ref, held, sems):
    places, half = out_ref.shape[2], out_ref.shape[5]
    copies = [
        pltpu.make_async_copy(weights.at[chosen[0, row]], held.at[row], sems.at[row])
        for row in range(held.shape[0])
    ]
    for copy in copies:
        copy.start()
    for row, copy in enumerate(copies):
        copy.wait()
        for core in (0, 1):
            at = slice(core * half, (core + 1) * half)
            out_ref[row // places, core, row % places] = low(held[row, :, :, at])


def pack_experts(chip_expert, weights, plane_count, tensor_count):
    _, pair, rows, cols = weights.shape
    count = plane_count * tensor_count
    out = outside((plane_count, 2, tensor_count, pair, rows, cols // 2), jnp.bfloat16)
    return pl.pallas_call(
        pack_experts_kernel,
        name="pack_experts",
        out_shape=out,
        in_specs=[SCALARS, OUTSIDE],
        out_specs=WHOLE,
        scratch_shapes=[
            pltpu.VMEM((count, pair, rows, cols), jnp.float32),
            pltpu.SemaphoreType.DMA((count,)),
        ],
        compiler_params=pltpu.CompilerParams(vmem_limit_bytes=16 * MEGA),
        cost_estimate=KERNEL_COST,
    )(chip_expert, *stay_outside((weights,)))


def sum_planes_kernel(*refs):
    *parts, out_ref = refs
    count = len(parts) // 2
    rows = parts[count].shape[1]

    def total(blocks, index, lines):
        return sum(block[index, lines].astype(jnp.float32) for block in blocks)

    for index in range(out_ref.shape[0]):
        out_ref[index, :rows] = low(total(parts[:count], index, slice(0, rows)))
        norms = sum(join_norms(block[index, rows : rows + 16]) for block in parts[:count])
        out_ref[index, rows : rows + 16] = split_norms(norms)
        out_ref[index, rows + 16 :] = low(total(parts[count:], index, slice(0, rows)))


def sum_planes(self_parts, cross_parts):
    blocks, rows, cols = self_parts[0].shape
    shape = (blocks, rows + cross_parts[0].shape[1], cols)
    return pl.pallas_call(
        sum_planes_kernel,
        name="sum_planes",
        out_shape=outside(shape, jnp.bfloat16),
        in_specs=[WHOLE] * (len(self_parts) + len(cross_parts)),
        out_specs=WHOLE,
        compiler_params=pltpu.CompilerParams(vmem_limit_bytes=16 * MEGA),
        cost_estimate=KERNEL_COST,
    )(*self_parts, *cross_parts)


def lamb_update(weight, moment, second, grad):
    moment = beta_one * moment + (1.0 - beta_one) * grad
    second = beta_two * second + (1.0 - beta_two) * grad * grad
    update = (
        moment / (1.0 - beta_one**STEP) / (jnp.sqrt(second / (1.0 - beta_two**STEP)) + epsilon)
        + decay * weight
    )
    return moment, second, update


def expert_lamb_kernel(
    chosen, grads, w_ref, m_ref, v_ref, m_out, v_out, u_out, squares, total
):
    step = pl.program_id(0)
    half = grads.shape[5]
    group = w_ref.shape[0]

    @pl.when(step == 0)
    def _():
        total[...] = jnp.zeros_like(total)
        for plane in range(grads.shape[0]):
            for place in range(grads.shape[2]):
                expert = chosen[plane * grads.shape[2] + place]
                for core in (0, 1):
                    at = slice(core * half, (core + 1) * half)
                    total[expert, :, :, at] = total[expert, :, :, at] + grads[
                        plane, core, place
                    ].astype(jnp.float32)

    for own in range(group):
        expert = step * group + own
        weight = w_ref[own]
        m_out[own], v_out[own], update = lamb_update(weight, m_ref[own], v_ref[own], total[expert])
        u_out[own] = low(update)
        squares[own] = jnp.concatenate(
            [jnp.sum(weight * weight, 1), jnp.sum(update * update, 1)], 0
        )


def expert_lamb(chip_expert, grads, weights, moments, seconds):
    experts, pair, rows, cols = weights.shape
    group = 4
    spec = pl.BlockSpec((group, pair, rows, cols), lambda step, chosen: (step, 0, 0, 0))
    return pl.pallas_call(
        expert_lamb_kernel,
        name="expert_lamb",
        out_shape=(outside(weights.shape, jnp.float32),) * 2
        + (outside(weights.shape, jnp.bfloat16),)
        + (jax.ShapeDtypeStruct((experts, 2 * pair, cols), jnp.float32),),
        grid_spec=pltpu.PrefetchScalarGridSpec(
            num_scalar_prefetch=1,
            grid=(experts // group,),
            in_specs=[WHOLE, spec, spec, spec],
            out_specs=(spec, spec, spec)
            + (pl.BlockSpec((group, 2 * pair, cols), lambda step, chosen: (step, 0, 0)),),
            scratch_shapes=[pltpu.VMEM(weights.shape, jnp.float32)],
        ),
        compiler_params=pltpu.CompilerParams(vmem_limit_bytes=24 * MEGA),
        cost_estimate=KERNEL_COST,
    )(chip_expert, *stay_outside((grads, weights, moments, seconds)))


def owner_lamb_kernel(odd, chips, *refs):
    w_ref, m_ref, v_ref, norms, norm_m, norm_v, expert_squares, *outs = refs
    m_out, v_out, u_out, norm_m_out, norm_v_out, norm_u_out, squares, sums = outs
    experts = expert_squares.shape[0]
    matrices = w_ref.shape[0] * w_ref.shape[1]
    kinds = matrices + 2 * experts + norms.shape[0]
    sums[...] = jnp.zeros_like(sums)
    heads = chips.shape[0] // 2
    left = head_lanes(0)
    rows = w_ref.shape[2]
    for branch in range(w_ref.shape[0]):
        for pack in (0, 1):
            begin = pack * rows + branch * (2 * rows + 16)
            totals = []
            for core in (0, 1):
                totals.append(
                    sum(
                        chips[core * heads + head, begin : begin + rows].astype(jnp.float32)
                        for head in range(heads)
                    )
                )
            first = jnp.where(left, totals[0], pltpu.roll(totals[1], HD, 1))
            second = jnp.where(left, pltpu.roll(totals[0], HD, 1), totals[1])
            swapped = odd[0, 0] == 1
            for kind, grad in (
                (0, jnp.where(swapped, second, first)),
                (1, jnp.where(swapped, first, second)),
            ):
                matrix = 2 * kind + pack
                weight = w_ref[branch, matrix]
                m_out[branch, matrix], v_out[branch, matrix], update = lamb_update(
                    weight, m_ref[branch, matrix], v_ref[branch, matrix], grad
                )
                u_out[branch, matrix] = update
                line = branch * w_ref.shape[1] + matrix
                sums[line : line + 1, :] = jnp.sum(weight * weight, 0, keepdims=True)
                line += kinds
                sums[line : line + 1, :] = jnp.sum(update * update, 0, keepdims=True)
    grad = sum(join_norms(chips[index, 2 * rows : 2 * rows + 16]) for index in range(2 * heads))
    count, cols = norms.shape
    norm_m_out[...], norm_v_out[...], update = lamb_update(
        norms[...], norm_m[...], norm_v[...], grad[:count, :cols]
    )
    norm_u_out[...] = update
    share = 1.0 / heads
    first = matrices + 2 * experts
    sums[first:kinds, :cols] = norms[...] * norms[...] * share
    sums[kinds + first : 2 * kinds, :cols] = update * update * share
    for expert in range(experts):
        held = expert_squares[expert]
        held = sum(held[:, at : at + 2 * HD] for at in range(0, held.shape[1], 2 * HD))
        line = matrices + 2 * expert
        sums[line : line + 2, :] = held[0:2]
        sums[kinds + line : kinds + line + 2, :] = held[2:4]
    total = jnp.sum(sums[...].T, 0, keepdims=True)
    squares[...] = jnp.broadcast_to(total, squares.shape)


def owner_lamb(odd, chips, attn, norm, expert_squares, devices):
    matrices, norms = attn[0].shape, norm[0].shape
    return pl.pallas_call(
        owner_lamb_kernel,
        name="owner_lamb",
        out_shape=(outside(matrices, jnp.float32),) * 3
        + (jax.ShapeDtypeStruct(norms, jnp.float32),) * 3
        + (jax.ShapeDtypeStruct((devices, 2 * HD), jnp.float32),),
        in_specs=[SCALARS] + [WHOLE] * 8,
        out_specs=(WHOLE,) * 7,
        scratch_shapes=[pltpu.VMEM((2 * HD, 2 * HD), jnp.float32)],
        compiler_params=pltpu.CompilerParams(vmem_limit_bytes=16 * MEGA),
        cost_estimate=KERNEL_COST,
    )(odd, *stay_outside((chips, *attn, *norm)), expert_squares)


def final_step_kernel(sizes, moves, w_ref, u_ref, attn, attn_u, norms, norm_u, *rest):
    count = (len(rest) - 4) // 3
    sources, (out_ref, attn_out, norm_out) = rest[: 2 * count], rest[2 * count : 2 * count + 3]
    settled, sems = rest[2 * count + 3 : -1], rest[-1]
    step = pl.program_id(0)

    def settle(source, place):
        return pltpu.make_async_copy(source, settled[place], sems.at[place])

    for place in range(count):
        for source, moved in zip(sources[2 * place : 2 * place + 2], (0, 1)):

            @pl.when((step == 0) & (moves[0, 0] == moved))
            def _(source=source, place=place):
                settle(source, place).start()

    @pl.when(step == pl.num_programs(0) - 1)
    def _():
        for place in range(count):
            settle(sources[2 * place], place).wait()

    group, pair = out_ref.shape[:2]
    attn_count = attn.shape[0] * attn.shape[1]
    for own in range(group):
        for kind in range(pair):
            size = sizes[0, attn_count + (step * group + own) * pair + kind]
            out_ref[own, kind] = w_ref[own, kind] - size * u_ref[own, kind].astype(jnp.float32)

    @pl.when(step == 0)
    def _():
        for branch in range(attn.shape[0]):
            for matrix in range(attn.shape[1]):
                size = sizes[0, branch * attn.shape[1] + matrix]
                attn_out[branch, matrix] = attn[branch, matrix] - size * attn_u[branch, matrix]
        first = sizes.shape[1] - norms.shape[0]
        for row in range(norms.shape[0]):
            at = slice(row, row + 1)
            norm_out[at, :] = norms[at, :] - sizes[0, first + row] * norm_u[at, :]


def final_step(sizes, moves, weights, updates, attn, norm, landed):
    experts, pair, rows, cols = weights.shape
    group = 4
    spec = pl.BlockSpec((group, pair, rows, cols), lambda step: (step, 0, 0, 0))
    return pl.pallas_call(
        final_step_kernel,
        name="final_step",
        grid=(experts // group,),
        out_shape=(
            outside(weights.shape, jnp.float32),
            outside(attn[0].shape, jnp.float32),
            jax.ShapeDtypeStruct(norm[0].shape, jnp.float32),
        )
        + tuple(outside(array.shape, array.dtype) for array in landed[::2]),
        in_specs=[SCALARS, SCALARS, spec, spec] + [WHOLE] * 4 + [ANYWHERE] * len(landed),
        out_specs=(spec, WHOLE, WHOLE) + (OUTSIDE,) * (len(landed) // 2),
        scratch_shapes=[pltpu.SemaphoreType.DMA((len(landed) // 2,))],
        compiler_params=pltpu.CompilerParams(vmem_limit_bytes=24 * MEGA),
        cost_estimate=KERNEL_COST,
    )(sizes, moves, *stay_outside((weights, updates, *attn, *norm)), *landed)


DEVICES = ("plane", "core", "tensor")
CHIP = ("core", "tensor")


def twin(values):
    return lax.ppermute(values, "core", ((0, 1), (1, 0)))


def exchange(values, axes):
    return lax.all_to_all(values, axes, 0, 0, tiled=True)


def swap_pairs(plane_count, tensor_count):
    pairs = []
    for plane in range(plane_count):
        for core in range(2):
            for place in range(tensor_count):
                target = (plane * 2 + place % 2) * tensor_count + place // 2 * 2 + core
                here = (plane * 2 + core) * tensor_count + place
                if target != here:
                    pairs.append((here, target))
    return pairs


def other_planes(blocks):
    planes = range(lax.axis_size("plane"))
    got = list(blocks)
    for distance in reversed(planes[1:]):
        got[distance] = lax.ppermute(
            blocks[distance], "plane", [(k, k ^ distance) for k in planes]
        )
    return got


def sum_devices(values, axes):
    for axis in axes:
        count, flip = lax.axis_size(axis), 1
        while flip < count:
            values = values + lax.ppermute(values, axis, [(k, k ^ flip) for k in range(count)])
            flip *= 2
    return values


def body_rows(
    tokens,
    memory,
    cotangent,
    tgt_lengths,
    mem_lengths,
    mem_keep,
    row_expert,
    attn_weights,
    attn_moment,
    attn_second,
    expert_weights,
    expert_moment,
    expert_second,
    norm_params,
    norm_moment,
    norm_second,
):
    plane_count, tensor_count = lax.axis_size("plane"), lax.axis_size("tensor")
    devices = plane_count * 2 * tensor_count
    core, place = lax.axis_index("core"), lax.axis_index("tensor")
    moves = swap_pairs(plane_count, tensor_count)

    moving = core != place % 2

    def swap(values):
        return lax.ppermute(values, DEVICES, moves)

    def own_row(values):
        return jnp.where(moving, swap(values), values)

    plane = lax.axis_index("plane")
    core_ref = jnp.stack([core, plane]).reshape(1, 2)
    odd = (place % 2).reshape(1, 1)
    packed = pack_attn(odd, attn_weights, norm_params, tensor_count)
    tokens_mine = own_row(tokens)
    owned = jnp.arange(plane_count * 2)[:, None] == plane * 2 + core
    owner_expert = sum_devices(jnp.where(owned, row_expert[None], 0), ("core", "plane"))
    chip_expert = owner_expert.reshape(plane_count, 2, 2).transpose(0, 2, 1).reshape(1, -1)
    facts = jnp.concatenate([tgt_lengths, mem_lengths, mem_keep], 1)
    facts = jnp.where(core == place % 2, facts, twin(facts))
    facts = lax.dynamic_slice_in_dim(facts, place // 2, 1, 0)
    facts, keep = facts[:, :16], facts[:, 16:]
    chips = exchange(packed, CHIP)
    tokens_theirs = twin(tokens_mine)
    chips, tokens_mine, tokens_theirs, memory, cotangent, chip_expert = lax.optimization_barrier(
        (chips, tokens_mine, tokens_theirs, memory, cotangent, chip_expert)
    )
    self_lines = 2 * attn_weights.shape[2] + 16
    self_weights = other_planes([chips[:, :self_lines]] * plane_count)
    memory_mine = own_row(memory)
    up_mine = own_row(cotangent)
    cross_weights = other_planes([chips[:, self_lines:]] * plane_count)
    chosen = pack_experts(chip_expert, expert_weights, plane_count, tensor_count)
    memory_mine, up_mine, chosen, *self_weights = lax.optimization_barrier(
        (memory_mine, up_mine, chosen, *self_weights)
    )
    hidden_cols = expert_weights.shape[3] // 2
    chosen = exchange(chosen.reshape(devices, 2, -1, hidden_cols), DEVICES)
    chosen = chosen.reshape(plane_count * 2, tensor_count, 2, -1, hidden_cols)
    tokens_row = ("cores", (tokens_mine, Moved(tokens_theirs)))

    def halves(*arrays):
        return [("halves", (array,)) for array in arrays]

    self_part, norms, *self_kept = attn_forward(
        "self_forward",
        self_forward_body,
        (core_ref, facts),
        [tokens_row],
        self_weights,
        ("one", (8, D), jnp.float32),
        False,
    )
    self_theirs = twin(self_part)
    memory_mine, up_mine, self_theirs, *cross_weights = lax.optimization_barrier(
        (memory_mine, up_mine, self_theirs, *cross_weights)
    )
    memory_row = ("cores", (memory_mine, Moved(twin(memory_mine))))
    up_theirs = twin(up_mine)
    up_row = ("cores", (up_mine, Moved(up_theirs)))
    norms_in, keep_in = ("small", (norms,)), ("small", (keep,))
    cross_part, first_sum, *cross_kept = attn_forward(
        "cross_forward",
        cross_forward_body,
        (core_ref, facts),
        [*halves(self_part, Moved(self_theirs)), tokens_row, norms_in, keep_in, memory_row],
        cross_weights,
        ("halves", (LEN, D), SUM),
        True,
    )
    second_sum, ffn_part, out_keep, out_give, row_grad = expert_layer(
        core_ref,
        (up_mine, up_theirs),
        (cross_part, twin(cross_part)),
        first_sum,
        norms,
        chosen,
    )
    layer_low = low(out_keep + twin(out_give))
    layer_out = swap(layer_low)
    row_grad = exchange(row_grad.reshape(devices, 2, -1, hidden_cols), DEVICES)
    row_grad = row_grad.reshape(plane_count, 2, tensor_count, 2, -1, hidden_cols)
    grad_cross, cross_part, memory_keep, memory_give, ffn_norm, *cross_grad = attn_backward(
        "cross_backward",
        cross_backward_body,
        (core_ref, facts),
        [*halves(ffn_part, Moved(twin(ffn_part)), second_sum), up_row, norms_in, keep_in, memory_row],
        cross_weights,
        cross_kept,
        [
            ("halves", (LEN, D), SUM),
            ("halves", (LEN, D), PART),
            ("cores", (LEN, D), jnp.bfloat16),
            ("one", (2, D), jnp.float32),
        ],
        True,
    )
    cross_grad = other_planes(cross_grad)
    own_grad, part_keep, part_give, *self_grad = attn_backward(
        "self_backward",
        self_backward_body,
        (core_ref, facts),
        [
            *halves(cross_part, Moved(twin(cross_part)), first_sum, grad_cross),
            tokens_row,
            ("small", (ffn_norm,)),
            norms_in,
        ],
        self_weights,
        self_kept,
        [("own", (LEN, D), jnp.float32), ("cores", (LEN, D), jnp.float32)],
        False,
    )
    self_grad, memory_give, cross_grad = lax.optimization_barrier(
        (self_grad, memory_give, cross_grad)
    )
    memory_low = low(memory_keep.astype(jnp.float32) + twin(memory_give).astype(jnp.float32))
    memory_grad = swap(memory_low)
    planes = other_planes(self_grad)
    back, _, _ = norm_back(
        tokens_mine.astype(jnp.float32), part_keep + twin(part_give), norms[0:1]
    )
    input_low = low(own_grad + back)
    input_grad = swap(input_low)
    input_grad, layer_out, memory_grad, *planes = lax.optimization_barrier(
        (input_grad, layer_out, memory_grad, *planes)
    )
    chips = sum_planes(planes, cross_grad)
    row_grad, chips = lax.optimization_barrier((row_grad, chips))
    chips = exchange(chips, CHIP)
    expert_moment_new, expert_second_new, expert_update, expert_squares = expert_lamb(
        chip_expert.reshape(-1), row_grad, expert_weights, expert_moment, expert_second
    )
    attn_moment_new, attn_second_new, attn_update, *norm_outs, squares = owner_lamb(
        odd,
        chips,
        (attn_weights, attn_moment, attn_second),
        (norm_params, norm_moment, norm_second),
        expert_squares,
        devices,
    )
    norm_moment_new, norm_second_new, norm_update = norm_outs
    count = 8 + 2 * E + 6
    squares = exchange(squares, DEVICES).sum(0)[: 2 * count]
    lamb_norms = jnp.sqrt(squares).reshape(2, count)
    sizes = (rate * (lamb_norms[0] / lamb_norms[1])).reshape(1, -1)
    expert_new, attn_new, norm_new, layer_out, memory_grad, input_grad = final_step(
        sizes,
        moving.astype(jnp.int32).reshape(1, 1),
        expert_weights,
        expert_update,
        (attn_weights, attn_update),
        (norm_params, norm_update),
        (layer_low, layer_out, memory_low, memory_grad, input_low, input_grad),
    )
    return (
        layer_out,
        input_grad,
        memory_grad,
        attn_new,
        attn_moment_new,
        attn_second_new,
        expert_new,
        expert_moment_new,
        expert_second_new,
        norm_new,
        norm_moment_new,
        norm_second_new,
        lamb_norms,
    )


def specs(rows, dp):
    tokens = P((*dp, "tensor"), None)
    matrix = P(None, None, dp, "tensor")
    row_items = (P(dp, None),) * 3 + (P(dp),)
    return dict(
        in_specs=(tokens,) * 3 + row_items + (matrix,) * 6 + (P(None, dp),) * 3,
        out_specs=(tokens,) * 3 + (matrix,) * 6 + (P(None, dp),) * 3 + (P(),),
        check_vma=False,
    )


def solution(mesh):
    def run(*args):
        rows = args[3].shape[0]
        dp_count, tensor_count = mesh.shape["dp"], mesh.shape["tensor"]
        if rows // dp_count * 2 == tensor_count and tensor_count % 2 == 0:
            fine = Mesh(
                mesh.devices.reshape(dp_count // 2, 2, tensor_count), ("plane", "core", "tensor")
            )
            return jax.shard_map(body_rows, mesh=fine, **specs(rows, ("plane", "core")))(*args)
        return jax.shard_map(body, mesh=mesh, **specs(rows, ("dp",)))(*args)

    return run
```

```python
import jax
import jax.numpy as jnp
from jax import lax
from jax.experimental import pallas as pl
from jax.experimental.pallas import tpu as pltpu
from jax.sharding import Mesh
from jax.sharding import PartitionSpec as P

D = 512
HD = 64
E = 16
LEN = 1024
MLEN = 1024
STEP = 10


beta_one = 0.9
beta_two = 0.999
epsilon = 1e-06
decay = 0.01
rate = 0.2


def norm_layer(values, gain_vec, shift_vec):
    centered = values - jnp.mean(values, -1, keepdims=True)
    variance = jnp.mean(centered * centered, -1, keepdims=True)
    return centered * lax.rsqrt(variance + 1e-05) * gain_vec + shift_vec


def doc_numbers(lengths, length_total):
    doc_ends = jnp.cumsum(lengths)
    places = jnp.arange(length_total, dtype=jnp.int32)
    numbers = jnp.sum((places[:, None] >= doc_ends[None, :]).astype(jnp.int32), 1)
    starts = doc_ends - lengths
    opening = jnp.any(places[:, None] == starts[None, :], 1)
    return (numbers, opening)


def build_allowed(tgt_len, mem_len, keep_row, cross):
    doc_ids, _ = doc_numbers(tgt_len, LEN)
    if cross:
        mem_docs, opening = doc_numbers(mem_len, MLEN)
        return (doc_ids[:, None] == mem_docs[None, :]) & ((keep_row == 1) | opening)[None, :]
    places = jnp.arange(LEN, dtype=jnp.int32)
    return (doc_ids[:, None] == doc_ids[None, :]) & (places[None, :] <= places[:, None])


def gather_rows(values):
    return lax.all_gather(values, "tensor", axis=0, tiled=True)


def spread_rows(values):
    return lax.psum_scatter(values, "tensor", scatter_dimension=0, tiled=True)


def project(left_side, right_side):
    return jnp.dot(left_side, right_side, preferred_element_type=jnp.float32)


def project_back(left_side, right_side):
    return lax.dot_general(
        left_side, right_side, (((1,), (1,)), ((), ())), preferred_element_type=jnp.float32
    )


def outer_grad(left_side, right_side):
    return lax.dot_general(
        left_side, right_side, (((0,), (0,)), ((), ())), preferred_element_type=jnp.float32
    )


def attend_one(queries, key_rows, value_rows, allowed):
    head_count = queries.shape[1] // HD
    keys_h = key_rows.reshape(key_rows.shape[0], head_count, HD)
    values_h = value_rows.reshape(value_rows.shape[0], head_count, HD)
    block_rows = min(LEN, 512)
    outputs = []
    totals = []
    for begin_at in range(0, LEN, block_rows):
        queries_h = queries[begin_at : begin_at + block_rows].reshape(block_rows, head_count, HD)
        scores = jnp.einsum(
            "qhd,khd->hqk", queries_h, keys_h, preferred_element_type=jnp.float32
        ) * HD ** (-0.5)
        scores = jnp.where(allowed[None, begin_at : begin_at + block_rows], scores, -1e30)
        top_score = jnp.max(scores, -1, keepdims=True)
        weights = jnp.exp(scores - top_score)
        row_total = jnp.sum(weights, -1, keepdims=True)
        prob_low = (weights / row_total).astype(jnp.bfloat16)
        blended = jnp.einsum("hqk,khd->qhd", prob_low, values_h, preferred_element_type=jnp.float32)
        outputs.append(blended.reshape(block_rows, head_count * HD))
        totals.append((top_score + jnp.log(row_total))[..., 0])
    return (jnp.concatenate(outputs, 0), jnp.concatenate(totals, 1))


def attend_back_one(queries, key_rows, value_rows, upstream, log_totals, allowed):
    head_count = queries.shape[1] // HD
    scale = HD ** (-0.5)
    keys_h = key_rows.reshape(key_rows.shape[0], head_count, HD)
    values_h = value_rows.reshape(value_rows.shape[0], head_count, HD)
    key_grad = jnp.zeros(keys_h.shape, jnp.float32)
    value_grad = jnp.zeros(values_h.shape, jnp.float32)
    block_rows = min(LEN, 512)
    query_grads = []
    for begin_at in range(0, LEN, block_rows):
        queries_h = queries[begin_at : begin_at + block_rows].reshape(block_rows, head_count, HD)
        upstream_h = upstream[begin_at : begin_at + block_rows].reshape(block_rows, head_count, HD)
        scores = (
            jnp.einsum("qhd,khd->hqk", queries_h, keys_h, preferred_element_type=jnp.float32)
            * scale
        )
        scores = jnp.where(allowed[None, begin_at : begin_at + block_rows], scores, -1e30)
        probs_full = jnp.exp(scores - log_totals[:, begin_at : begin_at + block_rows, None])
        prob_grad = jnp.einsum(
            "qhd,khd->hqk", upstream_h, values_h, preferred_element_type=jnp.float32
        )
        weighted = jnp.sum(probs_full * prob_grad, -1, keepdims=True)
        score_grad = (probs_full * (prob_grad - weighted)).astype(jnp.bfloat16)
        query_part = (
            jnp.einsum("hqk,khd->qhd", score_grad, keys_h, preferred_element_type=jnp.float32)
            * scale
        )
        query_grads.append(query_part.astype(jnp.bfloat16).reshape(block_rows, head_count * HD))
        key_grad = (
            key_grad
            + jnp.einsum("hqk,qhd->khd", score_grad, queries_h, preferred_element_type=jnp.float32)
            * scale
        )
        value_grad = value_grad + jnp.einsum(
            "hqk,qhd->khd",
            probs_full.astype(jnp.bfloat16),
            upstream_h,
            preferred_element_type=jnp.float32,
        )
    width = head_count * HD
    return (
        jnp.concatenate(query_grads, 0),
        key_grad.astype(jnp.bfloat16).reshape(-1, width),
        value_grad.astype(jnp.bfloat16).reshape(-1, width),
    )


def attend_rows(queries, key_rows, value_rows, tgt_lengths, mem_lengths, mem_keep, cross):
    row_count = tgt_lengths.shape[0]
    width = queries.shape[1]

    def one_row(row_item):
        row_q, row_k, row_v, tgt_len, mem_len, keep_row = row_item
        return attend_one(row_q, row_k, row_v, build_allowed(tgt_len, mem_len, keep_row, cross))

    blended, log_totals = lax.map(
        one_row,
        (
            queries.reshape(row_count, LEN, width),
            key_rows.reshape(row_count, -1, width),
            value_rows.reshape(row_count, -1, width),
            tgt_lengths,
            mem_lengths,
            mem_keep,
        ),
    )
    return (blended.reshape(row_count * LEN, width), log_totals)


def attend_back_rows(
    queries, key_rows, value_rows, upstream, log_totals, tgt_lengths, mem_lengths, mem_keep, cross
):
    row_count = tgt_lengths.shape[0]
    width = queries.shape[1]

    def one_row(row_item):
        row_q, row_k, row_v, row_up, row_log, tgt_len, mem_len, keep_row = row_item
        return attend_back_one(
            row_q, row_k, row_v, row_up, row_log, build_allowed(tgt_len, mem_len, keep_row, cross)
        )

    query_grad, key_grad, value_grad = lax.map(
        one_row,
        (
            queries.reshape(row_count, LEN, width),
            key_rows.reshape(row_count, -1, width),
            value_rows.reshape(row_count, -1, width),
            upstream.reshape(row_count, LEN, width),
            log_totals,
            tgt_lengths,
            mem_lengths,
            mem_keep,
        ),
    )
    return (
        query_grad.reshape(-1, width),
        key_grad.reshape(-1, width),
        value_grad.reshape(-1, width),
    )


def lamb_pieces(weight, moment, second, grad, axes):
    moment = beta_one * moment + (1.0 - beta_one) * grad
    second = beta_two * second + (1.0 - beta_two) * grad * grad
    update = (
        moment / (1.0 - beta_one**STEP) / (jnp.sqrt(second / (1.0 - beta_two**STEP)) + epsilon)
        + decay * weight
    )
    return (moment, second, update, jnp.sum(weight * weight, axes), jnp.sum(update * update, axes))


def body(
    tokens,
    memory,
    cotangent,
    tgt_lengths,
    mem_lengths,
    mem_keep,
    row_expert,
    attn_weights,
    attn_moment,
    attn_second,
    expert_weights,
    expert_moment,
    expert_second,
    norm_params,
    norm_moment,
    norm_second,
):
    row_count = tgt_lengths.shape[0]
    attn_low, expert_low = (
        lax.all_gather(attn_weights.astype(jnp.bfloat16), "dp", axis=2, tiled=True),
        lax.all_gather(expert_weights.astype(jnp.bfloat16), "dp", axis=2, tiled=True),
    )
    row_low = expert_low[row_expert]
    norms = lax.all_gather(norm_params, "dp", axis=1, tiled=True)
    residual = tokens.astype(jnp.float32)
    normed_self, back_self = jax.vjp(norm_layer, residual, norms[0], norms[1])
    self_rows = gather_rows(normed_self.astype(jnp.bfloat16))
    self_qkv = jnp.einsum(
        "td,jdc->jtc", self_rows, attn_low[0, :3], preferred_element_type=jnp.float32
    ).astype(jnp.bfloat16)
    self_mix, self_log = attend_rows(
        self_qkv[0], self_qkv[1], self_qkv[2], tgt_lengths, mem_lengths, mem_keep, False
    )
    self_low = self_mix.astype(jnp.bfloat16)
    first_sum = residual + spread_rows(project_back(self_low, attn_low[0, 3]))
    normed_cross, back_cross = jax.vjp(norm_layer, first_sum, norms[2], norms[3])
    cross_rows = gather_rows(normed_cross.astype(jnp.bfloat16))
    memory_rows = gather_rows(memory)
    cross_queries = project(cross_rows, attn_low[1, 0]).astype(jnp.bfloat16)
    cross_kv = jnp.einsum(
        "td,jdc->jtc", memory_rows, attn_low[1, 1:3], preferred_element_type=jnp.float32
    ).astype(jnp.bfloat16)
    cross_mix, cross_log = attend_rows(
        cross_queries, cross_kv[0], cross_kv[1], tgt_lengths, mem_lengths, mem_keep, True
    )
    cross_low = cross_mix.astype(jnp.bfloat16)
    second_sum = first_sum + spread_rows(project_back(cross_low, attn_low[1, 3]))
    normed_ffn, back_ffn = jax.vjp(norm_layer, second_sum, norms[4], norms[5])
    ffn_rows = gather_rows(normed_ffn.astype(jnp.bfloat16))

    def expert_forward(row_item):
        row_in, chosen = row_item
        inner_act = project(row_in, chosen[0])
        hidden = jax.nn.gelu(inner_act).astype(jnp.bfloat16)
        return (inner_act, project_back(hidden, chosen[1]))

    inner_all, branch_all = lax.map(expert_forward, (ffn_rows.reshape(row_count, LEN, D), row_low))
    layer_out = (second_sum + spread_rows(branch_all.reshape(row_count * LEN, D))).astype(
        jnp.bfloat16
    )
    grad_ffn = cotangent.astype(jnp.float32)
    upstream_ffn = gather_rows(cotangent)
    ffn_again = gather_rows(normed_ffn.astype(jnp.bfloat16))

    def expert_backward(row_item):
        row_in, inner_act, upstream, chosen = row_item
        hidden, gelu_back = jax.vjp(jax.nn.gelu, inner_act)
        inner_grad = gelu_back(project(upstream, chosen[1]))[0].astype(jnp.bfloat16)
        pair_grads = jnp.stack(
            [outer_grad(row_in, inner_grad), outer_grad(upstream, hidden.astype(jnp.bfloat16))]
        )
        return (pair_grads, project_back(inner_grad, chosen[0]))

    row_grads, ffn_part = lax.map(
        expert_backward,
        (
            ffn_again.reshape(row_count, LEN, D),
            inner_all,
            upstream_ffn.reshape(row_count, LEN, D),
            row_low,
        ),
    )
    normed_ffn_grad = spread_rows(ffn_part.reshape(row_count * LEN, D))
    back_tokens, gain_ffn, shift_ffn = back_ffn(normed_ffn_grad)
    grad_cross = grad_ffn + back_tokens
    upstream_cross = gather_rows(grad_cross.astype(jnp.bfloat16))
    cross_again = gather_rows(normed_cross.astype(jnp.bfloat16))
    memory_again = gather_rows(memory)
    cross_up = project(upstream_cross, attn_low[1, 3]).astype(jnp.bfloat16)
    cross_dq, cross_dk, cross_dv = attend_back_rows(
        cross_queries,
        cross_kv[0],
        cross_kv[1],
        cross_up,
        cross_log,
        tgt_lengths,
        mem_lengths,
        mem_keep,
        True,
    )
    cross_grads = jnp.stack(
        [
            outer_grad(cross_again, cross_dq),
            outer_grad(memory_again, cross_dk),
            outer_grad(memory_again, cross_dv),
            outer_grad(upstream_cross, cross_low),
        ]
    )
    normed_cross_grad, memory_total = (
        lax.psum_scatter(
            project_back(cross_dq, attn_low[1, 0]), "tensor", scatter_dimension=0, tiled=True
        ),
        lax.psum_scatter(
            project_back(cross_dk, attn_low[1, 1]) + project_back(cross_dv, attn_low[1, 2]),
            "tensor",
            scatter_dimension=0,
            tiled=True,
        ),
    )
    back_tokens, gain_cross, shift_cross = back_cross(normed_cross_grad)
    grad_self = grad_cross + back_tokens
    upstream_self = gather_rows(grad_self.astype(jnp.bfloat16))
    self_again = gather_rows(normed_self.astype(jnp.bfloat16))
    self_up = project(upstream_self, attn_low[0, 3]).astype(jnp.bfloat16)
    self_dq, self_dk, self_dv = attend_back_rows(
        self_qkv[0],
        self_qkv[1],
        self_qkv[2],
        self_up,
        self_log,
        tgt_lengths,
        mem_lengths,
        mem_keep,
        False,
    )
    self_grads = jnp.stack(
        [
            outer_grad(self_again, self_dq),
            outer_grad(self_again, self_dk),
            outer_grad(self_again, self_dv),
            outer_grad(upstream_self, self_low),
        ]
    )
    normed_self_grad = spread_rows(
        project_back(self_dq, attn_low[0, 0])
        + project_back(self_dk, attn_low[0, 1])
        + project_back(self_dv, attn_low[0, 2])
    )
    back_tokens, gain_self, shift_self = back_self(normed_self_grad)
    input_grad = (grad_self + back_tokens).astype(jnp.bfloat16)
    attn_grad = jnp.stack([self_grads, cross_grads])
    norm_grad = jnp.stack([gain_self, shift_self, gain_cross, shift_cross, gain_ffn, shift_ffn])
    norm_total = lax.psum(norm_grad, "tensor")
    selector = (row_expert[:, None] == jnp.arange(E, dtype=jnp.int32)[None, :]).astype(jnp.float32)
    expert_grad = jnp.einsum("re,rjdf->ejdf", selector, row_grads, precision=lax.Precision.HIGHEST)
    expert_shard = lax.psum_scatter(expert_grad, "dp", scatter_dimension=2, tiled=True)
    attn_shard, norm_shard = (
        lax.psum_scatter(attn_grad, "dp", scatter_dimension=2, tiled=True),
        lax.psum_scatter(norm_total, "dp", scatter_dimension=1, tiled=True),
    )
    attn_pieces = lamb_pieces(attn_weights, attn_moment, attn_second, attn_shard, (2, 3))
    expert_pieces = lamb_pieces(expert_weights, expert_moment, expert_second, expert_shard, (2, 3))
    norm_pieces = lamb_pieces(norm_params, norm_moment, norm_second, norm_shard, (1,))
    copy_share = 1.0 / lax.axis_size("tensor")
    weight_squares = jnp.concatenate(
        [attn_pieces[3].reshape(-1), expert_pieces[3].reshape(-1), norm_pieces[3] * copy_share]
    )
    update_squares = jnp.concatenate(
        [attn_pieces[4].reshape(-1), expert_pieces[4].reshape(-1), norm_pieces[4] * copy_share]
    )
    weight_total, update_total = lax.psum((weight_squares, update_squares), ("dp", "tensor"))
    weight_norm = jnp.sqrt(weight_total)
    update_norm = jnp.sqrt(update_total)
    trust_ratio = weight_norm / update_norm
    attn_ratio = trust_ratio[:8].reshape(2, 4, 1, 1)
    expert_ratio = trust_ratio[8 : 8 + 2 * E].reshape(E, 2, 1, 1)
    norm_ratio = trust_ratio[8 + 2 * E :].reshape(6, 1)
    attn_new = attn_weights - rate * attn_ratio * attn_pieces[2]
    expert_new = expert_weights - rate * expert_ratio * expert_pieces[2]
    norm_new = norm_params - rate * norm_ratio * norm_pieces[2]
    lamb_norms = jnp.stack([weight_norm, update_norm])
    return (
        layer_out,
        input_grad,
        memory_total.astype(jnp.bfloat16),
        attn_new,
        attn_pieces[0],
        attn_pieces[1],
        expert_new,
        expert_pieces[0],
        expert_pieces[1],
        norm_new,
        norm_pieces[0],
        norm_pieces[1],
        lamb_norms,
    )


MEGA = 1024 * 1024
QUERY_BLOCK = 256
WINDOWS = {False: (128, 256, 384, 512, 640, 768), True: (256, 384, 640, 1024)}
FORWARD_MEGA, BACKWARD_MEGA, EXPERT_MEGA = 26, 36, 28
PART = jnp.bfloat16
SUM = jnp.bfloat16
HALVES = (slice(0, LEN // 2), slice(LEN // 2, LEN))
KERNEL_COST = pl.CostEstimate(flops=10**6, bytes_accessed=1024, transcendentals=0)
WHOLE = pl.BlockSpec(memory_space=pltpu.VMEM)
OUTSIDE = pl.BlockSpec(memory_space=pltpu.HBM)
ANYWHERE = pl.BlockSpec(memory_space=pl.ANY)


def outside(shape, dtype):
    return pltpu.HBM(shape, dtype)


def stay_outside(arrays):
    return [pltpu.with_memory_space_constraint(array, pltpu.HBM) for array in arrays]


SCALARS = pl.BlockSpec(memory_space=pltpu.SMEM)


def mm(left, right):
    return lax.dot_general(left, right, (((1,), (0,)), ((), ())), preferred_element_type=jnp.float32)


def mt(left, right):
    return lax.dot_general(left, right, (((1,), (1,)), ((), ())), preferred_element_type=jnp.float32)


def tm(left, right):
    return lax.dot_general(left, right, (((0,), (0,)), ((), ())), preferred_element_type=jnp.float32)


def low(values):
    return values.astype(jnp.bfloat16)


def standardize(values):
    centered = values - jnp.mean(values, -1, keepdims=True)
    inverse = lax.rsqrt(jnp.mean(centered * centered, -1, keepdims=True) + 1e-05)
    return centered * inverse, inverse


def norm_back(values, grad, gain_vec):
    unit, inverse = standardize(values)
    inner = grad * gain_vec
    back = inverse * (
        inner
        - jnp.mean(inner, -1, keepdims=True)
        - unit * jnp.mean(inner * unit, -1, keepdims=True)
    )
    return back, jnp.sum(grad * unit, 0, keepdims=True), jnp.sum(grad, 0, keepdims=True)


def key_limits(facts, places, cross):
    zero = jnp.zeros(places.shape, jnp.int32)
    low_end, high_end, doc_end = zero, zero, 0
    for doc in range(8):
        begin, doc_end = doc_end, doc_end + facts[0, doc]
        if cross:
            low_end = low_end + jnp.where(places >= doc_end, facts[0, 8 + doc], 0)
            high_end = high_end + jnp.where(places >= begin, facts[0, 8 + doc], 0)
        else:
            low_end = jnp.where(places >= doc_end, doc_end, low_end)
    return low_end, (high_end if cross else places + 1)


def kept_keys(facts, keep, places):
    kept = keep == 1
    begin = 0
    for doc in range(8):
        kept = kept | (places == begin)
        begin = begin + facts[0, 8 + doc]
    return kept


def key_windows(facts, cross, run):
    def block(index, _):
        first_query = pl.multiple_of(index * QUERY_BLOCK, QUERY_BLOCK)
        lowest, _ = key_limits(facts, first_query, cross)
        _, highest = key_limits(facts, first_query + QUERY_BLOCK - 1, cross)
        begin = lax.div(lowest, 128) * 128
        need = highest - begin
        for last, width in zip((0, *WINDOWS[cross]), WINDOWS[cross]):
            start = pl.multiple_of(jnp.minimum(begin, MLEN - width), 128)

            @pl.when((need <= width) & (need > last))
            def _(start=start, width=width):
                run(first_query, start, width)

        return 0

    lax.fori_loop(0, LEN // QUERY_BLOCK, block, 0)


def allowed_bias(facts, keep_ref, cross, first_query, start, width):
    places = first_query + lax.broadcasted_iota(jnp.int32, (1, QUERY_BLOCK), 1)
    low_end, high_end = key_limits(facts, places, cross)
    keys = start + lax.broadcasted_iota(jnp.int32, (width, QUERY_BLOCK), 0)
    if cross:
        own = start + lax.broadcasted_iota(jnp.int32, (width, 1), 0)
        keys = jnp.where(kept_keys(facts, keep_ref[pl.ds(start, width), 0:1], own), keys, -1)
    return jnp.where((keys >= low_end) & (keys < high_end), 0.0, -1e30)


def head_lanes(half):
    lane = lax.broadcasted_iota(jnp.int32, (1, 2 * HD), 1)
    return (lane < HD) if half == 0 else (lane >= HD)


def head_tile(head):
    return slice(head // 2 * 2 * HD, (head // 2 + 1) * 2 * HD)


def value_lines(head):
    return slice((head ^ 1) * HD, ((head ^ 1) + 1) * HD)


def of_head(values, half):
    return jnp.where(head_lanes(half), values, jnp.zeros_like(values))


def gather_weights(plane, w_refs, pack, first, second):
    left = head_lanes(0)
    cores, rows = 2, D // (2 * len(w_refs))
    heads = w_refs[0].shape[0] // cores
    lines = slice(pack * rows, (pack + 1) * rows)
    for distance, w_ref in enumerate(w_refs):
        for core in range(cores):
            begin = pl.multiple_of(((plane ^ distance) * cores + core) * rows, rows)
            for pair in range(heads // 2):
                even = w_ref[core * heads + 2 * pair, lines]
                odd = w_ref[core * heads + 2 * pair + 1, lines]
                at = slice(pair * 2 * HD, (pair + 1) * 2 * HD)
                first[pl.ds(begin, rows), at] = jnp.where(left, even, odd)
                second[pl.ds(begin, rows), at] = jnp.where(left, odd, even)


def scatter_grads(plane, g_refs, pack, held, values):
    first, second = held
    first[:D, :], second[:D, :] = values
    left = head_lanes(0)
    cores, rows = 2, D // (2 * len(g_refs))
    heads = g_refs[0].shape[0] // cores
    lines = slice(pack * rows, (pack + 1) * rows)
    for distance, g_ref in enumerate(g_refs):
        for core in range(cores):
            begin = pl.multiple_of(((plane ^ distance) * cores + core) * rows, rows)
            for pair in range(heads // 2):
                at = slice(pair * 2 * HD, (pair + 1) * 2 * HD)
                one, two = first[pl.ds(begin, rows), at], second[pl.ds(begin, rows), at]
                g_ref[core * heads + 2 * pair, lines] = low(jnp.where(left, one, two))
                g_ref[core * heads + 2 * pair + 1, lines] = low(jnp.where(left, two, one))


def gather_norms(plane, w_refs, norms):
    left = head_lanes(0)
    heads = w_refs[0].shape[0] // 2
    first = 2 * D // (2 * len(w_refs))
    for distance, w_ref in enumerate(w_refs):
        parts = []
        for core in (0, 1):
            parts.append(join_norms(w_ref[core * heads, first : first + 16]))
        at = pl.ds(pl.multiple_of((plane ^ distance) * 2 * HD, 2 * HD), 2 * HD)
        norms[:, at] = jnp.where(left, *parts)


def split_norms(values):
    high = low(values).astype(jnp.float32)
    middle = low(values - high).astype(jnp.float32)
    least = low(values - high - middle).astype(jnp.float32)
    return low(jnp.concatenate([jnp.where(head_lanes(0), high, middle), least], 0))


def join_norms(held):
    held = held.astype(jnp.float32)
    return (held[0:8] + pltpu.roll(held[0:8], HD, 1)) + held[8:16]


def scatter_norms(plane, g_refs, norms):
    heads = g_refs[0].shape[0] // 2
    first = D // len(g_refs)
    for distance, g_ref in enumerate(g_refs):
        at = pl.ds(pl.multiple_of((plane ^ distance) * 2 * HD, 2 * HD), 2 * HD)
        tile = norms[:, at]
        for core in (0, 1):
            values = jnp.where(head_lanes(core), tile, pltpu.roll(tile, HD, 1))
            for head in range(heads):
                g_ref[core * heads + head, first : first + 16] = split_norms(values)


class Moved:
    def __init__(self, values):
        self.values, self.shape, self.dtype = values, values.shape, values.dtype


class Arriving:
    def __init__(self, held, copies):
        self.held, self.copies = held, list(copies)

    def half(self, which):
        copy, self.copies[which] = self.copies[which], None
        if copy is not None:
            copy.wait()
        return self.held

    def get(self):
        for which in range(len(self.copies)):
            self.half(which)
        return self.held


class Leaving:
    def __init__(self, held, copies):
        self.held, self.copies, self.sent = held, list(copies), 0

    def send(self, upto=None):
        while self.sent < (len(self.copies) if upto is None else upto):
            self.copies[self.sent].start()
            self.sent += 1

    def finish(self):
        for copy in self.copies:
            copy.wait()


def half_at(core_ref, other):
    half = LEN // 2
    core = core_ref[0, 0]
    return pl.ds(pl.multiple_of((1 - core if other else core) * half, half), half)


def copies_of(kind, refs, held, core_ref, sems):
    if kind in ("one", "small"):
        pairs = [(refs[0], held)]
    elif kind == "halves":
        pairs = [(refs[0].at[at], held.at[at]) for at in HALVES]
    else:
        pairs = [(ref, held.at[half_at(core_ref, other)]) for ref, other in zip(refs, (False, True))]
    return pairs, [next(sems) for _ in pairs]


def staged_call(body, name, scalars, inputs, outputs, scratch, mega):
    in_count = sum(len(arrays) for _, arrays in inputs)
    shapes = []
    for kind, shape, dtype in outputs:
        if kind == "cores":
            shapes += [outside((shape[0] // 2, *shape[1:]), dtype)] * 2
        elif kind == "own":
            shapes += [outside((shape[0] // 2, *shape[1:]), dtype)]
        else:
            shapes += [outside(shape, dtype)]
    held_in = []
    for kind, arrays in inputs:
        rows, *others = arrays[0].shape
        rows = 2 * rows if kind == "cores" else rows
        held_in.append(pltpu.VMEM((rows, *others), arrays[0].dtype))
    held_out = [pltpu.VMEM(shape, dtype) for _, shape, dtype in outputs]
    waits = 2 * (len(inputs) + len(outputs))

    def kernel(*refs):
        refs = list(refs)

        def take(count):
            taken = refs[:count]
            del refs[:count]
            return taken

        scalar_refs, in_refs, out_refs = take(len(scalars)), take(in_count), take(len(shapes))
        in_held, out_held, (sem_ref,) = take(len(inputs)), take(len(outputs)), take(1)
        sems = (sem_ref.at[place] for place in range(waits))
        core_ref = scalar_refs[0]
        arrivals, starts = [], []
        for (kind, arrays), held in zip(inputs, in_held):
            mine, in_refs = in_refs[: len(arrays)], in_refs[len(arrays) :]
            pairs, own = copies_of(kind, mine, held, core_ref, sems)
            copies = [pltpu.make_async_copy(a, b, sem) for (a, b), sem in zip(pairs, own)]
            turn = {"small": (0,), "halves": (1, 2), "cores": (2, 2), "one": (3,)}[kind]
            starts += zip(turn, copies)
            arrivals.append(Arriving(held, copies))
        for _, copy in sorted(starts, key=lambda item: item[0]):
            copy.start()
        departures = []
        for (kind, _, _), held in zip(outputs, out_held):
            mine = out_refs[: 2 if kind == "cores" else 1]
            out_refs = out_refs[len(mine) :]
            pairs, own = copies_of("cores" if kind == "own" else kind, mine, held, core_ref, sems)
            copies = [pltpu.make_async_copy(b, a, sem) for (a, b), sem in zip(pairs, own)]
            departures.append(Leaving(held, copies))
        body(scalar_refs, arrivals, departures, refs)
        for arrival in arrivals:
            arrival.get()
        for departure in departures:
            departure.send()
        for departure in departures:
            departure.finish()

    arrays = [array for _, group in inputs for array in group]
    moved = [place for place, array in enumerate(arrays) if isinstance(array, Moved)]
    arrays = [array.values if isinstance(array, Moved) else array for array in arrays]
    arrays = [
        array if place in moved else stay_outside([array])[0] for place, array in enumerate(arrays)
    ]
    return pl.pallas_call(
        kernel,
        name=name,
        out_shape=tuple(shapes),
        in_specs=[SCALARS] * len(scalars)
        + [ANYWHERE if place in moved else OUTSIDE for place in range(in_count)],
        out_specs=(OUTSIDE,) * len(shapes),
        scratch_shapes=held_in + held_out + [pltpu.SemaphoreType.DMA((waits,))] + scratch,
        compiler_params=pltpu.CompilerParams(vmem_limit_bytes=mega * MEGA),
        cost_estimate=KERNEL_COST,
    )(*scalars, *arrays)


def forward_heads(plane, facts, keep_ref, cross, query_rows, key_rows, w_refs, outs, scratch):
    w_q, w_k, w_v, w_o, values_turned, blended_turned = scratch
    part, queries_out, keys_out, values_out, blended_out, stats_out = outs
    q_ref, k_ref, o_ref, stats_ref = (
        out.held for out in (queries_out, keys_out, blended_out, stats_out)
    )
    w_refs = [w_ref.get() for w_ref in w_refs]
    gather_weights(plane, w_refs, 0, w_q, w_v)
    gather_weights(plane, w_refs, 1, w_k, w_o)
    for out, rows, weights in (
        (queries_out, query_rows, w_q),
        (keys_out, key_rows, w_k),
        (values_out, key_rows, w_v),
    ):
        out.held[...] = low(mm(rows[...], weights[...]))
        out.send()
    values_turned[...] = values_out.held[...].T
    stats_ref[...] = jnp.zeros_like(stats_ref)
    heads = q_ref.shape[1] // HD

    def one(first_query, start, width):
        at, keys_at = pl.ds(first_query, QUERY_BLOCK), pl.ds(start, width)
        bias = allowed_bias(facts, keep_ref, cross, first_query, start, width)
        scores = []
        for head in range(heads):
            tile = head_tile(head)
            queries = of_head(q_ref[at, tile] * HD ** (-0.5), head % 2)
            scores.append(mt(k_ref[keys_at, tile], queries) + bias)
        done = []
        for head in range(heads):
            top = jnp.max(scores[head], 0, keepdims=True)
            weights = jnp.exp(scores[head] - top)
            total = jnp.sum(weights, 0, keepdims=True)
            stats_ref[head : head + 1, at] = top + jnp.log(total)
            done.append((low(weights), 1.0 / total))
        for head, (weights, share) in enumerate(done):
            lines = value_lines(head)
            blended_turned[lines, at] = low(mm(values_turned[lines, keys_at], weights) * share)

    key_windows(facts, cross, one)
    for which, at in enumerate(HALVES):
        o_ref[at, :] = blended_turned[:, at].T
        part.held[at, :] = mt(o_ref[at, :], w_o[...]).astype(PART)
        part.send(which + 1)


def self_forward_body(scalars, ins, outs, scratch):
    core_ref, facts = scalars
    tokens, *w_refs = ins
    part, norms, rows, *heads = outs
    plane = core_ref[0, 1]
    tokens = tokens.get()
    units = [standardize(tokens[at, :].astype(jnp.float32))[0] for at in HALVES]
    gather_norms(plane, [w_ref.get() for w_ref in w_refs], norms.held)
    norms.send()
    for at, unit in zip(HALVES, units):
        rows.held[at, :] = low(unit * norms.held[0:1, :] + norms.held[1:2, :])
    rows.send()
    forward_heads(
        plane, facts, None, False, rows.held, rows.held, w_refs, (part, *heads), scratch
    )


def cross_forward_body(scalars, ins, outs, scratch):
    core_ref, facts = scalars
    part_mine, part_theirs, tokens, norms, keep, memory, *w_refs = ins
    part, total, rows, *heads = outs
    tokens, norms = tokens.get(), norms.get()
    for which, at in enumerate(HALVES):
        ours = part_mine.half(which)[at, :].astype(jnp.float32)
        value = tokens[at, :].astype(jnp.float32) + (
            ours + part_theirs.half(which)[at, :].astype(jnp.float32)
        )
        total.held[at, :] = value.astype(SUM)
        total.send(which + 1)
        unit, _ = standardize(value)
        rows.held[at, :] = low(unit * norms[2:3, :] + norms[3:4, :])
    rows.send()
    keep_turned, *scratch = scratch
    keep_turned[...] = jnp.broadcast_to(keep.get()[...], (128, MLEN)).T
    forward_heads(
        core_ref[0, 1],
        facts,
        keep_turned,
        True,
        rows.held,
        memory.get(),
        w_refs,
        (part, *heads),
        scratch,
    )


def attn_forward(name, body, scalars, inputs, weights, extra, cross):
    cols = weights[0].shape[0] // 2 * HD
    bfloat16 = jnp.bfloat16
    outputs = [
        ("halves", (LEN, D), PART),
        extra,
        ("one", (LEN, D), bfloat16),
        *[("one", (LEN, cols), bfloat16)] * 4,
        ("one", (8, LEN), jnp.float32),
    ]
    scratch = [pltpu.VMEM((D, cols), bfloat16)] * 4
    scratch += [pltpu.VMEM((cols, MLEN), bfloat16), pltpu.VMEM((cols, LEN), bfloat16)]
    if cross:
        scratch = [pltpu.VMEM((MLEN, 128), jnp.int32)] + scratch
    inputs = inputs + [("one", (Moved(block),)) for block in weights]
    return staged_call(body, name, scalars, inputs, outputs, scratch, FORWARD_MEGA)


def backward_heads(plane, facts, keep_ref, cross, up_rows, w_refs, heads, scratch):
    w_q, w_k, w_v, w_o, weighted, up, keys_turned, q_turned, dq, k_sum, v_sum, dk, dv = scratch
    w_refs = [w_ref.get() for w_ref in w_refs]
    gather_weights(plane, w_refs, 0, w_q, w_v)
    gather_weights(plane, w_refs, 1, w_k, w_o)
    scale = HD ** (-0.5)
    up[...] = low(mm(up_rows[...], w_o[...]))
    q_ref, k_ref, v_ref, o_ref, stats_ref = (head.get() for head in heads)
    keys_turned[...] = k_ref[...].T
    k_sum[...] = jnp.zeros_like(k_sum)
    v_sum[...] = jnp.zeros_like(v_sum)

    products = (up[...].astype(jnp.float32) * o_ref[...].astype(jnp.float32)).T
    heads = q_ref.shape[1] // HD
    for head in range(heads):
        weighted[head : head + 1, :] = jnp.sum(products[value_lines(head), :], 0, keepdims=True)

    def one(first_query, start, width):
        at, keys_at = pl.ds(first_query, QUERY_BLOCK), pl.ds(start, width)
        bias = allowed_bias(facts, keep_ref, cross, first_query, start, width)
        ready, done, adds = [], [], []
        for head in range(heads):
            tile = head_tile(head)
            queries = of_head(q_ref[at, tile], head % 2)
            upstream = of_head(up[at, tile], 1 - head % 2)
            scores = mt(k_ref[keys_at, tile], queries * scale)
            ready.append((queries, upstream, scores, mt(v_ref[keys_at, tile], upstream)))
        for head, (_, _, scores, prob_grad) in enumerate(ready):
            probs = jnp.exp(scores + bias - stats_ref[head : head + 1, at])
            score_grad = low(probs * (prob_grad - weighted[head : head + 1, at]))
            done.append((low(probs), score_grad))
        for head, (probs, score_grad) in enumerate(done):
            queries, upstream, _, _ = ready[head]
            lines = slice(head * HD, (head + 1) * HD)
            q_turned[lines, at] = low(mm(keys_turned[lines, keys_at], score_grad) * scale)
            adds.append((mm(score_grad, queries), mm(probs, upstream)))
        for head in range(0, heads, 2):
            tile = head_tile(head)
            (key_one, value_one), (key_two, value_two) = adds[head : head + 2]
            k_sum[keys_at, tile] = k_sum[keys_at, tile] + (key_one + key_two)
            v_sum[keys_at, tile] = v_sum[keys_at, tile] + (value_one + value_two)

    key_windows(facts, cross, one)
    dq[...] = q_turned[...].T
    dk[...] = low(k_sum[...] * scale)
    dv[...] = low(v_sum[...])


def norm_step(parts, total, norms, row, upstream, finish):
    gains = jnp.zeros((1, D), jnp.float32)
    shifts = jnp.zeros((1, D), jnp.float32)
    for which, at in enumerate(HALVES):
        mine, theirs = (part.half(which)[at, :].astype(jnp.float32) for part in parts)
        back, gain, shift = norm_back(
            total.half(which)[at, :].astype(jnp.float32), mine + theirs, norms[row : row + 1, :]
        )
        gains, shifts = gains + gain, shifts + shift
        finish(which, at, upstream(which, at) + back)
    return gains, shifts


def cross_backward_body(scalars, ins, outs, scratch):
    core_ref, facts = scalars
    part_mine, part_theirs, total, cotangent, norms, keep, memory, *rest = ins
    planes = len(rest) - 6
    w_refs, (rows, *heads) = rest[:planes], rest[planes:]
    up_rows, part, memory_part, norm_out, *g_outs = outs
    turned, memory_turned, keep_turned, *scratch = scratch
    keep_turned[...] = jnp.broadcast_to(keep.get()[...], (128, MLEN)).T
    norms, cotangent = norms.get(), cotangent.get()
    plane = core_ref[0, 1]

    def finish(which, at, value):
        up_rows.held[at, :] = low(value)
        up_rows.send(which + 1)

    gains, shifts = norm_step(
        (part_mine, part_theirs),
        total,
        norms,
        4,
        lambda which, at: cotangent[at, :].astype(jnp.float32),
        finish,
    )
    norm_out.held[0:1, :] = 0.5 * gains
    norm_out.held[1:2, :] = 0.5 * shifts
    norm_out.send()
    backward_heads(plane, facts, keep_turned, True, up_rows.held, w_refs, heads, scratch)
    w_q, w_k, w_v, *_ = scratch
    dq, *held, dk, dv = scratch[-5:]
    for which, at in enumerate(HALVES):
        part.held[at, :] = mt(dq[at, :], w_q[...]).astype(PART)
        part.send(which + 1)
    memory_part.held[...] = low(mt(dk[...], w_k[...]) + mt(dv[...], w_v[...]))
    memory_part.send()
    g_refs = [out.held for out in g_outs]
    turned[...] = rows.get()[...].T
    memory_turned[...] = memory.get()[...].T
    scatter_grads(
        plane, g_refs, 0, held, (mm(turned[...], dq[...]), mm(memory_turned[...], dv[...]))
    )
    turned[...] = up_rows.held[...].T
    out_grad = mm(turned[...], heads[3].get()[...])
    scatter_grads(plane, g_refs, 1, held, (mm(memory_turned[...], dk[...]), out_grad))


def self_backward_body(scalars, ins, outs, scratch):
    core_ref, facts = scalars
    part_mine, part_theirs, total, grad, tokens, ffn_norm, norms, *rest = ins
    planes = len(rest) - 6
    w_refs, (rows, *heads) = rest[:planes], rest[planes:]
    grad_out, part, *g_outs = outs
    norm_grad, up_rows, turned, *scratch = scratch
    norms = norms.get()
    plane = core_ref[0, 1]

    def finish(which, at, value):
        grad_out.held[at, :] = value
        up_rows[at, :] = low(value)

    gains, shifts = norm_step(
        (part_mine, part_theirs),
        total,
        norms,
        2,
        lambda which, at: grad.half(which)[at, :].astype(jnp.float32),
        finish,
    )
    grad_out.send()
    norm_grad[2:3, :] = 0.5 * gains
    norm_grad[3:4, :] = 0.5 * shifts
    norm_grad[4:6, :] = ffn_norm.get()[...]
    norm_grad[6:8, :] = jnp.zeros((2, D), jnp.float32)
    backward_heads(plane, facts, None, False, up_rows, w_refs, heads, scratch)
    w_q, w_k, w_v, *_ = scratch
    dq, *held, dk, dv = scratch[-5:]
    tokens = tokens.get()
    gains = jnp.zeros((1, D), jnp.float32)
    shifts = jnp.zeros((1, D), jnp.float32)
    for at in HALVES:
        value = mt(dq[at, :], w_q[...]) + mt(dk[at, :], w_k[...]) + mt(dv[at, :], w_v[...])
        part.held[at, :] = value
        unit, _ = standardize(tokens[at, :].astype(jnp.float32))
        gains = gains + jnp.sum(value * unit, 0, keepdims=True)
        shifts = shifts + jnp.sum(value, 0, keepdims=True)
    part.send()
    norm_grad[0:1, :] = gains
    norm_grad[1:2, :] = shifts
    g_refs = [out.held for out in g_outs]
    scatter_norms(plane, g_refs, norm_grad)
    turned[...] = rows.get()[...].T
    scatter_grads(plane, g_refs, 0, held, (mm(turned[...], dq[...]), mm(turned[...], dv[...])))
    key_grad = mm(turned[...], dk[...])
    turned[...] = up_rows[...].T
    scatter_grads(plane, g_refs, 1, held, (key_grad, mm(turned[...], heads[3].get()[...])))


def attn_backward(name, body, scalars, inputs, weights, kept, outputs, cross):
    cols = weights[0].shape[0] // 2 * HD
    bfloat16 = jnp.bfloat16
    block = (weights[0].shape[0], D // len(weights) + (0 if cross else 16), 2 * HD)
    outputs = outputs + [("one", block, bfloat16)] * len(weights)
    scratch = [pltpu.VMEM((D, LEN), bfloat16)]
    if not cross:
        scratch = [pltpu.VMEM((8, D), jnp.float32), pltpu.VMEM((LEN, D), bfloat16)] + scratch
    if cross:
        scratch += [pltpu.VMEM((D, MLEN), bfloat16), pltpu.VMEM((MLEN, 128), jnp.int32)]
    scratch += [pltpu.VMEM((D, cols), bfloat16)] * 4 + [
        pltpu.VMEM((8, LEN), jnp.float32),
        pltpu.VMEM((LEN, cols), bfloat16),
        pltpu.VMEM((cols, MLEN), bfloat16),
        pltpu.VMEM((cols, LEN), bfloat16),
        pltpu.VMEM((LEN, cols), bfloat16),
        pltpu.VMEM((MLEN, cols), jnp.float32),
        pltpu.VMEM((MLEN, cols), jnp.float32),
        pltpu.VMEM((MLEN, cols), bfloat16),
        pltpu.VMEM((MLEN, cols), bfloat16),
    ]
    inputs = inputs + [("one", (array,)) for array in (*map(Moved, weights), *kept)]
    return staged_call(body, name, scalars, inputs, outputs, scratch, BACKWARD_MEGA)


def add_to(ref, step, update):
    @pl.when(step == 0)
    def _():
        ref[...] = update

    @pl.when(step != 0)
    def _():
        ref[...] = ref[...] + update


def gelu_pieces(values):
    factor = 0.7978845608028654
    square = values * values
    slope = jnp.tanh(factor * values * (1.0 + 0.044715 * square))
    half = 0.5 * (1.0 + slope)
    grad = half + 0.5 * values * (1.0 - slope * slope) * factor * (1.0 + 3 * 0.044715 * square)
    return values * half, grad


def expert_kernel(
    core_ref,
    mine,
    theirs,
    part_mine,
    part_theirs,
    first_sum,
    norms,
    w_ref,
    sum_out,
    grad_out,
    out_keep,
    out_give,
    w_grad_ref,
    ours,
    others,
    sum_ref,
    exact,
    rows,
    up,
    grad_ref,
    out_total,
    grad_low,
    sems,
    out_sems,
):
    step = pl.program_id(0)

    def leaving(place):
        held, target = (
            (sum_ref, sum_out),
            (grad_low, grad_out),
            (out_total.at[half_at(core_ref, False)], out_keep),
            (out_total.at[half_at(core_ref, True)], out_give),
        )[place]
        return pltpu.make_async_copy(held, target, out_sems.at[place])

    @pl.when(step == 0)
    def _():
        up_copies = [
            pltpu.make_async_copy(a, up.at[half_at(core_ref, other)], sems.at[place])
            for place, (a, other) in enumerate(((mine, False), (theirs, True)))
        ]
        copies = [
            pltpu.make_async_copy(a.at[at], b.at[at], sems.at[2 + 3 * which + place])
            for which, at in enumerate(HALVES)
            for place, (a, b) in enumerate(
                ((part_mine, ours), (part_theirs, others), (first_sum, sum_ref))
            )
        ]
        for copy in copies[:3] + up_copies + copies[3:]:
            copy.start()
        for which, at in enumerate(HALVES):
            for copy in copies[3 * which : 3 * which + 3]:
                copy.wait()
            total = sum_ref[at, :].astype(jnp.float32) + (
                ours[at, :].astype(jnp.float32) + others[at, :].astype(jnp.float32)
            )
            exact[at, :] = total
            sum_ref[at, :] = total.astype(SUM)
            unit, _ = standardize(total)
            rows[at, :] = low(unit * norms[4:5, :] + norms[5:6, :])
        leaving(0).start()
        for copy in up_copies:
            copy.wait()

    shape = (D, w_ref.shape[4])
    w_in, w_out = w_ref[:, 0, 0].reshape(shape), w_ref[:, 0, 1].reshape(shape)
    back = mm(up[...], w_out)
    hidden, slope = gelu_pieces(mm(rows[...], w_in))
    hidden = low(hidden)
    inner_grad = low(slope * back)
    add_to(grad_ref, step, mt(inner_grad, w_in))
    add_to(out_total, step, mt(hidden, w_out))

    @pl.when(step == pl.num_programs(0) - 1)
    def _():
        grad_low[...] = grad_ref[...].astype(PART)
        at = half_at(core_ref, False)
        out_total[at, :] = out_total[at, :] + exact[at, :]
        for place in (1, 2, 3):
            leaving(place).start()

    grads = w_grad_ref.shape[0], -1, w_ref.shape[4]
    w_grad_ref[:, 0, 0] = low(tm(rows[...], inner_grad)).reshape(grads)
    w_grad_ref[:, 0, 1] = low(tm(up[...], hidden)).reshape(grads)

    @pl.when(step == pl.num_programs(0) - 1)
    def _():
        for place in range(4):
            leaving(place).wait()


def expert_layer(core_ref, rows, parts, first_sum, norms, weights):
    owners, steps, _, line_count, cols = weights.shape
    half = outside((LEN // 2, D), jnp.float32)
    w_spec = pl.BlockSpec((owners, 1, 2, line_count, cols), lambda step: (0, step, 0, 0, 0))
    low_rows = pltpu.VMEM((LEN, D), jnp.bfloat16)
    wide = pltpu.VMEM((LEN, D), jnp.float32)
    return pl.pallas_call(
        expert_kernel,
        name="expert",
        grid=(steps,),
        out_shape=(
            outside((LEN, D), SUM),
            outside((LEN, D), PART),
            half,
            half,
            outside(weights.shape, jnp.bfloat16),
        ),
        in_specs=[SCALARS, OUTSIDE, ANYWHERE, OUTSIDE, OUTSIDE, OUTSIDE, WHOLE, w_spec],
        out_specs=(OUTSIDE,) * 4 + (w_spec,),
        scratch_shapes=[pltpu.VMEM((LEN, D), PART)] * 2
        + [pltpu.VMEM((LEN, D), SUM), wide, low_rows, low_rows]
        + [wide, wide, pltpu.VMEM((LEN, D), PART)]
        + [pltpu.SemaphoreType.DMA((8,)), pltpu.SemaphoreType.DMA((4,))],
        compiler_params=pltpu.CompilerParams(vmem_limit_bytes=EXPERT_MEGA * MEGA),
        cost_estimate=KERNEL_COST,
    )(
        core_ref,
        *stay_outside(rows[:1]),
        rows[1],
        *stay_outside(parts),
        *stay_outside((first_sum, norms, weights)),
    )


def pack_attn_kernel(places, weights, norms, out_ref):
    odd = places[0, 0] == 1
    left = head_lanes(0)
    rows = weights.shape[2]
    count = norms.shape[0]
    values = jnp.concatenate(
        [norms[...], jnp.zeros((8 - count, norms.shape[1]), jnp.float32)], 0
    )
    facts = split_norms(jnp.concatenate([values, values], 1))
    blocks = out_ref.shape[0] // 2
    for core in (0, 1):
        for branch in range(weights.shape[0]):
            for pack in (0, 1):
                first, second = weights[branch, pack], weights[branch, 2 + pack]
                one = jnp.where(odd, second, first)
                two = jnp.where(odd, first, second)
                if core == 0:
                    tile = jnp.where(left, one, pltpu.roll(two, HD, 1))
                else:
                    tile = jnp.where(left, pltpu.roll(one, HD, 1), two)
                begin = pack * rows + branch * (2 * rows + 16)
                for block in range(blocks):
                    out_ref[core * blocks + block, begin : begin + rows] = low(tile)
        for block in range(blocks):
            out_ref[core * blocks + block, 2 * rows : 2 * rows + 16] = facts


def pack_attn(odd, weights, norms, tensor_count):
    shape = (2 * tensor_count, 4 * weights.shape[2] + 16, 2 * HD)
    return pl.pallas_call(
        pack_attn_kernel,
        name="pack_attn",
        out_shape=outside(shape, jnp.bfloat16),
        in_specs=[SCALARS, WHOLE, WHOLE],
        out_specs=WHOLE,
        compiler_params=pltpu.CompilerParams(vmem_limit_bytes=16 * MEGA),
        cost_estimate=KERNEL_COST,
    )(odd, *stay_outside((weights, norms)))


def pack_experts_kernel(chosen, weights, out_ref, held, sems):
    places, half = out_ref.shape[2], out_ref.shape[5]
    copies = [
        pltpu.make_async_copy(weights.at[chosen[0, row]], held.at[row], sems.at[row])
        for row in range(held.shape[0])
    ]
    for copy in copies:
        copy.start()
    for row, copy in enumerate(copies):
        copy.wait()
        for core in (0, 1):
            at = slice(core * half, (core + 1) * half)
            out_ref[row // places, core, row % places] = low(held[row, :, :, at])


def pack_experts(chip_expert, weights, plane_count, tensor_count):
    _, pair, rows, cols = weights.shape
    count = plane_count * tensor_count
    out = outside((plane_count, 2, tensor_count, pair, rows, cols // 2), jnp.bfloat16)
    return pl.pallas_call(
        pack_experts_kernel,
        name="pack_experts",
        out_shape=out,
        in_specs=[SCALARS, OUTSIDE],
        out_specs=WHOLE,
        scratch_shapes=[
            pltpu.VMEM((count, pair, rows, cols), jnp.float32),
            pltpu.SemaphoreType.DMA((count,)),
        ],
        compiler_params=pltpu.CompilerParams(vmem_limit_bytes=16 * MEGA),
        cost_estimate=KERNEL_COST,
    )(chip_expert, *stay_outside((weights,)))


def sum_planes_kernel(*refs):
    *parts, out_ref = refs
    count = len(parts) // 2
    rows = parts[count].shape[1]

    def total(blocks, index, lines):
        return sum(block[index, lines].astype(jnp.float32) for block in blocks)

    for index in range(out_ref.shape[0]):
        out_ref[index, :rows] = low(total(parts[:count], index, slice(0, rows)))
        norms = sum(join_norms(block[index, rows : rows + 16]) for block in parts[:count])
        out_ref[index, rows : rows + 16] = split_norms(norms)
        out_ref[index, rows + 16 :] = low(total(parts[count:], index, slice(0, rows)))


def sum_planes(self_parts, cross_parts):
    blocks, rows, cols = self_parts[0].shape
    shape = (blocks, rows + cross_parts[0].shape[1], cols)
    return pl.pallas_call(
        sum_planes_kernel,
        name="sum_planes",
        out_shape=outside(shape, jnp.bfloat16),
        in_specs=[WHOLE] * (len(self_parts) + len(cross_parts)),
        out_specs=WHOLE,
        compiler_params=pltpu.CompilerParams(vmem_limit_bytes=16 * MEGA),
        cost_estimate=KERNEL_COST,
    )(*self_parts, *cross_parts)


def lamb_update(weight, moment, second, grad):
    moment = beta_one * moment + (1.0 - beta_one) * grad
    second = beta_two * second + (1.0 - beta_two) * grad * grad
    update = (
        moment / (1.0 - beta_one**STEP) / (jnp.sqrt(second / (1.0 - beta_two**STEP)) + epsilon)
        + decay * weight
    )
    return moment, second, update


def expert_lamb_kernel(
    chosen, grads, w_ref, m_ref, v_ref, m_out, v_out, u_out, squares, total
):
    step = pl.program_id(0)
    half = grads.shape[5]
    group = w_ref.shape[0]

    @pl.when(step == 0)
    def _():
        total[...] = jnp.zeros_like(total)
        for plane in range(grads.shape[0]):
            for place in range(grads.shape[2]):
                expert = chosen[plane * grads.shape[2] + place]
                for core in (0, 1):
                    at = slice(core * half, (core + 1) * half)
                    total[expert, :, :, at] = total[expert, :, :, at] + grads[
                        plane, core, place
                    ].astype(jnp.float32)

    for own in range(group):
        expert = step * group + own
        weight = w_ref[own]
        m_out[own], v_out[own], update = lamb_update(weight, m_ref[own], v_ref[own], total[expert])
        u_out[own] = low(update)
        squares[own] = jnp.concatenate(
            [jnp.sum(weight * weight, 1), jnp.sum(update * update, 1)], 0
        )


def expert_lamb(chip_expert, grads, weights, moments, seconds):
    experts, pair, rows, cols = weights.shape
    group = 4
    spec = pl.BlockSpec((group, pair, rows, cols), lambda step, chosen: (step, 0, 0, 0))
    return pl.pallas_call(
        expert_lamb_kernel,
        name="expert_lamb",
        out_shape=(outside(weights.shape, jnp.float32),) * 2
        + (outside(weights.shape, jnp.bfloat16),)
        + (jax.ShapeDtypeStruct((experts, 2 * pair, cols), jnp.float32),),
        grid_spec=pltpu.PrefetchScalarGridSpec(
            num_scalar_prefetch=1,
            grid=(experts // group,),
            in_specs=[WHOLE, spec, spec, spec],
            out_specs=(spec, spec, spec)
            + (pl.BlockSpec((group, 2 * pair, cols), lambda step, chosen: (step, 0, 0)),),
            scratch_shapes=[pltpu.VMEM(weights.shape, jnp.float32)],
        ),
        compiler_params=pltpu.CompilerParams(vmem_limit_bytes=24 * MEGA),
        cost_estimate=KERNEL_COST,
    )(chip_expert, *stay_outside((grads, weights, moments, seconds)))


def owner_lamb_kernel(odd, chips, *refs):
    w_ref, m_ref, v_ref, norms, norm_m, norm_v, expert_squares, *outs = refs
    m_out, v_out, u_out, norm_m_out, norm_v_out, norm_u_out, squares, sums = outs
    experts = expert_squares.shape[0]
    matrices = w_ref.shape[0] * w_ref.shape[1]
    kinds = matrices + 2 * experts + norms.shape[0]
    sums[...] = jnp.zeros_like(sums)
    heads = chips.shape[0] // 2
    left = head_lanes(0)
    rows = w_ref.shape[2]
    for branch in range(w_ref.shape[0]):
        for pack in (0, 1):
            begin = pack * rows + branch * (2 * rows + 16)
            totals = []
            for core in (0, 1):
                totals.append(
                    sum(
                        chips[core * heads + head, begin : begin + rows].astype(jnp.float32)
                        for head in range(heads)
                    )
                )
            first = jnp.where(left, totals[0], pltpu.roll(totals[1], HD, 1))
            second = jnp.where(left, pltpu.roll(totals[0], HD, 1), totals[1])
            swapped = odd[0, 0] == 1
            for kind, grad in (
                (0, jnp.where(swapped, second, first)),
                (1, jnp.where(swapped, first, second)),
            ):
                matrix = 2 * kind + pack
                weight = w_ref[branch, matrix]
                m_out[branch, matrix], v_out[branch, matrix], update = lamb_update(
                    weight, m_ref[branch, matrix], v_ref[branch, matrix], grad
                )
                u_out[branch, matrix] = update
                line = branch * w_ref.shape[1] + matrix
                sums[line : line + 1, :] = jnp.sum(weight * weight, 0, keepdims=True)
                line += kinds
                sums[line : line + 1, :] = jnp.sum(update * update, 0, keepdims=True)
    grad = sum(join_norms(chips[index, 2 * rows : 2 * rows + 16]) for index in range(2 * heads))
    count, cols = norms.shape
    norm_m_out[...], norm_v_out[...], update = lamb_update(
        norms[...], norm_m[...], norm_v[...], grad[:count, :cols]
    )
    norm_u_out[...] = update
    share = 1.0 / heads
    first = matrices + 2 * experts
    sums[first:kinds, :cols] = norms[...] * norms[...] * share
    sums[kinds + first : 2 * kinds, :cols] = update * update * share
    for expert in range(experts):
        held = expert_squares[expert]
        held = sum(held[:, at : at + 2 * HD] for at in range(0, held.shape[1], 2 * HD))
        line = matrices + 2 * expert
        sums[line : line + 2, :] = held[0:2]
        sums[kinds + line : kinds + line + 2, :] = held[2:4]
    total = jnp.sum(sums[...].T, 0, keepdims=True)
    squares[...] = jnp.broadcast_to(total, squares.shape)


def owner_lamb(odd, chips, attn, norm, expert_squares, devices):
    matrices, norms = attn[0].shape, norm[0].shape
    return pl.pallas_call(
        owner_lamb_kernel,
        name="owner_lamb",
        out_shape=(outside(matrices, jnp.float32),) * 3
        + (jax.ShapeDtypeStruct(norms, jnp.float32),) * 3
        + (jax.ShapeDtypeStruct((devices, 2 * HD), jnp.float32),),
        in_specs=[SCALARS] + [WHOLE] * 8,
        out_specs=(WHOLE,) * 7,
        scratch_shapes=[pltpu.VMEM((2 * HD, 2 * HD), jnp.float32)],
        compiler_params=pltpu.CompilerParams(vmem_limit_bytes=16 * MEGA),
        cost_estimate=KERNEL_COST,
    )(odd, *stay_outside((chips, *attn, *norm)), expert_squares)


def final_step_kernel(sizes, moves, w_ref, u_ref, attn, attn_u, norms, norm_u, *rest):
    count = (len(rest) - 4) // 3
    sources, (out_ref, attn_out, norm_out) = rest[: 2 * count], rest[2 * count : 2 * count + 3]
    settled, sems = rest[2 * count + 3 : -1], rest[-1]
    step = pl.program_id(0)

    def settle(source, place):
        return pltpu.make_async_copy(source, settled[place], sems.at[place])

    for place in range(count):
        for source, moved in zip(sources[2 * place : 2 * place + 2], (0, 1)):

            @pl.when((step == 0) & (moves[0, 0] == moved))
            def _(source=source, place=place):
                settle(source, place).start()

    @pl.when(step == pl.num_programs(0) - 1)
    def _():
        for place in range(count):
            settle(sources[2 * place], place).wait()

    group, pair = out_ref.shape[:2]
    attn_count = attn.shape[0] * attn.shape[1]
    for own in range(group):
        for kind in range(pair):
            size = sizes[0, attn_count + (step * group + own) * pair + kind]
            out_ref[own, kind] = w_ref[own, kind] - size * u_ref[own, kind].astype(jnp.float32)

    @pl.when(step == 0)
    def _():
        for branch in range(attn.shape[0]):
            for matrix in range(attn.shape[1]):
                size = sizes[0, branch * attn.shape[1] + matrix]
                attn_out[branch, matrix] = attn[branch, matrix] - size * attn_u[branch, matrix]
        first = sizes.shape[1] - norms.shape[0]
        for row in range(norms.shape[0]):
            at = slice(row, row + 1)
            norm_out[at, :] = norms[at, :] - sizes[0, first + row] * norm_u[at, :]


def final_step(sizes, moves, weights, updates, attn, norm, landed):
    experts, pair, rows, cols = weights.shape
    group = 4
    spec = pl.BlockSpec((group, pair, rows, cols), lambda step: (step, 0, 0, 0))
    return pl.pallas_call(
        final_step_kernel,
        name="final_step",
        grid=(experts // group,),
        out_shape=(
            outside(weights.shape, jnp.float32),
            outside(attn[0].shape, jnp.float32),
            jax.ShapeDtypeStruct(norm[0].shape, jnp.float32),
        )
        + tuple(outside(array.shape, array.dtype) for array in landed[::2]),
        in_specs=[SCALARS, SCALARS, spec, spec] + [WHOLE] * 4 + [ANYWHERE] * len(landed),
        out_specs=(spec, WHOLE, WHOLE) + (OUTSIDE,) * (len(landed) // 2),
        scratch_shapes=[pltpu.SemaphoreType.DMA((len(landed) // 2,))],
        compiler_params=pltpu.CompilerParams(vmem_limit_bytes=24 * MEGA),
        cost_estimate=KERNEL_COST,
    )(sizes, moves, *stay_outside((weights, updates, *attn, *norm)), *landed)


DEVICES = ("plane", "core", "tensor")
CHIP = ("core", "tensor")


def twin(values):
    return lax.ppermute(values, "core", ((0, 1), (1, 0)))


def exchange(values, axes):
    return lax.all_to_all(values, axes, 0, 0, tiled=True)


def swap_pairs(plane_count, tensor_count):
    pairs = []
    for plane in range(plane_count):
        for core in range(2):
            for place in range(tensor_count):
                target = (plane * 2 + place % 2) * tensor_count + place // 2 * 2 + core
                here = (plane * 2 + core) * tensor_count + place
                if target != here:
                    pairs.append((here, target))
    return pairs


def other_planes(blocks):
    planes = range(lax.axis_size("plane"))
    got = list(blocks)
    for distance in reversed(planes[1:]):
        got[distance] = lax.ppermute(
            blocks[distance], "plane", [(k, k ^ distance) for k in planes]
        )
    return got


def sum_devices(values, axes):
    for axis in axes:
        count, flip = lax.axis_size(axis), 1
        while flip < count:
            values = values + lax.ppermute(values, axis, [(k, k ^ flip) for k in range(count)])
            flip *= 2
    return values


def body_rows(
    tokens,
    memory,
    cotangent,
    tgt_lengths,
    mem_lengths,
    mem_keep,
    row_expert,
    attn_weights,
    attn_moment,
    attn_second,
    expert_weights,
    expert_moment,
    expert_second,
    norm_params,
    norm_moment,
    norm_second,
):
    plane_count, tensor_count = lax.axis_size("plane"), lax.axis_size("tensor")
    devices = plane_count * 2 * tensor_count
    core, place = lax.axis_index("core"), lax.axis_index("tensor")
    moves = swap_pairs(plane_count, tensor_count)

    moving = core != place % 2

    def swap(values):
        return lax.ppermute(values, DEVICES, moves)

    def own_row(values):
        return jnp.where(moving, swap(values), values)

    plane = lax.axis_index("plane")
    core_ref = jnp.stack([core, plane]).reshape(1, 2)
    odd = (place % 2).reshape(1, 1)
    packed = pack_attn(odd, attn_weights, norm_params, tensor_count)
    tokens_mine = own_row(tokens)
    owned = jnp.arange(plane_count * 2)[:, None] == plane * 2 + core
    owner_expert = sum_devices(jnp.where(owned, row_expert[None], 0), ("core", "plane"))
    chip_expert = owner_expert.reshape(plane_count, 2, 2).transpose(0, 2, 1).reshape(1, -1)
    facts = jnp.concatenate([tgt_lengths, mem_lengths, mem_keep], 1)
    facts = jnp.where(core == place % 2, facts, twin(facts))
    facts = lax.dynamic_slice_in_dim(facts, place // 2, 1, 0)
    facts, keep = facts[:, :16], facts[:, 16:]
    chips = exchange(packed, CHIP)
    tokens_theirs = twin(tokens_mine)
    chips, tokens_mine, tokens_theirs, memory, cotangent, chip_expert = lax.optimization_barrier(
        (chips, tokens_mine, tokens_theirs, memory, cotangent, chip_expert)
    )
    self_lines = 2 * attn_weights.shape[2] + 16
    self_weights = other_planes([chips[:, :self_lines]] * plane_count)
    memory_mine = own_row(memory)
    up_mine = own_row(cotangent)
    cross_weights = other_planes([chips[:, self_lines:]] * plane_count)
    chosen = pack_experts(chip_expert, expert_weights, plane_count, tensor_count)
    memory_mine, up_mine, chosen, *self_weights = lax.optimization_barrier(
        (memory_mine, up_mine, chosen, *self_weights)
    )
    hidden_cols = expert_weights.shape[3] // 2
    chosen = exchange(chosen.reshape(devices, 2, -1, hidden_cols), DEVICES)
    chosen = chosen.reshape(plane_count * 2, tensor_count, 2, -1, hidden_cols)
    tokens_row = ("cores", (tokens_mine, Moved(tokens_theirs)))

    def halves(*arrays):
        return [("halves", (array,)) for array in arrays]

    self_part, norms, *self_kept = attn_forward(
        "self_forward",
        self_forward_body,
        (core_ref, facts),
        [tokens_row],
        self_weights,
        ("one", (8, D), jnp.float32),
        False,
    )
    self_theirs = twin(self_part)
    memory_mine, up_mine, self_theirs, *cross_weights = lax.optimization_barrier(
        (memory_mine, up_mine, self_theirs, *cross_weights)
    )
    memory_row = ("cores", (memory_mine, Moved(twin(memory_mine))))
    up_theirs = twin(up_mine)
    up_row = ("cores", (up_mine, Moved(up_theirs)))
    norms_in, keep_in = ("small", (norms,)), ("small", (keep,))
    cross_part, first_sum, *cross_kept = attn_forward(
        "cross_forward",
        cross_forward_body,
        (core_ref, facts),
        [*halves(self_part, Moved(self_theirs)), tokens_row, norms_in, keep_in, memory_row],
        cross_weights,
        ("halves", (LEN, D), SUM),
        True,
    )
    second_sum, ffn_part, out_keep, out_give, row_grad = expert_layer(
        core_ref,
        (up_mine, up_theirs),
        (cross_part, twin(cross_part)),
        first_sum,
        norms,
        chosen,
    )
    layer_low = low(out_keep + twin(out_give))
    layer_out = swap(layer_low)
    row_grad = exchange(row_grad.reshape(devices, 2, -1, hidden_cols), DEVICES)
    row_grad = row_grad.reshape(plane_count, 2, tensor_count, 2, -1, hidden_cols)
    grad_cross, cross_part, memory_keep, memory_give, ffn_norm, *cross_grad = attn_backward(
        "cross_backward",
        cross_backward_body,
        (core_ref, facts),
        [*halves(ffn_part, Moved(twin(ffn_part)), second_sum), up_row, norms_in, keep_in, memory_row],
        cross_weights,
        cross_kept,
        [
            ("halves", (LEN, D), SUM),
            ("halves", (LEN, D), PART),
            ("cores", (LEN, D), jnp.bfloat16),
            ("one", (2, D), jnp.float32),
        ],
        True,
    )
    cross_grad = other_planes(cross_grad)
    own_grad, part_keep, part_give, *self_grad = attn_backward(
        "self_backward",
        self_backward_body,
        (core_ref, facts),
        [
            *halves(cross_part, Moved(twin(cross_part)), first_sum, grad_cross),
            tokens_row,
            ("small", (ffn_norm,)),
            norms_in,
        ],
        self_weights,
        self_kept,
        [("own", (LEN, D), jnp.float32), ("cores", (LEN, D), jnp.float32)],
        False,
    )
    self_grad, memory_give, cross_grad = lax.optimization_barrier(
        (self_grad, memory_give, cross_grad)
    )
    memory_low = low(memory_keep.astype(jnp.float32) + twin(memory_give).astype(jnp.float32))
    memory_grad = swap(memory_low)
    planes = other_planes(self_grad)
    back, _, _ = norm_back(
        tokens_mine.astype(jnp.float32), part_keep + twin(part_give), norms[0:1]
    )
    input_low = low(own_grad + back)
    input_grad = swap(input_low)
    input_grad, layer_out, memory_grad, *planes = lax.optimization_barrier(
        (input_grad, layer_out, memory_grad, *planes)
    )
    chips = sum_planes(planes, cross_grad)
    row_grad, chips = lax.optimization_barrier((row_grad, chips))
    chips = exchange(chips, CHIP)
    expert_moment_new, expert_second_new, expert_update, expert_squares = expert_lamb(
        chip_expert.reshape(-1), row_grad, expert_weights, expert_moment, expert_second
    )
    attn_moment_new, attn_second_new, attn_update, *norm_outs, squares = owner_lamb(
        odd,
        chips,
        (attn_weights, attn_moment, attn_second),
        (norm_params, norm_moment, norm_second),
        expert_squares,
        devices,
    )
    norm_moment_new, norm_second_new, norm_update = norm_outs
    count = 8 + 2 * E + 6
    squares = exchange(squares, DEVICES).sum(0)[: 2 * count]
    lamb_norms = jnp.sqrt(squares).reshape(2, count)
    sizes = (rate * (lamb_norms[0] / lamb_norms[1])).reshape(1, -1)
    expert_new, attn_new, norm_new, layer_out, memory_grad, input_grad = final_step(
        sizes,
        moving.astype(jnp.int32).reshape(1, 1),
        expert_weights,
        expert_update,
        (attn_weights, attn_update),
        (norm_params, norm_update),
        (layer_low, layer_out, memory_low, memory_grad, input_low, input_grad),
    )
    return (
        layer_out,
        input_grad,
        memory_grad,
        attn_new,
        attn_moment_new,
        attn_second_new,
        expert_new,
        expert_moment_new,
        expert_second_new,
        norm_new,
        norm_moment_new,
        norm_second_new,
        lamb_norms,
    )


def specs(rows, dp):
    tokens = P((*dp, "tensor"), None)
    matrix = P(None, None, dp, "tensor")
    row_items = (P(dp, None),) * 3 + (P(dp),)
    return dict(
        in_specs=(tokens,) * 3 + row_items + (matrix,) * 6 + (P(None, dp),) * 3,
        out_specs=(tokens,) * 3 + (matrix,) * 6 + (P(None, dp),) * 3 + (P(),),
        check_vma=False,
    )


def solution(mesh):
    def run(*args):
        rows = args[3].shape[0]
        dp_count, tensor_count = mesh.shape["dp"], mesh.shape["tensor"]
        if rows // dp_count * 2 == tensor_count and tensor_count % 2 == 0:
            fine = Mesh(
                mesh.devices.reshape(dp_count // 2, 2, tensor_count), ("plane", "core", "tensor")
            )
            return jax.shard_map(body_rows, mesh=fine, **specs(rows, ("plane", "core")))(*args)
        return jax.shard_map(body, mesh=mesh, **specs(rows, ("dp",)))(*args)

    return run
```

```python
import jax
import jax.numpy as jnp
from jax import lax
from jax.experimental import pallas as pl
from jax.experimental.pallas import tpu as pltpu
from jax.sharding import Mesh
from jax.sharding import PartitionSpec as P

D = 512
HD = 64
E = 16
LEN = 1024
MLEN = 1024
STEP = 10


beta_one = 0.9
beta_two = 0.999
epsilon = 1e-06
decay = 0.01
rate = 0.2


def norm_layer(values, gain_vec, shift_vec):
    centered = values - jnp.mean(values, -1, keepdims=True)
    variance = jnp.mean(centered * centered, -1, keepdims=True)
    return centered * lax.rsqrt(variance + 1e-05) * gain_vec + shift_vec


def doc_numbers(lengths, length_total):
    doc_ends = jnp.cumsum(lengths)
    places = jnp.arange(length_total, dtype=jnp.int32)
    numbers = jnp.sum((places[:, None] >= doc_ends[None, :]).astype(jnp.int32), 1)
    starts = doc_ends - lengths
    opening = jnp.any(places[:, None] == starts[None, :], 1)
    return (numbers, opening)


def build_allowed(tgt_len, mem_len, keep_row, cross):
    doc_ids, _ = doc_numbers(tgt_len, LEN)
    if cross:
        mem_docs, opening = doc_numbers(mem_len, MLEN)
        return (doc_ids[:, None] == mem_docs[None, :]) & ((keep_row == 1) | opening)[None, :]
    places = jnp.arange(LEN, dtype=jnp.int32)
    return (doc_ids[:, None] == doc_ids[None, :]) & (places[None, :] <= places[:, None])


def gather_rows(values):
    return lax.all_gather(values, "tensor", axis=0, tiled=True)


def spread_rows(values):
    return lax.psum_scatter(values, "tensor", scatter_dimension=0, tiled=True)


def project(left_side, right_side):
    return jnp.dot(left_side, right_side, preferred_element_type=jnp.float32)


def project_back(left_side, right_side):
    return lax.dot_general(
        left_side, right_side, (((1,), (1,)), ((), ())), preferred_element_type=jnp.float32
    )


def outer_grad(left_side, right_side):
    return lax.dot_general(
        left_side, right_side, (((0,), (0,)), ((), ())), preferred_element_type=jnp.float32
    )


def attend_one(queries, key_rows, value_rows, allowed):
    head_count = queries.shape[1] // HD
    keys_h = key_rows.reshape(key_rows.shape[0], head_count, HD)
    values_h = value_rows.reshape(value_rows.shape[0], head_count, HD)
    block_rows = min(LEN, 512)
    outputs = []
    totals = []
    for begin_at in range(0, LEN, block_rows):
        queries_h = queries[begin_at : begin_at + block_rows].reshape(block_rows, head_count, HD)
        scores = jnp.einsum(
            "qhd,khd->hqk", queries_h, keys_h, preferred_element_type=jnp.float32
        ) * HD ** (-0.5)
        scores = jnp.where(allowed[None, begin_at : begin_at + block_rows], scores, -1e30)
        top_score = jnp.max(scores, -1, keepdims=True)
        weights = jnp.exp(scores - top_score)
        row_total = jnp.sum(weights, -1, keepdims=True)
        prob_low = (weights / row_total).astype(jnp.bfloat16)
        blended = jnp.einsum("hqk,khd->qhd", prob_low, values_h, preferred_element_type=jnp.float32)
        outputs.append(blended.reshape(block_rows, head_count * HD))
        totals.append((top_score + jnp.log(row_total))[..., 0])
    return (jnp.concatenate(outputs, 0), jnp.concatenate(totals, 1))


def attend_back_one(queries, key_rows, value_rows, upstream, log_totals, allowed):
    head_count = queries.shape[1] // HD
    scale = HD ** (-0.5)
    keys_h = key_rows.reshape(key_rows.shape[0], head_count, HD)
    values_h = value_rows.reshape(value_rows.shape[0], head_count, HD)
    key_grad = jnp.zeros(keys_h.shape, jnp.float32)
    value_grad = jnp.zeros(values_h.shape, jnp.float32)
    block_rows = min(LEN, 512)
    query_grads = []
    for begin_at in range(0, LEN, block_rows):
        queries_h = queries[begin_at : begin_at + block_rows].reshape(block_rows, head_count, HD)
        upstream_h = upstream[begin_at : begin_at + block_rows].reshape(block_rows, head_count, HD)
        scores = (
            jnp.einsum("qhd,khd->hqk", queries_h, keys_h, preferred_element_type=jnp.float32)
            * scale
        )
        scores = jnp.where(allowed[None, begin_at : begin_at + block_rows], scores, -1e30)
        probs_full = jnp.exp(scores - log_totals[:, begin_at : begin_at + block_rows, None])
        prob_grad = jnp.einsum(
            "qhd,khd->hqk", upstream_h, values_h, preferred_element_type=jnp.float32
        )
        weighted = jnp.sum(probs_full * prob_grad, -1, keepdims=True)
        score_grad = (probs_full * (prob_grad - weighted)).astype(jnp.bfloat16)
        query_part = (
            jnp.einsum("hqk,khd->qhd", score_grad, keys_h, preferred_element_type=jnp.float32)
            * scale
        )
        query_grads.append(query_part.astype(jnp.bfloat16).reshape(block_rows, head_count * HD))
        key_grad = (
            key_grad
            + jnp.einsum("hqk,qhd->khd", score_grad, queries_h, preferred_element_type=jnp.float32)
            * scale
        )
        value_grad = value_grad + jnp.einsum(
            "hqk,qhd->khd",
            probs_full.astype(jnp.bfloat16),
            upstream_h,
            preferred_element_type=jnp.float32,
        )
    width = head_count * HD
    return (
        jnp.concatenate(query_grads, 0),
        key_grad.astype(jnp.bfloat16).reshape(-1, width),
        value_grad.astype(jnp.bfloat16).reshape(-1, width),
    )


def attend_rows(queries, key_rows, value_rows, tgt_lengths, mem_lengths, mem_keep, cross):
    row_count = tgt_lengths.shape[0]
    width = queries.shape[1]

    def one_row(row_item):
        row_q, row_k, row_v, tgt_len, mem_len, keep_row = row_item
        return attend_one(row_q, row_k, row_v, build_allowed(tgt_len, mem_len, keep_row, cross))

    blended, log_totals = lax.map(
        one_row,
        (
            queries.reshape(row_count, LEN, width),
            key_rows.reshape(row_count, -1, width),
            value_rows.reshape(row_count, -1, width),
            tgt_lengths,
            mem_lengths,
            mem_keep,
        ),
    )
    return (blended.reshape(row_count * LEN, width), log_totals)


def attend_back_rows(
    queries, key_rows, value_rows, upstream, log_totals, tgt_lengths, mem_lengths, mem_keep, cross
):
    row_count = tgt_lengths.shape[0]
    width = queries.shape[1]

    def one_row(row_item):
        row_q, row_k, row_v, row_up, row_log, tgt_len, mem_len, keep_row = row_item
        return attend_back_one(
            row_q, row_k, row_v, row_up, row_log, build_allowed(tgt_len, mem_len, keep_row, cross)
        )

    query_grad, key_grad, value_grad = lax.map(
        one_row,
        (
            queries.reshape(row_count, LEN, width),
            key_rows.reshape(row_count, -1, width),
            value_rows.reshape(row_count, -1, width),
            upstream.reshape(row_count, LEN, width),
            log_totals,
            tgt_lengths,
            mem_lengths,
            mem_keep,
        ),
    )
    return (
        query_grad.reshape(-1, width),
        key_grad.reshape(-1, width),
        value_grad.reshape(-1, width),
    )


def lamb_pieces(weight, moment, second, grad, axes):
    moment = beta_one * moment + (1.0 - beta_one) * grad
    second = beta_two * second + (1.0 - beta_two) * grad * grad
    update = (
        moment / (1.0 - beta_one**STEP) / (jnp.sqrt(second / (1.0 - beta_two**STEP)) + epsilon)
        + decay * weight
    )
    return (moment, second, update, jnp.sum(weight * weight, axes), jnp.sum(update * update, axes))


def body(
    tokens,
    memory,
    cotangent,
    tgt_lengths,
    mem_lengths,
    mem_keep,
    row_expert,
    attn_weights,
    attn_moment,
    attn_second,
    expert_weights,
    expert_moment,
    expert_second,
    norm_params,
    norm_moment,
    norm_second,
):
    row_count = tgt_lengths.shape[0]
    attn_low, expert_low = (
        lax.all_gather(attn_weights.astype(jnp.bfloat16), "dp", axis=2, tiled=True),
        lax.all_gather(expert_weights.astype(jnp.bfloat16), "dp", axis=2, tiled=True),
    )
    row_low = expert_low[row_expert]
    norms = lax.all_gather(norm_params, "dp", axis=1, tiled=True)
    residual = tokens.astype(jnp.float32)
    normed_self, back_self = jax.vjp(norm_layer, residual, norms[0], norms[1])
    self_rows = gather_rows(normed_self.astype(jnp.bfloat16))
    self_qkv = jnp.einsum(
        "td,jdc->jtc", self_rows, attn_low[0, :3], preferred_element_type=jnp.float32
    ).astype(jnp.bfloat16)
    self_mix, self_log = attend_rows(
        self_qkv[0], self_qkv[1], self_qkv[2], tgt_lengths, mem_lengths, mem_keep, False
    )
    self_low = self_mix.astype(jnp.bfloat16)
    first_sum = residual + spread_rows(project_back(self_low, attn_low[0, 3]))
    normed_cross, back_cross = jax.vjp(norm_layer, first_sum, norms[2], norms[3])
    cross_rows = gather_rows(normed_cross.astype(jnp.bfloat16))
    memory_rows = gather_rows(memory)
    cross_queries = project(cross_rows, attn_low[1, 0]).astype(jnp.bfloat16)
    cross_kv = jnp.einsum(
        "td,jdc->jtc", memory_rows, attn_low[1, 1:3], preferred_element_type=jnp.float32
    ).astype(jnp.bfloat16)
    cross_mix, cross_log = attend_rows(
        cross_queries, cross_kv[0], cross_kv[1], tgt_lengths, mem_lengths, mem_keep, True
    )
    cross_low = cross_mix.astype(jnp.bfloat16)
    second_sum = first_sum + spread_rows(project_back(cross_low, attn_low[1, 3]))
    normed_ffn, back_ffn = jax.vjp(norm_layer, second_sum, norms[4], norms[5])
    ffn_rows = gather_rows(normed_ffn.astype(jnp.bfloat16))

    def expert_forward(row_item):
        row_in, chosen = row_item
        inner_act = project(row_in, chosen[0])
        hidden = jax.nn.gelu(inner_act).astype(jnp.bfloat16)
        return (inner_act, project_back(hidden, chosen[1]))

    inner_all, branch_all = lax.map(expert_forward, (ffn_rows.reshape(row_count, LEN, D), row_low))
    layer_out = (second_sum + spread_rows(branch_all.reshape(row_count * LEN, D))).astype(
        jnp.bfloat16
    )
    grad_ffn = cotangent.astype(jnp.float32)
    upstream_ffn = gather_rows(cotangent)
    ffn_again = gather_rows(normed_ffn.astype(jnp.bfloat16))

    def expert_backward(row_item):
        row_in, inner_act, upstream, chosen = row_item
        hidden, gelu_back = jax.vjp(jax.nn.gelu, inner_act)
        inner_grad = gelu_back(project(upstream, chosen[1]))[0].astype(jnp.bfloat16)
        pair_grads = jnp.stack(
            [outer_grad(row_in, inner_grad), outer_grad(upstream, hidden.astype(jnp.bfloat16))]
        )
        return (pair_grads, project_back(inner_grad, chosen[0]))

    row_grads, ffn_part = lax.map(
        expert_backward,
        (
            ffn_again.reshape(row_count, LEN, D),
            inner_all,
            upstream_ffn.reshape(row_count, LEN, D),
            row_low,
        ),
    )
    normed_ffn_grad = spread_rows(ffn_part.reshape(row_count * LEN, D))
    back_tokens, gain_ffn, shift_ffn = back_ffn(normed_ffn_grad)
    grad_cross = grad_ffn + back_tokens
    upstream_cross = gather_rows(grad_cross.astype(jnp.bfloat16))
    cross_again = gather_rows(normed_cross.astype(jnp.bfloat16))
    memory_again = gather_rows(memory)
    cross_up = project(upstream_cross, attn_low[1, 3]).astype(jnp.bfloat16)
    cross_dq, cross_dk, cross_dv = attend_back_rows(
        cross_queries,
        cross_kv[0],
        cross_kv[1],
        cross_up,
        cross_log,
        tgt_lengths,
        mem_lengths,
        mem_keep,
        True,
    )
    cross_grads = jnp.stack(
        [
            outer_grad(cross_again, cross_dq),
            outer_grad(memory_again, cross_dk),
            outer_grad(memory_again, cross_dv),
            outer_grad(upstream_cross, cross_low),
        ]
    )
    normed_cross_grad, memory_total = (
        lax.psum_scatter(
            project_back(cross_dq, attn_low[1, 0]), "tensor", scatter_dimension=0, tiled=True
        ),
        lax.psum_scatter(
            project_back(cross_dk, attn_low[1, 1]) + project_back(cross_dv, attn_low[1, 2]),
            "tensor",
            scatter_dimension=0,
            tiled=True,
        ),
    )
    back_tokens, gain_cross, shift_cross = back_cross(normed_cross_grad)
    grad_self = grad_cross + back_tokens
    upstream_self = gather_rows(grad_self.astype(jnp.bfloat16))
    self_again = gather_rows(normed_self.astype(jnp.bfloat16))
    self_up = project(upstream_self, attn_low[0, 3]).astype(jnp.bfloat16)
    self_dq, self_dk, self_dv = attend_back_rows(
        self_qkv[0],
        self_qkv[1],
        self_qkv[2],
        self_up,
        self_log,
        tgt_lengths,
        mem_lengths,
        mem_keep,
        False,
    )
    self_grads = jnp.stack(
        [
            outer_grad(self_again, self_dq),
            outer_grad(self_again, self_dk),
            outer_grad(self_again, self_dv),
            outer_grad(upstream_self, self_low),
        ]
    )
    normed_self_grad = spread_rows(
        project_back(self_dq, attn_low[0, 0])
        + project_back(self_dk, attn_low[0, 1])
        + project_back(self_dv, attn_low[0, 2])
    )
    back_tokens, gain_self, shift_self = back_self(normed_self_grad)
    input_grad = (grad_self + back_tokens).astype(jnp.bfloat16)
    attn_grad = jnp.stack([self_grads, cross_grads])
    norm_grad = jnp.stack([gain_self, shift_self, gain_cross, shift_cross, gain_ffn, shift_ffn])
    norm_total = lax.psum(norm_grad, "tensor")
    selector = (row_expert[:, None] == jnp.arange(E, dtype=jnp.int32)[None, :]).astype(jnp.float32)
    expert_grad = jnp.einsum("re,rjdf->ejdf", selector, row_grads, precision=lax.Precision.HIGHEST)
    expert_shard = lax.psum_scatter(expert_grad, "dp", scatter_dimension=2, tiled=True)
    attn_shard, norm_shard = (
        lax.psum_scatter(attn_grad, "dp", scatter_dimension=2, tiled=True),
        lax.psum_scatter(norm_total, "dp", scatter_dimension=1, tiled=True),
    )
    attn_pieces = lamb_pieces(attn_weights, attn_moment, attn_second, attn_shard, (2, 3))
    expert_pieces = lamb_pieces(expert_weights, expert_moment, expert_second, expert_shard, (2, 3))
    norm_pieces = lamb_pieces(norm_params, norm_moment, norm_second, norm_shard, (1,))
    copy_share = 1.0 / lax.axis_size("tensor")
    weight_squares = jnp.concatenate(
        [attn_pieces[3].reshape(-1), expert_pieces[3].reshape(-1), norm_pieces[3] * copy_share]
    )
    update_squares = jnp.concatenate(
        [attn_pieces[4].reshape(-1), expert_pieces[4].reshape(-1), norm_pieces[4] * copy_share]
    )
    weight_total, update_total = lax.psum((weight_squares, update_squares), ("dp", "tensor"))
    weight_norm = jnp.sqrt(weight_total)
    update_norm = jnp.sqrt(update_total)
    trust_ratio = weight_norm / update_norm
    attn_ratio = trust_ratio[:8].reshape(2, 4, 1, 1)
    expert_ratio = trust_ratio[8 : 8 + 2 * E].reshape(E, 2, 1, 1)
    norm_ratio = trust_ratio[8 + 2 * E :].reshape(6, 1)
    attn_new = attn_weights - rate * attn_ratio * attn_pieces[2]
    expert_new = expert_weights - rate * expert_ratio * expert_pieces[2]
    norm_new = norm_params - rate * norm_ratio * norm_pieces[2]
    lamb_norms = jnp.stack([weight_norm, update_norm])
    return (
        layer_out,
        input_grad,
        memory_total.astype(jnp.bfloat16),
        attn_new,
        attn_pieces[0],
        attn_pieces[1],
        expert_new,
        expert_pieces[0],
        expert_pieces[1],
        norm_new,
        norm_pieces[0],
        norm_pieces[1],
        lamb_norms,
    )


MEGA = 1024 * 1024
QUERY_BLOCK = 256
WINDOWS = {False: (256, 384, 512, 640, 768), True: (256, 384, 640, 1024)}
FORWARD_MEGA, BACKWARD_MEGA, EXPERT_MEGA = 26, 36, 28
PART = jnp.bfloat16
SUM = jnp.bfloat16
HALVES = (slice(0, LEN // 2), slice(LEN // 2, LEN))
KERNEL_COST = pl.CostEstimate(flops=10**6, bytes_accessed=1024, transcendentals=0)
WHOLE = pl.BlockSpec(memory_space=pltpu.VMEM)
OUTSIDE = pl.BlockSpec(memory_space=pltpu.HBM)
ANYWHERE = pl.BlockSpec(memory_space=pl.ANY)


def outside(shape, dtype):
    return pltpu.HBM(shape, dtype)


def stay_outside(arrays):
    return [pltpu.with_memory_space_constraint(array, pltpu.HBM) for array in arrays]


SCALARS = pl.BlockSpec(memory_space=pltpu.SMEM)


def mm(left, right):
    return lax.dot_general(left, right, (((1,), (0,)), ((), ())), preferred_element_type=jnp.float32)


def mt(left, right):
    return lax.dot_general(left, right, (((1,), (1,)), ((), ())), preferred_element_type=jnp.float32)


def tm(left, right):
    return lax.dot_general(left, right, (((0,), (0,)), ((), ())), preferred_element_type=jnp.float32)


def low(values):
    return values.astype(jnp.bfloat16)


def standardize(values):
    centered = values - jnp.mean(values, -1, keepdims=True)
    inverse = lax.rsqrt(jnp.mean(centered * centered, -1, keepdims=True) + 1e-05)
    return centered * inverse, inverse


def norm_back(values, grad, gain_vec):
    unit, inverse = standardize(values)
    inner = grad * gain_vec
    back = inverse * (
        inner
        - jnp.mean(inner, -1, keepdims=True)
        - unit * jnp.mean(inner * unit, -1, keepdims=True)
    )
    return back, jnp.sum(grad * unit, 0, keepdims=True), jnp.sum(grad, 0, keepdims=True)


def key_limits(facts, places, cross):
    zero = jnp.zeros(places.shape, jnp.int32)
    low_end, high_end, doc_end = zero, zero, 0
    for doc in range(8):
        begin, doc_end = doc_end, doc_end + facts[0, doc]
        if cross:
            low_end = low_end + jnp.where(places >= doc_end, facts[0, 8 + doc], 0)
            high_end = high_end + jnp.where(places >= begin, facts[0, 8 + doc], 0)
        else:
            low_end = jnp.where(places >= doc_end, doc_end, low_end)
    return low_end, (high_end if cross else places + 1)


def kept_keys(facts, keep, places):
    kept = keep == 1
    begin = 0
    for doc in range(8):
        kept = kept | (places == begin)
        begin = begin + facts[0, 8 + doc]
    return kept


def key_windows(facts, cross, run):
    def block(index, _):
        first_query = pl.multiple_of(index * QUERY_BLOCK, QUERY_BLOCK)
        lowest, _ = key_limits(facts, first_query, cross)
        _, highest = key_limits(facts, first_query + QUERY_BLOCK - 1, cross)
        begin = lax.div(lowest, 128) * 128
        need = highest - begin
        for last, width in zip((0, *WINDOWS[cross]), WINDOWS[cross]):
            start = pl.multiple_of(jnp.minimum(begin, MLEN - width), 128)

            @pl.when((need <= width) & (need > last))
            def _(start=start, width=width):
                run(first_query, start, width)

        return 0

    lax.fori_loop(0, LEN // QUERY_BLOCK, block, 0)


def allowed_bias(facts, keep_ref, cross, first_query, start, width):
    places = first_query + lax.broadcasted_iota(jnp.int32, (1, QUERY_BLOCK), 1)
    low_end, high_end = key_limits(facts, places, cross)
    keys = start + lax.broadcasted_iota(jnp.int32, (width, QUERY_BLOCK), 0)
    if cross:
        own = start + lax.broadcasted_iota(jnp.int32, (width, 1), 0)
        keys = jnp.where(kept_keys(facts, keep_ref[pl.ds(start, width), 0:1], own), keys, -1)
    return jnp.where((keys >= low_end) & (keys < high_end), 0.0, -1e30)


def head_lanes(half):
    lane = lax.broadcasted_iota(jnp.int32, (1, 2 * HD), 1)
    return (lane < HD) if half == 0 else (lane >= HD)


def head_tile(head):
    return slice(head // 2 * 2 * HD, (head // 2 + 1) * 2 * HD)


def value_lines(head):
    return slice((head ^ 1) * HD, ((head ^ 1) + 1) * HD)


def of_head(values, half):
    return jnp.where(head_lanes(half), values, jnp.zeros_like(values))


def gather_weights(plane, w_refs, pack, first, second):
    left = head_lanes(0)
    cores, rows = 2, D // (2 * len(w_refs))
    heads = w_refs[0].shape[0] // cores
    lines = slice(pack * rows, (pack + 1) * rows)
    for distance, w_ref in enumerate(w_refs):
        for core in range(cores):
            begin = pl.multiple_of(((plane ^ distance) * cores + core) * rows, rows)
            for pair in range(heads // 2):
                even = w_ref[core * heads + 2 * pair, lines]
                odd = w_ref[core * heads + 2 * pair + 1, lines]
                at = slice(pair * 2 * HD, (pair + 1) * 2 * HD)
                first[pl.ds(begin, rows), at] = jnp.where(left, even, odd)
                second[pl.ds(begin, rows), at] = jnp.where(left, odd, even)


def scatter_grads(plane, g_refs, pack, held, values):
    first, second = held
    first[:D, :], second[:D, :] = values
    left = head_lanes(0)
    cores, rows = 2, D // (2 * len(g_refs))
    heads = g_refs[0].shape[0] // cores
    lines = slice(pack * rows, (pack + 1) * rows)
    for distance, g_ref in enumerate(g_refs):
        for core in range(cores):
            begin = pl.multiple_of(((plane ^ distance) * cores + core) * rows, rows)
            for pair in range(heads // 2):
                at = slice(pair * 2 * HD, (pair + 1) * 2 * HD)
                one, two = first[pl.ds(begin, rows), at], second[pl.ds(begin, rows), at]
                g_ref[core * heads + 2 * pair, lines] = low(jnp.where(left, one, two))
                g_ref[core * heads + 2 * pair + 1, lines] = low(jnp.where(left, two, one))


def gather_norms(plane, w_refs, norms):
    left = head_lanes(0)
    heads = w_refs[0].shape[0] // 2
    first = 2 * D // (2 * len(w_refs))
    for distance, w_ref in enumerate(w_refs):
        parts = []
        for core in (0, 1):
            parts.append(join_norms(w_ref[core * heads, first : first + 16]))
        at = pl.ds(pl.multiple_of((plane ^ distance) * 2 * HD, 2 * HD), 2 * HD)
        norms[:, at] = jnp.where(left, *parts)


def split_norms(values):
    high = low(values).astype(jnp.float32)
    middle = low(values - high).astype(jnp.float32)
    least = low(values - high - middle).astype(jnp.float32)
    return low(jnp.concatenate([jnp.where(head_lanes(0), high, middle), least], 0))


def join_norms(held):
    held = held.astype(jnp.float32)
    return (held[0:8] + pltpu.roll(held[0:8], HD, 1)) + held[8:16]


def scatter_norms(plane, g_refs, norms):
    heads = g_refs[0].shape[0] // 2
    first = D // len(g_refs)
    for distance, g_ref in enumerate(g_refs):
        at = pl.ds(pl.multiple_of((plane ^ distance) * 2 * HD, 2 * HD), 2 * HD)
        tile = norms[:, at]
        for core in (0, 1):
            values = jnp.where(head_lanes(core), tile, pltpu.roll(tile, HD, 1))
            for head in range(heads):
                g_ref[core * heads + head, first : first + 16] = split_norms(values)


class Moved:
    def __init__(self, values):
        self.values, self.shape, self.dtype = values, values.shape, values.dtype


class Arriving:
    def __init__(self, held, copies):
        self.held, self.copies = held, list(copies)

    def half(self, which):
        copy, self.copies[which] = self.copies[which], None
        if copy is not None:
            copy.wait()
        return self.held

    def get(self):
        for which in range(len(self.copies)):
            self.half(which)
        return self.held


class Leaving:
    def __init__(self, held, copies):
        self.held, self.copies, self.sent = held, list(copies), 0

    def send(self, upto=None):
        while self.sent < (len(self.copies) if upto is None else upto):
            self.copies[self.sent].start()
            self.sent += 1

    def finish(self):
        for copy in self.copies:
            copy.wait()


def half_at(core_ref, other):
    half = LEN // 2
    core = core_ref[0, 0]
    return pl.ds(pl.multiple_of((1 - core if other else core) * half, half), half)


def copies_of(kind, refs, held, core_ref, sems):
    if kind in ("one", "small"):
        pairs = [(refs[0], held)]
    elif kind == "halves":
        pairs = [(refs[0].at[at], held.at[at]) for at in HALVES]
    else:
        pairs = [(ref, held.at[half_at(core_ref, other)]) for ref, other in zip(refs, (False, True))]
    return pairs, [next(sems) for _ in pairs]


def staged_call(body, name, scalars, inputs, outputs, scratch, mega):
    in_count = sum(len(arrays) for _, arrays in inputs)
    shapes = []
    for kind, shape, dtype in outputs:
        if kind == "cores":
            shapes += [outside((shape[0] // 2, *shape[1:]), dtype)] * 2
        elif kind == "own":
            shapes += [outside((shape[0] // 2, *shape[1:]), dtype)]
        else:
            shapes += [outside(shape, dtype)]
    held_in = []
    for kind, arrays in inputs:
        rows, *others = arrays[0].shape
        rows = 2 * rows if kind == "cores" else rows
        held_in.append(pltpu.VMEM((rows, *others), arrays[0].dtype))
    held_out = [pltpu.VMEM(shape, dtype) for _, shape, dtype in outputs]
    waits = 2 * (len(inputs) + len(outputs))

    def kernel(*refs):
        refs = list(refs)

        def take(count):
            taken = refs[:count]
            del refs[:count]
            return taken

        scalar_refs, in_refs, out_refs = take(len(scalars)), take(in_count), take(len(shapes))
        in_held, out_held, (sem_ref,) = take(len(inputs)), take(len(outputs)), take(1)
        sems = (sem_ref.at[place] for place in range(waits))
        core_ref = scalar_refs[0]
        arrivals, starts = [], []
        for (kind, arrays), held in zip(inputs, in_held):
            mine, in_refs = in_refs[: len(arrays)], in_refs[len(arrays) :]
            pairs, own = copies_of(kind, mine, held, core_ref, sems)
            copies = [pltpu.make_async_copy(a, b, sem) for (a, b), sem in zip(pairs, own)]
            turn = {"small": (0,), "halves": (1, 2), "cores": (2, 2), "one": (3,)}[kind]
            starts += zip(turn, copies)
            arrivals.append(Arriving(held, copies))
        for _, copy in sorted(starts, key=lambda item: item[0]):
            copy.start()
        departures = []
        for (kind, _, _), held in zip(outputs, out_held):
            mine = out_refs[: 2 if kind == "cores" else 1]
            out_refs = out_refs[len(mine) :]
            pairs, own = copies_of("cores" if kind == "own" else kind, mine, held, core_ref, sems)
            copies = [pltpu.make_async_copy(b, a, sem) for (a, b), sem in zip(pairs, own)]
            departures.append(Leaving(held, copies))
        body(scalar_refs, arrivals, departures, refs)
        for arrival in arrivals:
            arrival.get()
        for departure in departures:
            departure.send()
        for departure in departures:
            departure.finish()

    arrays = [array for _, group in inputs for array in group]
    moved = [place for place, array in enumerate(arrays) if isinstance(array, Moved)]
    arrays = [array.values if isinstance(array, Moved) else array for array in arrays]
    arrays = [
        array if place in moved else stay_outside([array])[0] for place, array in enumerate(arrays)
    ]
    return pl.pallas_call(
        kernel,
        name=name,
        out_shape=tuple(shapes),
        in_specs=[SCALARS] * len(scalars)
        + [ANYWHERE if place in moved else OUTSIDE for place in range(in_count)],
        out_specs=(OUTSIDE,) * len(shapes),
        scratch_shapes=held_in + held_out + [pltpu.SemaphoreType.DMA((waits,))] + scratch,
        compiler_params=pltpu.CompilerParams(vmem_limit_bytes=mega * MEGA),
        cost_estimate=KERNEL_COST,
    )(*scalars, *arrays)


def forward_heads(plane, facts, keep_ref, cross, query_rows, key_rows, w_refs, outs, scratch):
    w_q, w_k, w_v, w_o, values_turned, blended_turned = scratch
    part, queries_out, keys_out, values_out, blended_out, stats_out = outs
    q_ref, k_ref, o_ref, stats_ref = (
        out.held for out in (queries_out, keys_out, blended_out, stats_out)
    )
    w_refs = [w_ref.get() for w_ref in w_refs]
    gather_weights(plane, w_refs, 0, w_q, w_v)
    gather_weights(plane, w_refs, 1, w_k, w_o)
    for out, rows, weights in (
        (queries_out, query_rows, w_q),
        (keys_out, key_rows, w_k),
        (values_out, key_rows, w_v),
    ):
        out.held[...] = low(mm(rows[...], weights[...]))
        out.send()
    values_turned[...] = values_out.held[...].T
    stats_ref[...] = jnp.zeros_like(stats_ref)
    heads = q_ref.shape[1] // HD

    def one(first_query, start, width):
        at, keys_at = pl.ds(first_query, QUERY_BLOCK), pl.ds(start, width)
        bias = allowed_bias(facts, keep_ref, cross, first_query, start, width)
        scores = []
        for head in range(heads):
            tile = head_tile(head)
            queries = of_head(q_ref[at, tile] * HD ** (-0.5), head % 2)
            scores.append(mt(k_ref[keys_at, tile], queries) + bias)
        done = []
        for head in range(heads):
            top = jnp.max(scores[head], 0, keepdims=True)
            weights = jnp.exp(scores[head] - top)
            total = jnp.sum(weights, 0, keepdims=True)
            stats_ref[head : head + 1, at] = top + jnp.log(total)
            done.append((low(weights), 1.0 / total))
        for head, (weights, share) in enumerate(done):
            lines = value_lines(head)
            blended_turned[lines, at] = low(mm(values_turned[lines, keys_at], weights) * share)

    key_windows(facts, cross, one)
    for which, at in enumerate(HALVES):
        o_ref[at, :] = blended_turned[:, at].T
        part.held[at, :] = mt(o_ref[at, :], w_o[...]).astype(PART)
        part.send(which + 1)


def self_forward_body(scalars, ins, outs, scratch):
    core_ref, facts = scalars
    tokens, *w_refs = ins
    part, norms, rows, *heads = outs
    plane = core_ref[0, 1]
    tokens = tokens.get()
    units = [standardize(tokens[at, :].astype(jnp.float32))[0] for at in HALVES]
    gather_norms(plane, [w_ref.get() for w_ref in w_refs], norms.held)
    norms.send()
    for at, unit in zip(HALVES, units):
        rows.held[at, :] = low(unit * norms.held[0:1, :] + norms.held[1:2, :])
    rows.send()
    forward_heads(
        plane, facts, None, False, rows.held, rows.held, w_refs, (part, *heads), scratch
    )


def cross_forward_body(scalars, ins, outs, scratch):
    core_ref, facts = scalars
    part_mine, part_theirs, tokens, norms, keep, memory, *w_refs = ins
    part, total, rows, *heads = outs
    tokens, norms = tokens.get(), norms.get()
    for which, at in enumerate(HALVES):
        ours = part_mine.half(which)[at, :].astype(jnp.float32)
        value = tokens[at, :].astype(jnp.float32) + (
            ours + part_theirs.half(which)[at, :].astype(jnp.float32)
        )
        total.held[at, :] = value.astype(SUM)
        total.send(which + 1)
        unit, _ = standardize(value)
        rows.held[at, :] = low(unit * norms[2:3, :] + norms[3:4, :])
    rows.send()
    keep_turned, *scratch = scratch
    keep_turned[...] = jnp.broadcast_to(keep.get()[...], (128, MLEN)).T
    forward_heads(
        core_ref[0, 1],
        facts,
        keep_turned,
        True,
        rows.held,
        memory.get(),
        w_refs,
        (part, *heads),
        scratch,
    )


def attn_forward(name, body, scalars, inputs, weights, extra, cross):
    cols = weights[0].shape[0] // 2 * HD
    bfloat16 = jnp.bfloat16
    outputs = [
        ("halves", (LEN, D), PART),
        extra,
        ("one", (LEN, D), bfloat16),
        *[("one", (LEN, cols), bfloat16)] * 4,
        ("one", (8, LEN), jnp.float32),
    ]
    scratch = [pltpu.VMEM((D, cols), bfloat16)] * 4
    scratch += [pltpu.VMEM((cols, MLEN), bfloat16), pltpu.VMEM((cols, LEN), bfloat16)]
    if cross:
        scratch = [pltpu.VMEM((MLEN, 128), jnp.int32)] + scratch
    inputs = inputs + [("one", (Moved(block),)) for block in weights]
    return staged_call(body, name, scalars, inputs, outputs, scratch, FORWARD_MEGA)


def backward_heads(plane, facts, keep_ref, cross, up_rows, w_refs, heads, scratch):
    w_q, w_k, w_v, w_o, weighted, up, keys_turned, q_turned, dq, k_sum, v_sum, dk, dv = scratch
    w_refs = [w_ref.get() for w_ref in w_refs]
    gather_weights(plane, w_refs, 0, w_q, w_v)
    gather_weights(plane, w_refs, 1, w_k, w_o)
    scale = HD ** (-0.5)
    up[...] = low(mm(up_rows[...], w_o[...]))
    q_ref, k_ref, v_ref, o_ref, stats_ref = (head.get() for head in heads)
    keys_turned[...] = k_ref[...].T
    k_sum[...] = jnp.zeros_like(k_sum)
    v_sum[...] = jnp.zeros_like(v_sum)

    products = (up[...].astype(jnp.float32) * o_ref[...].astype(jnp.float32)).T
    heads = q_ref.shape[1] // HD
    for head in range(heads):
        weighted[head : head + 1, :] = jnp.sum(products[value_lines(head), :], 0, keepdims=True)

    def one(first_query, start, width):
        at, keys_at = pl.ds(first_query, QUERY_BLOCK), pl.ds(start, width)
        bias = allowed_bias(facts, keep_ref, cross, first_query, start, width)
        ready, done, adds = [], [], []
        for head in range(heads):
            tile = head_tile(head)
            queries = of_head(q_ref[at, tile], head % 2)
            upstream = of_head(up[at, tile], 1 - head % 2)
            scores = mt(k_ref[keys_at, tile], queries * scale)
            ready.append((queries, upstream, scores, mt(v_ref[keys_at, tile], upstream)))
        for head, (_, _, scores, prob_grad) in enumerate(ready):
            probs = jnp.exp(scores + bias - stats_ref[head : head + 1, at])
            score_grad = low(probs * (prob_grad - weighted[head : head + 1, at]))
            done.append((low(probs), score_grad))
        for head, (probs, score_grad) in enumerate(done):
            queries, upstream, _, _ = ready[head]
            lines = slice(head * HD, (head + 1) * HD)
            q_turned[lines, at] = low(mm(keys_turned[lines, keys_at], score_grad) * scale)
            adds.append((mm(score_grad, queries), mm(probs, upstream)))
        for head in range(0, heads, 2):
            tile = head_tile(head)
            (key_one, value_one), (key_two, value_two) = adds[head : head + 2]
            k_sum[keys_at, tile] = k_sum[keys_at, tile] + (key_one + key_two)
            v_sum[keys_at, tile] = v_sum[keys_at, tile] + (value_one + value_two)

    key_windows(facts, cross, one)
    dq[...] = q_turned[...].T
    dk[...] = low(k_sum[...] * scale)
    dv[...] = low(v_sum[...])


def norm_step(parts, total, norms, row, upstream, finish):
    gains = jnp.zeros((1, D), jnp.float32)
    shifts = jnp.zeros((1, D), jnp.float32)
    for which, at in enumerate(HALVES):
        mine, theirs = (part.half(which)[at, :].astype(jnp.float32) for part in parts)
        back, gain, shift = norm_back(
            total.half(which)[at, :].astype(jnp.float32), mine + theirs, norms[row : row + 1, :]
        )
        gains, shifts = gains + gain, shifts + shift
        finish(which, at, upstream(which, at) + back)
    return gains, shifts


def cross_backward_body(scalars, ins, outs, scratch):
    core_ref, facts = scalars
    part_mine, part_theirs, total, cotangent, norms, keep, memory, *rest = ins
    planes = len(rest) - 6
    w_refs, (rows, *heads) = rest[:planes], rest[planes:]
    up_rows, part, memory_part, norm_out, *g_outs = outs
    turned, memory_turned, keep_turned, *scratch = scratch
    keep_turned[...] = jnp.broadcast_to(keep.get()[...], (128, MLEN)).T
    norms, cotangent = norms.get(), cotangent.get()
    plane = core_ref[0, 1]

    def finish(which, at, value):
        up_rows.held[at, :] = low(value)
        up_rows.send(which + 1)

    gains, shifts = norm_step(
        (part_mine, part_theirs),
        total,
        norms,
        4,
        lambda which, at: cotangent[at, :].astype(jnp.float32),
        finish,
    )
    norm_out.held[0:1, :] = 0.5 * gains
    norm_out.held[1:2, :] = 0.5 * shifts
    norm_out.send()
    backward_heads(plane, facts, keep_turned, True, up_rows.held, w_refs, heads, scratch)
    w_q, w_k, w_v, *_ = scratch
    dq, *held, dk, dv = scratch[-5:]
    for which, at in enumerate(HALVES):
        part.held[at, :] = mt(dq[at, :], w_q[...]).astype(PART)
        part.send(which + 1)
    memory_part.held[...] = low(mt(dk[...], w_k[...]) + mt(dv[...], w_v[...]))
    memory_part.send()
    g_refs = [out.held for out in g_outs]
    turned[...] = rows.get()[...].T
    memory_turned[...] = memory.get()[...].T
    scatter_grads(
        plane, g_refs, 0, held, (mm(turned[...], dq[...]), mm(memory_turned[...], dv[...]))
    )
    turned[...] = up_rows.held[...].T
    out_grad = mm(turned[...], heads[3].get()[...])
    scatter_grads(plane, g_refs, 1, held, (mm(memory_turned[...], dk[...]), out_grad))


def self_backward_body(scalars, ins, outs, scratch):
    core_ref, facts = scalars
    part_mine, part_theirs, total, grad, tokens, ffn_norm, norms, *rest = ins
    planes = len(rest) - 6
    w_refs, (rows, *heads) = rest[:planes], rest[planes:]
    grad_out, part, *g_outs = outs
    norm_grad, up_rows, turned, *scratch = scratch
    norms = norms.get()
    plane = core_ref[0, 1]

    def finish(which, at, value):
        grad_out.held[at, :] = value
        up_rows[at, :] = low(value)

    gains, shifts = norm_step(
        (part_mine, part_theirs),
        total,
        norms,
        2,
        lambda which, at: grad.half(which)[at, :].astype(jnp.float32),
        finish,
    )
    grad_out.send()
    norm_grad[2:3, :] = 0.5 * gains
    norm_grad[3:4, :] = 0.5 * shifts
    norm_grad[4:6, :] = ffn_norm.get()[...]
    norm_grad[6:8, :] = jnp.zeros((2, D), jnp.float32)
    backward_heads(plane, facts, None, False, up_rows, w_refs, heads, scratch)
    w_q, w_k, w_v, *_ = scratch
    dq, *held, dk, dv = scratch[-5:]
    tokens = tokens.get()
    gains = jnp.zeros((1, D), jnp.float32)
    shifts = jnp.zeros((1, D), jnp.float32)
    for at in HALVES:
        value = mt(dq[at, :], w_q[...]) + mt(dk[at, :], w_k[...]) + mt(dv[at, :], w_v[...])
        part.held[at, :] = value
        unit, _ = standardize(tokens[at, :].astype(jnp.float32))
        gains = gains + jnp.sum(value * unit, 0, keepdims=True)
        shifts = shifts + jnp.sum(value, 0, keepdims=True)
    part.send()
    norm_grad[0:1, :] = gains
    norm_grad[1:2, :] = shifts
    g_refs = [out.held for out in g_outs]
    scatter_norms(plane, g_refs, norm_grad)
    turned[...] = rows.get()[...].T
    scatter_grads(plane, g_refs, 0, held, (mm(turned[...], dq[...]), mm(turned[...], dv[...])))
    key_grad = mm(turned[...], dk[...])
    turned[...] = up_rows[...].T
    scatter_grads(plane, g_refs, 1, held, (key_grad, mm(turned[...], heads[3].get()[...])))


def attn_backward(name, body, scalars, inputs, weights, kept, outputs, cross):
    cols = weights[0].shape[0] // 2 * HD
    bfloat16 = jnp.bfloat16
    block = (weights[0].shape[0], D // len(weights) + (0 if cross else 16), 2 * HD)
    outputs = outputs + [("one", block, bfloat16)] * len(weights)
    scratch = [pltpu.VMEM((D, LEN), bfloat16)]
    if not cross:
        scratch = [pltpu.VMEM((8, D), jnp.float32), pltpu.VMEM((LEN, D), bfloat16)] + scratch
    if cross:
        scratch += [pltpu.VMEM((D, MLEN), bfloat16), pltpu.VMEM((MLEN, 128), jnp.int32)]
    scratch += [pltpu.VMEM((D, cols), bfloat16)] * 4 + [
        pltpu.VMEM((8, LEN), jnp.float32),
        pltpu.VMEM((LEN, cols), bfloat16),
        pltpu.VMEM((cols, MLEN), bfloat16),
        pltpu.VMEM((cols, LEN), bfloat16),
        pltpu.VMEM((LEN, cols), bfloat16),
        pltpu.VMEM((MLEN, cols), jnp.float32),
        pltpu.VMEM((MLEN, cols), jnp.float32),
        pltpu.VMEM((MLEN, cols), bfloat16),
        pltpu.VMEM((MLEN, cols), bfloat16),
    ]
    inputs = inputs + [("one", (array,)) for array in (*map(Moved, weights), *kept)]
    return staged_call(body, name, scalars, inputs, outputs, scratch, BACKWARD_MEGA)


def add_to(ref, step, update):
    @pl.when(step == 0)
    def _():
        ref[...] = update

    @pl.when(step != 0)
    def _():
        ref[...] = ref[...] + update


def gelu_pieces(values):
    factor = 0.7978845608028654
    square = values * values
    slope = jnp.tanh(factor * values * (1.0 + 0.044715 * square))
    half = 0.5 * (1.0 + slope)
    grad = half + 0.5 * values * (1.0 - slope * slope) * factor * (1.0 + 3 * 0.044715 * square)
    return values * half, grad


def expert_kernel(
    core_ref,
    mine,
    theirs,
    part_mine,
    part_theirs,
    first_sum,
    norms,
    w_ref,
    sum_out,
    grad_out,
    out_keep,
    out_give,
    w_grad_ref,
    ours,
    others,
    sum_ref,
    exact,
    rows,
    up,
    grad_ref,
    out_total,
    grad_low,
    sems,
    out_sems,
):
    step = pl.program_id(0)

    def leaving(place):
        held, target = (
            (sum_ref, sum_out),
            (grad_low, grad_out),
            (out_total.at[half_at(core_ref, False)], out_keep),
            (out_total.at[half_at(core_ref, True)], out_give),
        )[place]
        return pltpu.make_async_copy(held, target, out_sems.at[place])

    @pl.when(step == 0)
    def _():
        up_copies = [
            pltpu.make_async_copy(a, up.at[half_at(core_ref, other)], sems.at[place])
            for place, (a, other) in enumerate(((mine, False), (theirs, True)))
        ]
        copies = [
            pltpu.make_async_copy(a.at[at], b.at[at], sems.at[2 + 3 * which + place])
            for which, at in enumerate(HALVES)
            for place, (a, b) in enumerate(
                ((part_mine, ours), (part_theirs, others), (first_sum, sum_ref))
            )
        ]
        for copy in copies[:3] + up_copies + copies[3:]:
            copy.start()
        for which, at in enumerate(HALVES):
            for copy in copies[3 * which : 3 * which + 3]:
                copy.wait()
            total = sum_ref[at, :].astype(jnp.float32) + (
                ours[at, :].astype(jnp.float32) + others[at, :].astype(jnp.float32)
            )
            exact[at, :] = total
            sum_ref[at, :] = total.astype(SUM)
            unit, _ = standardize(total)
            rows[at, :] = low(unit * norms[4:5, :] + norms[5:6, :])
        leaving(0).start()
        for copy in up_copies:
            copy.wait()

    shape = (D, w_ref.shape[4])
    w_in, w_out = w_ref[:, 0, 0].reshape(shape), w_ref[:, 0, 1].reshape(shape)
    back = mm(up[...], w_out)
    hidden, slope = gelu_pieces(mm(rows[...], w_in))
    hidden = low(hidden)
    inner_grad = low(slope * back)
    add_to(grad_ref, step, mt(inner_grad, w_in))
    add_to(out_total, step, mt(hidden, w_out))

    @pl.when(step == pl.num_programs(0) - 1)
    def _():
        grad_low[...] = grad_ref[...].astype(PART)
        at = half_at(core_ref, False)
        out_total[at, :] = out_total[at, :] + exact[at, :]
        for place in (1, 2, 3):
            leaving(place).start()

    grads = w_grad_ref.shape[0], -1, w_ref.shape[4]
    w_grad_ref[:, 0, 0] = low(tm(rows[...], inner_grad)).reshape(grads)
    w_grad_ref[:, 0, 1] = low(tm(up[...], hidden)).reshape(grads)

    @pl.when(step == pl.num_programs(0) - 1)
    def _():
        for place in range(4):
            leaving(place).wait()


def expert_layer(core_ref, rows, parts, first_sum, norms, weights):
    owners, steps, _, line_count, cols = weights.shape
    half = outside((LEN // 2, D), jnp.float32)
    w_spec = pl.BlockSpec((owners, 1, 2, line_count, cols), lambda step: (0, step, 0, 0, 0))
    low_rows = pltpu.VMEM((LEN, D), jnp.bfloat16)
    wide = pltpu.VMEM((LEN, D), jnp.float32)
    return pl.pallas_call(
        expert_kernel,
        name="expert",
        grid=(steps,),
        out_shape=(
            outside((LEN, D), SUM),
            outside((LEN, D), PART),
            half,
            half,
            outside(weights.shape, jnp.bfloat16),
        ),
        in_specs=[SCALARS, OUTSIDE, ANYWHERE, OUTSIDE, OUTSIDE, OUTSIDE, WHOLE, w_spec],
        out_specs=(OUTSIDE,) * 4 + (w_spec,),
        scratch_shapes=[pltpu.VMEM((LEN, D), PART)] * 2
        + [pltpu.VMEM((LEN, D), SUM), wide, low_rows, low_rows]
        + [wide, wide, pltpu.VMEM((LEN, D), PART)]
        + [pltpu.SemaphoreType.DMA((8,)), pltpu.SemaphoreType.DMA((4,))],
        compiler_params=pltpu.CompilerParams(vmem_limit_bytes=EXPERT_MEGA * MEGA),
        cost_estimate=KERNEL_COST,
    )(
        core_ref,
        *stay_outside(rows[:1]),
        rows[1],
        *stay_outside(parts),
        *stay_outside((first_sum, norms, weights)),
    )


def pack_attn_kernel(places, weights, norms, out_ref):
    odd = places[0, 0] == 1
    left = head_lanes(0)
    rows = weights.shape[2]
    count = norms.shape[0]
    values = jnp.concatenate(
        [norms[...], jnp.zeros((8 - count, norms.shape[1]), jnp.float32)], 0
    )
    facts = split_norms(jnp.concatenate([values, values], 1))
    blocks = out_ref.shape[0] // 2
    for core in (0, 1):
        for branch in range(weights.shape[0]):
            for pack in (0, 1):
                first, second = weights[branch, pack], weights[branch, 2 + pack]
                one = jnp.where(odd, second, first)
                two = jnp.where(odd, first, second)
                if core == 0:
                    tile = jnp.where(left, one, pltpu.roll(two, HD, 1))
                else:
                    tile = jnp.where(left, pltpu.roll(one, HD, 1), two)
                begin = pack * rows + branch * (2 * rows + 16)
                for block in range(blocks):
                    out_ref[core * blocks + block, begin : begin + rows] = low(tile)
        for block in range(blocks):
            out_ref[core * blocks + block, 2 * rows : 2 * rows + 16] = facts


def pack_attn(odd, weights, norms, tensor_count):
    shape = (2 * tensor_count, 4 * weights.shape[2] + 16, 2 * HD)
    return pl.pallas_call(
        pack_attn_kernel,
        name="pack_attn",
        out_shape=outside(shape, jnp.bfloat16),
        in_specs=[SCALARS, WHOLE, WHOLE],
        out_specs=WHOLE,
        compiler_params=pltpu.CompilerParams(vmem_limit_bytes=16 * MEGA),
        cost_estimate=KERNEL_COST,
    )(odd, *stay_outside((weights, norms)))


def pack_experts_kernel(chosen, weights, out_ref, held, sems):
    places, half = out_ref.shape[2], out_ref.shape[5]
    copies = [
        pltpu.make_async_copy(weights.at[chosen[0, row]], held.at[row], sems.at[row])
        for row in range(held.shape[0])
    ]
    for copy in copies:
        copy.start()
    for row, copy in enumerate(copies):
        copy.wait()
        for core in (0, 1):
            at = slice(core * half, (core + 1) * half)
            out_ref[row // places, core, row % places] = low(held[row, :, :, at])


def pack_experts(chip_expert, weights, plane_count, tensor_count):
    _, pair, rows, cols = weights.shape
    count = plane_count * tensor_count
    out = outside((plane_count, 2, tensor_count, pair, rows, cols // 2), jnp.bfloat16)
    return pl.pallas_call(
        pack_experts_kernel,
        name="pack_experts",
        out_shape=out,
        in_specs=[SCALARS, OUTSIDE],
        out_specs=WHOLE,
        scratch_shapes=[
            pltpu.VMEM((count, pair, rows, cols), jnp.float32),
            pltpu.SemaphoreType.DMA((count,)),
        ],
        compiler_params=pltpu.CompilerParams(vmem_limit_bytes=16 * MEGA),
        cost_estimate=KERNEL_COST,
    )(chip_expert, *stay_outside((weights,)))


def sum_planes_kernel(*refs):
    *parts, out_ref = refs
    count = len(parts) // 2
    rows = parts[count].shape[1]

    def total(blocks, index, lines):
        return sum(block[index, lines].astype(jnp.float32) for block in blocks)

    for index in range(out_ref.shape[0]):
        out_ref[index, :rows] = low(total(parts[:count], index, slice(0, rows)))
        norms = sum(join_norms(block[index, rows : rows + 16]) for block in parts[:count])
        out_ref[index, rows : rows + 16] = split_norms(norms)
        out_ref[index, rows + 16 :] = low(total(parts[count:], index, slice(0, rows)))


def sum_planes(self_parts, cross_parts):
    blocks, rows, cols = self_parts[0].shape
    shape = (blocks, rows + cross_parts[0].shape[1], cols)
    return pl.pallas_call(
        sum_planes_kernel,
        name="sum_planes",
        out_shape=outside(shape, jnp.bfloat16),
        in_specs=[WHOLE] * (len(self_parts) + len(cross_parts)),
        out_specs=WHOLE,
        compiler_params=pltpu.CompilerParams(vmem_limit_bytes=16 * MEGA),
        cost_estimate=KERNEL_COST,
    )(*self_parts, *cross_parts)


def lamb_update(weight, moment, second, grad):
    moment = beta_one * moment + (1.0 - beta_one) * grad
    second = beta_two * second + (1.0 - beta_two) * grad * grad
    update = (
        moment / (1.0 - beta_one**STEP) / (jnp.sqrt(second / (1.0 - beta_two**STEP)) + epsilon)
        + decay * weight
    )
    return moment, second, update


def expert_lamb_kernel(
    chosen, grads, w_ref, m_ref, v_ref, m_out, v_out, u_out, squares, total
):
    step = pl.program_id(0)
    half = grads.shape[5]
    group = w_ref.shape[0]

    @pl.when(step == 0)
    def _():
        total[...] = jnp.zeros_like(total)
        for plane in range(grads.shape[0]):
            for place in range(grads.shape[2]):
                expert = chosen[plane * grads.shape[2] + place]
                for core in (0, 1):
                    at = slice(core * half, (core + 1) * half)
                    total[expert, :, :, at] = total[expert, :, :, at] + grads[
                        plane, core, place
                    ].astype(jnp.float32)

    for own in range(group):
        expert = step * group + own
        weight = w_ref[own]
        m_out[own], v_out[own], update = lamb_update(weight, m_ref[own], v_ref[own], total[expert])
        u_out[own] = low(update)
        squares[own] = jnp.concatenate(
            [jnp.sum(weight * weight, 1), jnp.sum(update * update, 1)], 0
        )


def expert_lamb(chip_expert, grads, weights, moments, seconds):
    experts, pair, rows, cols = weights.shape
    group = 4
    spec = pl.BlockSpec((group, pair, rows, cols), lambda step, chosen: (step, 0, 0, 0))
    return pl.pallas_call(
        expert_lamb_kernel,
        name="expert_lamb",
        out_shape=(outside(weights.shape, jnp.float32),) * 2
        + (outside(weights.shape, jnp.bfloat16),)
        + (jax.ShapeDtypeStruct((experts, 2 * pair, cols), jnp.float32),),
        grid_spec=pltpu.PrefetchScalarGridSpec(
            num_scalar_prefetch=1,
            grid=(experts // group,),
            in_specs=[WHOLE, spec, spec, spec],
            out_specs=(spec, spec, spec)
            + (pl.BlockSpec((group, 2 * pair, cols), lambda step, chosen: (step, 0, 0)),),
            scratch_shapes=[pltpu.VMEM(weights.shape, jnp.float32)],
        ),
        compiler_params=pltpu.CompilerParams(vmem_limit_bytes=24 * MEGA),
        cost_estimate=KERNEL_COST,
    )(chip_expert, *stay_outside((grads, weights, moments, seconds)))


def owner_lamb_kernel(odd, chips, *refs):
    w_ref, m_ref, v_ref, norms, norm_m, norm_v, expert_squares, *outs = refs
    m_out, v_out, u_out, norm_m_out, norm_v_out, norm_u_out, squares, sums = outs
    experts = expert_squares.shape[0]
    matrices = w_ref.shape[0] * w_ref.shape[1]
    kinds = matrices + 2 * experts + norms.shape[0]
    sums[...] = jnp.zeros_like(sums)
    heads = chips.shape[0] // 2
    left = head_lanes(0)
    rows = w_ref.shape[2]
    for branch in range(w_ref.shape[0]):
        for pack in (0, 1):
            begin = pack * rows + branch * (2 * rows + 16)
            totals = []
            for core in (0, 1):
                totals.append(
                    sum(
                        chips[core * heads + head, begin : begin + rows].astype(jnp.float32)
                        for head in range(heads)
                    )
                )
            first = jnp.where(left, totals[0], pltpu.roll(totals[1], HD, 1))
            second = jnp.where(left, pltpu.roll(totals[0], HD, 1), totals[1])
            swapped = odd[0, 0] == 1
            for kind, grad in (
                (0, jnp.where(swapped, second, first)),
                (1, jnp.where(swapped, first, second)),
            ):
                matrix = 2 * kind + pack
                weight = w_ref[branch, matrix]
                m_out[branch, matrix], v_out[branch, matrix], update = lamb_update(
                    weight, m_ref[branch, matrix], v_ref[branch, matrix], grad
                )
                u_out[branch, matrix] = update
                line = branch * w_ref.shape[1] + matrix
                sums[line : line + 1, :] = jnp.sum(weight * weight, 0, keepdims=True)
                line += kinds
                sums[line : line + 1, :] = jnp.sum(update * update, 0, keepdims=True)
    grad = sum(join_norms(chips[index, 2 * rows : 2 * rows + 16]) for index in range(2 * heads))
    count, cols = norms.shape
    norm_m_out[...], norm_v_out[...], update = lamb_update(
        norms[...], norm_m[...], norm_v[...], grad[:count, :cols]
    )
    norm_u_out[...] = update
    share = 1.0 / heads
    first = matrices + 2 * experts
    sums[first:kinds, :cols] = norms[...] * norms[...] * share
    sums[kinds + first : 2 * kinds, :cols] = update * update * share
    for expert in range(experts):
        held = expert_squares[expert]
        held = sum(held[:, at : at + 2 * HD] for at in range(0, held.shape[1], 2 * HD))
        line = matrices + 2 * expert
        sums[line : line + 2, :] = held[0:2]
        sums[kinds + line : kinds + line + 2, :] = held[2:4]
    total = jnp.sum(sums[...].T, 0, keepdims=True)
    squares[...] = jnp.broadcast_to(total, squares.shape)


def owner_lamb(odd, chips, attn, norm, expert_squares, devices):
    matrices, norms = attn[0].shape, norm[0].shape
    return pl.pallas_call(
        owner_lamb_kernel,
        name="owner_lamb",
        out_shape=(outside(matrices, jnp.float32),) * 3
        + (jax.ShapeDtypeStruct(norms, jnp.float32),) * 3
        + (jax.ShapeDtypeStruct((devices, 2 * HD), jnp.float32),),
        in_specs=[SCALARS] + [WHOLE] * 8,
        out_specs=(WHOLE,) * 7,
        scratch_shapes=[pltpu.VMEM((2 * HD, 2 * HD), jnp.float32)],
        compiler_params=pltpu.CompilerParams(vmem_limit_bytes=16 * MEGA),
        cost_estimate=KERNEL_COST,
    )(odd, *stay_outside((chips, *attn, *norm)), expert_squares)


def final_step_kernel(sizes, moves, w_ref, u_ref, attn, attn_u, norms, norm_u, *rest):
    count = (len(rest) - 4) // 3
    sources, (out_ref, attn_out, norm_out) = rest[: 2 * count], rest[2 * count : 2 * count + 3]
    settled, sems = rest[2 * count + 3 : -1], rest[-1]
    step = pl.program_id(0)

    def settle(source, place):
        return pltpu.make_async_copy(source, settled[place], sems.at[place])

    for place in range(count):
        for source, moved in zip(sources[2 * place : 2 * place + 2], (0, 1)):

            @pl.when((step == 0) & (moves[0, 0] == moved))
            def _(source=source, place=place):
                settle(source, place).start()

    @pl.when(step == pl.num_programs(0) - 1)
    def _():
        for place in range(count):
            settle(sources[2 * place], place).wait()

    group, pair = out_ref.shape[:2]
    attn_count = attn.shape[0] * attn.shape[1]
    for own in range(group):
        for kind in range(pair):
            size = sizes[0, attn_count + (step * group + own) * pair + kind]
            out_ref[own, kind] = w_ref[own, kind] - size * u_ref[own, kind].astype(jnp.float32)

    @pl.when(step == 0)
    def _():
        for branch in range(attn.shape[0]):
            for matrix in range(attn.shape[1]):
                size = sizes[0, branch * attn.shape[1] + matrix]
                attn_out[branch, matrix] = attn[branch, matrix] - size * attn_u[branch, matrix]
        first = sizes.shape[1] - norms.shape[0]
        for row in range(norms.shape[0]):
            at = slice(row, row + 1)
            norm_out[at, :] = norms[at, :] - sizes[0, first + row] * norm_u[at, :]


def final_step(sizes, moves, weights, updates, attn, norm, landed):
    experts, pair, rows, cols = weights.shape
    group = 4
    spec = pl.BlockSpec((group, pair, rows, cols), lambda step: (step, 0, 0, 0))
    return pl.pallas_call(
        final_step_kernel,
        name="final_step",
        grid=(experts // group,),
        out_shape=(
            outside(weights.shape, jnp.float32),
            outside(attn[0].shape, jnp.float32),
            jax.ShapeDtypeStruct(norm[0].shape, jnp.float32),
        )
        + tuple(outside(array.shape, array.dtype) for array in landed[::2]),
        in_specs=[SCALARS, SCALARS, spec, spec] + [WHOLE] * 4 + [ANYWHERE] * len(landed),
        out_specs=(spec, WHOLE, WHOLE) + (OUTSIDE,) * (len(landed) // 2),
        scratch_shapes=[pltpu.SemaphoreType.DMA((len(landed) // 2,))],
        compiler_params=pltpu.CompilerParams(vmem_limit_bytes=24 * MEGA),
        cost_estimate=KERNEL_COST,
    )(sizes, moves, *stay_outside((weights, updates, *attn, *norm)), *landed)


DEVICES = ("plane", "core", "tensor")
CHIP = ("core", "tensor")


def twin(values):
    return lax.ppermute(values, "core", ((0, 1), (1, 0)))


def exchange(values, axes):
    return lax.all_to_all(values, axes, 0, 0, tiled=True)


def swap_pairs(plane_count, tensor_count):
    pairs = []
    for plane in range(plane_count):
        for core in range(2):
            for place in range(tensor_count):
                target = (plane * 2 + place % 2) * tensor_count + place // 2 * 2 + core
                here = (plane * 2 + core) * tensor_count + place
                if target != here:
                    pairs.append((here, target))
    return pairs


def other_planes(blocks):
    planes = range(lax.axis_size("plane"))
    got = list(blocks)
    for distance in reversed(planes[1:]):
        got[distance] = lax.ppermute(
            blocks[distance], "plane", [(k, k ^ distance) for k in planes]
        )
    return got


def sum_devices(values, axes):
    for axis in axes:
        count, flip = lax.axis_size(axis), 1
        while flip < count:
            values = values + lax.ppermute(values, axis, [(k, k ^ flip) for k in range(count)])
            flip *= 2
    return values


def body_rows(
    tokens,
    memory,
    cotangent,
    tgt_lengths,
    mem_lengths,
    mem_keep,
    row_expert,
    attn_weights,
    attn_moment,
    attn_second,
    expert_weights,
    expert_moment,
    expert_second,
    norm_params,
    norm_moment,
    norm_second,
):
    plane_count, tensor_count = lax.axis_size("plane"), lax.axis_size("tensor")
    devices = plane_count * 2 * tensor_count
    core, place = lax.axis_index("core"), lax.axis_index("tensor")
    moves = swap_pairs(plane_count, tensor_count)

    moving = core != place % 2

    def swap(values):
        return lax.ppermute(values, DEVICES, moves)

    def own_row(values):
        return jnp.where(moving, swap(values), values)

    plane = lax.axis_index("plane")
    core_ref = jnp.stack([core, plane]).reshape(1, 2)
    odd = (place % 2).reshape(1, 1)
    packed = pack_attn(odd, attn_weights, norm_params, tensor_count)
    tokens_mine = own_row(tokens)
    owned = jnp.arange(plane_count * 2)[:, None] == plane * 2 + core
    owner_expert = sum_devices(jnp.where(owned, row_expert[None], 0), ("core", "plane"))
    chip_expert = owner_expert.reshape(plane_count, 2, 2).transpose(0, 2, 1).reshape(1, -1)
    facts = jnp.concatenate([tgt_lengths, mem_lengths, mem_keep], 1)
    facts = jnp.where(core == place % 2, facts, twin(facts))
    facts = lax.dynamic_slice_in_dim(facts, place // 2, 1, 0)
    facts, keep = facts[:, :16], facts[:, 16:]
    chips = exchange(packed, CHIP)
    tokens_theirs = twin(tokens_mine)
    chips, tokens_mine, tokens_theirs, memory, cotangent, chip_expert = lax.optimization_barrier(
        (chips, tokens_mine, tokens_theirs, memory, cotangent, chip_expert)
    )
    self_lines = 2 * attn_weights.shape[2] + 16
    self_weights = other_planes([chips[:, :self_lines]] * plane_count)
    memory_mine = own_row(memory)
    up_mine = own_row(cotangent)
    cross_weights = other_planes([chips[:, self_lines:]] * plane_count)
    chosen = pack_experts(chip_expert, expert_weights, plane_count, tensor_count)
    memory_mine, up_mine, chosen, *self_weights = lax.optimization_barrier(
        (memory_mine, up_mine, chosen, *self_weights)
    )
    hidden_cols = expert_weights.shape[3] // 2
    chosen = exchange(chosen.reshape(devices, 2, -1, hidden_cols), DEVICES)
    chosen = chosen.reshape(plane_count * 2, tensor_count, 2, -1, hidden_cols)
    tokens_row = ("cores", (tokens_mine, Moved(tokens_theirs)))

    def halves(*arrays):
        return [("halves", (array,)) for array in arrays]

    self_part, norms, *self_kept = attn_forward(
        "self_forward",
        self_forward_body,
        (core_ref, facts),
        [tokens_row],
        self_weights,
        ("one", (8, D), jnp.float32),
        False,
    )
    self_theirs = twin(self_part)
    memory_mine, up_mine, self_theirs, *cross_weights = lax.optimization_barrier(
        (memory_mine, up_mine, self_theirs, *cross_weights)
    )
    memory_row = ("cores", (memory_mine, Moved(twin(memory_mine))))
    up_theirs = twin(up_mine)
    up_row = ("cores", (up_mine, Moved(up_theirs)))
    norms_in, keep_in = ("small", (norms,)), ("small", (keep,))
    cross_part, first_sum, *cross_kept = attn_forward(
        "cross_forward",
        cross_forward_body,
        (core_ref, facts),
        [*halves(self_part, Moved(self_theirs)), tokens_row, norms_in, keep_in, memory_row],
        cross_weights,
        ("halves", (LEN, D), SUM),
        True,
    )
    second_sum, ffn_part, out_keep, out_give, row_grad = expert_layer(
        core_ref,
        (up_mine, up_theirs),
        (cross_part, twin(cross_part)),
        first_sum,
        norms,
        chosen,
    )
    layer_low = low(out_keep + twin(out_give))
    layer_out = swap(layer_low)
    row_grad = exchange(row_grad.reshape(devices, 2, -1, hidden_cols), DEVICES)
    row_grad = row_grad.reshape(plane_count, 2, tensor_count, 2, -1, hidden_cols)
    grad_cross, cross_part, memory_keep, memory_give, ffn_norm, *cross_grad = attn_backward(
        "cross_backward",
        cross_backward_body,
        (core_ref, facts),
        [*halves(ffn_part, Moved(twin(ffn_part)), second_sum), up_row, norms_in, keep_in, memory_row],
        cross_weights,
        cross_kept,
        [
            ("halves", (LEN, D), SUM),
            ("halves", (LEN, D), PART),
            ("cores", (LEN, D), jnp.bfloat16),
            ("one", (2, D), jnp.float32),
        ],
        True,
    )
    cross_grad = other_planes(cross_grad)
    own_grad, part_keep, part_give, *self_grad = attn_backward(
        "self_backward",
        self_backward_body,
        (core_ref, facts),
        [
            *halves(cross_part, Moved(twin(cross_part)), first_sum, grad_cross),
            tokens_row,
            ("small", (ffn_norm,)),
            norms_in,
        ],
        self_weights,
        self_kept,
        [("own", (LEN, D), jnp.float32), ("cores", (LEN, D), jnp.float32)],
        False,
    )
    self_grad, memory_give, cross_grad = lax.optimization_barrier(
        (self_grad, memory_give, cross_grad)
    )
    memory_low = low(memory_keep.astype(jnp.float32) + twin(memory_give).astype(jnp.float32))
    memory_grad = swap(memory_low)
    planes = other_planes(self_grad)
    back, _, _ = norm_back(
        tokens_mine.astype(jnp.float32), part_keep + twin(part_give), norms[0:1]
    )
    input_low = low(own_grad + back)
    input_grad = swap(input_low)
    input_grad, layer_out, memory_grad, *planes = lax.optimization_barrier(
        (input_grad, layer_out, memory_grad, *planes)
    )
    chips = sum_planes(planes, cross_grad)
    row_grad, chips = lax.optimization_barrier((row_grad, chips))
    chips = exchange(chips, CHIP)
    expert_moment_new, expert_second_new, expert_update, expert_squares = expert_lamb(
        chip_expert.reshape(-1), row_grad, expert_weights, expert_moment, expert_second
    )
    attn_moment_new, attn_second_new, attn_update, *norm_outs, squares = owner_lamb(
        odd,
        chips,
        (attn_weights, attn_moment, attn_second),
        (norm_params, norm_moment, norm_second),
        expert_squares,
        devices,
    )
    norm_moment_new, norm_second_new, norm_update = norm_outs
    count = 8 + 2 * E + 6
    squares = exchange(squares, DEVICES).sum(0)[: 2 * count]
    lamb_norms = jnp.sqrt(squares).reshape(2, count)
    sizes = (rate * (lamb_norms[0] / lamb_norms[1])).reshape(1, -1)
    expert_new, attn_new, norm_new, layer_out, memory_grad, input_grad = final_step(
        sizes,
        moving.astype(jnp.int32).reshape(1, 1),
        expert_weights,
        expert_update,
        (attn_weights, attn_update),
        (norm_params, norm_update),
        (layer_low, layer_out, memory_low, memory_grad, input_low, input_grad),
    )
    return (
        layer_out,
        input_grad,
        memory_grad,
        attn_new,
        attn_moment_new,
        attn_second_new,
        expert_new,
        expert_moment_new,
        expert_second_new,
        norm_new,
        norm_moment_new,
        norm_second_new,
        lamb_norms,
    )


def specs(rows, dp):
    tokens = P((*dp, "tensor"), None)
    matrix = P(None, None, dp, "tensor")
    row_items = (P(dp, None),) * 3 + (P(dp),)
    return dict(
        in_specs=(tokens,) * 3 + row_items + (matrix,) * 6 + (P(None, dp),) * 3,
        out_specs=(tokens,) * 3 + (matrix,) * 6 + (P(None, dp),) * 3 + (P(),),
        check_vma=False,
    )


def solution(mesh):
    def run(*args):
        rows = args[3].shape[0]
        dp_count, tensor_count = mesh.shape["dp"], mesh.shape["tensor"]
        if rows // dp_count * 2 == tensor_count and tensor_count % 2 == 0:
            fine = Mesh(
                mesh.devices.reshape(dp_count // 2, 2, tensor_count), ("plane", "core", "tensor")
            )
            return jax.shard_map(body_rows, mesh=fine, **specs(rows, ("plane", "core")))(*args)
        return jax.shard_map(body, mesh=mesh, **specs(rows, ("dp",)))(*args)

    return run
```
